128 devices in a mesh: seq: 16 (over x, y), mp: 8 (over z, core).
Axes of the slice: x: 4, y: 4, z: 4, core: 2. Of those that a mesh axis runs over, the one named last changes fastest.
Arguments:
- tokens: bfloat16 [16, 16, 64, 1024], P('seq'), may hold values from -25 to 25
- proj_main: bfloat16 [1024, 2, 2048], P('seq', None, 'mp'), may hold values from -0.1875 to 0.1875
- proj_shared: bfloat16 [1024, 2, 128], P('seq'), may hold values from -0.0078125 to 0.0078125
- proj_step: bfloat16 [1024, 32], P('seq', 'mp'), may hold values from -0.1875 to 0.1875
- step_bias: float32 [32], P('mp'), may hold values from -1.5 to 0.5
- decay_rate: float32 [2, 32], P(None, 'mp'), as said below
- skip_gain: float32 [32], P('mp'), may hold values from -1 to 2
- cotangent: bfloat16 [16, 16, 64, 2048], P('seq', None, None, 'mp'), may hold values from -6 to 6
Outputs:
- gated: bfloat16 [16, 16, 64, 2048], P('seq', None, None, 'mp')
- input_grad: bfloat16 [16, 16, 64, 1024], P('seq', None, None, 'mp')
- grad_main: float32 [1024, 2, 2048], P('seq', None, 'mp')
- grad_shared: float32 [1024, 2, 128], P('seq')
- grad_step: float32 [1024, 32], P('seq', 'mp')
The draws below stay inside these ranges and needn't reach their ends.
Inputs may be any that keep to these rules, and one draw needn't show every extreme that they name: `decay_rate`: positive decay rates.
All inputs are finite; a program needn't handle non-finite values.
Results may differ from the reference program's by a relative error of at most 0.023.
Values may be sent and summed in bfloat16 or wider, within the bound.
A program may use at most 256 MiB of HBM per device.

```python
import math
import jax
import jax.numpy as jnp
from jax import lax

D = 1024
INNER = 2048
HEADS = 32
STATE = 128
HEADDIM = 64
BLOCK = 256
WID = 64
FRAMES = 16
HGT = 16
TOKENS = 16384


def draw_tokens(key, part):
    key = jax.random.fold_in(key, 11)
    base_key, frame_key, row_key = jax.random.split(key, 3)
    shape = (FRAMES, HGT, WID, D)
    base = jnp.clip(jax.random.normal(base_key, shape, jnp.float32), -6.0, 6.0)
    frame_scale = jnp.exp(jax.random.uniform(frame_key, (FRAMES, 1, 1, 1), jnp.float32, -0.7, 0.7))
    row_scale = jnp.exp(jax.random.uniform(row_key, (1, HGT, 1, 1), jnp.float32, -0.7, 0.7))
    return (base * frame_scale * row_scale).astype(jnp.bfloat16)


def draw_decay_rate(key, part):
    key = jax.random.fold_in(key, 7)
    pick_key, slow_key, fast_key = jax.random.split(key, 3)
    choose = jax.random.uniform(pick_key, (2, HEADS), jnp.float32)
    slow = jax.random.uniform(slow_key, (2, HEADS), jnp.float32, 0.8, 2.0) / TOKENS
    fast = jnp.exp(jax.random.uniform(fast_key, (2, HEADS), jnp.float32, math.log(0.003), math.log(0.06)))
    share = 0.5
    return jnp.where(choose < share, slow, fast).astype(jnp.float32)


def shard_levels(key, extent, cuts, least, high):
    level = 1.0
    for axis_at, shards_of in cuts:
        heights = jax.random.uniform(jax.random.fold_in(jax.random.fold_in(key, 6), axis_at), (shards_of,), jnp.float32, least / len(cuts), high / len(cuts))
        level = level * jnp.repeat(jnp.exp(heights), extent[axis_at] // shards_of).reshape((-1,) + (1,) * (len(extent) - 1 - axis_at))
    return level


def normal_values(own_key, shape, scale, bound, cuts=(), dtype=jnp.bfloat16):
    level = shard_levels(own_key, shape, cuts, -0.22, 0.18) if cuts else 1.0
    result = jax.random.normal(own_key, shape, jnp.float32) * scale * level
    return jnp.minimum(jnp.maximum(result, -bound), bound).astype(dtype)


def setup_inputs(seed: int = 0) -> dict:
    keys = jax.random.split(jax.random.key(seed), 9)
    return {
        "tokens": draw_tokens(jax.random.fold_in(keys[8], 71), 0),
        "proj_main": normal_values(keys[1], (D, 2, INNER), D ** -0.5, 0.1875, ((0, 16), (2, 8))),
        "proj_shared": normal_values(keys[2], (D, 2, STATE), (D * STATE * 4) ** -0.5, 0.0078125, ((0, 16),)),
        "proj_step": normal_values(keys[3], (D, HEADS), D ** -0.5, 0.1875, ((0, 16), (1, 8))),
        "step_bias": jnp.clip(-1.5 + 2.0 * jax.random.uniform(keys[4], (HEADS,), jnp.float32) ** shard_levels(keys[4], (HEADS,), ((0, 8),), -0.2, 0.2), -1.5, 0.5),
        "decay_rate": draw_decay_rate(jax.random.fold_in(keys[8], 71), 0),
        "skip_gain": jnp.clip(-1.0 + 3.0 * jax.random.uniform(keys[6], (HEADS,), jnp.float32) ** shard_levels(keys[6], (HEADS,), ((0, 8),), -0.2, 0.2), -1.0, 2.0),
        "cotangent": normal_values(keys[7], (FRAMES, HGT, WID, INNER), 1.0, 6.0, ((0, 16), (3, 8))),
    }


HIGH = lax.Precision.HIGHEST

def scan_blocks(x_float, b_float, c_float, step_size, rate, block):
    count, heads, head_width = x_float.shape
    state_dim = b_float.shape[1]
    blocks = count // block
    log_decay = -step_size * rate[None, :]
    pieces = (x_float.reshape(blocks, block, heads, head_width), b_float.reshape(blocks, block, state_dim), c_float.reshape(blocks, block, state_dim), log_decay.reshape(blocks, block, heads), step_size.reshape(blocks, block, heads))
    lower = jnp.arange(block)[:, None] >= jnp.arange(block)[None, :]

    def advance(carry, piece):
        state, offset = carry
        x_block, b_block, c_block, log_block, step_block = piece
        running = jnp.cumsum(log_block, axis=0)
        scaled = x_block * step_block[:, :, None]
        spread = running.T[:, :, None] - running.T[:, None, :]
        decay = jnp.where(lower[None], jnp.exp(jnp.where(lower[None], spread, 0.0)), 0.0)
        scores = jnp.dot(c_block, b_block.T, precision=HIGH)
        inside = jnp.einsum('hij,jhp->ihp', decay * scores[None], scaled, precision=HIGH)
        entry = jnp.exp(running)[:, :, None] * jnp.einsum('in,hpn->ihp', c_block, state, precision=HIGH)
        final = running[-1]
        tail = jnp.exp(final[None, :] - running)
        fresh = jnp.einsum('jhp,jn->hpn', scaled * tail[:, :, None], b_block, precision=HIGH)
        state = jnp.exp(final)[:, None, None] * state + fresh
        return ((state, offset + final), (inside + entry, offset[None, :] + running))
    init = (jnp.zeros((heads, head_width, state_dim), jnp.float32), jnp.zeros((heads,), jnp.float32))
    carried, stacked = lax.scan(jax.checkpoint(advance), init, pieces)
    return stacked[0].reshape(count, heads, head_width)

def rows_order(array):
    return array.reshape(FRAMES, HGT, WID, -1).transpose(1, 2, 0, 3).reshape(TOKENS, -1)

def frames_order(array):
    return array.reshape(HGT, WID, FRAMES, -1).transpose(2, 0, 1, 3).reshape(TOKENS, -1)

def reference(tokens, proj_main, proj_shared, proj_step, step_bias, decay_rate, skip_gain, cotangent):
    flat_tokens = tokens.reshape(TOKENS, D)
    main_weight = proj_main.reshape(D, 2 * INNER)
    shared_weight = proj_shared.reshape(D, 2 * STATE)
    both = jnp.dot(flat_tokens, main_weight, preferred_element_type=jnp.float32)
    x_half = both[:, :INNER].astype(jnp.bfloat16)
    z_half = both[:, INNER:].astype(jnp.bfloat16)
    shared_half = jnp.dot(flat_tokens, shared_weight, preferred_element_type=jnp.float32).astype(jnp.bfloat16)
    step_raw = jnp.dot(flat_tokens, proj_step, preferred_element_type=jnp.float32) + step_bias[None, :]
    step_size = jax.nn.softplus(step_raw)
    x_float = x_half.astype(jnp.float32)
    shared_float = shared_half.astype(jnp.float32)
    z_float = z_half.astype(jnp.float32)
    sigma = jax.nn.sigmoid(z_float)
    gate = z_float * sigma
    grad_out = cotangent.reshape(TOKENS, INNER).astype(jnp.float32)
    dy_half = (grad_out * gate).astype(jnp.bfloat16)

    def raster_run(x_in, b_in, c_in, step_in):
        return scan_blocks(x_in, b_in, c_in, step_in, decay_rate[0], BLOCK)

    def temporal_run(x_in, b_in, c_in, step_in):
        return scan_blocks(x_in, b_in, c_in, step_in, decay_rate[1], BLOCK)
    y_raster, pull_raster = jax.vjp(raster_run, x_float.reshape(TOKENS, HEADS, HEADDIM), shared_float[:, :STATE], shared_float[:, STATE:], step_size)
    x_rows = rows_order(x_float).reshape(TOKENS, HEADS, HEADDIM)
    shared_rows = rows_order(shared_float)
    y_temporal, pull_temporal = jax.vjp(temporal_run, x_rows, shared_rows[:, :STATE], shared_rows[:, STATE:], rows_order(step_size))
    y_temporal_b = frames_order(y_temporal.reshape(TOKENS, INNER).astype(jnp.bfloat16))
    skip_term = (skip_gain[None, :, None] * x_float.reshape(TOKENS, HEADS, HEADDIM)).reshape(TOKENS, INNER)
    y_total = y_raster.reshape(TOKENS, INNER) + y_temporal_b.astype(jnp.float32) + skip_term
    gated = (y_total * gate).astype(jnp.bfloat16)
    dz_half = (grad_out * y_total * sigma * (1.0 + z_float * (1.0 - sigma))).astype(jnp.bfloat16)
    dy_float = dy_half.astype(jnp.float32)
    dx_r, db_r, dc_r, dstep_r = pull_raster(dy_float.reshape(TOKENS, HEADS, HEADDIM))
    dy_rows = rows_order(dy_half).astype(jnp.float32).reshape(TOKENS, HEADS, HEADDIM)
    dx_t, db_t, dc_t, dstep_t = pull_temporal(dy_rows)
    dx_temporal_b = frames_order(dx_t.reshape(TOKENS, INNER).astype(jnp.bfloat16))
    skip_grad = (skip_gain[None, :, None] * dy_float.reshape(TOKENS, HEADS, HEADDIM)).reshape(TOKENS, INNER)
    dx_half = (dx_r.reshape(TOKENS, INNER) + dx_temporal_b.astype(jnp.float32) + skip_grad).astype(jnp.bfloat16)
    shared_grad = jnp.concatenate([db_r, dc_r], axis=1) + frames_order(jnp.concatenate([db_t, dc_t], axis=1))
    shared_grad_b = shared_grad.astype(jnp.bfloat16)
    step_grad = dstep_r + frames_order(dstep_t)
    dstep_half = (step_grad * jax.nn.sigmoid(step_raw)).astype(jnp.bfloat16)
    main_grads = jnp.concatenate([dx_half, dz_half], axis=1)
    grad_main = jnp.dot(flat_tokens.T, main_grads, preferred_element_type=jnp.float32).reshape(D, 2, INNER)
    grad_shared = jnp.dot(flat_tokens.T, shared_grad_b, preferred_element_type=jnp.float32).reshape(D, 2, STATE)
    grad_step = jnp.dot(flat_tokens.T, dstep_half, preferred_element_type=jnp.float32)
    input_grad = jnp.dot(main_grads, main_weight.T, preferred_element_type=jnp.float32) + jnp.dot(shared_grad_b, shared_weight.T, preferred_element_type=jnp.float32) + jnp.dot(dstep_half, proj_step.T, preferred_element_type=jnp.float32)
    return (gated.reshape(FRAMES, HGT, WID, INNER), input_grad.astype(jnp.bfloat16).reshape(FRAMES, HGT, WID, D), grad_main, grad_shared, grad_step)
```

```python
import jax
import jax.numpy as jnp
from jax import lax
from jax.experimental import pallas as pl
from jax.experimental.pallas import tpu as pltpu
from jax.sharding import PartitionSpec as P

MESH = pl.DeviceIdType.MESH
BF = jnp.bfloat16
F32 = jnp.float32

SEQ = 16
MP = 8
TOK = 1024
WID = 64
DM = 1024
INNER = 256
HEADS = 4
STATE = 128
LANES = 128
CHUNK = 256
CHUNKS = TOK // CHUNK
COLS = CHUNK // SEQ
SHARD = DM // SEQ
X0, Y0, S0, L0, PAY = 0, 256, 512, 768, 896


def iota(shape, axis):
    return lax.broadcasted_iota(jnp.int32, shape, axis)


def mm(a, b):
    return lax.dot_general(a, b, (((1,), (0,)), ((), ())), preferred_element_type=F32)


def mm_nt(a, b):
    return lax.dot_general(a, b, (((1,), (1,)), ((), ())), preferred_element_type=F32)


def mm_tn(a, b):
    return lax.dot_general(a, b, (((0,), (0,)), ((), ())), preferred_element_type=F32)


def halves(v):
    hi = v.astype(BF)
    return hi, (v - hi.astype(F32)).astype(BF)


def as_pair(v):
    lane = iota(v.shape, 1)
    hi = v.astype(BF).astype(F32)
    return jnp.where(lane < 4, hi, jnp.where(lane < 8, v - hi, 0.0)).astype(BF)


def fori(low, high, step):
    def run(i, carry):
        step(i)
        return carry

    lax.fori_loop(low, high, run, 0)


class SeqExchange:
    def __init__(self, source, landing, sems):
        self.source, self.landing = source, landing
        self.send, self.recv = sems
        self.me = lax.axis_index("seq")

    def copy(self, d):
        peer = lax.rem(self.me + d, SEQ)
        return pltpu.make_async_remote_copy(
            src_ref=self.source(peer),
            dst_ref=self.landing(self.me),
            send_sem=self.send.at[d],
            recv_sem=self.recv.at[d],
            device_id={"seq": peer},
            device_id_type=MESH,
        )

    def arrival(self, d):
        origin = lax.rem(self.me - d + SEQ, SEQ)
        return pltpu.make_async_remote_copy(
            src_ref=self.landing(origin),
            dst_ref=self.landing(origin),
            send_sem=self.send.at[d],
            recv_sem=self.recv.at[d],
            device_id={"seq": origin},
            device_id_type=MESH,
        )

    def start(self):
        fori(1, SEQ, lambda d: self.copy(d).start())

    def wait_recv(self):
        fori(1, SEQ, lambda d: self.arrival(d).wait_recv())

    def wait_send(self):
        fori(1, SEQ, lambda d: self.copy(d).wait_send())


def mp_copy(source, landing, send, recv, peer):
    return pltpu.make_async_remote_copy(
        src_ref=source,
        dst_ref=landing,
        send_sem=send,
        recv_sem=recv,
        device_id={"mp": peer},
        device_id_type=MESH,
    )


def scan_scratch():
    v = pltpu.VMEM
    return dict(
        xs=v((CHUNKS, CHUNK, INNER), BF),
        xt=v((CHUNKS, CHUNK, INNER), BF),
        ed=v((CHUNKS, CHUNK, INNER), BF),
        er=v((CHUNKS, CHUNK, INNER), F32),
        tail=v((CHUNKS, CHUNK, INNER), F32),
        rcol=v((CHUNKS, CHUNK, LANES), F32),
        fresh=v((CHUNKS, INNER, STATE), F32),
        back=v((CHUNKS, INNER, STATE), F32),
        eR=v((CHUNKS, INNER, STATE), F32),
        RC=v((INNER, STATE), F32),
        st=v((2, INNER + 16, STATE), BF),
        sx=v((SEQ, INNER + 16, STATE), BF),
        y=v((CHUNKS, CHUNK, INNER), F32),
        dx=v((CHUNKS, CHUNK, INNER), F32),
        dbc=v((CHUNKS, CHUNK, 2 * STATE), F32),
        dd=v((CHUNKS, CHUNK, LANES), F32),
        gin=v((CHUNKS, INNER, STATE), F32),
        sin=v((INNER, STATE), F32),
    )


def main_scratch():
    v = pltpu.VMEM
    dma = pltpu.SemaphoreType.DMA
    seq_sems = lambda: dma((2, SEQ))
    return dict(
        tok=v((TOK, DM), BF),
        cot=v((TOK, INNER), BF),
        w=v((DM, 768), BF),
        sw_rx=v((SEQ, 16, LANES), BF),
        sw=v((LANES, DM), BF),
        z=v((TOK, INNER), BF),
        sraw=v((TOK, LANES), F32),
        pay=v((TOK, PAY), BF),
        trx=v((SEQ, WID, PAY), BF),
        bpay=v((SEQ, WID, PAY), BF),
        brx=v((SEQ, WID, PAY), BF),
        tri=v((2, CHUNK, CHUNK), BF),
        R=scan_scratch(),
        T=scan_scratch(),
        g=v((TOK, 2 * INNER), BF),
        dst=v((TOK, LANES), BF),
        dbp=v((TOK, 2 * STATE), BF),
        mrx=v((MP, TOK // MP, 2 * STATE), BF),
        dbf=v((TOK, 2 * STATE), BF),
        gp=v((DM, 2 * INNER), BF),
        gq=v((DM, 2 * STATE), BF),
        gs=v((MP, 16, LANES), BF),
        gp_rx=v((SEQ, SHARD, 2 * INNER), BF),
        gq_rx=v((SEQ, SHARD, 2 * STATE), BF),
        gs_rx=v((SEQ, 16, LANES), BF),
        ip=v((MP, TOK, LANES), BF),
        prx=v((4, TOK, LANES), BF),
        zs=v((4, TOK, LANES), BF),
        zrx=v((4, TOK, LANES), BF),
        s_local=dma((4,)),
        s_w=seq_sems(),
        s_sw=seq_sems(),
        s_pay=seq_sems(),
        s_sr=seq_sems(),
        s_st=seq_sems(),
        s_back=seq_sems(),
        s_gp=seq_sems(),
        s_gq=seq_sems(),
        s_gs=seq_sems(),
        s_mr=dma((2, MP)),
        s_ma=dma((2, MP)),
        s_pair=dma((2, 4)),
        s_z=dma((2, 4)),
    )


def sems(ref):
    return ref.at[0], ref.at[1]


def head_sum():
    c, h = iota((INNER, LANES), 0), iota((INNER, LANES), 1)
    return jnp.where((h < 8) & ((h & 3) == (c >> 6)), 1.0, 0.0).astype(BF)


def pair_expand():
    k, c = iota((LANES, INNER), 0), iota((LANES, INNER), 1)
    return jnp.where((k < 8) & ((k & 3) == (c >> 6)), 1.0, 0.0).astype(BF)


def pair_merge():
    k, h = iota((LANES, LANES), 0), iota((LANES, LANES), 1)
    return jnp.where((k < 8) & (h < 8) & ((k & 3) == (h & 3)), 1.0, 0.0).astype(BF)


def summary(b, tri, load, rate, ratex, q):
    x = load(X0, 256, q).astype(F32)
    dy = load(Y0, 256, q).astype(F32)
    bmat = load(S0, STATE, q)
    cmat = load(S0 + STATE, STATE, q)
    pair = load(L0, LANES, q)
    dexp = mm(pair, pair_expand())
    lhi, llo = halves(-dexp * ratex)
    chi, clo = halves(-mm(pair, pair_merge()) * rate)
    rexp = mm(tri, lhi) + mm(tri, llo)
    b["rcol"][q] = mm(tri, chi) + mm(tri, clo)
    total = jnp.sum(lhi.astype(F32) + llo.astype(F32), axis=0, keepdims=True)
    er = jnp.exp(rexp)
    tail = jnp.exp(jnp.minimum(total - rexp, 0.0))
    xs = (x * dexp).astype(BF)
    xt = (xs.astype(F32) * tail).astype(BF)
    ed = (er * dy).astype(BF)
    b["er"][q] = er
    b["tail"][q] = tail
    b["xs"][q] = xs
    b["xt"][q] = xt
    b["ed"][q] = ed
    b["fresh"][q] = mm_tn(xt, bmat)
    b["back"][q] = mm_tn(ed, cmat)
    ones = jnp.ones((CHUNK, STATE), BF)
    rows = mm_tn(lhi, ones) + mm_tn(llo, ones)
    b["eR"][q] = jnp.exp(rows)
    b["RC"][...] += rows


def pack_states(b):
    e = [b["eR"][q] for q in range(CHUNKS)]
    end = b["fresh"][0]
    for q in range(1, CHUNKS):
        end = end * e[q] + b["fresh"][q]
    first = b["back"][CHUNKS - 1]
    for q in range(CHUNKS - 2, -1, -1):
        first = first * e[q] + b["back"][q]
    rc = b["RC"][...]
    row = iota((16, STATE), 0)
    value = jnp.zeros((16, STATE), F32)
    for h in range(HEADS):
        value = jnp.where((row & 3) == h, jnp.broadcast_to(rc[64 * h : 64 * h + 1], (16, STATE)), value)
    hi = value.astype(BF).astype(F32)
    tile = jnp.where(row < 4, hi, jnp.where(row < 8, value - hi, 0.0)).astype(BF)
    b["st"][0, pl.ds(0, INNER)] = end.astype(BF)
    b["st"][1, pl.ds(0, INNER)] = first.astype(BF)
    b["st"][0, pl.ds(INNER, 16)] = tile
    b["st"][1, pl.ds(INNER, 16)] = tile


def entering_states(b, me):
    c, k = iota((INNER, 16), 0), iota((INNER, 16), 1)
    spread = jnp.where((k < 8) & ((k & 3) == (c >> 6)), 1.0, 0.0).astype(BF)

    def lap(k, state):
        decay = jnp.exp(mm(spread, b["sx"][k, pl.ds(INNER, 16)]))
        return state * decay + b["sx"][k, pl.ds(0, INNER)].astype(F32)

    zero = jnp.zeros((INNER, STATE), F32)
    b["sin"][...] = lax.fori_loop(0, me, lap, zero)
    grad = lax.fori_loop(0, SEQ - 1 - me, lambda k, s: lap(SEQ - 1 - k, s), zero)
    for q in range(CHUNKS - 1, -1, -1):
        b["gin"][q] = grad
        if q > 0:
            grad = grad * b["eR"][q] + b["back"][q]


def inside(b, tri, load, q):
    dy = load(Y0, 256, q)
    bmat = load(S0, STATE, q)
    cmat = load(S0 + STATE, STATE, q)
    xs = b["xs"][q]
    trif = tri.astype(F32)
    scores = mm_nt(cmat, bmat) * trif
    rcol = b["rcol"][q]
    rrow = rcol.T
    head = iota((CHUNK, INNER), 1) >> 6
    zero = jnp.zeros((), BF)
    y = jnp.zeros((CHUNK, INNER), F32)
    dxs = jnp.zeros((CHUNK, INNER), F32)
    pairs = jnp.zeros((CHUNK, CHUNK), F32)
    for h in range(HEADS):
        decay = jnp.exp(jnp.minimum(rcol[:, h : h + 1] - rrow[h : h + 1, :], 0.0))
        m = (decay * scores).astype(BF)
        dyh = jnp.where(head == h, dy, zero)
        xsh = jnp.where(head == h, xs, zero)
        y += mm(m, xsh)
        dxs += mm_tn(m, dyh)
        pairs += decay * mm_nt(dyh, xs)
    pairs = (pairs * trif).astype(BF)
    b["y"][q] = y
    b["dx"][q] = dxs
    b["dbc"][q, :, pl.ds(0, STATE)] = mm_tn(pairs, cmat)
    b["dbc"][q, :, pl.ds(STATE, STATE)] = mm(pairs, bmat)


def outside(b, tri, load, rate, q, put):
    x = load(X0, 256, q).astype(F32)
    dy = load(Y0, 256, q).astype(F32)
    bmat = load(S0, STATE, q)
    cmat = load(S0 + STATE, STATE, q)
    dexp = mm(load(L0, LANES, q), pair_expand())
    xs = b["xs"][q].astype(F32)
    state = b["sin"][...]
    grad = b["gin"][q]
    state_b, grad_b = state.astype(BF), grad.astype(BF)
    sums = head_sum()
    y = b["y"][q] + b["er"][q] * mm_nt(cmat, state_b)
    inner = b["dx"][q]
    outer = b["tail"][q] * mm_nt(bmat, grad_b)
    dxs = inner + outer
    db = b["dbc"][q, :, pl.ds(0, STATE)] + mm(b["xt"][q], grad_b)
    dc = b["dbc"][q, :, pl.ds(STATE, STATE)] + mm(b["ed"][q], state_b)

    def by_head(v):
        hi, lo = halves(v)
        return mm(hi, sums) + mm(lo, sums)

    late = by_head(dy * y - xs * inner)
    early = by_head(xs * outer)
    decayed = b["eR"][q] * state
    across = jnp.sum(mm_tn((decayed * grad).astype(BF), sums), axis=0, keepdims=True)
    late_hi, late_lo = halves(late)
    early_hi, early_lo = halves(early)
    dl = mm_tn(tri, late_hi) + mm_tn(tri, late_lo) + mm(tri, early_hi) + mm(tri, early_lo) - early + across
    ddelta = by_head(x * dxs) - rate * dl
    b["sin"][...] = decayed + b["fresh"][q]
    put(q, y, dexp * dxs, db, dc, ddelta)


def kernel(tok_hbm, cot_hbm, wp, swp, bias, rates, ratex, skipx, gated_o, ig_o, gm_o, gsh_o, gst_o, m):
    seq, mp = lax.axis_index("seq"), lax.axis_index("mp")
    core = lax.rem(mp, 2)
    chip = mp // 2
    partner = mp + 1 - 2 * core

    load_tok = pltpu.make_async_copy(tok_hbm, m["tok"], m["s_local"].at[0])
    load_cot = pltpu.make_async_copy(cot_hbm, m["cot"], m["s_local"].at[1])
    load_tok.start()
    load_cot.start()

    barrier = pltpu.get_barrier_semaphore()

    def greet_seq(d):
        pl.semaphore_signal(
            barrier, inc=1, device_id={"seq": lax.rem(seq + d, SEQ)}, device_id_type=MESH
        )

    def greet_mp(d):
        pl.semaphore_signal(barrier, inc=1, device_id={"mp": lax.rem(mp + d, MP)}, device_id_type=MESH)

    fori(1, SEQ, greet_seq)
    fori(1, MP, greet_mp)
    pl.semaphore_wait(barrier, SEQ + MP - 2)

    def w_rows(k):
        return m["w"].at[pl.ds(pl.multiple_of(k * SHARD, SHARD), SHARD)]

    send_w = SeqExchange(lambda p: wp, w_rows, sems(m["s_w"]))
    send_sw = SeqExchange(lambda p: swp, lambda k: m["sw_rx"].at[k], sems(m["s_sw"]))
    send_w.start()
    send_sw.start()
    m["w"][pl.ds(pl.multiple_of(seq * SHARD, SHARD), SHARD)] = wp[...]
    m["sw_rx"][seq] = swp[...]

    i, j = iota((CHUNK, CHUNK), 0), iota((CHUNK, CHUNK), 1)
    m["tri"][0] = jnp.where(i >= j, 1.0, 0.0).astype(BF)
    it, jt = (i & 15) * 16 + (i >> 4), (j & 15) * 16 + (j >> 4)
    m["tri"][1] = jnp.where(it >= jt, 1.0, 0.0).astype(BF)
    m["sw"][...] = jnp.zeros((LANES, DM), BF)
    m["R"]["RC"][...] = jnp.zeros((INNER, STATE), F32)
    m["T"]["RC"][...] = jnp.zeros((INNER, STATE), F32)
    load_tok.wait()
    load_cot.wait()
    send_w.wait_recv()
    send_sw.wait_recv()
    for k in range(SEQ // 2):
        m["sw"][pl.ds(0, 16), pl.ds(k * LANES, LANES)] = m["sw_rx"][2 * k] + m["sw_rx"][2 * k + 1]

    def rows_of(q):
        return pl.ds(pl.multiple_of(q * CHUNK, CHUNK), CHUNK)

    def project(q):
        rows = rows_of(q)
        u = m["tok"][rows, :]
        z = mm(u, m["w"][:, pl.ds(256, 256)]).astype(BF)
        m["z"][rows, :] = z
        zf = z.astype(F32)
        gate = zf * jax.nn.sigmoid(zf)
        m["pay"][rows, pl.ds(Y0, 256)] = (m["cot"][rows, :].astype(F32) * gate).astype(BF)
        m["pay"][rows, pl.ds(X0, 256)] = mm(u, m["w"][:, pl.ds(0, 256)]).astype(BF)
        m["pay"][rows, pl.ds(S0, 256)] = mm(u, m["w"][:, pl.ds(512, 256)]).astype(BF)
        raw = mm_nt(u, m["sw"][...]) + bias[...]
        m["sraw"][rows, :] = raw
        delta = jnp.maximum(raw, 0.0) + jnp.log1p(jnp.exp(-jnp.abs(raw)))
        m["pay"][rows, pl.ds(L0, LANES)] = as_pair(delta)

    fori(0, CHUNKS, project)

    send_pay = SeqExchange(
        lambda p: m["pay"].at[pl.ds(pl.multiple_of(p * WID, WID), WID)],
        lambda k: m["trx"].at[k],
        sems(m["s_pay"]),
    )
    send_pay.start()
    m["trx"][seq] = m["pay"][pl.ds(pl.multiple_of(seq * WID, WID), WID), :]

    def load_r(at, width, q):
        return m["pay"][rows_of(q), pl.ds(at, width)]

    def cols_of(q):
        return pl.ds(pl.multiple_of(q * COLS, COLS), COLS)

    def load_t(at, width, q):
        return m["trx"][:, cols_of(q), pl.ds(at, width)].reshape(CHUNK, width)

    def states_exchange(b, sem):
        return SeqExchange(
            lambda p: b["st"].at[jnp.where(seq < p, 0, 1)], lambda k: b["sx"].at[k], sems(sem)
        )

    r, t = m["R"], m["T"]
    tri_r, tri_t = m["tri"].at[0], m["tri"].at[1]
    rate_r, rate_t = rates[pl.ds(0, 1), :], rates[pl.ds(1, 1), :]
    ratex_r, ratex_t = ratex[pl.ds(0, 1), :], ratex[pl.ds(1, 1), :]
    fori(0, CHUNKS, lambda q: summary(r, tri_r[...], load_r, rate_r, ratex_r, q))
    pack_states(r)
    send_sr = states_exchange(r, m["s_sr"])
    send_sr.start()
    fori(0, CHUNKS, lambda q: inside(r, tri_r[...], load_r, q))

    send_pay.wait_recv()
    fori(0, CHUNKS, lambda q: summary(t, tri_t[...], load_t, rate_t, ratex_t, q))
    pack_states(t)
    send_st = states_exchange(t, m["s_st"])
    send_st.start()
    fori(0, CHUNKS, lambda q: inside(t, tri_t[...], load_t, q))
    send_st.wait_recv()
    entering_states(t, seq)

    def put_t(q, y, dx, db, dc, dd):
        def put(at, v):
            m["bpay"][:, cols_of(q), pl.ds(at, v.shape[1])] = v.astype(BF).reshape(SEQ, COLS, v.shape[1])

        put(X0, y)
        put(Y0, dx)
        put(S0, db)
        put(S0 + STATE, dc)
        put(L0, as_pair(dd))

    fori(0, CHUNKS, lambda q: outside(t, tri_t[...], load_t, rate_t, q, put_t))
    send_back = SeqExchange(lambda p: m["bpay"].at[p], lambda k: m["brx"].at[k], sems(m["s_back"]))
    send_back.start()
    m["brx"][seq] = m["bpay"][seq]

    send_sr.wait_recv()
    entering_states(r, seq)

    def put_r(q, y, dx, db, dc, dd):
        r["y"][q] = y
        r["dx"][q] = dx
        r["dbc"][q, :, pl.ds(0, STATE)] = db
        r["dbc"][q, :, pl.ds(STATE, STATE)] = dc
        r["dd"][q] = dd

    fori(0, CHUNKS, lambda q: outside(r, tri_r[...], load_r, rate_r, q, put_r))
    send_back.wait_recv()

    def combine(q):
        rows = rows_of(q)

        def back(at, width):
            return m["brx"][pl.ds(q * 4, 4), :, pl.ds(at, width)].reshape(CHUNK, width)

        x = load_r(X0, 256, q).astype(F32)
        dy = load_r(Y0, 256, q).astype(F32)
        z = m["z"][rows, :].astype(F32)
        cot = m["cot"][rows, :].astype(F32)
        skip = skipx[...]
        y = r["y"][q] + back(X0, 256).astype(F32) + skip * x
        sigma = jax.nn.sigmoid(z)
        gated_o[rows, :] = (y * (z * sigma)).astype(BF)
        m["g"][rows, pl.ds(256, 256)] = (cot * y * sigma * (1.0 + z * (1.0 - sigma))).astype(BF)
        m["g"][rows, pl.ds(0, 256)] = (r["dx"][q] + back(Y0, 256).astype(F32) + skip * dy).astype(BF)
        m["dbp"][rows, :] = (r["dbc"][q] + back(S0, 256).astype(F32)).astype(BF)
        dd = r["dd"][q] + mm(back(L0, LANES), pair_merge())
        dstep = dd * jax.nn.sigmoid(m["sraw"][rows, :])
        m["dst"][rows, :] = jnp.where(iota((CHUNK, LANES), 1) < HEADS, dstep, 0.0).astype(BF)

    fori(0, CHUNKS, combine)

    part = TOK // MP

    def part_rows(k):
        return pl.ds(pl.multiple_of(k * part, part), part)

    def mp_peer(d):
        return lax.rem(mp + d, MP)

    def mr_copy(d):
        peer = mp_peer(d)
        return mp_copy(
            m["dbp"].at[part_rows(peer)], m["mrx"].at[mp], m["s_mr"].at[0, d], m["s_mr"].at[1, d], peer
        )

    def mr_arrival(d):
        origin = lax.rem(mp - d + MP, MP)
        return mp_copy(
            m["mrx"].at[origin], m["mrx"].at[origin], m["s_mr"].at[0, d], m["s_mr"].at[1, d], origin
        )

    fori(1, MP, lambda d: mr_copy(d).start())
    m["mrx"][mp] = m["dbp"][part_rows(mp), :]

    def input_part(q):
        rows = rows_of(q)
        g = m["g"][rows, :]
        ds = m["dst"][rows, :]
        for c in range(4):
            cols = pl.ds(c * 256, 256)
            v = mm_nt(g, m["w"][cols, pl.ds(0, 512)]) + mm(ds, m["sw"][:, cols])
            v = v.astype(BF)
            m["ip"][2 * c, rows, :] = v[:, :LANES]
            m["ip"][2 * c + 1, rows, :] = v[:, LANES:]

    fori(0, CHUNKS, input_part)

    def pair_copy(k):
        return mp_copy(
            m["ip"].at[2 * k + 1 - core],
            m["prx"].at[k],
            m["s_pair"].at[0, k],
            m["s_pair"].at[1, k],
            partner,
        )

    fori(0, 4, lambda k: pair_copy(k).start())

    def grads(k):
        cols = pl.ds(k * 256, 256)
        u = m["tok"][:, cols]
        m["gp"][pl.ds(k * 256, 256), :] = mm_tn(u, m["g"][...]).astype(BF)
        gs = mm_tn(m["dst"][...], u)[:16].astype(BF)
        m["gs"][2 * k] = gs[:, :LANES]
        m["gs"][2 * k + 1] = gs[:, LANES:]

    for k in range(4):
        grads(k)

    def shard_rows(ref):
        return lambda p: ref.at[pl.ds(pl.multiple_of(p * SHARD, SHARD), SHARD)]

    send_gp = SeqExchange(shard_rows(m["gp"]), lambda k: m["gp_rx"].at[k], sems(m["s_gp"]))
    send_gs = SeqExchange(lambda p: m["gs"].at[p // 2], lambda k: m["gs_rx"].at[k], sems(m["s_gs"]))
    send_gp.start()
    send_gs.start()
    own = pl.ds(pl.multiple_of(seq * SHARD, SHARD), SHARD)
    m["gp_rx"][seq] = m["gp"][own, :]
    m["gs_rx"][seq] = m["gs"][seq // 2]

    fori(1, MP, lambda d: mr_arrival(d).wait_recv())
    total = m["mrx"][0].astype(F32)
    for k in range(1, MP):
        total += m["mrx"][k].astype(F32)
    m["dbf"][part_rows(mp), :] = total.astype(BF)

    def ma_copy(d):
        return mp_copy(
            m["dbf"].at[part_rows(mp)],
            m["dbf"].at[part_rows(mp)],
            m["s_ma"].at[0, d],
            m["s_ma"].at[1, d],
            mp_peer(d),
        )

    def ma_arrival(d):
        origin = lax.rem(mp - d + MP, MP)
        return mp_copy(
            m["dbf"].at[part_rows(origin)],
            m["dbf"].at[part_rows(origin)],
            m["s_ma"].at[0, d],
            m["s_ma"].at[1, d],
            origin,
        )

    fori(1, MP, lambda d: ma_copy(d).start())

    def z_peer(d):
        return lax.rem(chip + d, 4)

    def z_copy(d):
        return mp_copy(
            m["zs"].at[z_peer(d)],
            m["zrx"].at[chip],
            m["s_z"].at[0, d],
            m["s_z"].at[1, d],
            2 * z_peer(d) + core,
        )

    def z_arrival(d):
        origin = lax.rem(chip - d + 4, 4)
        return mp_copy(
            m["zrx"].at[origin],
            m["zrx"].at[origin],
            m["s_z"].at[0, d],
            m["s_z"].at[1, d],
            2 * origin + core,
        )

    fori(0, 4, lambda k: pair_copy(k).wait_recv())

    def pair_sum(k):
        m["zs"][k] = (m["ip"][2 * k + core].astype(F32) + m["prx"][k].astype(F32)).astype(BF)

    def pair_send(d):
        pair_sum(z_peer(d))
        z_copy(d).start()

    fori(1, 4, pair_send)
    pair_sum(chip)
    m["zrx"][chip] = m["zs"][chip]

    fori(1, MP, lambda d: ma_arrival(d).wait_recv())
    for k in range(4):
        m["gq"][pl.ds(k * 256, 256), :] = mm_tn(m["tok"][:, pl.ds(k * 256, 256)], m["dbf"][...]).astype(BF)
    send_gq = SeqExchange(shard_rows(m["gq"]), lambda k: m["gq_rx"].at[k], sems(m["s_gq"]))
    send_gq.start()
    m["gq_rx"][seq] = m["gq"][own, :]

    fori(1, 4, lambda d: z_arrival(d).wait_recv())
    w_mine = m["w"][part_rows(mp), pl.ds(512, 256)]

    def input_sum(q):
        rows = rows_of(q)
        v = mm_nt(m["dbf"][rows, :], w_mine)
        for k in range(4):
            v += m["zrx"][k, rows, :].astype(F32)
        ig_o[rows, :] = v.astype(BF)

    fori(0, CHUNKS, input_sum)

    def total_of(ref):
        v = ref[0].astype(F32)
        for k in range(1, SEQ):
            v += ref[k].astype(F32)
        return v

    send_gp.wait_recv()
    gm_o[...] = total_of(m["gp_rx"])
    send_gs.wait_recv()
    gst_o[...] = total_of(m["gs_rx"])
    send_gq.wait_recv()
    gsh_o[...] = total_of(m["gq_rx"])

    for e in (send_w, send_sw, send_pay, send_sr, send_st, send_back, send_gp, send_gs, send_gq):
        e.wait_send()
    fori(1, MP, lambda d: mr_copy(d).wait_send())
    fori(1, MP, lambda d: ma_copy(d).wait_send())
    fori(0, 4, lambda k: pair_copy(k).wait_send())
    fori(1, 4, lambda d: z_copy(d).wait_send())


def eight(v):
    return jnp.concatenate([v, v, jnp.zeros((v.shape[0], LANES - 8), v.dtype)], axis=1)


def body(tokens, proj_main, proj_shared, proj_step, step_bias, decay_rate, skip_gain, cotangent):
    seq = lax.axis_index("seq")
    wp = jnp.concatenate([proj_main.reshape(SHARD, 512), proj_shared.reshape(SHARD, 256)], axis=1)
    step_t = proj_step.T
    step_t = jnp.concatenate([step_t, step_t, jnp.zeros((8, SHARD), BF)], axis=0)
    low = lax.rem(seq, 2) == 0
    nothing = jnp.zeros_like(step_t)
    swp = jnp.concatenate([jnp.where(low, step_t, nothing), jnp.where(low, nothing, step_t)], axis=1)
    bias = eight(step_bias[None, :])
    rates = eight(decay_rate)
    ratex = jnp.repeat(decay_rate, 64, axis=1)
    skipx = jnp.repeat(skip_gain[None, :], 64, axis=1)
    vm = pl.BlockSpec(memory_space=pltpu.VMEM)
    hbm = pl.BlockSpec(memory_space=pl.ANY)
    gated, ig, gm, gsh, gst = pl.pallas_call(
        kernel,
        out_shape=(
            jax.ShapeDtypeStruct((TOK, INNER), BF),
            jax.ShapeDtypeStruct((TOK, LANES), BF),
            jax.ShapeDtypeStruct((SHARD, 512), F32),
            jax.ShapeDtypeStruct((SHARD, 256), F32),
            jax.ShapeDtypeStruct((16, LANES), F32),
        ),
        in_specs=[hbm, hbm] + [vm] * 6,
        out_specs=(vm,) * 5,
        scratch_shapes=[main_scratch()],
        compiler_params=pltpu.CompilerParams(
            collective_id=0, has_side_effects=True, vmem_limit_bytes=62 * 1024 * 1024
        ),
    )(tokens.reshape(TOK, DM), cotangent.reshape(TOK, INNER), wp, swp, bias, rates, ratex, skipx)
    grad_step = jnp.where(low, gst[:4, :64], gst[:4, 64:]).T
    return (
        gated.reshape(1, 16, WID, INNER),
        ig.reshape(1, 16, WID, LANES),
        gm.reshape(SHARD, 2, INNER),
        gsh.reshape(SHARD, 2, STATE),
        grad_step,
    )


def solution(mesh):
    placed = (
        P("seq", None, None, None),
        P("seq", None, "mp"),
        P("seq", None, None),
        P("seq", "mp"),
        P("mp"),
        P(None, "mp"),
        P("mp"),
        P("seq", None, None, "mp"),
    )
    return jax.shard_map(
        body,
        mesh=mesh,
        in_specs=placed,
        out_specs=(
            P("seq", None, None, "mp"),
            P("seq", None, None, "mp"),
            P("seq", None, "mp"),
            P("seq", None, None),
            P("seq", "mp"),
        ),
        check_vma=False,
    )
```

```python
import jax
import jax.numpy as jnp
from jax import lax
from jax.experimental import pallas as pl
from jax.experimental.pallas import tpu as pltpu
from jax.sharding import PartitionSpec as P

MESH = pl.DeviceIdType.MESH
BF = jnp.bfloat16
F32 = jnp.float32

SEQ = 16
MP = 8
TOK = 1024
WID = 64
DM = 1024
INNER = 256
HEADS = 4
STATE = 128
LANES = 128
CHUNK = 256
CHUNKS = TOK // CHUNK
COLS = CHUNK // SEQ
SHARD = DM // SEQ
BX, BY, BB, BC, ROWS_L, ROWS = 0, 2, 4, 5, 384, 400
PIECE = INNER // SEQ


def iota(shape, axis):
    return lax.broadcasted_iota(jnp.int32, shape, axis)


def mm(a, b):
    return lax.dot_general(a, b, (((1,), (0,)), ((), ())), preferred_element_type=F32)


def mm_nt(a, b):
    return lax.dot_general(a, b, (((1,), (1,)), ((), ())), preferred_element_type=F32)


def mm_tn(a, b):
    return lax.dot_general(a, b, (((0,), (0,)), ((), ())), preferred_element_type=F32)


def halves(v):
    hi = v.astype(BF)
    return hi, (v - hi.astype(F32)).astype(BF)


def as_pair(v):
    lane = iota(v.shape, 1)
    hi = v.astype(BF).astype(F32)
    return jnp.where(lane < 4, hi, jnp.where(lane < 8, v - hi, 0.0)).astype(BF)


def fori(low, high, step):
    def run(i, carry):
        step(i)
        return carry

    lax.fori_loop(low, high, run, 0)


class SeqExchange:
    def __init__(self, source, landing, sems):
        self.source, self.landing = source, landing
        self.send, self.recv = sems
        self.me = lax.axis_index("seq")

    def copy(self, d):
        peer = lax.rem(self.me + d, SEQ)
        return pltpu.make_async_remote_copy(
            src_ref=self.source(peer),
            dst_ref=self.landing(self.me),
            send_sem=self.send.at[d],
            recv_sem=self.recv.at[d],
            device_id={"seq": peer},
            device_id_type=MESH,
        )

    def arrival(self, d):
        origin = lax.rem(self.me - d + SEQ, SEQ)
        return pltpu.make_async_remote_copy(
            src_ref=self.landing(origin),
            dst_ref=self.landing(origin),
            send_sem=self.send.at[d],
            recv_sem=self.recv.at[d],
            device_id={"seq": origin},
            device_id_type=MESH,
        )

    def start(self):
        fori(1, SEQ, lambda d: self.copy(d).start())

    def wait_recv(self):
        fori(1, SEQ, lambda d: self.arrival(d).wait_recv())

    def wait_send(self):
        fori(1, SEQ, lambda d: self.copy(d).wait_send())


def mp_copy(source, landing, send, recv, peer):
    return pltpu.make_async_remote_copy(
        src_ref=source,
        dst_ref=landing,
        send_sem=send,
        recv_sem=recv,
        device_id={"mp": peer},
        device_id_type=MESH,
    )


def scan_scratch():
    v = pltpu.VMEM
    return dict(
        xs=v((CHUNKS, CHUNK, INNER), BF),
        xt=v((CHUNKS, CHUNK, INNER), BF),
        ed=v((CHUNKS, CHUNK, INNER), BF),
        er=v((CHUNKS, CHUNK, INNER), F32),
        tail=v((CHUNKS, CHUNK, INNER), F32),
        rcol=v((CHUNKS, CHUNK, LANES), F32),
        fresh=v((CHUNKS, INNER, STATE), F32),
        back=v((CHUNKS, INNER, STATE), F32),
        eR=v((CHUNKS, INNER, STATE), F32),
        RC=v((INNER, STATE), F32),
        st=v((SEQ, 48, STATE), BF),
        sx=v((SEQ, 48, STATE), BF),
        sy=v((SEQ, 32, STATE), BF),
        sz=v((SEQ, 32, STATE), BF),
        y=v((CHUNKS, CHUNK, INNER), F32),
        dx=v((CHUNKS, CHUNK, INNER), F32),
        dbc=v((CHUNKS, CHUNK, 2 * STATE), F32),
        dd=v((CHUNKS, CHUNK, LANES), F32),
        gin=v((CHUNKS, INNER, STATE), F32),
        sin=v((INNER, STATE), F32),
    )


def main_scratch():
    v = pltpu.VMEM
    dma = pltpu.SemaphoreType.DMA
    seq_sems = lambda: dma((2, SEQ))
    return dict(
        tok=v((TOK, DM), BF),
        cot=v((TOK, INNER), BF),
        w=v((DM, 768), BF),
        sw_rx=v((SEQ, 16, LANES), BF),
        sw=v((LANES, DM), BF),
        z=v((TOK, INNER), BF),
        sraw=v((TOK, LANES), F32),
        pay=v((SEQ, ROWS, LANES), BF),
        trx=v((SEQ, ROWS, LANES), BF),
        bpay=v((SEQ, ROWS, LANES), BF),
        brx=v((SEQ, ROWS, LANES), BF),
        tri=v((2, CHUNK, CHUNK), BF),
        lp=v((TOK, LANES), BF),
        lacc=v((CHUNK, LANES), F32),
        wp=v((SHARD, 768), BF),
        swp=v((16, LANES), BF),
        rows=v((8, INNER), F32),
        R=scan_scratch(),
        T=scan_scratch(),
        g=v((TOK, 2 * INNER), BF),
        dst=v((TOK, LANES), BF),
        dbp=v((TOK, 2 * STATE), BF),
        mrx=v((MP, TOK // MP, 2 * STATE), BF),
        dbf=v((TOK, 2 * STATE), BF),
        gp=v((DM, 2 * INNER), BF),
        gq=v((DM, 2 * STATE), BF),
        gs=v((MP, 16, LANES), BF),
        gp_rx=v((SEQ, SHARD, 2 * INNER), BF),
        gq_rx=v((SEQ, SHARD, 2 * STATE), BF),
        gs_rx=v((SEQ, 16, LANES), BF),
        ip=v((MP, TOK, LANES), BF),
        prx=v((4, TOK, LANES), BF),
        zs=v((4, TOK, LANES), BF),
        zrx=v((4, TOK, LANES), BF),
        s_local=dma((4,)),
        s_w=seq_sems(),
        s_sw=seq_sems(),
        s_pay=seq_sems(),
        s_sr=seq_sems(),
        s_st=seq_sems(),
        s_ur=seq_sems(),
        s_ut=seq_sems(),
        s_back=seq_sems(),
        s_gp=seq_sems(),
        s_gq=seq_sems(),
        s_gs=seq_sems(),
        s_mr=dma((2, MP)),
        s_ma=dma((2, MP)),
        s_pair=dma((2, 4, CHUNKS)),
        s_z=dma((2, 4)),
    )


def sems(ref):
    return ref.at[0], ref.at[1]


def head_sum():
    c, h = iota((INNER, LANES), 0), iota((INNER, LANES), 1)
    return jnp.where((h < 8) & ((h & 3) == (c >> 6)), 1.0, 0.0).astype(BF)


def pair_expand(shift):
    k, c = iota((LANES, INNER), 0) - shift, iota((LANES, INNER), 1)
    return jnp.where((k >= 0) & (k < 8) & ((k & 3) == (c >> 6)), 1.0, 0.0).astype(BF)


def pair_merge(shift):
    k, h = iota((LANES, LANES), 0) - shift, iota((LANES, LANES), 1)
    return jnp.where((k >= 0) & (k < 8) & (h < 8) & ((k & 3) == (h & 3)), 1.0, 0.0).astype(BF)


def pair_place(shift):
    k, lane = iota((LANES, LANES), 0), iota((LANES, LANES), 1)
    return jnp.where((k < 8) & (lane == k + shift), 1.0, 0.0).astype(BF)


def wide(load, block, q):
    return jnp.concatenate([load(block, q), load(block + 1, q)], axis=1)


def summary(b, tri, load, pair_of, rate, ratex, q):
    x = wide(load, BX, q).astype(F32)
    dy = wide(load, BY, q).astype(F32)
    pair, shift = pair_of(q)
    dexp = mm(pair, pair_expand(shift))
    logs = (-dexp * ratex).astype(BF)
    rexp = mm(tri, logs)
    b["rcol"][q] = mm(tri, (-mm(pair, pair_merge(shift)) * rate).astype(BF))
    total = jnp.sum(logs.astype(F32), axis=0, keepdims=True)
    er = jnp.exp(rexp)
    tail = jnp.exp(jnp.minimum(total - rexp, 0.0))
    xs = (x * dexp).astype(BF)
    xt = (xs.astype(F32) * tail).astype(BF)
    ed = (er * dy).astype(BF)
    b["er"][q] = er
    b["tail"][q] = tail
    b["xs"][q] = xs
    b["xt"][q] = xt
    b["ed"][q] = ed
    b["fresh"][q] = mm_tn(xt, load(BB, q))
    b["back"][q] = mm_tn(ed, load(BC, q))
    rows = mm_tn(logs, jnp.ones((CHUNK, STATE), BF))
    b["eR"][q] = jnp.exp(rows)
    b["RC"][...] += rows


def pack_states(b):
    e = [b["eR"][q] for q in range(CHUNKS)]
    end = b["fresh"][0]
    for q in range(1, CHUNKS):
        end = end * e[q] + b["fresh"][q]
    first = b["back"][CHUNKS - 1]
    for q in range(CHUNKS - 2, -1, -1):
        first = first * e[q] + b["back"][q]
    rc = b["RC"][...].reshape(SEQ, PIECE, STATE)
    hi = rc.astype(BF).astype(F32)
    logs = jnp.where(iota((SEQ, PIECE, STATE), 1) < 8, hi, rc - hi)
    b["st"][:, pl.ds(0, PIECE), :] = end.astype(BF).reshape(SEQ, PIECE, STATE)
    b["st"][:, pl.ds(PIECE, PIECE), :] = first.astype(BF).reshape(SEQ, PIECE, STATE)
    b["st"][:, pl.ds(2 * PIECE, PIECE), :] = logs.astype(BF)


def chain_states(b):
    decay = []
    for k in range(SEQ):
        logs = b["sx"][k, pl.ds(2 * PIECE, PIECE)].astype(F32)
        one = jnp.exp(logs[:8] + logs[8:])
        decay.append(jnp.concatenate([one, one], axis=0))
    state = jnp.zeros((PIECE, STATE), F32)
    grad = jnp.zeros((PIECE, STATE), F32)
    for k in range(SEQ):
        b["sy"][k, pl.ds(0, PIECE)] = state.astype(BF)
        state = state * decay[k] + b["sx"][k, pl.ds(0, PIECE)].astype(F32)
        n = SEQ - 1 - k
        b["sy"][n, pl.ds(PIECE, PIECE)] = grad.astype(BF)
        grad = grad * decay[n] + b["sx"][n, pl.ds(PIECE, PIECE)].astype(F32)


def entering_states(b):
    b["sin"][...] = b["sz"][:, pl.ds(0, PIECE), :].reshape(INNER, STATE).astype(F32)
    grad = b["sz"][:, pl.ds(PIECE, PIECE), :].reshape(INNER, STATE).astype(F32)
    for q in range(CHUNKS - 1, -1, -1):
        b["gin"][q] = grad
        if q > 0:
            grad = grad * b["eR"][q] + b["back"][q]


def inside(b, tri, load, q):
    dy = wide(load, BY, q)
    bmat = load(BB, q)
    cmat = load(BC, q)
    xs = b["xs"][q]
    trif = tri.astype(F32)
    scores = mm_nt(cmat, bmat) * trif
    rcol = b["rcol"][q]
    rrow = rcol.T
    head = iota((CHUNK, INNER), 1) >> 6
    zero = jnp.zeros((), BF)
    y = jnp.zeros((CHUNK, INNER), F32)
    dxs = jnp.zeros((CHUNK, INNER), F32)
    pairs = jnp.zeros((CHUNK, CHUNK), F32)
    for h in range(HEADS):
        decay = jnp.exp(jnp.minimum(rcol[:, h : h + 1] - rrow[h : h + 1, :], 0.0))
        m = (decay * scores).astype(BF)
        dyh = jnp.where(head == h, dy, zero)
        xsh = jnp.where(head == h, xs, zero)
        y += mm(m, xsh)
        dxs += mm_tn(m, dyh)
        pairs += decay * mm_nt(dyh, xs)
    pairs = (pairs * trif).astype(BF)
    b["y"][q] = y
    b["dx"][q] = dxs
    b["dbc"][q, :, pl.ds(0, STATE)] = mm_tn(pairs, cmat)
    b["dbc"][q, :, pl.ds(STATE, STATE)] = mm(pairs, bmat)


def outside(b, tri, load, pair_of, rate, q, put):
    x = wide(load, BX, q).astype(F32)
    dy = wide(load, BY, q).astype(F32)
    bmat = load(BB, q)
    cmat = load(BC, q)
    pair, shift = pair_of(q)
    dexp = mm(pair, pair_expand(shift))
    xs = b["xs"][q].astype(F32)
    state = b["sin"][...]
    grad = b["gin"][q]
    state_b, grad_b = state.astype(BF), grad.astype(BF)
    sums = head_sum()
    y = b["y"][q] + b["er"][q] * mm_nt(cmat, state_b)
    inner = b["dx"][q]
    outer = b["tail"][q] * mm_nt(bmat, grad_b)
    dxs = inner + outer
    db = b["dbc"][q, :, pl.ds(0, STATE)] + mm(b["xt"][q], grad_b)
    dc = b["dbc"][q, :, pl.ds(STATE, STATE)] + mm(b["ed"][q], state_b)

    def by_head(v):
        return mm(v.astype(BF), sums)

    late = by_head(dy * y - xs * inner).astype(BF)
    early = by_head(xs * outer).astype(BF)
    decayed = b["eR"][q] * state
    across = jnp.sum(mm_tn((decayed * grad).astype(BF), sums), axis=0, keepdims=True)
    dl = mm_tn(tri, late) + mm(tri, early) - early.astype(F32) + across
    ddelta = by_head(x * dxs) - rate * dl
    b["sin"][...] = decayed + b["fresh"][q]
    put(q, y, dexp * dxs, db, dc, ddelta)


def kernel(tok_hbm, cot_hbm, pm, ps, pt, bias_s, rate_s, skip_s, gated_o, ig_o, gm_o, gsh_o, gst_o, m):
    seq, mp = lax.axis_index("seq"), lax.axis_index("mp")
    core = lax.rem(mp, 2)
    chip = mp // 2
    partner = mp + 1 - 2 * core
    plane = seq // 4
    low = lax.rem(seq, 2)

    load_tok = pltpu.make_async_copy(tok_hbm, m["tok"], m["s_local"].at[0])
    load_cot = pltpu.make_async_copy(cot_hbm, m["cot"], m["s_local"].at[1])
    load_tok.start()
    load_cot.start()

    barrier = pltpu.get_barrier_semaphore()

    def greet_seq(d):
        pl.semaphore_signal(
            barrier, inc=1, device_id={"seq": lax.rem(seq + d, SEQ)}, device_id_type=MESH
        )

    def greet_mp(d):
        pl.semaphore_signal(barrier, inc=1, device_id={"mp": lax.rem(mp + d, MP)}, device_id_type=MESH)

    fori(1, SEQ, greet_seq)
    fori(1, MP, greet_mp)

    wp, swp = m["wp"], m["swp"]
    wp[:, pl.ds(0, 256)] = pm[:, 0, :]
    wp[:, pl.ds(256, 256)] = pm[:, 1, :]
    wp[:, pl.ds(512, 128)] = ps[:, 0, :]
    wp[:, pl.ds(640, 128)] = ps[:, 1, :]
    at, lane = iota((SHARD, LANES), 0), iota((SHARD, LANES), 1)
    place = jnp.where(lane == at + SHARD * low, 1.0, 0.0).astype(BF)
    shifted = mm(pt[...], place).astype(BF)
    swp[...] = jnp.concatenate([shifted, shifted, jnp.zeros((8, LANES), BF)], axis=0)
    pl.semaphore_wait(barrier, SEQ + MP - 2)

    def w_rows(k):
        return m["w"].at[pl.ds(pl.multiple_of(k * SHARD, SHARD), SHARD)]

    send_w = SeqExchange(lambda p: wp, w_rows, sems(m["s_w"]))
    send_sw = SeqExchange(lambda p: swp, lambda k: m["sw_rx"].at[k], sems(m["s_sw"]))
    send_w.start()
    send_sw.start()
    m["w"][pl.ds(pl.multiple_of(seq * SHARD, SHARD), SHARD)] = wp[...]
    m["sw_rx"][seq] = swp[...]

    i, j = iota((CHUNK, CHUNK), 0), iota((CHUNK, CHUNK), 1)
    m["tri"][0] = jnp.where(i >= j, 1.0, 0.0).astype(BF)
    it, jt = (i & 15) * 16 + (i >> 4), (j & 15) * 16 + (j >> 4)
    m["tri"][1] = jnp.where(it >= jt, 1.0, 0.0).astype(BF)
    m["sw"][...] = jnp.zeros((LANES, DM), BF)
    m["R"]["RC"][...] = jnp.zeros((INNER, STATE), F32)
    m["T"]["RC"][...] = jnp.zeros((INNER, STATE), F32)
    m["lacc"][...] = jnp.zeros((CHUNK, LANES), F32)

    head_l = iota((1, LANES), 1)
    head_c = iota((1, INNER), 1) >> 6

    def lanes_of(value):
        v = jnp.zeros((1, LANES), F32)
        for h in range(HEADS):
            v = jnp.where((head_l < 8) & ((head_l & 3) == h), value(h), v)
        return v

    def features_of(value):
        v = jnp.zeros((1, INNER), F32)
        for h in range(HEADS):
            v = jnp.where(head_c == h, value(h), v)
        return v

    bias = lanes_of(lambda h: bias_s[h])
    rate_r, rate_t = lanes_of(lambda h: rate_s[0, h]), lanes_of(lambda h: rate_s[1, h])
    ratex_r, ratex_t = features_of(lambda h: rate_s[0, h]), features_of(lambda h: rate_s[1, h])
    skip = features_of(lambda h: skip_s[h])

    load_tok.wait()
    load_cot.wait()
    send_w.wait_recv()
    send_sw.wait_recv()
    for k in range(SEQ // 2):
        m["sw"][pl.ds(0, 16), pl.ds(k * LANES, LANES)] = m["sw_rx"][2 * k] + m["sw_rx"][2 * k + 1]

    def rows_of(q):
        return pl.ds(pl.multiple_of(q * CHUNK, CHUNK), CHUNK)

    def rest(v):
        return v.reshape(4, WID, LANES)

    send_pay = SeqExchange(lambda p: m["pay"].at[p], lambda k: m["trx"].at[k], sems(m["s_pay"]))

    def start_four(exchange, q):
        def one(n):
            d = lax.rem(4 * q + n - seq + SEQ, SEQ)

            @pl.when(d != 0)
            def _():
                exchange.copy(d).start()

        fori(0, 4, one)

    def project(n):
        q = lax.rem(plane + n, 4)
        rows = rows_of(q)
        u = m["tok"][rows, :]
        four = pl.ds(4 * q, 4)

        def put(block, v):
            v = v.astype(BF)
            for k in range(v.shape[1] // LANES):
                m["pay"][four, pl.ds((block + k) * WID, WID), :] = rest(v[:, k * LANES : (k + 1) * LANES])

        z = mm(u, m["w"][:, pl.ds(256, 256)]).astype(BF)
        m["z"][rows, :] = z
        zf = z.astype(F32)
        gate = zf * jax.nn.sigmoid(zf)
        put(BY, m["cot"][rows, :].astype(F32) * gate)
        put(BX, mm(u, m["w"][:, pl.ds(0, 256)]))
        put(BB, mm(u, m["w"][:, pl.ds(512, 256)]))
        raw = mm_nt(u, m["sw"][...]) + bias
        m["sraw"][rows, :] = raw
        pair = as_pair(jnp.maximum(raw, 0.0) + jnp.log1p(jnp.exp(-jnp.abs(raw))))
        m["lp"][rows, :] = pair
        folded = jnp.zeros((64, LANES), F32)
        for g in range(4):
            part = rest(pair)[:, g * COLS : (g + 1) * COLS, :].reshape(64, LANES)
            folded += mm(part, pair_place(8 * g))
        m["pay"][four, pl.ds(ROWS_L, COLS), :] = folded.astype(BF).reshape(4, COLS, LANES)
        start_four(send_pay, q)

    fori(0, CHUNKS, project)
    m["trx"][seq] = m["pay"][seq]

    def load_r(block, q):
        return m["pay"][pl.ds(4 * q, 4), pl.ds(block * WID, WID), :].reshape(CHUNK, LANES)

    def pair_r(q):
        return m["lp"][rows_of(q), :], 0

    def cols_of(block, q):
        return pl.ds(pl.multiple_of(block * WID + q * COLS, COLS), COLS)

    def load_t(block, q):
        return m["trx"][:, cols_of(block, q), :].reshape(CHUNK, LANES)

    def pair_t(q):
        return m["trx"][:, pl.ds(ROWS_L, COLS), :].reshape(CHUNK, LANES), 8 * q

    def pieces_exchange(source, landing, sem):
        return SeqExchange(lambda p: source.at[p], lambda k: landing.at[k], sems(sem))

    r, t = m["R"], m["T"]
    tri_r, tri_t = m["tri"].at[0], m["tri"].at[1]

    def start_pieces(b, sem):
        pack_states(b)
        e = pieces_exchange(b["st"], b["sx"], sem)
        e.start()
        b["sx"][seq] = b["st"][seq]
        return e

    def start_entering(b, sem):
        chain_states(b)
        e = pieces_exchange(b["sy"], b["sz"], sem)
        e.start()
        b["sz"][seq] = b["sy"][seq]
        return e

    fori(0, CHUNKS, lambda q: summary(r, tri_r[...], load_r, pair_r, rate_r, ratex_r, q))
    send_sr = start_pieces(r, m["s_sr"])
    fori(0, CHUNKS, lambda q: inside(r, tri_r[...], load_r, q))
    send_sr.wait_recv()
    send_ur = start_entering(r, m["s_ur"])

    send_pay.wait_recv()
    fori(0, CHUNKS, lambda q: summary(t, tri_t[...], load_t, pair_t, rate_t, ratex_t, q))
    send_st = start_pieces(t, m["s_st"])
    fori(0, 2, lambda q: inside(t, tri_t[...], load_t, q))
    send_st.wait_recv()
    send_ut = start_entering(t, m["s_ut"])
    fori(2, CHUNKS, lambda q: inside(t, tri_t[...], load_t, q))
    send_ut.wait_recv()
    entering_states(t)

    def put_t(q, y, dx, db, dc, dd):
        def put(block, v):
            v = v.astype(BF)
            for k in range(v.shape[1] // LANES):
                part = v[:, k * LANES : (k + 1) * LANES]
                m["bpay"][:, cols_of(block + k, q), :] = part.reshape(SEQ, COLS, LANES)

        put(BX, y)
        put(BY, dx)
        put(BB, db)
        put(BC, dc)
        m["lacc"][...] += mm(as_pair(dd), pair_place(8 * q))

    fori(0, CHUNKS, lambda q: outside(t, tri_t[...], load_t, pair_t, rate_t, q, put_t))
    m["bpay"][:, pl.ds(ROWS_L, COLS), :] = m["lacc"][...].astype(BF).reshape(SEQ, COLS, LANES)
    send_back = SeqExchange(lambda p: m["bpay"].at[p], lambda k: m["brx"].at[k], sems(m["s_back"]))
    send_back.start()
    m["brx"][seq] = m["bpay"][seq]

    send_ur.wait_recv()
    entering_states(r)

    def put_r(q, y, dx, db, dc, dd):
        r["y"][q] = y
        r["dx"][q] = dx
        r["dbc"][q, :, pl.ds(0, STATE)] = db
        r["dbc"][q, :, pl.ds(STATE, STATE)] = dc
        r["dd"][q] = dd

    fori(0, CHUNKS, lambda q: outside(r, tri_r[...], load_r, pair_r, rate_r, q, put_r))
    send_back.wait_recv()

    def back(block, q):
        return m["brx"][pl.ds(4 * q, 4), pl.ds(block * WID, WID), :].reshape(CHUNK, LANES)

    def combine(q):
        rows = rows_of(q)
        x = wide(load_r, BX, q).astype(F32)
        dy = wide(load_r, BY, q).astype(F32)
        z = m["z"][rows, :].astype(F32)
        cot = m["cot"][rows, :].astype(F32)
        y = r["y"][q] + wide(back, BX, q).astype(F32) + skip * x
        sigma = jax.nn.sigmoid(z)
        gated_o[rows, :] = (y * (z * sigma)).astype(BF)
        m["g"][rows, pl.ds(256, 256)] = (cot * y * sigma * (1.0 + z * (1.0 - sigma))).astype(BF)
        m["g"][rows, pl.ds(0, 256)] = (r["dx"][q] + wide(back, BY, q).astype(F32) + skip * dy).astype(BF)
        m["dbp"][rows, :] = (r["dbc"][q] + wide(back, BB, q).astype(F32)).astype(BF)
        folded = m["brx"][pl.ds(4 * q, 4), pl.ds(ROWS_L, COLS), :].reshape(64, LANES)
        parts = [mm(folded, pair_merge(8 * g)).reshape(4, COLS, LANES) for g in range(4)]
        dd = r["dd"][q] + jnp.concatenate(parts, axis=1).reshape(CHUNK, LANES)
        dstep = dd * jax.nn.sigmoid(m["sraw"][rows, :])
        m["dst"][rows, :] = jnp.where(iota((CHUNK, LANES), 1) < HEADS, dstep, 0.0).astype(BF)

    part = TOK // MP

    def part_rows(k):
        return pl.ds(pl.multiple_of(k * part, part), part)

    def mp_peer(d):
        return lax.rem(mp + d, MP)

    def mr_copy(d):
        peer = mp_peer(d)
        return mp_copy(
            m["dbp"].at[part_rows(peer)], m["mrx"].at[mp], m["s_mr"].at[0, d], m["s_mr"].at[1, d], peer
        )

    def mr_arrival(d):
        origin = lax.rem(mp - d + MP, MP)
        return mp_copy(
            m["mrx"].at[origin], m["mrx"].at[origin], m["s_mr"].at[0, d], m["s_mr"].at[1, d], origin
        )

    def pair_copy(k, q):
        rows = rows_of(q)
        return mp_copy(
            m["ip"].at[2 * k + 1 - core, rows],
            m["prx"].at[k, rows],
            m["s_pair"].at[0, k, q],
            m["s_pair"].at[1, k, q],
            partner,
        )

    def finish(n):
        q = lax.rem(chip + n, 4)
        combine(q)
        for k in range(2):
            d = lax.rem(2 * q + k - mp + MP, MP)

            @pl.when(d != 0)
            def _():
                mr_copy(d).start()

        rows = rows_of(q)
        g = m["g"][rows, :]
        ds = m["dst"][rows, :]
        for c in range(4):
            cols = pl.ds(c * 256, 256)
            v = mm_nt(g, m["w"][cols, pl.ds(0, 512)]) + mm(ds, m["sw"][:, cols])
            v = v.astype(BF)
            m["ip"][2 * c, rows, :] = v[:, :LANES]
            m["ip"][2 * c + 1, rows, :] = v[:, LANES:]
        fori(0, 4, lambda k: pair_copy(k, q).start())

    fori(0, CHUNKS, finish)
    m["mrx"][mp] = m["dbp"][part_rows(mp), :]

    def z_peer(d):
        return lax.rem(chip + d, 4)

    def z_copy(d):
        return mp_copy(
            m["zs"].at[z_peer(d)],
            m["zrx"].at[chip],
            m["s_z"].at[0, d],
            m["s_z"].at[1, d],
            2 * z_peer(d) + core,
        )

    def z_arrival(d):
        origin = lax.rem(chip - d + 4, 4)
        return mp_copy(
            m["zrx"].at[origin],
            m["zrx"].at[origin],
            m["s_z"].at[0, d],
            m["s_z"].at[1, d],
            2 * origin + core,
        )

    def pair_sum(k):
        fori(0, CHUNKS, lambda q: pair_copy(k, q).wait_recv())
        m["zs"][k] = (m["ip"][2 * k + core].astype(F32) + m["prx"][k].astype(F32)).astype(BF)

    def pair_send(d):
        pair_sum(z_peer(d))
        z_copy(d).start()

    fori(1, 4, pair_send)
    pair_sum(chip)
    m["zrx"][chip] = m["zs"][chip]

    fori(1, MP, lambda d: mr_arrival(d).wait_recv())
    total = m["mrx"][0].astype(F32)
    for k in range(1, MP):
        total += m["mrx"][k].astype(F32)
    m["dbf"][part_rows(mp), :] = total.astype(BF)

    def ma_copy(d):
        return mp_copy(
            m["dbf"].at[part_rows(mp)],
            m["dbf"].at[part_rows(mp)],
            m["s_ma"].at[0, d],
            m["s_ma"].at[1, d],
            mp_peer(d),
        )

    def ma_arrival(d):
        origin = lax.rem(mp - d + MP, MP)
        return mp_copy(
            m["dbf"].at[part_rows(origin)],
            m["dbf"].at[part_rows(origin)],
            m["s_ma"].at[0, d],
            m["s_ma"].at[1, d],
            origin,
        )

    fori(1, MP, lambda d: ma_copy(d).start())

    def shard_rows(ref):
        return lambda p: ref.at[pl.ds(pl.multiple_of(p * SHARD, SHARD), SHARD)]

    send_gp = SeqExchange(shard_rows(m["gp"]), lambda k: m["gp_rx"].at[k], sems(m["s_gp"]))
    send_gs = SeqExchange(lambda p: m["gs"].at[p // 2], lambda k: m["gs_rx"].at[k], sems(m["s_gs"]))
    send_gq = SeqExchange(shard_rows(m["gq"]), lambda k: m["gq_rx"].at[k], sems(m["s_gq"]))

    def grads(n):
        k = lax.rem(plane + n, 4)
        cols = rows_of(k)
        u = m["tok"][:, cols]
        m["gp"][cols, :] = mm_tn(u, m["g"][...]).astype(BF)
        gs = mm_tn(m["dst"][...], u)[:16].astype(BF)
        m["gs"][2 * k] = gs[:, :LANES]
        m["gs"][2 * k + 1] = gs[:, LANES:]
        start_four(send_gp, k)
        start_four(send_gs, k)

    fori(0, 4, grads)
    own = pl.ds(pl.multiple_of(seq * SHARD, SHARD), SHARD)
    m["gp_rx"][seq] = m["gp"][own, :]
    m["gs_rx"][seq] = m["gs"][seq // 2]

    fori(1, MP, lambda d: ma_arrival(d).wait_recv())

    def shared_grads(n):
        k = lax.rem(plane + n, 4)
        cols = rows_of(k)
        m["gq"][cols, :] = mm_tn(m["tok"][:, cols], m["dbf"][...]).astype(BF)
        start_four(send_gq, k)

    fori(0, 4, shared_grads)
    m["gq_rx"][seq] = m["gq"][own, :]

    w_mine = m["w"][part_rows(mp), pl.ds(512, 256)]
    fori(1, 4, lambda d: z_arrival(d).wait_recv())

    def input_sum(q):
        rows = rows_of(q)
        v = mm_nt(m["dbf"][rows, :], w_mine)
        for k in range(4):
            v += m["zrx"][k, rows, :].astype(F32)
        ig_o[rows, :] = v.astype(BF)

    fori(0, CHUNKS, input_sum)

    def total_of(ref):
        v = ref[0].astype(F32)
        for k in range(1, SEQ):
            v += ref[k].astype(F32)
        return v

    send_gp.wait_recv()
    main = total_of(m["gp_rx"])
    gm_o[:, 0, :] = main[:, :INNER]
    gm_o[:, 1, :] = main[:, INNER:]
    send_gs.wait_recv()
    step = total_of(m["gs_rx"])
    gst_o[...] = jnp.where(low == 0, step[:HEADS, :SHARD], step[:HEADS, SHARD:])
    send_gq.wait_recv()
    shared = total_of(m["gq_rx"])
    gsh_o[:, 0, :] = shared[:, :STATE]
    gsh_o[:, 1, :] = shared[:, STATE:]

    sent = (send_w, send_sw, send_pay, send_sr, send_ur, send_st, send_ut, send_back, send_gp, send_gs, send_gq)
    for e in sent:
        e.wait_send()
    fori(1, MP, lambda d: mr_copy(d).wait_send())
    fori(1, MP, lambda d: ma_copy(d).wait_send())
    for k in range(4):
        fori(0, CHUNKS, lambda q: pair_copy(k, q).wait_send())
    fori(1, 4, lambda d: z_copy(d).wait_send())


def hand_over(*refs):
    n = (len(refs) - 1) // 2
    copies = [pltpu.make_async_copy(refs[k], refs[n + k], refs[-1].at[k]) for k in range(n)]
    for c in copies:
        c.start()
    for c in copies:
        c.wait()


def body(tokens, proj_main, proj_shared, proj_step, step_bias, decay_rate, skip_gain, cotangent):
    vm = pl.BlockSpec(memory_space=pltpu.VMEM)
    sm = pl.BlockSpec(memory_space=pltpu.SMEM)
    hbm = pl.BlockSpec(memory_space=pl.ANY)
    shapes = (
        jax.ShapeDtypeStruct((TOK, INNER), BF),
        jax.ShapeDtypeStruct((TOK, LANES), BF),
        jax.ShapeDtypeStruct((SHARD, 2, INNER), F32),
        jax.ShapeDtypeStruct((SHARD, 2, STATE), F32),
        jax.ShapeDtypeStruct((HEADS, SHARD), F32),
    )
    results = pl.pallas_call(
        kernel,
        out_shape=shapes,
        in_specs=[hbm, hbm, vm, vm, vm, sm, sm, sm],
        out_specs=(vm,) * 5,
        scratch_shapes=[main_scratch()],
        compiler_params=pltpu.CompilerParams(
            collective_id=0, has_side_effects=True, vmem_limit_bytes=62 * 1024 * 1024
        ),
    )(
        tokens.reshape(TOK, DM),
        cotangent.reshape(TOK, INNER),
        proj_main,
        proj_shared,
        proj_step.T,
        step_bias,
        decay_rate,
        skip_gain,
    )
    gated, ig, gm, gsh, gst = pl.pallas_call(
        hand_over,
        out_shape=shapes,
        in_specs=[hbm] * 5,
        out_specs=(hbm,) * 5,
        scratch_shapes=[pltpu.SemaphoreType.DMA((5,))],
    )(*results)
    return (
        gated.reshape(1, 16, WID, INNER),
        ig.reshape(1, 16, WID, LANES),
        gm,
        gsh,
        gst.T,
    )


def solution(mesh):
    placed = (
        P("seq", None, None, None),
        P("seq", None, "mp"),
        P("seq", None, None),
        P("seq", "mp"),
        P("mp"),
        P(None, "mp"),
        P("mp"),
        P("seq", None, None, "mp"),
    )
    return jax.shard_map(
        body,
        mesh=mesh,
        in_specs=placed,
        out_specs=(
            P("seq", None, None, "mp"),
            P("seq", None, None, "mp"),
            P("seq", None, "mp"),
            P("seq", None, None),
            P("seq", "mp"),
        ),
        check_vma=False,
    )
```

```python
import jax
import jax.numpy as jnp
from jax import lax
from jax.experimental import pallas as pl
from jax.experimental.pallas import tpu as pltpu
from jax.sharding import PartitionSpec as P

MESH = pl.DeviceIdType.MESH
BF = jnp.bfloat16
F32 = jnp.float32

SEQ = 16
MP = 8
TOK = 1024
WID = 64
DM = 1024
INNER = 256
HEADS = 4
STATE = 128
LANES = 128
CHUNK = 256
CHUNKS = TOK // CHUNK
COLS = CHUNK // SEQ
SHARD = DM // SEQ
BX, BY, BB, BC, ROWS_L, ROWS = 0, 2, 4, 5, 384, 400
PIECE = STATE // SEQ
HALF = 3 * LANES
LOG2E = 1.4426950408889634


def iota(shape, axis):
    return lax.broadcasted_iota(jnp.int32, shape, axis)


def mm(a, b):
    return lax.dot_general(a, b, (((1,), (0,)), ((), ())), preferred_element_type=F32)


def mm_nt(a, b):
    return lax.dot_general(a, b, (((1,), (1,)), ((), ())), preferred_element_type=F32)


def mm_tn(a, b):
    return lax.dot_general(a, b, (((0,), (0,)), ((), ())), preferred_element_type=F32)


def halves(v):
    hi = v.astype(BF)
    return hi, (v - hi.astype(F32)).astype(BF)


def as_pair(v):
    lane = iota(v.shape, 1)
    hi = v.astype(BF).astype(F32)
    return jnp.where(lane < 4, hi, jnp.where(lane < 8, v - hi, 0.0)).astype(BF)


def fori(low, high, step):
    def run(i, carry):
        step(i)
        return carry

    lax.fori_loop(low, high, run, 0)


class SeqExchange:
    def __init__(self, source, landing, sems):
        self.source, self.landing = source, landing
        self.send, self.recv = sems
        self.me = lax.axis_index("seq")

    def copy(self, d):
        peer = lax.rem(self.me + d, SEQ)
        return pltpu.make_async_remote_copy(
            src_ref=self.source(peer),
            dst_ref=self.landing(self.me),
            send_sem=self.send.at[d],
            recv_sem=self.recv.at[d],
            device_id={"seq": peer},
            device_id_type=MESH,
        )

    def arrival(self, d):
        origin = lax.rem(self.me - d + SEQ, SEQ)
        return pltpu.make_async_remote_copy(
            src_ref=self.landing(origin),
            dst_ref=self.landing(origin),
            send_sem=self.send.at[d],
            recv_sem=self.recv.at[d],
            device_id={"seq": origin},
            device_id_type=MESH,
        )

    def start(self):
        fori(1, SEQ, lambda d: self.copy(d).start())

    def wait_recv(self):
        fori(1, SEQ, lambda d: self.arrival(d).wait_recv())

    def wait_send(self):
        fori(1, SEQ, lambda d: self.copy(d).wait_send())


class Ring:
    def __init__(self, me, to, whole, part, sems):
        self.whole, self.part, self.sems, self.to = whole, part, sems, to
        self.me, self.right, self.left = me, lax.rem(me + 1, 4), lax.rem(me + 3, 4)
        self.far = lax.rem(me + 2, 4)

    def copy(self, ref, k, peer):
        return pltpu.make_async_remote_copy(
            src_ref=ref,
            dst_ref=ref,
            send_sem=self.sems.at[0, k],
            recv_sem=self.sems.at[1, k],
            device_id={"seq": self.to(peer)},
            device_id_type=MESH,
        )

    def start(self):
        self.copy(self.whole(self.me), 0, self.right).start()
        self.copy(self.whole(self.me), 1, self.left).start()

    def forward(self):
        self.copy(self.whole(self.left), 0, self.left).wait_recv()
        self.copy(self.part(self.left, 0), 2, self.right).start()
        self.copy(self.whole(self.right), 1, self.right).wait_recv()
        self.copy(self.part(self.right, 1), 3, self.left).start()

    def finish(self):
        self.copy(self.part(self.far, 0), 2, self.left).wait_recv()
        self.copy(self.part(self.far, 1), 3, self.right).wait_recv()

    def wait_send(self):
        self.copy(self.whole(self.me), 0, self.right).wait_send()
        self.copy(self.whole(self.me), 1, self.left).wait_send()
        self.copy(self.part(self.left, 0), 2, self.right).wait_send()
        self.copy(self.part(self.right, 1), 3, self.left).wait_send()


def mp_copy(source, landing, send, recv, peer):
    return pltpu.make_async_remote_copy(
        src_ref=source,
        dst_ref=landing,
        send_sem=send,
        recv_sem=recv,
        device_id={"mp": peer},
        device_id_type=MESH,
    )


def scan_scratch():
    v = pltpu.VMEM
    return dict(
        xs=v((CHUNKS, CHUNK, INNER), BF),
        xt=v((CHUNKS, CHUNK, INNER), BF),
        ed=v((CHUNKS, CHUNK, INNER), BF),
        er=v((CHUNKS, CHUNK, INNER), F32),
        tail=v((CHUNKS, CHUNK, INNER), F32),
        rcol=v((CHUNKS, CHUNK, LANES), F32),
        fresh=v((CHUNKS, STATE, INNER), F32),
        back=v((CHUNKS, STATE, INNER), F32),
        eR=v((CHUNKS, 8, INNER), F32),
        RC=v((8, INNER), F32),
        st=v((SEQ, 4 * PIECE, INNER), BF),
        sx=v((SEQ, 4 * PIECE, INNER), BF),
        sy=v((SEQ, 2 * PIECE, INNER), BF),
        sz=v((SEQ, 2 * PIECE, INNER), BF),
        y=v((CHUNKS, CHUNK, INNER), F32),
        dx=v((CHUNKS, CHUNK, INNER), F32),
        dbc=v((CHUNKS, CHUNK, 2 * STATE), F32),
        dd=v((CHUNKS, CHUNK, LANES), F32),
        gin=v((CHUNKS, STATE, INNER), F32),
        sin=v((STATE, INNER), F32),
    )


def main_scratch():
    v = pltpu.VMEM
    dma = pltpu.SemaphoreType.DMA
    seq_sems = lambda: dma((2, SEQ))
    return dict(
        tok=v((TOK, DM), BF),
        cot=v((TOK, INNER), BF),
        wa=v((4, 4, SHARD, HALF), BF),
        wb=v((4, 4, SHARD, HALF), BF),
        sw_rx=v((SEQ, 16, LANES), BF),
        sw=v((LANES, DM), BF),
        z=v((TOK, INNER), BF),
        sraw=v((TOK, LANES), F32),
        pay=v((SEQ, ROWS, LANES), BF),
        trx=v((SEQ, ROWS, LANES), BF),
        bpay=v((SEQ, ROWS, LANES), BF),
        brx=v((SEQ, ROWS, LANES), BF),
        tri=v((4, CHUNK, CHUNK), BF),
        lp=v((TOK, LANES), BF),
        lacc=v((CHUNK, LANES), F32),
        swp=v((16, LANES), BF),
        R=scan_scratch(),
        T=scan_scratch(),
        g=v((TOK, 2 * INNER), BF),
        dst=v((TOK, LANES), BF),
        dbp=v((TOK, 2 * STATE), BF),
        mrx=v((MP, TOK // MP, 2 * STATE), BF),
        dbf=v((TOK, 2 * STATE), BF),
        gp=v((DM, 2 * INNER), BF),
        gq=v((DM, 2 * STATE), BF),
        gs=v((MP, 16, LANES), BF),
        gp_rx=v((SEQ, SHARD, 2 * INNER), BF),
        gq_rx=v((SEQ, SHARD, 2 * STATE), BF),
        gs_rx=v((SEQ, 16, LANES), BF),
        ip=v((MP, TOK, LANES), BF),
        prx=v((4, TOK, LANES), BF),
        zs=v((4, TOK, LANES), BF),
        zrx=v((4, TOK, LANES), BF),
        s_local=dma((4,)),
        s_w=dma((4, 2, 4)),
        s_sw=seq_sems(),
        s_pay=seq_sems(),
        s_sr=seq_sems(),
        s_st=seq_sems(),
        s_ur=seq_sems(),
        s_ut=seq_sems(),
        s_back=seq_sems(),
        s_back2=seq_sems(),
        s_gp=seq_sems(),
        s_gq=seq_sems(),
        s_gs=seq_sems(),
        s_mr=dma((2, MP)),
        s_ma=dma((2, MP)),
        s_pair=dma((2, 4, CHUNKS)),
        s_z=dma((2, 4)),
    )


def sems(ref):
    return ref.at[0], ref.at[1]


def head_sum():
    c, h = iota((INNER, LANES), 0), iota((INNER, LANES), 1)
    return jnp.where((h < 8) & ((h & 3) == (c >> 6)), 1.0, 0.0).astype(BF)


def pair_expand(shift):
    k, c = iota((LANES, INNER), 0) - shift, iota((LANES, INNER), 1)
    return jnp.where((k >= 0) & (k < 8) & ((k & 3) == (c >> 6)), 1.0, 0.0).astype(BF)


def pair_merge(shift):
    k, h = iota((LANES, LANES), 0) - shift, iota((LANES, LANES), 1)
    return jnp.where((k >= 0) & (k < 8) & (h < 8) & ((k & 3) == (h & 3)), 1.0, 0.0).astype(BF)


def pair_place(shift):
    k, lane = iota((LANES, LANES), 0), iota((LANES, LANES), 1)
    return jnp.where((k < 8) & (lane == k + shift), 1.0, 0.0).astype(BF)


def wide(load, block, q):
    return jnp.concatenate([load(block, q), load(block + 1, q)], axis=1)


def summary(b, tri, load, pair_of, rate, ratex, q):
    x = wide(load, BX, q).astype(F32)
    dy = wide(load, BY, q).astype(F32)
    pair, shift = pair_of(q)
    dexp = mm(pair, pair_expand(shift))
    logs = (-dexp * ratex).astype(BF)
    rexp = mm(tri, logs)
    b["rcol"][q] = mm(tri, (-mm(pair, pair_merge(shift)) * rate).astype(BF))
    total = jnp.sum(logs.astype(F32), axis=0, keepdims=True)
    er = jnp.exp2(rexp)
    tail = jnp.exp2(jnp.minimum(total - rexp, 0.0))
    xs = (x * dexp).astype(BF)
    xt = (xs.astype(F32) * tail).astype(BF)
    ed = (er * dy).astype(BF)
    b["er"][q] = er
    b["tail"][q] = tail
    b["xs"][q] = xs
    b["xt"][q] = xt
    b["ed"][q] = ed
    b["fresh"][q] = mm_tn(load(BB, q), xt)
    b["back"][q] = mm_tn(load(BC, q), ed)
    rows = jnp.broadcast_to(total, (8, INNER))
    b["eR"][q] = jnp.exp2(rows)
    b["RC"][...] += rows


def pack_states(b):
    e = [b["eR"][q][:1] for q in range(CHUNKS)]
    end = b["fresh"][0]
    for q in range(1, CHUNKS):
        end = end * e[q] + b["fresh"][q]
    first = b["back"][CHUNKS - 1]
    for q in range(CHUNKS - 2, -1, -1):
        first = first * e[q] + b["back"][q]
    rc = b["RC"][...]
    hi = rc.astype(BF).astype(F32)
    logs = jnp.concatenate([hi, rc - hi], axis=0).astype(BF)
    pieces = [v.reshape(SEQ, PIECE, INNER) for v in (end, first)]
    b["st"][:, pl.ds(0, 2 * PIECE), :] = jnp.concatenate(pieces, axis=1).astype(BF)
    for k in range(SEQ):
        b["st"][k, pl.ds(2 * PIECE, 2 * PIECE)] = logs


def chain_states(b):
    own = [b["sx"][k, pl.ds(0, 2 * PIECE)].astype(F32) for k in range(SEQ)]
    logs = [b["sx"][k, pl.ds(2 * PIECE, 2 * PIECE)].astype(F32) for k in range(SEQ)]
    decay = [jnp.exp2(v[:PIECE] + v[PIECE:]) for v in logs]
    state = [jnp.zeros((PIECE, INNER), F32)]
    grad = [jnp.zeros((PIECE, INNER), F32)]
    for k in range(SEQ - 1):
        state.append(state[k] * decay[k] + own[k][:PIECE])
        n = SEQ - 1 - k
        grad.append(grad[k] * decay[n] + own[n][PIECE:])
    for k in range(SEQ):
        b["sy"][k] = jnp.concatenate([state[k], grad[SEQ - 1 - k]], axis=0).astype(BF)


def entering_states(b):
    both = b["sz"][...].astype(F32)
    b["sin"][...] = both[:, :PIECE, :].reshape(STATE, INNER)
    grad = both[:, PIECE:, :].reshape(STATE, INNER)
    for q in range(CHUNKS - 1, -1, -1):
        b["gin"][q] = grad
        if q > 0:
            grad = grad * b["eR"][q][:1] + b["back"][q]


def inside(b, tri, load, q):
    dy = wide(load, BY, q)
    bmat = load(BB, q)
    cmat = load(BC, q)
    xs = b["xs"][q]
    trif = tri.astype(F32)
    scores = mm_nt(cmat, bmat) * trif
    rcol = b["rcol"][q]
    rrow = rcol.T
    head = iota((CHUNK, INNER), 1) >> 6
    zero = jnp.zeros((), BF)
    y = jnp.zeros((CHUNK, INNER), F32)
    dxs = jnp.zeros((CHUNK, INNER), F32)
    pairs = jnp.zeros((CHUNK, CHUNK), F32)
    for h in range(HEADS):
        decay = jnp.exp2(jnp.minimum(rcol[:, h : h + 1] - rrow[h : h + 1, :], 0.0))
        m = (decay * scores).astype(BF)
        dyh = jnp.where(head == h, dy, zero)
        xsh = jnp.where(head == h, xs, zero)
        y += mm(m, xsh)
        dxs += mm_tn(m, dyh)
        pairs += decay * mm_nt(dyh, xs)
    pairs = (pairs * trif).astype(BF)
    b["y"][q] = y
    b["dx"][q] = dxs
    b["dbc"][q, :, pl.ds(0, STATE)] = mm_tn(pairs, cmat)
    b["dbc"][q, :, pl.ds(STATE, STATE)] = mm(pairs, bmat)


def outside(b, tri, tri_up, load, pair_of, rate, q, put):
    x = wide(load, BX, q).astype(F32)
    dy = wide(load, BY, q).astype(F32)
    bmat = load(BB, q)
    cmat = load(BC, q)
    pair, shift = pair_of(q)
    dexp = mm(pair, pair_expand(shift))
    xs = b["xs"][q].astype(F32)
    state = b["sin"][...]
    grad = b["gin"][q]
    state_b, grad_b = state.astype(BF), grad.astype(BF)
    sums = head_sum()
    y = b["y"][q] + b["er"][q] * mm(cmat, state_b)
    inner = b["dx"][q]
    outer = b["tail"][q] * mm(bmat, grad_b)
    dxs = inner + outer
    db = b["dbc"][q, :, pl.ds(0, STATE)] + mm_nt(b["xt"][q], grad_b)
    dc = b["dbc"][q, :, pl.ds(STATE, STATE)] + mm_nt(b["ed"][q], state_b)

    def by_head(v):
        return mm(v.astype(BF), sums)

    late = by_head(dy * y - xs * inner).astype(BF)
    early = by_head(xs * outer).astype(BF)
    decayed = b["eR"][q][:1] * state
    across = jnp.sum(decayed * grad, axis=0, keepdims=True)
    across = mm(jnp.broadcast_to(across, (16, INNER)).astype(BF), sums)[:1]
    dl = mm(tri_up, late) + mm(tri, early) - early.astype(F32) + across
    ddelta = by_head(x * dxs) - rate * dl
    b["sin"][...] = decayed + b["fresh"][q]
    put(q, y, dexp * dxs, db, dc, ddelta)


def kernel(tok_hbm, cot_hbm, pm, ps, pt, bias_s, rate_s, skip_s, gated_o, ig_o, gm_o, gsh_o, gst_o, m):
    seq, mp = lax.axis_index("seq"), lax.axis_index("mp")
    core = lax.rem(mp, 2)
    chip = mp // 2
    partner = mp + 1 - 2 * core
    plane, line = seq // 4, lax.rem(seq, 4)
    low = lax.rem(seq, 2)

    load_tok = pltpu.make_async_copy(tok_hbm, m["tok"], m["s_local"].at[0])
    load_cot = pltpu.make_async_copy(cot_hbm, m["cot"], m["s_local"].at[1])
    load_tok.start()
    load_cot.start()

    barrier = pltpu.get_barrier_semaphore()

    def greet_seq(d):
        pl.semaphore_signal(
            barrier, inc=1, device_id={"seq": lax.rem(seq + d, SEQ)}, device_id_type=MESH
        )

    def greet_mp(d):
        pl.semaphore_signal(barrier, inc=1, device_id={"mp": lax.rem(mp + d, MP)}, device_id_type=MESH)

    fori(1, SEQ, greet_seq)
    fori(1, MP, greet_mp)

    wa, wb, swp = m["wa"], m["wb"], m["swp"]
    wa[plane, line, :, pl.ds(0, 256)] = pm[:, 0, :]
    wb[plane, line, :, pl.ds(0, 256)] = pm[:, 1, :]
    wa[plane, line, :, pl.ds(256, 128)] = ps[:, 0, :]
    wb[plane, line, :, pl.ds(256, 128)] = ps[:, 1, :]
    at, lane = iota((SHARD, LANES), 0), iota((SHARD, LANES), 1)
    place = jnp.where(lane == at + SHARD * low, 1.0, 0.0).astype(BF)
    shifted = mm(pt[...], place).astype(BF)
    swp[...] = jnp.concatenate([shifted, shifted, jnp.zeros((8, LANES), BF)], axis=0)
    pl.semaphore_wait(barrier, SEQ + MP - 2)

    def along_x(k):
        return 4 * k + line

    def along_y(k):
        return 4 * plane + k

    half = SHARD // 2
    ring_a1 = Ring(plane, along_x, lambda k: wa.at[k, line], lambda k, n: wa.at[k, line, pl.ds(half * n, half)], m["s_w"].at[0])
    ring_b1 = Ring(line, along_y, lambda k: wb.at[plane, k], lambda k, n: wb.at[plane, k, pl.ds(half * n, half)], m["s_w"].at[1])
    ring_a2 = Ring(line, along_y, lambda k: wa.at[:, k], lambda k, n: wa.at[pl.ds(2 * n, 2), k], m["s_w"].at[2])
    ring_b2 = Ring(plane, along_x, lambda k: wb.at[k], lambda k, n: wb.at[k, pl.ds(2 * n, 2)], m["s_w"].at[3])
    rings = (ring_a1, ring_b1, ring_a2, ring_b2)
    ring_a1.start()
    ring_b1.start()
    send_sw = SeqExchange(lambda p: swp, lambda k: m["sw_rx"].at[k], sems(m["s_sw"]))
    send_sw.start()
    m["sw_rx"][seq] = swp[...]

    ring_a1.forward()
    ring_b1.forward()
    ring_a1.finish()
    ring_a2.start()
    ring_b1.finish()
    ring_b2.start()

    i, j = iota((CHUNK, CHUNK), 0), iota((CHUNK, CHUNK), 1)
    m["tri"][0] = jnp.where(i >= j, 1.0, 0.0).astype(BF)
    it, jt = (i & 15) * 16 + (i >> 4), (j & 15) * 16 + (j >> 4)
    m["tri"][1] = jnp.where(it >= jt, 1.0, 0.0).astype(BF)
    m["tri"][2] = jnp.where(i <= j, 1.0, 0.0).astype(BF)
    m["tri"][3] = jnp.where(it <= jt, 1.0, 0.0).astype(BF)
    m["sw"][...] = jnp.zeros((LANES, DM), BF)
    m["R"]["RC"][...] = jnp.zeros((8, INNER), F32)
    m["T"]["RC"][...] = jnp.zeros((8, INNER), F32)
    m["lacc"][...] = jnp.zeros((CHUNK, LANES), F32)

    head_l = iota((1, LANES), 1)
    head_c = iota((1, INNER), 1) >> 6

    def lanes_of(value):
        v = jnp.zeros((1, LANES), F32)
        for h in range(HEADS):
            v = jnp.where((head_l < 8) & ((head_l & 3) == h), value(h), v)
        return v

    def features_of(value):
        v = jnp.zeros((1, INNER), F32)
        for h in range(HEADS):
            v = jnp.where(head_c == h, value(h), v)
        return v

    bias = lanes_of(lambda h: bias_s[h])
    rate_r, rate_t = lanes_of(lambda h: rate_s[0, h]), lanes_of(lambda h: rate_s[1, h])
    ratex_r = features_of(lambda h: rate_s[0, h]) * LOG2E
    ratex_t = features_of(lambda h: rate_s[1, h]) * LOG2E
    skip = features_of(lambda h: skip_s[h])

    load_tok.wait()
    load_cot.wait()
    ring_a2.forward()
    ring_b2.forward()
    ring_a2.finish()
    ring_b2.finish()
    send_sw.wait_recv()
    for k in range(SEQ // 2):
        m["sw"][pl.ds(0, 16), pl.ds(k * LANES, LANES)] = m["sw_rx"][2 * k] + m["sw_rx"][2 * k + 1]

    def rows_of(q):
        return pl.ds(pl.multiple_of(q * CHUNK, CHUNK), CHUNK)

    def columns(ref, at, width):
        return ref[:, :, :, pl.ds(at, width)].reshape(DM, width)

    def rest(v):
        return v.reshape(4, WID, LANES)

    send_pay = SeqExchange(lambda p: m["pay"].at[p], lambda k: m["trx"].at[k], sems(m["s_pay"]))

    def start_four(exchange, q):
        def one(n):
            d = lax.rem(4 * q + n - seq + SEQ, SEQ)

            @pl.when(d != 0)
            def _():
                exchange.copy(d).start()

        fori(0, 4, one)

    def project(n):
        q = lax.rem(plane + n, 4)
        rows = rows_of(q)
        u = m["tok"][rows, :]
        four = pl.ds(4 * q, 4)

        def put(block, v):
            v = v.astype(BF)
            for k in range(v.shape[1] // LANES):
                m["pay"][four, pl.ds((block + k) * WID, WID), :] = rest(v[:, k * LANES : (k + 1) * LANES])

        z = mm(u, columns(wb, 0, 256)).astype(BF)
        m["z"][rows, :] = z
        zf = z.astype(F32)
        gate = zf * jax.nn.sigmoid(zf)
        put(BY, m["cot"][rows, :].astype(F32) * gate)
        put(BX, mm(u, columns(wa, 0, 256)))
        put(BB, mm(u, columns(wa, 256, 128)))
        put(BC, mm(u, columns(wb, 256, 128)))
        raw = mm_nt(u, m["sw"][...]) + bias
        m["sraw"][rows, :] = raw
        pair = as_pair(jnp.maximum(raw, 0.0) + jnp.log1p(jnp.exp(-jnp.abs(raw))))
        m["lp"][rows, :] = pair
        folded = jnp.zeros((64, LANES), F32)
        for g in range(4):
            part = rest(pair)[:, g * COLS : (g + 1) * COLS, :].reshape(64, LANES)
            folded += mm(part, pair_place(8 * g))
        m["pay"][four, pl.ds(ROWS_L, COLS), :] = folded.astype(BF).reshape(4, COLS, LANES)
        start_four(send_pay, q)

    fori(0, CHUNKS, project)
    m["trx"][seq] = m["pay"][seq]

    def load_r(block, q):
        return m["pay"][pl.ds(4 * q, 4), pl.ds(block * WID, WID), :].reshape(CHUNK, LANES)

    def pair_r(q):
        return m["lp"][rows_of(q), :], 0

    def cols_of(block, q):
        return pl.ds(pl.multiple_of(block * WID + q * COLS, COLS), COLS)

    def load_t(block, q):
        return m["trx"][:, cols_of(block, q), :].reshape(CHUNK, LANES)

    def pair_t(q):
        return m["trx"][:, pl.ds(ROWS_L, COLS), :].reshape(CHUNK, LANES), 8 * q

    def pieces_exchange(source, landing, sem):
        return SeqExchange(lambda p: source.at[p], lambda k: landing.at[k], sems(sem))

    r, t = m["R"], m["T"]
    tri_r, tri_t, up_r, up_t = (m["tri"].at[k] for k in range(4))

    def chunks(low, high, step):
        for q in range(low, high):
            step(q)


    def start_pieces(b, sem):
        pack_states(b)
        e = pieces_exchange(b["st"], b["sx"], sem)
        e.start()
        b["sx"][seq] = b["st"][seq]
        return e

    def start_entering(b, sem):
        chain_states(b)
        e = pieces_exchange(b["sy"], b["sz"], sem)
        e.start()
        b["sz"][seq] = b["sy"][seq]
        return e

    chunks(0, CHUNKS, lambda q: summary(r, tri_r[...], load_r, pair_r, rate_r * LOG2E, ratex_r, q))
    send_sr = start_pieces(r, m["s_sr"])
    chunks(0, CHUNKS, lambda q: inside(r, tri_r[...], load_r, q))
    send_sr.wait_recv()
    send_ur = start_entering(r, m["s_ur"])

    send_pay.wait_recv()
    chunks(0, CHUNKS, lambda q: summary(t, tri_t[...], load_t, pair_t, rate_t * LOG2E, ratex_t, q))
    send_st = start_pieces(t, m["s_st"])
    chunks(0, 2, lambda q: inside(t, tri_t[...], load_t, q))
    send_st.wait_recv()
    send_ut = start_entering(t, m["s_ut"])
    chunks(2, CHUNKS, lambda q: inside(t, tri_t[...], load_t, q))
    send_ut.wait_recv()
    entering_states(t)

    def put_t(q, y, dx, db, dc, dd):
        def put(block, v):
            v = v.astype(BF)
            for k in range(v.shape[1] // LANES):
                part = v[:, k * LANES : (k + 1) * LANES]
                at = 192 * (q // 2) + 32 * (block + k) + COLS * (q % 2)
                m["bpay"][:, pl.ds(at, COLS), :] = part.reshape(SEQ, COLS, LANES)

        put(BX, y)
        put(BY, dx)
        put(BB, db)
        put(BC, dc)
        m["lacc"][...] += mm(as_pair(dd), pair_place(8 * q))

    def half_back(at, count, sem):
        rows = pl.ds(at, count)
        return SeqExchange(lambda p: m["bpay"].at[p, rows], lambda k: m["brx"].at[k, rows], sems(sem))

    send_back = half_back(0, 192, m["s_back"])
    send_back2 = half_back(192, 208, m["s_back2"])
    chunks(0, 2, lambda q: outside(t, tri_t[...], up_t[...], load_t, pair_t, rate_t, q, put_t))
    send_back.start()
    chunks(2, 4, lambda q: outside(t, tri_t[...], up_t[...], load_t, pair_t, rate_t, q, put_t))
    m["bpay"][:, pl.ds(ROWS_L, COLS), :] = m["lacc"][...].astype(BF).reshape(SEQ, COLS, LANES)
    send_back2.start()
    m["brx"][seq] = m["bpay"][seq]

    send_ur.wait_recv()
    entering_states(r)

    def put_r(q, y, dx, db, dc, dd):
        r["y"][q] = y
        r["dx"][q] = dx
        r["dbc"][q, :, pl.ds(0, STATE)] = db
        r["dbc"][q, :, pl.ds(STATE, STATE)] = dc
        r["dd"][q] = dd

    chunks(0, CHUNKS, lambda q: outside(r, tri_r[...], up_r[...], load_r, pair_r, rate_r, q, put_r))
    send_back.wait_recv()
    send_back2.wait_recv()

    def back(block, q):
        parts = [m["brx"][pl.ds(4 * q, 4), pl.ds(192 * n + 32 * block, 32), :] for n in range(2)]
        return jnp.concatenate(parts, axis=1).reshape(CHUNK, LANES)

    def combine(q):
        rows = rows_of(q)
        x = wide(load_r, BX, q).astype(F32)
        dy = wide(load_r, BY, q).astype(F32)
        z = m["z"][rows, :].astype(F32)
        cot = m["cot"][rows, :].astype(F32)
        y = r["y"][q] + wide(back, BX, q).astype(F32) + skip * x
        sigma = jax.nn.sigmoid(z)
        gated_o[rows, :] = (y * (z * sigma)).astype(BF)
        m["g"][rows, pl.ds(256, 256)] = (cot * y * sigma * (1.0 + z * (1.0 - sigma))).astype(BF)
        m["g"][rows, pl.ds(0, 256)] = (r["dx"][q] + wide(back, BY, q).astype(F32) + skip * dy).astype(BF)
        m["dbp"][rows, :] = (r["dbc"][q] + wide(back, BB, q).astype(F32)).astype(BF)
        folded = m["brx"][pl.ds(4 * q, 4), pl.ds(ROWS_L, COLS), :].reshape(64, LANES)
        parts = [mm(folded, pair_merge(8 * g)).reshape(4, COLS, LANES) for g in range(4)]
        dd = r["dd"][q] + jnp.concatenate(parts, axis=1).reshape(CHUNK, LANES)
        dstep = dd * jax.nn.sigmoid(m["sraw"][rows, :])
        m["dst"][rows, :] = jnp.where(iota((CHUNK, LANES), 1) < HEADS, dstep, 0.0).astype(BF)

    part = TOK // MP

    def part_rows(k):
        return pl.ds(pl.multiple_of(k * part, part), part)

    def mp_peer(d):
        return lax.rem(mp + d, MP)

    def mr_copy(d):
        peer = mp_peer(d)
        return mp_copy(
            m["dbp"].at[part_rows(peer)], m["mrx"].at[mp], m["s_mr"].at[0, d], m["s_mr"].at[1, d], peer
        )

    def mr_arrival(d):
        origin = lax.rem(mp - d + MP, MP)
        return mp_copy(
            m["mrx"].at[origin], m["mrx"].at[origin], m["s_mr"].at[0, d], m["s_mr"].at[1, d], origin
        )

    def pair_copy(k, q):
        rows = rows_of(q)
        return mp_copy(
            m["ip"].at[2 * k + 1 - core, rows],
            m["prx"].at[k, rows],
            m["s_pair"].at[0, k, q],
            m["s_pair"].at[1, k, q],
            partner,
        )

    def finish(n):
        q = lax.rem(chip + n, 4)
        combine(q)
        for k in range(2):
            d = lax.rem(2 * q + k - mp + MP, MP)

            @pl.when(d != 0)
            def _():
                mr_copy(d).start()

        rows = rows_of(q)
        g = m["g"][rows, :]
        ds = m["dst"][rows, :]
        for c in range(4):
            cols = pl.ds(c * 256, 256)
            v = mm_nt(g[:, :256], wa[c, :, :, pl.ds(0, 256)].reshape(256, 256))
            v += mm_nt(g[:, 256:], wb[c, :, :, pl.ds(0, 256)].reshape(256, 256))
            v += mm(ds, m["sw"][:, cols])
            v = v.astype(BF)
            m["ip"][2 * c, rows, :] = v[:, :LANES]
            m["ip"][2 * c + 1, rows, :] = v[:, LANES:]
        fori(0, 4, lambda k: pair_copy(k, q).start())

    fori(0, CHUNKS, finish)
    m["mrx"][mp] = m["dbp"][part_rows(mp), :]

    def z_peer(d):
        return lax.rem(chip + d, 4)

    def z_copy(d):
        return mp_copy(
            m["zs"].at[z_peer(d)],
            m["zrx"].at[chip],
            m["s_z"].at[0, d],
            m["s_z"].at[1, d],
            2 * z_peer(d) + core,
        )

    def z_arrival(d):
        origin = lax.rem(chip - d + 4, 4)
        return mp_copy(
            m["zrx"].at[origin],
            m["zrx"].at[origin],
            m["s_z"].at[0, d],
            m["s_z"].at[1, d],
            2 * origin + core,
        )

    def pair_sum(k):
        fori(0, CHUNKS, lambda q: pair_copy(k, q).wait_recv())
        m["zs"][k] = (m["ip"][2 * k + core].astype(F32) + m["prx"][k].astype(F32)).astype(BF)

    def pair_send(d):
        pair_sum(z_peer(d))
        z_copy(d).start()

    fori(1, 4, pair_send)
    pair_sum(chip)
    m["zrx"][chip] = m["zs"][chip]

    fori(1, MP, lambda d: mr_arrival(d).wait_recv())
    total = m["mrx"][0].astype(F32)
    for k in range(1, MP):
        total += m["mrx"][k].astype(F32)
    m["dbf"][part_rows(mp), :] = total.astype(BF)

    def ma_copy(d):
        return mp_copy(
            m["dbf"].at[part_rows(mp)],
            m["dbf"].at[part_rows(mp)],
            m["s_ma"].at[0, d],
            m["s_ma"].at[1, d],
            mp_peer(d),
        )

    def ma_arrival(d):
        origin = lax.rem(mp - d + MP, MP)
        return mp_copy(
            m["dbf"].at[part_rows(origin)],
            m["dbf"].at[part_rows(origin)],
            m["s_ma"].at[0, d],
            m["s_ma"].at[1, d],
            origin,
        )

    fori(1, MP, lambda d: ma_copy(d).start())

    def shard_rows(ref):
        return lambda p: ref.at[pl.ds(pl.multiple_of(p * SHARD, SHARD), SHARD)]

    send_gp = SeqExchange(shard_rows(m["gp"]), lambda k: m["gp_rx"].at[k], sems(m["s_gp"]))
    send_gs = SeqExchange(lambda p: m["gs"].at[p // 2], lambda k: m["gs_rx"].at[k], sems(m["s_gs"]))
    send_gq = SeqExchange(shard_rows(m["gq"]), lambda k: m["gq_rx"].at[k], sems(m["s_gq"]))

    def grads(n):
        k = lax.rem(plane + n, 4)
        cols = rows_of(k)
        u = m["tok"][:, cols]
        m["gp"][cols, :] = mm_tn(u, m["g"][...]).astype(BF)
        gs = mm_tn(m["dst"][...], u)[:16].astype(BF)
        m["gs"][2 * k] = gs[:, :LANES]
        m["gs"][2 * k + 1] = gs[:, LANES:]
        start_four(send_gp, k)
        start_four(send_gs, k)

    fori(0, 4, grads)
    own = pl.ds(pl.multiple_of(seq * SHARD, SHARD), SHARD)
    m["gp_rx"][seq] = m["gp"][own, :]
    m["gs_rx"][seq] = m["gs"][seq // 2]

    fori(1, MP, lambda d: ma_arrival(d).wait_recv())

    def shared_grads(n):
        k = lax.rem(plane + n, 4)
        cols = rows_of(k)
        m["gq"][cols, :] = mm_tn(m["tok"][:, cols], m["dbf"][...]).astype(BF)
        start_four(send_gq, k)

    fori(0, 4, shared_grads)
    m["gq_rx"][seq] = m["gq"][own, :]

    mine = pl.ds(2 * core, 2)
    w_mine = [w[chip, mine, :, pl.ds(256, 128)].reshape(part, LANES) for w in (wa, wb)]
    fori(1, 4, lambda d: z_arrival(d).wait_recv())

    def input_sum(q):
        rows = rows_of(q)
        v = mm_nt(m["dbf"][rows, pl.ds(0, STATE)], w_mine[0])
        v += mm_nt(m["dbf"][rows, pl.ds(STATE, STATE)], w_mine[1])
        for k in range(4):
            v += m["zrx"][k, rows, :].astype(F32)
        ig_o[rows, :] = v.astype(BF)

    fori(0, CHUNKS, input_sum)

    def total_of(ref):
        v = ref[0].astype(F32)
        for k in range(1, SEQ):
            v += ref[k].astype(F32)
        return v

    send_gp.wait_recv()
    main = total_of(m["gp_rx"])
    gm_o[:, 0, :] = main[:, :INNER]
    gm_o[:, 1, :] = main[:, INNER:]
    send_gs.wait_recv()
    step = total_of(m["gs_rx"])
    gst_o[...] = jnp.where(low == 0, step[:HEADS, :SHARD], step[:HEADS, SHARD:])
    send_gq.wait_recv()
    shared = total_of(m["gq_rx"])
    gsh_o[:, 0, :] = shared[:, :STATE]
    gsh_o[:, 1, :] = shared[:, STATE:]

    sent = rings + (send_sw, send_pay, send_sr, send_ur, send_st, send_ut, send_back, send_back2, send_gp, send_gs, send_gq)
    for e in sent:
        e.wait_send()
    fori(1, MP, lambda d: mr_copy(d).wait_send())
    fori(1, MP, lambda d: ma_copy(d).wait_send())
    for k in range(4):
        fori(0, CHUNKS, lambda q: pair_copy(k, q).wait_send())
    fori(1, 4, lambda d: z_copy(d).wait_send())


def hand_over(*refs):
    n = len(refs) // 2
    for k in range(n):
        refs[n + k][...] = refs[k][...]


def body(tokens, proj_main, proj_shared, proj_step, step_bias, decay_rate, skip_gain, cotangent):
    vm = pl.BlockSpec(memory_space=pltpu.VMEM)
    sm = pl.BlockSpec(memory_space=pltpu.SMEM)
    hbm = pl.BlockSpec(memory_space=pl.ANY)
    shapes = (
        jax.ShapeDtypeStruct((TOK, INNER), BF),
        jax.ShapeDtypeStruct((TOK, LANES), BF),
        jax.ShapeDtypeStruct((SHARD, 2, INNER), F32),
        jax.ShapeDtypeStruct((SHARD, 2, STATE), F32),
        jax.ShapeDtypeStruct((HEADS, SHARD), F32),
    )
    results = pl.pallas_call(
        kernel,
        out_shape=shapes,
        in_specs=[hbm, hbm, vm, vm, vm, sm, sm, sm],
        out_specs=(vm,) * 5,
        scratch_shapes=[main_scratch()],
        compiler_params=pltpu.CompilerParams(
            collective_id=0, has_side_effects=True, vmem_limit_bytes=62 * 1024 * 1024
        ),
    )(
        tokens.reshape(TOK, DM),
        cotangent.reshape(TOK, INNER),
        proj_main,
        proj_shared,
        proj_step.T,
        step_bias,
        decay_rate,
        skip_gain,
    )
    gated, ig, gm, gsh, gst = pl.pallas_call(
        hand_over,
        out_shape=shapes,
        in_specs=[vm] * 5,
        out_specs=(vm,) * 5,
    )(*results)
    return (
        gated.reshape(1, 16, WID, INNER),
        ig.reshape(1, 16, WID, LANES),
        gm,
        gsh,
        gst.T,
    )


def solution(mesh):
    placed = (
        P("seq", None, None, None),
        P("seq", None, "mp"),
        P("seq", None, None),
        P("seq", "mp"),
        P("mp"),
        P(None, "mp"),
        P("mp"),
        P("seq", None, None, "mp"),
    )
    return jax.shard_map(
        body,
        mesh=mesh,
        in_specs=placed,
        out_specs=(
            P("seq", None, None, "mp"),
            P("seq", None, None, "mp"),
            P("seq", None, "mp"),
            P("seq", None, None),
            P("seq", "mp"),
        ),
        check_vma=False,
    )
```

```python
import jax
import jax.numpy as jnp
from jax import lax
from jax.experimental import pallas as pl
from jax.experimental.pallas import tpu as pltpu
from jax.sharding import PartitionSpec as P

MESH = pl.DeviceIdType.MESH
BF = jnp.bfloat16
F32 = jnp.float32

SEQ = 16
MP = 8
TOK = 1024
WID = 64
DM = 1024
INNER = 256
HEADS = 4
STATE = 128
LANES = 128
CHUNK = 256
CHUNKS = TOK // CHUNK
COLS = CHUNK // SEQ
SHARD = DM // SEQ
BX, BY, BB, BC, ROWS_L, ROWS = 0, 2, 4, 5, 256, 272
PIECE = STATE // SEQ
HALF = 3 * LANES
LOG2E = 1.4426950408889634


def iota(shape, axis):
    return lax.broadcasted_iota(jnp.int32, shape, axis)


def mm(a, b):
    return lax.dot_general(a, b, (((1,), (0,)), ((), ())), preferred_element_type=F32)


def mm_nt(a, b):
    return lax.dot_general(a, b, (((1,), (1,)), ((), ())), preferred_element_type=F32)


def mm_tn(a, b):
    return lax.dot_general(a, b, (((0,), (0,)), ((), ())), preferred_element_type=F32)


def halves(v):
    hi = v.astype(BF)
    return hi, (v - hi.astype(F32)).astype(BF)


def as_pair(v):
    lane = iota(v.shape, 1)
    hi = v.astype(BF).astype(F32)
    return jnp.where(lane < 4, hi, jnp.where(lane < 8, v - hi, 0.0)).astype(BF)


def fori(low, high, step):
    def run(i, carry):
        step(i)
        return carry

    lax.fori_loop(low, high, run, 0)


class SeqExchange:
    def __init__(self, source, landing, sems):
        self.source, self.landing = source, landing
        self.send, self.recv = sems
        self.me = lax.axis_index("seq")

    def copy(self, d):
        peer = lax.rem(self.me + d, SEQ)
        return pltpu.make_async_remote_copy(
            src_ref=self.source(peer),
            dst_ref=self.landing(self.me),
            send_sem=self.send.at[d],
            recv_sem=self.recv.at[d],
            device_id={"seq": peer},
            device_id_type=MESH,
        )

    def arrival(self, d):
        origin = lax.rem(self.me - d + SEQ, SEQ)
        return pltpu.make_async_remote_copy(
            src_ref=self.landing(origin),
            dst_ref=self.landing(origin),
            send_sem=self.send.at[d],
            recv_sem=self.recv.at[d],
            device_id={"seq": origin},
            device_id_type=MESH,
        )

    def start(self):
        fori(1, SEQ, lambda d: self.copy(d).start())

    def wait_recv(self):
        fori(1, SEQ, lambda d: self.arrival(d).wait_recv())

    def wait_send(self):
        fori(1, SEQ, lambda d: self.copy(d).wait_send())


class Ring:
    def __init__(self, me, to, whole, part, sems):
        self.whole, self.part, self.sems, self.to = whole, part, sems, to
        self.me, self.right, self.left = me, lax.rem(me + 1, 4), lax.rem(me + 3, 4)
        self.far = lax.rem(me + 2, 4)

    def copy(self, ref, k, peer):
        return pltpu.make_async_remote_copy(
            src_ref=ref,
            dst_ref=ref,
            send_sem=self.sems.at[0, k],
            recv_sem=self.sems.at[1, k],
            device_id={"seq": self.to(peer)},
            device_id_type=MESH,
        )

    def start(self):
        self.copy(self.whole(self.me), 0, self.right).start()
        self.copy(self.whole(self.me), 1, self.left).start()

    def forward(self):
        self.copy(self.whole(self.left), 0, self.left).wait_recv()
        self.copy(self.part(self.left, 0), 2, self.right).start()
        self.copy(self.whole(self.right), 1, self.right).wait_recv()
        self.copy(self.part(self.right, 1), 3, self.left).start()

    def finish(self):
        self.copy(self.part(self.far, 0), 2, self.left).wait_recv()
        self.copy(self.part(self.far, 1), 3, self.right).wait_recv()

    def wait_send(self):
        self.copy(self.whole(self.me), 0, self.right).wait_send()
        self.copy(self.whole(self.me), 1, self.left).wait_send()
        self.copy(self.part(self.left, 0), 2, self.right).wait_send()
        self.copy(self.part(self.right, 1), 3, self.left).wait_send()


def mp_copy(source, landing, send, recv, peer):
    return pltpu.make_async_remote_copy(
        src_ref=source,
        dst_ref=landing,
        send_sem=send,
        recv_sem=recv,
        device_id={"mp": peer},
        device_id_type=MESH,
    )


class MpExchange:
    def __init__(self, source, landing, sems):
        self.source, self.landing = source, landing
        self.send, self.recv = sems
        self.me = lax.axis_index("mp")

    def copy(self, d):
        peer = lax.rem(self.me + d, MP)
        return mp_copy(self.source(peer), self.landing(self.me), self.send.at[d], self.recv.at[d], peer)

    def arrival(self, d):
        origin = lax.rem(self.me - d + MP, MP)
        ref = self.landing(origin)
        return mp_copy(ref, ref, self.send.at[d], self.recv.at[d], origin)

    def start(self):
        fori(1, MP, lambda d: self.copy(d).start())

    def wait_recv(self):
        fori(1, MP, lambda d: self.arrival(d).wait_recv())

    def wait_send(self):
        fori(1, MP, lambda d: self.copy(d).wait_send())


def scan_scratch():
    v = pltpu.VMEM
    return dict(
        xs=v((CHUNKS, CHUNK, INNER), BF),
        xt=v((CHUNKS, CHUNK, INNER), BF),
        ed=v((CHUNKS, CHUNK, INNER), BF),
        er=v((CHUNKS, CHUNK, INNER), F32),
        tail=v((CHUNKS, CHUNK, INNER), F32),
        rcol=v((CHUNKS, CHUNK, LANES), F32),
        fresh=v((CHUNKS, STATE, INNER), F32),
        back=v((CHUNKS, STATE, INNER), F32),
        eR=v((CHUNKS, 8, INNER), F32),
        RC=v((8, INNER), F32),
        st=v((SEQ, 4 * PIECE, INNER), BF),
        sx=v((SEQ, 4 * PIECE, INNER), BF),
        sy=v((SEQ, 2 * PIECE, INNER), BF),
        sz=v((SEQ, 2 * PIECE, INNER), BF),
        y=v((CHUNKS, CHUNK, INNER), F32),
        dx=v((CHUNKS, CHUNK, INNER), F32),
        dbc=v((CHUNKS, CHUNK, 2 * STATE), F32),
        dd=v((CHUNKS, CHUNK, LANES), F32),
        gin=v((CHUNKS, STATE, INNER), F32),
        sin=v((STATE, INNER), F32),
    )


def main_scratch():
    v = pltpu.VMEM
    dma = pltpu.SemaphoreType.DMA
    seq_sems = lambda: dma((2, SEQ))
    return dict(
        tok3=v((SEQ, WID, DM), BF),
        cot=v((TOK, INNER), BF),
        wa=v((4, 4, SHARD, HALF), BF),
        wb=v((4, 4, SHARD, HALF), BF),
        sw_rx=v((SEQ, 16, LANES), BF),
        sw=v((LANES, DM), BF),
        z=v((TOK, INNER), BF),
        sraw=v((TOK, LANES), F32),
        pay=v((SEQ, ROWS, LANES), BF),
        trx=v((SEQ, ROWS, LANES), BF),
        bpay=v((SEQ, ROWS, LANES), BF),
        brx=v((SEQ, ROWS, LANES), BF),
        tri=v((4, CHUNK, CHUNK), BF),
        lp=v((TOK, LANES), BF),
        bcr=v((2, SEQ, WID, LANES), BF),
        bct=v((2, SEQ, WID, LANES), BF),
        wsh=v((DM, LANES), BF),
        tdb=v((2, CHUNKS, CHUNK, LANES), BF),
        trs=v((MP, CHUNK, LANES), BF),
        tpiece=v((SEQ, COLS, LANES), BF),
        rpiece=v((SEQ, COLS, LANES), BF),
        rdb=v((2, SEQ, WID, LANES), BF),
        rrs=v((MP, SEQ, COLS, LANES), BF),
        dpiece=v((SEQ, COLS, LANES), BF),
        lacc=v((CHUNK, LANES), F32),
        swp=v((16, LANES), BF),
        R=scan_scratch(),
        T=scan_scratch(),
        g=v((TOK, 2 * INNER), BF),
        dst=v((TOK, LANES), BF),
        gp=v((DM, 640), BF),
        gs=v((MP, 16, LANES), BF),
        gp_rx=v((SEQ, SHARD, 640), BF),
        gs_rx=v((SEQ, 16, LANES), BF),
        ip=v((MP, TOK, LANES), BF),
        prx=v((4, TOK, LANES), BF),
        zs=v((4, TOK, LANES), BF),
        zrx=v((4, TOK, LANES), BF),
        fsh=v((SHARD, LANES), F32),
        frx=v((MP, SHARD, LANES), F32),
        s_local=dma((4,)),
        s_w=dma((4, 2, 4)),
        s_sw=seq_sems(),
        s_pay=seq_sems(),
        s_sr=seq_sems(),
        s_st=seq_sems(),
        s_ur=seq_sems(),
        s_ut=seq_sems(),
        s_back=seq_sems(),
        s_back2=seq_sems(),
        s_gp=seq_sems(),
        s_bc=seq_sems(),
        s_bp=seq_sems(),
        s_gs=seq_sems(),
        s_bm=dma((2, MP)),
        s_tr=dma((2, MP)),
        s_rr=dma((2, MP)),
        s_fin=dma((2, MP)),
        s_pair=dma((2, 4, CHUNKS)),
        s_z=dma((2, 4, CHUNKS)),
    )


def sems(ref):
    return ref.at[0], ref.at[1]


def head_sum():
    c, h = iota((INNER, LANES), 0), iota((INNER, LANES), 1)
    return jnp.where((h < 8) & ((h & 3) == (c >> 6)), 1.0, 0.0).astype(BF)


def pair_expand(shift):
    k, c = iota((LANES, INNER), 0) - shift, iota((LANES, INNER), 1)
    return jnp.where((k >= 0) & (k < 8) & ((k & 3) == (c >> 6)), 1.0, 0.0).astype(BF)


def pair_merge(shift):
    k, h = iota((LANES, LANES), 0) - shift, iota((LANES, LANES), 1)
    return jnp.where((k >= 0) & (k < 8) & (h < 8) & ((k & 3) == (h & 3)), 1.0, 0.0).astype(BF)


def pair_place(shift):
    k, lane = iota((LANES, LANES), 0), iota((LANES, LANES), 1)
    return jnp.where((k < 8) & (lane == k + shift), 1.0, 0.0).astype(BF)


def wide(load, block, q):
    return jnp.concatenate([load(block, q), load(block + 1, q)], axis=1)


def summary(b, tri, load, pair_of, rate, ratex, q):
    x = wide(load, BX, q).astype(F32)
    dy = wide(load, BY, q).astype(F32)
    pair, shift = pair_of(q)
    dexp = mm(pair, pair_expand(shift))
    logs = (-dexp * ratex).astype(BF)
    rexp = mm(tri, logs)
    b["rcol"][q] = mm(tri, (-mm(pair, pair_merge(shift)) * rate).astype(BF))
    total = jnp.sum(logs.astype(F32), axis=0, keepdims=True)
    er = jnp.exp2(rexp)
    tail = jnp.exp2(jnp.minimum(total - rexp, 0.0))
    xs = (x * dexp).astype(BF)
    xt = (xs.astype(F32) * tail).astype(BF)
    ed = (er * dy).astype(BF)
    b["er"][q] = er
    b["tail"][q] = tail
    b["xs"][q] = xs
    b["xt"][q] = xt
    b["ed"][q] = ed
    b["fresh"][q] = mm_tn(load(BB, q), xt)
    b["back"][q] = mm_tn(load(BC, q), ed)
    rows = jnp.broadcast_to(total, (8, INNER))
    b["eR"][q] = jnp.exp2(rows)
    b["RC"][...] += rows


def pack_states(b):
    e = [b["eR"][q][:1] for q in range(CHUNKS)]
    end = b["fresh"][0]
    for q in range(1, CHUNKS):
        end = end * e[q] + b["fresh"][q]
    first = b["back"][CHUNKS - 1]
    for q in range(CHUNKS - 2, -1, -1):
        first = first * e[q] + b["back"][q]
    rc = b["RC"][...]
    hi = rc.astype(BF).astype(F32)
    logs = jnp.concatenate([hi, rc - hi], axis=0).astype(BF)
    pieces = [v.reshape(SEQ, PIECE, INNER) for v in (end, first)]
    b["st"][:, pl.ds(0, 2 * PIECE), :] = jnp.concatenate(pieces, axis=1).astype(BF)
    for k in range(SEQ):
        b["st"][k, pl.ds(2 * PIECE, 2 * PIECE)] = logs


def chain_states(b):
    own = [b["sx"][k, pl.ds(0, 2 * PIECE)].astype(F32) for k in range(SEQ)]
    logs = [b["sx"][k, pl.ds(2 * PIECE, 2 * PIECE)].astype(F32) for k in range(SEQ)]
    decay = [jnp.exp2(v[:PIECE] + v[PIECE:]) for v in logs]
    state = [jnp.zeros((PIECE, INNER), F32)]
    grad = [jnp.zeros((PIECE, INNER), F32)]
    for k in range(SEQ - 1):
        state.append(state[k] * decay[k] + own[k][:PIECE])
        n = SEQ - 1 - k
        grad.append(grad[k] * decay[n] + own[n][PIECE:])
    for k in range(SEQ):
        b["sy"][k] = jnp.concatenate([state[k], grad[SEQ - 1 - k]], axis=0).astype(BF)


def entering_states(b):
    both = b["sz"][...].astype(F32)
    b["sin"][...] = both[:, :PIECE, :].reshape(STATE, INNER)
    grad = both[:, PIECE:, :].reshape(STATE, INNER)
    for q in range(CHUNKS - 1, -1, -1):
        b["gin"][q] = grad
        if q > 0:
            grad = grad * b["eR"][q][:1] + b["back"][q]


def inside(b, tri, load, q):
    dy = wide(load, BY, q)
    bmat = load(BB, q)
    cmat = load(BC, q)
    xs = b["xs"][q]
    trif = tri.astype(F32)
    scores = mm_nt(cmat, bmat) * trif
    rcol = b["rcol"][q]
    rrow = rcol.T
    head = iota((CHUNK, INNER), 1) >> 6
    zero = jnp.zeros((), BF)
    y = jnp.zeros((CHUNK, INNER), F32)
    dxs = jnp.zeros((CHUNK, INNER), F32)
    pairs = jnp.zeros((CHUNK, CHUNK), F32)
    for h in range(HEADS):
        decay = jnp.exp2(jnp.minimum(rcol[:, h : h + 1] - rrow[h : h + 1, :], 0.0))
        m = (decay * scores).astype(BF)
        dyh = jnp.where(head == h, dy, zero)
        xsh = jnp.where(head == h, xs, zero)
        y += mm(m, xsh)
        dxs += mm_tn(m, dyh)
        pairs += decay * mm_nt(dyh, xs)
    pairs = (pairs * trif).astype(BF)
    b["y"][q] = y
    b["dx"][q] = dxs
    b["dbc"][q, :, pl.ds(0, STATE)] = mm_tn(pairs, cmat)
    b["dbc"][q, :, pl.ds(STATE, STATE)] = mm(pairs, bmat)


def outside(b, tri, tri_up, load, pair_of, rate, q, put):
    x = wide(load, BX, q).astype(F32)
    dy = wide(load, BY, q).astype(F32)
    bmat = load(BB, q)
    cmat = load(BC, q)
    pair, shift = pair_of(q)
    dexp = mm(pair, pair_expand(shift))
    xs = b["xs"][q].astype(F32)
    state = b["sin"][...]
    grad = b["gin"][q]
    state_b, grad_b = state.astype(BF), grad.astype(BF)
    sums = head_sum()
    y = b["y"][q] + b["er"][q] * mm(cmat, state_b)
    inner = b["dx"][q]
    outer = b["tail"][q] * mm(bmat, grad_b)
    dxs = inner + outer
    db = b["dbc"][q, :, pl.ds(0, STATE)] + mm_nt(b["xt"][q], grad_b)
    dc = b["dbc"][q, :, pl.ds(STATE, STATE)] + mm_nt(b["ed"][q], state_b)

    def by_head(v):
        return mm(v.astype(BF), sums)

    late = by_head(dy * y - xs * inner).astype(BF)
    early = by_head(xs * outer).astype(BF)
    decayed = b["eR"][q][:1] * state
    across = jnp.sum(decayed * grad, axis=0, keepdims=True)
    across = mm(jnp.broadcast_to(across, (16, INNER)).astype(BF), sums)[:1]
    dl = mm(tri_up, late) + mm(tri, early) - early.astype(F32) + across
    ddelta = by_head(x * dxs) - rate * dl
    b["sin"][...] = decayed + b["fresh"][q]
    put(q, y, dexp * dxs, db, dc, ddelta)


def kernel(tok_hbm, cot_hbm, pm, ps, pt, bias_s, rate_s, skip_s, gated_o, ig_o, gm_o, gsh_o, gst_o, m):
    seq, mp = lax.axis_index("seq"), lax.axis_index("mp")
    core = lax.rem(mp, 2)
    chip = mp // 2
    partner = mp + 1 - 2 * core
    plane, line = seq // 4, lax.rem(seq, 4)
    low = lax.rem(seq, 2)

    load_tok = pltpu.make_async_copy(tok_hbm, m["tok3"], m["s_local"].at[0])
    load_cot = pltpu.make_async_copy(cot_hbm, m["cot"], m["s_local"].at[1])
    load_tok.start()
    load_cot.start()

    barrier = pltpu.get_barrier_semaphore()

    def greet_seq(d):
        pl.semaphore_signal(
            barrier, inc=1, device_id={"seq": lax.rem(seq + d, SEQ)}, device_id_type=MESH
        )

    def greet_mp(d):
        pl.semaphore_signal(barrier, inc=1, device_id={"mp": lax.rem(mp + d, MP)}, device_id_type=MESH)

    fori(1, SEQ, greet_seq)
    fori(1, MP, greet_mp)

    wa, wb, swp = m["wa"], m["wb"], m["swp"]
    wa[plane, line, :, pl.ds(0, 256)] = pm[:, 0, :]
    wb[plane, line, :, pl.ds(0, 256)] = pm[:, 1, :]
    wa[plane, line, :, pl.ds(256, 128)] = ps[:, 0, :]
    wb[plane, line, :, pl.ds(256, 128)] = ps[:, 1, :]
    at, lane = iota((SHARD, LANES), 0), iota((SHARD, LANES), 1)
    place = jnp.where(lane == at + SHARD * low, 1.0, 0.0).astype(BF)
    shifted = mm(pt[...], place).astype(BF)
    swp[...] = jnp.concatenate([shifted, shifted, jnp.zeros((8, LANES), BF)], axis=0)
    pl.semaphore_wait(barrier, SEQ + MP - 2)

    def along_x(k):
        return 4 * k + line

    def along_y(k):
        return 4 * plane + k

    half = SHARD // 2
    ring_a1 = Ring(plane, along_x, lambda k: wa.at[k, line], lambda k, n: wa.at[k, line, pl.ds(half * n, half)], m["s_w"].at[0])
    ring_b1 = Ring(line, along_y, lambda k: wb.at[plane, k], lambda k, n: wb.at[plane, k, pl.ds(half * n, half)], m["s_w"].at[1])
    ring_a2 = Ring(line, along_y, lambda k: wa.at[:, k], lambda k, n: wa.at[pl.ds(2 * n, 2), k], m["s_w"].at[2])
    ring_b2 = Ring(plane, along_x, lambda k: wb.at[k], lambda k, n: wb.at[k, pl.ds(2 * n, 2)], m["s_w"].at[3])
    rings = (ring_a1, ring_b1, ring_a2, ring_b2)
    ring_a1.start()
    ring_b1.start()
    send_sw = SeqExchange(lambda p: swp, lambda k: m["sw_rx"].at[k], sems(m["s_sw"]))
    send_sw.start()
    m["sw_rx"][seq] = swp[...]

    ring_a1.forward()
    ring_b1.forward()
    ring_a1.finish()
    ring_a2.start()
    ring_b1.finish()
    ring_b2.start()

    i, j = iota((CHUNK, CHUNK), 0), iota((CHUNK, CHUNK), 1)
    m["tri"][0] = jnp.where(i >= j, 1.0, 0.0).astype(BF)
    it, jt = (i & 15) * 16 + (i >> 4), (j & 15) * 16 + (j >> 4)
    m["tri"][1] = jnp.where(it >= jt, 1.0, 0.0).astype(BF)
    m["tri"][2] = jnp.where(i <= j, 1.0, 0.0).astype(BF)
    m["tri"][3] = jnp.where(it <= jt, 1.0, 0.0).astype(BF)
    m["sw"][...] = jnp.zeros((LANES, DM), BF)
    m["R"]["RC"][...] = jnp.zeros((8, INNER), F32)
    m["T"]["RC"][...] = jnp.zeros((8, INNER), F32)
    m["lacc"][...] = jnp.zeros((CHUNK, LANES), F32)

    head_l = iota((1, LANES), 1)
    head_c = iota((1, INNER), 1) >> 6

    def lanes_of(value):
        v = jnp.zeros((1, LANES), F32)
        for h in range(HEADS):
            v = jnp.where((head_l < 8) & ((head_l & 3) == h), value(h), v)
        return v

    def features_of(value):
        v = jnp.zeros((1, INNER), F32)
        for h in range(HEADS):
            v = jnp.where(head_c == h, value(h), v)
        return v

    bias = lanes_of(lambda h: bias_s[h])
    rate_r, rate_t = lanes_of(lambda h: rate_s[0, h]), lanes_of(lambda h: rate_s[1, h])
    ratex_r = features_of(lambda h: rate_s[0, h]) * LOG2E
    ratex_t = features_of(lambda h: rate_s[1, h]) * LOG2E
    skip = features_of(lambda h: skip_s[h])

    load_tok.wait()
    load_cot.wait()
    ring_a2.forward()
    ring_b2.forward()
    ring_a2.finish()
    ring_b2.finish()
    send_sw.wait_recv()
    for k in range(SEQ // 2):
        m["sw"][pl.ds(0, 16), pl.ds(k * LANES, LANES)] = m["sw_rx"][2 * k] + m["sw_rx"][2 * k + 1]

    def rows_of(q):
        return pl.ds(pl.multiple_of(q * CHUNK, CHUNK), CHUNK)

    def columns(ref, at, width):
        return ref[:, :, :, pl.ds(at, width)].reshape(DM, width)

    def rest(v):
        return v.reshape(4, WID, LANES)

    send_pay = SeqExchange(lambda p: m["pay"].at[p], lambda k: m["trx"].at[k], sems(m["s_pay"]))
    quarter = pl.ds(pl.multiple_of(chip * COLS, COLS), COLS)
    bcr, bct = m["bcr"], m["bct"]
    send_bc = SeqExchange(
        lambda p: bcr.at[core, p, quarter], lambda k: bct.at[core, k, quarter], sems(m["s_bc"])
    )

    def piece_of(ref, k):
        return ref.at[lax.rem(k, 2), :, pl.ds(pl.multiple_of(k // 2 * COLS, COLS), COLS)]

    send_bm = MpExchange(lambda p: piece_of(bct, mp), lambda k: piece_of(bct, k), sems(m["s_bm"]))
    m["wsh"][...] = jnp.where(core == 0, columns(wa, 256, 128), columns(wb, 256, 128))

    def start_four(exchange, q):
        def one(n):
            d = lax.rem(4 * q + n - seq + SEQ, SEQ)

            @pl.when(d != 0)
            def _():
                exchange.copy(d).start()

        fori(0, 4, one)

    def project(n):
        q = lax.rem(plane + n, 4)
        rows = rows_of(q)
        u = m["tok3"][pl.ds(4 * q, 4)].reshape(CHUNK, DM)
        four = pl.ds(4 * q, 4)

        def put(block, v):
            v = v.astype(BF)
            for k in range(v.shape[1] // LANES):
                m["pay"][four, pl.ds((block + k) * WID, WID), :] = rest(v[:, k * LANES : (k + 1) * LANES])

        bcr[0, four] = rest(mm(u, columns(wa, 256, 128)).astype(BF))
        bcr[1, four] = rest(mm(u, columns(wb, 256, 128)).astype(BF))
        start_four(send_bc, q)
        z = mm(u, columns(wb, 0, 256)).astype(BF)
        m["z"][rows, :] = z
        zf = z.astype(F32)
        gate = zf * jax.nn.sigmoid(zf)
        put(BY, m["cot"][rows, :].astype(F32) * gate)
        put(BX, mm(u, columns(wa, 0, 256)))
        raw = mm_nt(u, m["sw"][...]) + bias
        m["sraw"][rows, :] = raw
        pair = as_pair(jnp.maximum(raw, 0.0) + jnp.log1p(jnp.exp(-jnp.abs(raw))))
        m["lp"][rows, :] = pair
        folded = jnp.zeros((64, LANES), F32)
        for g in range(4):
            part = rest(pair)[:, g * COLS : (g + 1) * COLS, :].reshape(64, LANES)
            folded += mm(part, pair_place(8 * g))
        m["pay"][four, pl.ds(ROWS_L, COLS), :] = folded.astype(BF).reshape(4, COLS, LANES)
        start_four(send_pay, q)

    fori(0, CHUNKS, project)
    m["trx"][seq] = m["pay"][seq]
    bct[core, seq, quarter] = bcr[core, seq, quarter]

    def load_r(block, q):
        if block >= BB:
            return bcr[block - BB, pl.ds(4 * q, 4)].reshape(CHUNK, LANES)
        return m["pay"][pl.ds(4 * q, 4), pl.ds(block * WID, WID), :].reshape(CHUNK, LANES)

    def pair_r(q):
        return m["lp"][rows_of(q), :], 0

    def cols_of(block, q):
        return pl.ds(pl.multiple_of(block * WID + q * COLS, COLS), COLS)

    def load_t(block, q):
        if block >= BB:
            return bct[block - BB, :, pl.ds(q * COLS, COLS), :].reshape(CHUNK, LANES)
        return m["trx"][:, cols_of(block, q), :].reshape(CHUNK, LANES)

    def pair_t(q):
        return m["trx"][:, pl.ds(ROWS_L, COLS), :].reshape(CHUNK, LANES), 8 * q

    def pieces_exchange(source, landing, sem):
        return SeqExchange(lambda p: source.at[p], lambda k: landing.at[k], sems(sem))

    r, t = m["R"], m["T"]
    tri_r, tri_t, up_r, up_t = (m["tri"].at[k] for k in range(4))

    def chunks(low, high, step):
        for q in range(low, high):
            step(q)


    def start_pieces(b, sem):
        pack_states(b)
        e = pieces_exchange(b["st"], b["sx"], sem)
        e.start()
        b["sx"][seq] = b["st"][seq]
        return e

    def start_entering(b, sem):
        chain_states(b)
        e = pieces_exchange(b["sy"], b["sz"], sem)
        e.start()
        b["sz"][seq] = b["sy"][seq]
        return e

    chunks(0, CHUNKS, lambda q: summary(r, tri_r[...], load_r, pair_r, rate_r * LOG2E, ratex_r, q))
    send_sr = start_pieces(r, m["s_sr"])
    send_bc.wait_recv()
    send_bm.start()
    chunks(0, CHUNKS, lambda q: inside(r, tri_r[...], load_r, q))
    send_sr.wait_recv()
    send_ur = start_entering(r, m["s_ur"])

    send_pay.wait_recv()
    send_bm.wait_recv()
    chunks(0, CHUNKS, lambda q: summary(t, tri_t[...], load_t, pair_t, rate_t * LOG2E, ratex_t, q))
    send_st = start_pieces(t, m["s_st"])
    chunks(0, 2, lambda q: inside(t, tri_t[...], load_t, q))
    send_st.wait_recv()
    send_ut = start_entering(t, m["s_ut"])
    chunks(2, CHUNKS, lambda q: inside(t, tri_t[...], load_t, q))
    send_ut.wait_recv()
    entering_states(t)

    def put_t(q, y, dx, db, dc, dd):
        def put(block, v):
            v = v.astype(BF)
            for k in range(v.shape[1] // LANES):
                part = v[:, k * LANES : (k + 1) * LANES]
                at = 128 * (q // 2) + 32 * (block + k) + COLS * (q % 2)
                m["bpay"][:, pl.ds(at, COLS), :] = part.reshape(SEQ, COLS, LANES)

        put(BX, y)
        put(BY, dx)
        m["tdb"][0, q] = db.astype(BF)
        m["tdb"][1, q] = dc.astype(BF)
        for n in range(2):
            d = lax.rem(2 * q + n - mp + MP, MP)

            @pl.when(d != 0)
            def _():
                send_tr.copy(d).start()

        m["lacc"][...] += mm(as_pair(dd), pair_place(8 * q))

    def half_back(at, count, sem):
        rows = pl.ds(at, count)
        return SeqExchange(lambda p: m["bpay"].at[p, rows], lambda k: m["brx"].at[k, rows], sems(sem))

    send_back = half_back(0, 128, m["s_back"])
    send_back2 = half_back(128, 144, m["s_back2"])
    send_tr = MpExchange(
        lambda p: m["tdb"].at[lax.rem(p, 2), p // 2], lambda k: m["trs"].at[k], sems(m["s_tr"])
    )
    send_bp = SeqExchange(lambda p: m["tpiece"].at[p], lambda k: m["rpiece"].at[k], sems(m["s_bp"]))
    send_rr = MpExchange(lambda p: piece_of(m["rdb"], p), lambda k: m["rrs"].at[k], sems(m["s_rr"]))

    def group_total(ref):
        v = ref[0].astype(F32)
        for k in range(1, MP):
            v += ref[k].astype(F32)
        return v

    chunks(0, 2, lambda q: outside(t, tri_t[...], up_t[...], load_t, pair_t, rate_t, q, put_t))
    send_back.start()
    chunks(2, 4, lambda q: outside(t, tri_t[...], up_t[...], load_t, pair_t, rate_t, q, put_t))
    m["bpay"][:, pl.ds(ROWS_L, COLS), :] = m["lacc"][...].astype(BF).reshape(SEQ, COLS, LANES)
    send_back2.start()
    m["brx"][seq] = m["bpay"][seq]
    m["trs"][mp] = m["tdb"][core, chip]

    send_ur.wait_recv()
    entering_states(r)

    def put_r(q, y, dx, db, dc, dd):
        r["y"][q] = y
        r["dx"][q] = dx
        m["rdb"][0, pl.ds(4 * q, 4)] = rest(db.astype(BF))
        m["rdb"][1, pl.ds(4 * q, 4)] = rest(dc.astype(BF))
        r["dd"][q] = dd

    def outside_r(q):
        outside(r, tri_r[...], up_r[...], load_r, pair_r, rate_r, q, put_r)

    chunks(0, 1, outside_r)
    send_tr.wait_recv()
    m["tpiece"][...] = group_total(m["trs"]).astype(BF).reshape(SEQ, COLS, LANES)
    send_bp.start()
    m["rpiece"][seq] = m["tpiece"][seq]
    chunks(1, CHUNKS, outside_r)
    send_rr.start()
    m["rrs"][mp] = m["rdb"][core, :, quarter]
    send_back.wait_recv()
    send_back2.wait_recv()
    send_bp.wait_recv()
    send_rr.wait_recv()
    m["dpiece"][...] = (group_total(m["rrs"]) + m["rpiece"][...].astype(F32)).astype(BF)

    def back(block, q):
        parts = [m["brx"][pl.ds(4 * q, 4), pl.ds(128 * n + 32 * block, 32), :] for n in range(2)]
        return jnp.concatenate(parts, axis=1).reshape(CHUNK, LANES)

    def combine(q):
        rows = rows_of(q)
        x = wide(load_r, BX, q).astype(F32)
        dy = wide(load_r, BY, q).astype(F32)
        z = m["z"][rows, :].astype(F32)
        cot = m["cot"][rows, :].astype(F32)
        y = r["y"][q] + wide(back, BX, q).astype(F32) + skip * x
        sigma = jax.nn.sigmoid(z)
        gated_o[rows, :] = (y * (z * sigma)).astype(BF)
        m["g"][rows, pl.ds(256, 256)] = (cot * y * sigma * (1.0 + z * (1.0 - sigma))).astype(BF)
        m["g"][rows, pl.ds(0, 256)] = (r["dx"][q] + wide(back, BY, q).astype(F32) + skip * dy).astype(BF)
        folded = m["brx"][pl.ds(4 * q, 4), pl.ds(ROWS_L, COLS), :].reshape(64, LANES)
        parts = [mm(folded, pair_merge(8 * g)).reshape(4, COLS, LANES) for g in range(4)]
        dd = r["dd"][q] + jnp.concatenate(parts, axis=1).reshape(CHUNK, LANES)
        dstep = dd * jax.nn.sigmoid(m["sraw"][rows, :])
        m["dst"][rows, :] = jnp.where(iota((CHUNK, LANES), 1) < HEADS, dstep, 0.0).astype(BF)

    def pair_copy(k, q):
        rows = rows_of(q)
        return mp_copy(
            m["ip"].at[2 * k + 1 - core, rows],
            m["prx"].at[k, rows],
            m["s_pair"].at[0, k, q],
            m["s_pair"].at[1, k, q],
            partner,
        )

    def z_peer(d):
        return lax.rem(chip + d, 4)

    def z_copy(d, q):
        return mp_copy(
            m["zs"].at[z_peer(d), rows_of(q)],
            m["zrx"].at[chip, rows_of(q)],
            m["s_z"].at[0, d, q],
            m["s_z"].at[1, d, q],
            2 * z_peer(d) + core,
        )

    def z_arrival(d, q):
        origin = lax.rem(chip - d + 4, 4)
        ref = m["zrx"].at[origin, rows_of(q)]
        return mp_copy(ref, ref, m["s_z"].at[0, d, q], m["s_z"].at[1, d, q], 2 * origin + core)

    def pair_sum(k, q):
        rows = rows_of(q)
        pair_copy(k, q).wait_recv()
        return (m["ip"][2 * k + core, rows, :].astype(F32) + m["prx"][k, rows, :].astype(F32)).astype(BF)

    def pass_on(q):
        def to(d):
            m["zs"][z_peer(d), rows_of(q), :] = pair_sum(z_peer(d), q)
            z_copy(d, q).start()

        fori(1, 4, to)
        m["zrx"][chip, rows_of(q), :] = pair_sum(chip, q)

    def finish(q):
        combine(q)
        rows = rows_of(q)
        g = m["g"][rows, :]
        ds = m["dst"][rows, :]
        piece = m["dpiece"][pl.ds(4 * q, 4)]
        here = (iota((4, WID, LANES), 1) >> 4) == chip
        piece = jnp.where(here, jnp.concatenate([piece] * 4, axis=1), jnp.zeros((), BF)).reshape(CHUNK, LANES)
        for c in range(4):
            cols = pl.ds(c * 256, 256)
            v = mm_nt(g[:, :256], wa[c, :, :, pl.ds(0, 256)].reshape(256, 256))
            v += mm_nt(g[:, 256:], wb[c, :, :, pl.ds(0, 256)].reshape(256, 256))
            v += mm(ds, m["sw"][:, cols])
            v += mm_nt(piece, m["wsh"][cols, :])
            v = v.astype(BF)
            m["ip"][2 * c, rows, :] = v[:, :LANES]
            m["ip"][2 * c + 1, rows, :] = v[:, LANES:]
        fori(0, 4, lambda k: pair_copy(k, q).start())

    for q in range(CHUNKS):
        finish(q)
        if q > 0:
            pass_on(q - 1)

    def shard_rows(ref):
        return lambda p: ref.at[pl.ds(pl.multiple_of(p * SHARD, SHARD), SHARD)]

    send_gp = SeqExchange(shard_rows(m["gp"]), lambda k: m["gp_rx"].at[k], sems(m["s_gp"]))
    send_gs = SeqExchange(lambda p: m["gs"].at[p // 2], lambda k: m["gs_rx"].at[k], sems(m["s_gs"]))

    def grads(n):
        k = lax.rem(plane + n, 4)
        cols = rows_of(k)
        u = m["tok3"][:, :, cols].reshape(TOK, 256)
        m["gp"][cols, pl.ds(0, 512)] = mm_tn(u, m["g"][...]).astype(BF)
        some = m["tok3"][:, quarter, cols].reshape(CHUNK, 256)
        m["gp"][cols, pl.ds(512, 128)] = mm_tn(some, piece_rows).astype(BF)
        gs = mm_tn(m["dst"][...], u)[:16].astype(BF)
        m["gs"][2 * k] = gs[:, :LANES]
        m["gs"][2 * k + 1] = gs[:, LANES:]
        start_four(send_gp, k)
        start_four(send_gs, k)

    piece_rows = m["dpiece"][...].reshape(CHUNK, LANES)
    grads(0)
    pass_on(CHUNKS - 1)
    fori(1, 4, grads)
    own = pl.ds(pl.multiple_of(seq * SHARD, SHARD), SHARD)
    m["gp_rx"][seq] = m["gp"][own, :]
    m["gs_rx"][seq] = m["gs"][seq // 2]

    def input_sum(q):
        rows = rows_of(q)
        fori(1, 4, lambda d: z_arrival(d, q).wait_recv())
        v = m["zrx"][0, rows, :].astype(F32)
        for k in range(1, 4):
            v += m["zrx"][k, rows, :].astype(F32)
        ig_o[rows, :] = v.astype(BF)

    fori(0, CHUNKS, input_sum)

    def total_of(ref):
        v = ref[0].astype(F32)
        for k in range(1, SEQ):
            v += ref[k].astype(F32)
        return v

    send_gp.wait_recv()
    main = total_of(m["gp_rx"])
    m["fsh"][...] = main[:, 512:]
    send_fin = MpExchange(lambda p: m["fsh"], lambda k: m["frx"].at[k], sems(m["s_fin"]))
    send_fin.start()
    m["frx"][mp] = main[:, 512:]
    gm_o[:, 0, :] = main[:, :INNER]
    gm_o[:, 1, :] = main[:, INNER : 2 * INNER]
    send_gs.wait_recv()
    step = total_of(m["gs_rx"])
    gst_o[...] = jnp.where(low == 0, step[:HEADS, :SHARD], step[:HEADS, SHARD:])
    send_fin.wait_recv()
    for n in range(2):
        gsh_o[:, n, :] = m["frx"][n] + m["frx"][2 + n] + m["frx"][4 + n] + m["frx"][6 + n]

    sent = rings + (send_sw, send_pay, send_bc, send_bm, send_sr, send_ur, send_st, send_ut)
    sent += (send_back, send_back2, send_tr, send_bp, send_rr, send_gp, send_gs, send_fin)
    for e in sent:
        e.wait_send()
    for q in range(CHUNKS):
        fori(0, 4, lambda k: pair_copy(k, q).wait_send())
        fori(1, 4, lambda d: z_copy(d, q).wait_send())


def hand_over(*refs):
    n = len(refs) // 2
    for k in range(n):
        refs[n + k][...] = refs[k][...]


def body(tokens, proj_main, proj_shared, proj_step, step_bias, decay_rate, skip_gain, cotangent):
    vm = pl.BlockSpec(memory_space=pltpu.VMEM)
    sm = pl.BlockSpec(memory_space=pltpu.SMEM)
    hbm = pl.BlockSpec(memory_space=pl.ANY)
    shapes = (
        jax.ShapeDtypeStruct((TOK, INNER), BF),
        jax.ShapeDtypeStruct((TOK, LANES), BF),
        jax.ShapeDtypeStruct((SHARD, 2, INNER), F32),
        jax.ShapeDtypeStruct((SHARD, 2, STATE), F32),
        jax.ShapeDtypeStruct((HEADS, SHARD), F32),
    )
    results = pl.pallas_call(
        kernel,
        out_shape=shapes,
        in_specs=[hbm, hbm, vm, vm, vm, sm, sm, sm],
        out_specs=(vm,) * 5,
        scratch_shapes=[main_scratch()],
        compiler_params=pltpu.CompilerParams(
            collective_id=0, has_side_effects=True, vmem_limit_bytes=62 * 1024 * 1024
        ),
    )(
        tokens.reshape(SEQ, WID, DM),
        cotangent.reshape(TOK, INNER),
        proj_main,
        proj_shared,
        proj_step.T,
        step_bias,
        decay_rate,
        skip_gain,
    )
    gated, ig, gm, gsh, gst = pl.pallas_call(
        hand_over,
        out_shape=shapes,
        in_specs=[vm] * 5,
        out_specs=(vm,) * 5,
    )(*results)
    return (
        gated.reshape(1, 16, WID, INNER),
        ig.reshape(1, 16, WID, LANES),
        gm,
        gsh,
        gst.T,
    )


def solution(mesh):
    placed = (
        P("seq", None, None, None),
        P("seq", None, "mp"),
        P("seq", None, None),
        P("seq", "mp"),
        P("mp"),
        P(None, "mp"),
        P("mp"),
        P("seq", None, None, "mp"),
    )
    return jax.shard_map(
        body,
        mesh=mesh,
        in_specs=placed,
        out_specs=(
            P("seq", None, None, "mp"),
            P("seq", None, None, "mp"),
            P("seq", None, "mp"),
            P("seq", None, None),
            P("seq", "mp"),
        ),
        check_vma=False,
    )
```

```python
import jax
import jax.numpy as jnp
from jax import lax
from jax.experimental import pallas as pl
from jax.experimental.pallas import tpu as pltpu
from jax.sharding import PartitionSpec as P

MESH = pl.DeviceIdType.MESH
BF = jnp.bfloat16
F32 = jnp.float32

SEQ = 16
MP = 8
TOK = 1024
WID = 64
DM = 1024
INNER = 256
HEADS = 4
STATE = 128
LANES = 128
CHUNK = 256
CHUNKS = TOK // CHUNK
COLS = CHUNK // SEQ
SHARD = DM // SEQ
BX, BY, BB, BC, ROWS_L, ROWS = 0, 2, 4, 5, 256, 272
PIECE = STATE // SEQ
HALF = 3 * LANES
LOG2E = 1.4426950408889634


def iota(shape, axis):
    return lax.broadcasted_iota(jnp.int32, shape, axis)


def mm(a, b):
    return lax.dot_general(a, b, (((1,), (0,)), ((), ())), preferred_element_type=F32)


def mm_nt(a, b):
    return lax.dot_general(a, b, (((1,), (1,)), ((), ())), preferred_element_type=F32)


def mm_tn(a, b):
    return lax.dot_general(a, b, (((0,), (0,)), ((), ())), preferred_element_type=F32)


def halves(v):
    hi = v.astype(BF)
    return hi, (v - hi.astype(F32)).astype(BF)


def as_pair(v):
    lane = iota(v.shape, 1)
    hi = v.astype(BF).astype(F32)
    return jnp.where(lane < 4, hi, jnp.where(lane < 8, v - hi, 0.0)).astype(BF)


def fori(low, high, step):
    def run(i, carry):
        step(i)
        return carry

    lax.fori_loop(low, high, run, 0)


class SeqExchange:
    def __init__(self, source, landing, sems):
        self.source, self.landing = source, landing
        self.send, self.recv = sems
        self.me = lax.axis_index("seq")

    def copy(self, d):
        peer = lax.rem(self.me + d, SEQ)
        return pltpu.make_async_remote_copy(
            src_ref=self.source(peer),
            dst_ref=self.landing(self.me),
            send_sem=self.send.at[d],
            recv_sem=self.recv.at[d],
            device_id={"seq": peer},
            device_id_type=MESH,
        )

    def arrival(self, d):
        origin = lax.rem(self.me - d + SEQ, SEQ)
        return pltpu.make_async_remote_copy(
            src_ref=self.landing(origin),
            dst_ref=self.landing(origin),
            send_sem=self.send.at[d],
            recv_sem=self.recv.at[d],
            device_id={"seq": origin},
            device_id_type=MESH,
        )

    def start(self):
        fori(1, SEQ, lambda d: self.copy(d).start())

    def wait_recv(self):
        fori(1, SEQ, lambda d: self.arrival(d).wait_recv())

    def wait_send(self):
        fori(1, SEQ, lambda d: self.copy(d).wait_send())


class Ring:
    def __init__(self, me, to, whole, part, sems):
        self.whole, self.part, self.sems, self.to = whole, part, sems, to
        self.me, self.right, self.left = me, lax.rem(me + 1, 4), lax.rem(me + 3, 4)
        self.far = lax.rem(me + 2, 4)

    def copy(self, ref, k, peer):
        return pltpu.make_async_remote_copy(
            src_ref=ref,
            dst_ref=ref,
            send_sem=self.sems.at[0, k],
            recv_sem=self.sems.at[1, k],
            device_id={"seq": self.to(peer)},
            device_id_type=MESH,
        )

    def start(self):
        self.copy(self.whole(self.me), 0, self.right).start()
        self.copy(self.whole(self.me), 1, self.left).start()

    def forward(self):
        self.copy(self.whole(self.left), 0, self.left).wait_recv()
        self.copy(self.part(self.left, 0), 2, self.right).start()
        self.copy(self.whole(self.right), 1, self.right).wait_recv()
        self.copy(self.part(self.right, 1), 3, self.left).start()

    def finish(self):
        self.copy(self.part(self.far, 0), 2, self.left).wait_recv()
        self.copy(self.part(self.far, 1), 3, self.right).wait_recv()

    def wait_send(self):
        self.copy(self.whole(self.me), 0, self.right).wait_send()
        self.copy(self.whole(self.me), 1, self.left).wait_send()
        self.copy(self.part(self.left, 0), 2, self.right).wait_send()
        self.copy(self.part(self.right, 1), 3, self.left).wait_send()


def mp_copy(source, landing, send, recv, peer):
    return pltpu.make_async_remote_copy(
        src_ref=source,
        dst_ref=landing,
        send_sem=send,
        recv_sem=recv,
        device_id={"mp": peer},
        device_id_type=MESH,
    )


class MpExchange:
    def __init__(self, source, landing, sems):
        self.source, self.landing = source, landing
        self.send, self.recv = sems
        self.me = lax.axis_index("mp")

    def copy(self, d):
        peer = lax.rem(self.me + d, MP)
        return mp_copy(self.source(peer), self.landing(self.me), self.send.at[d], self.recv.at[d], peer)

    def arrival(self, d):
        origin = lax.rem(self.me - d + MP, MP)
        ref = self.landing(origin)
        return mp_copy(ref, ref, self.send.at[d], self.recv.at[d], origin)

    def start(self):
        fori(1, MP, lambda d: self.copy(d).start())

    def wait_recv(self):
        fori(1, MP, lambda d: self.arrival(d).wait_recv())

    def wait_send(self):
        fori(1, MP, lambda d: self.copy(d).wait_send())


def scan_scratch():
    v = pltpu.VMEM
    return dict(
        xs=v((CHUNKS, CHUNK, INNER), BF),
        xt=v((CHUNKS, CHUNK, INNER), BF),
        ed=v((CHUNKS, CHUNK, INNER), BF),
        er=v((CHUNKS, CHUNK, INNER), F32),
        tail=v((CHUNKS, CHUNK, INNER), F32),
        rcol=v((CHUNKS, CHUNK, LANES), F32),
        fresh=v((CHUNKS, STATE, INNER), F32),
        back=v((CHUNKS, STATE, INNER), F32),
        eR=v((CHUNKS, 8, INNER), F32),
        RC=v((8, INNER), F32),
        st=v((SEQ, 4 * PIECE, INNER), BF),
        sx=v((SEQ, 4 * PIECE, INNER), BF),
        sy=v((SEQ, 2 * PIECE, INNER), BF),
        sz=v((SEQ, 2 * PIECE, INNER), BF),
        y=v((CHUNKS, CHUNK, INNER), F32),
        dx=v((CHUNKS, CHUNK, INNER), F32),
        dbc=v((CHUNKS, CHUNK, 2 * STATE), F32),
        dd=v((CHUNKS, CHUNK, LANES), F32),
        gin=v((CHUNKS, STATE, INNER), F32),
        sin=v((STATE, INNER), F32),
    )


def main_scratch():
    v = pltpu.VMEM
    dma = pltpu.SemaphoreType.DMA
    seq_sems = lambda: dma((2, SEQ))
    return dict(
        tok3=v((SEQ, WID, DM), BF),
        cot=v((TOK, INNER), BF),
        wa=v((4, 4, SHARD, HALF), BF),
        wb=v((4, 4, SHARD, HALF), BF),
        sw_rx=v((SEQ, 16, LANES), BF),
        sw=v((LANES, DM), BF),
        z=v((TOK, INNER), BF),
        sraw=v((TOK, LANES), F32),
        pay=v((SEQ, ROWS, LANES), BF),
        trx=v((SEQ, ROWS, LANES), BF),
        bpay=v((SEQ, ROWS, LANES), BF),
        brx=v((SEQ, ROWS, LANES), BF),
        tri=v((4, CHUNK, CHUNK), BF),
        lp=v((TOK, LANES), BF),
        bcr=v((2, SEQ, WID, LANES), BF),
        bct=v((2, SEQ, WID, LANES), BF),
        wx=v((DM, 2 * LANES), BF),
        tdb=v((2, CHUNKS, CHUNK, LANES), BF),
        trs=v((MP, CHUNK, LANES), BF),
        tpiece=v((SEQ, COLS, LANES), BF),
        rpiece=v((SEQ, COLS, LANES), BF),
        rdb=v((2, SEQ, WID, LANES), BF),
        rrs=v((MP, SEQ, COLS, LANES), BF),
        dpiece=v((SEQ, COLS, LANES), BF),
        lacc=v((CHUNK, LANES), F32),
        swp=v((16, LANES), BF),
        R=scan_scratch(),
        T=scan_scratch(),
        g=v((TOK, 768), BF),
        tokt=v((DM, TOK), BF),
        gp=v((DM, 640), BF),
        gs=v((MP, 16, LANES), BF),
        gp_rx=v((SEQ, SHARD, 640), BF),
        gs_rx=v((SEQ, 16, LANES), BF),
        ip=v((MP, TOK, LANES), BF),
        prx=v((4, TOK, LANES), BF),
        zs=v((4, TOK, LANES), BF),
        zrx=v((4, TOK, LANES), BF),
        fsh=v((SHARD, LANES), F32),
        frx=v((MP, SHARD, LANES), F32),
        s_local=dma((4,)),
        s_w=dma((4, 2, 4)),
        s_sw=seq_sems(),
        s_pay=seq_sems(),
        s_sr=seq_sems(),
        s_st=seq_sems(),
        s_ur=seq_sems(),
        s_ut=seq_sems(),
        s_back=seq_sems(),
        s_back2=seq_sems(),
        s_gp=seq_sems(),
        s_bc=seq_sems(),
        s_bp=seq_sems(),
        s_gs=seq_sems(),
        s_bm=dma((2, MP)),
        s_tr=dma((2, MP)),
        s_rr=dma((2, MP)),
        s_fin=dma((2, MP)),
        s_pair=dma((2, 4, CHUNKS)),
        s_z=dma((2, 4, CHUNKS)),
    )


def sems(ref):
    return ref.at[0], ref.at[1]


def head_sum():
    c, h = iota((INNER, LANES), 0), iota((INNER, LANES), 1)
    return jnp.where((h < 8) & ((h & 3) == (c >> 6)), 1.0, 0.0).astype(BF)


def pair_expand(shift):
    k, c = iota((LANES, INNER), 0) - shift, iota((LANES, INNER), 1)
    return jnp.where((k >= 0) & (k < 8) & ((k & 3) == (c >> 6)), 1.0, 0.0).astype(BF)


def pair_merge(shift):
    k, h = iota((LANES, LANES), 0) - shift, iota((LANES, LANES), 1)
    return jnp.where((k >= 0) & (k < 8) & (h < 8) & ((k & 3) == (h & 3)), 1.0, 0.0).astype(BF)


def pair_place(shift):
    k, lane = iota((LANES, LANES), 0), iota((LANES, LANES), 1)
    return jnp.where((k < 8) & (lane == k + shift), 1.0, 0.0).astype(BF)


def wide(load, block, q):
    return jnp.concatenate([load(block, q), load(block + 1, q)], axis=1)


def summary(b, tri, load, pair_of, rate, ratex, q):
    x = wide(load, BX, q).astype(F32)
    dy = wide(load, BY, q).astype(F32)
    pair, shift = pair_of(q)
    dexp = mm(pair, pair_expand(shift))
    logs = (-dexp * ratex).astype(BF)
    rexp = mm(tri, logs)
    b["rcol"][q] = mm(tri, (-mm(pair, pair_merge(shift)) * rate).astype(BF))
    total = jnp.sum(logs.astype(F32), axis=0, keepdims=True)
    er = jnp.exp2(rexp)
    tail = jnp.exp2(jnp.minimum(total - rexp, 0.0))
    xs = (x * dexp).astype(BF)
    xt = (xs.astype(F32) * tail).astype(BF)
    ed = (er * dy).astype(BF)
    b["er"][q] = er
    b["tail"][q] = tail
    b["xs"][q] = xs
    b["xt"][q] = xt
    b["ed"][q] = ed
    b["fresh"][q] = mm_tn(load(BB, q), xt)
    b["back"][q] = mm_tn(load(BC, q), ed)
    rows = jnp.broadcast_to(total, (8, INNER))
    b["eR"][q] = jnp.exp2(rows)
    b["RC"][...] += rows


def pack_states(b):
    e = [b["eR"][q][:1] for q in range(CHUNKS)]
    end = b["fresh"][0]
    for q in range(1, CHUNKS):
        end = end * e[q] + b["fresh"][q]
    first = b["back"][CHUNKS - 1]
    for q in range(CHUNKS - 2, -1, -1):
        first = first * e[q] + b["back"][q]
    rc = b["RC"][...]
    hi = rc.astype(BF).astype(F32)
    logs = jnp.concatenate([hi, rc - hi], axis=0).astype(BF)
    pieces = [v.reshape(SEQ, PIECE, INNER) for v in (end, first)]
    b["st"][:, pl.ds(0, 2 * PIECE), :] = jnp.concatenate(pieces, axis=1).astype(BF)
    for k in range(SEQ):
        b["st"][k, pl.ds(2 * PIECE, 2 * PIECE)] = logs


def chain_states(b):
    own = [b["sx"][k, pl.ds(0, 2 * PIECE)].astype(F32) for k in range(SEQ)]
    logs = [b["sx"][k, pl.ds(2 * PIECE, 2 * PIECE)].astype(F32) for k in range(SEQ)]
    decay = [jnp.exp2(v[:PIECE] + v[PIECE:]) for v in logs]
    state = [jnp.zeros((PIECE, INNER), F32)]
    grad = [jnp.zeros((PIECE, INNER), F32)]
    for k in range(SEQ - 1):
        state.append(state[k] * decay[k] + own[k][:PIECE])
        n = SEQ - 1 - k
        grad.append(grad[k] * decay[n] + own[n][PIECE:])
    for k in range(SEQ):
        b["sy"][k] = jnp.concatenate([state[k], grad[SEQ - 1 - k]], axis=0).astype(BF)


def entering_states(b):
    both = b["sz"][...].astype(F32)
    b["sin"][...] = both[:, :PIECE, :].reshape(STATE, INNER)
    grad = both[:, PIECE:, :].reshape(STATE, INNER)
    for q in range(CHUNKS - 1, -1, -1):
        b["gin"][q] = grad
        if q > 0:
            grad = grad * b["eR"][q][:1] + b["back"][q]


def head_rows(h):
    one = jnp.where((iota((16, INNER), 1) >> 6) == h, 1.0, 0.0).astype(BF)
    return jnp.concatenate([one] * (CHUNK // 16), axis=0)


def inside(b, tri, load, q):
    dy = wide(load, BY, q)
    bmat = load(BB, q)
    cmat = load(BC, q)
    xs = b["xs"][q]
    trif = tri.astype(F32)
    scores = mm_nt(cmat, bmat) * trif
    rcol = b["rcol"][q]
    rrow = rcol.T
    pairs = None
    ms, dys, xss = [], [], []
    for h in range(HEADS):
        decay = jnp.exp2(jnp.minimum(rcol[:, h : h + 1] - rrow[h : h + 1, :], 0.0))
        ms.append((decay * scores).astype(BF))
        mask = head_rows(h)
        dys.append(dy * mask)
        xss.append(xs * mask)
        term = decay * mm_nt(dys[h], xs)
        pairs = term if h == 0 else pairs + term
    dy4 = jnp.concatenate(dys, axis=0)
    y = mm(jnp.concatenate(ms, axis=1), jnp.concatenate(xss, axis=0))
    dxs = mm_tn(jnp.concatenate(ms, axis=0), dy4)
    pairs = (pairs * trif).astype(BF)
    b["y"][q] = y
    b["dx"][q] = dxs
    b["dbc"][q, :, pl.ds(0, STATE)] = mm_tn(pairs, cmat)
    b["dbc"][q, :, pl.ds(STATE, STATE)] = mm(pairs, bmat)


def outside(b, tri, tri_up, load, pair_of, rate, q, put):
    x = wide(load, BX, q).astype(F32)
    dy = wide(load, BY, q).astype(F32)
    bmat = load(BB, q)
    cmat = load(BC, q)
    pair, shift = pair_of(q)
    dexp = mm(pair, pair_expand(shift))
    xs = b["xs"][q].astype(F32)
    state = b["sin"][...]
    grad = b["gin"][q]
    state_b, grad_b = state.astype(BF), grad.astype(BF)
    sums = head_sum()
    y = b["y"][q] + b["er"][q] * mm(cmat, state_b)
    inner = b["dx"][q]
    outer = b["tail"][q] * mm(bmat, grad_b)
    dxs = inner + outer
    db = b["dbc"][q, :, pl.ds(0, STATE)] + mm_nt(b["xt"][q], grad_b)
    dc = b["dbc"][q, :, pl.ds(STATE, STATE)] + mm_nt(b["ed"][q], state_b)

    def by_head(v):
        return mm(v.astype(BF), sums)

    late = by_head(dy * y - xs * inner).astype(BF)
    early = by_head(xs * outer).astype(BF)
    decayed = b["eR"][q][:1] * state
    across = jnp.sum(decayed * grad, axis=0, keepdims=True)
    across = mm(jnp.broadcast_to(across, (16, INNER)).astype(BF), sums)[:1]
    dl = mm(tri_up, late) + mm(tri, early) - early.astype(F32) + across
    ddelta = by_head(x * dxs) - rate * dl
    b["sin"][...] = decayed + b["fresh"][q]
    put(q, y, dexp * dxs, db, dc, ddelta)


def kernel(tok_hbm, cot_hbm, pm, ps, pt, bias_s, rate_s, skip_s, gated_o, ig_o, gm_o, gsh_o, gst_o, m):
    seq, mp = lax.axis_index("seq"), lax.axis_index("mp")
    core = lax.rem(mp, 2)
    chip = mp // 2
    partner = mp + 1 - 2 * core
    plane, line = seq // 4, lax.rem(seq, 4)
    low = lax.rem(seq, 2)

    load_tok = pltpu.make_async_copy(tok_hbm, m["tok3"], m["s_local"].at[0])
    load_cot = pltpu.make_async_copy(cot_hbm, m["cot"], m["s_local"].at[1])
    load_tok.start()
    load_cot.start()

    barrier = pltpu.get_barrier_semaphore()

    def greet_seq(d):
        pl.semaphore_signal(
            barrier, inc=1, device_id={"seq": lax.rem(seq + d, SEQ)}, device_id_type=MESH
        )

    def greet_mp(d):
        pl.semaphore_signal(barrier, inc=1, device_id={"mp": lax.rem(mp + d, MP)}, device_id_type=MESH)

    fori(1, SEQ, greet_seq)
    fori(1, MP, greet_mp)

    wa, wb, swp = m["wa"], m["wb"], m["swp"]
    wa[plane, line, :, pl.ds(0, 256)] = pm[:, 0, :]
    wb[plane, line, :, pl.ds(0, 256)] = pm[:, 1, :]
    wa[plane, line, :, pl.ds(256, 128)] = ps[:, 0, :]
    wb[plane, line, :, pl.ds(256, 128)] = ps[:, 1, :]
    at, lane = iota((SHARD, LANES), 0), iota((SHARD, LANES), 1)
    place = jnp.where(lane == at + SHARD * low, 1.0, 0.0).astype(BF)
    shifted = mm(pt[...], place).astype(BF)
    swp[...] = jnp.concatenate([shifted, shifted, jnp.zeros((8, LANES), BF)], axis=0)
    pl.semaphore_wait(barrier, SEQ + MP - 2)

    def along_x(k):
        return 4 * k + line

    def along_y(k):
        return 4 * plane + k

    half = SHARD // 2
    ring_a1 = Ring(plane, along_x, lambda k: wa.at[k, line], lambda k, n: wa.at[k, line, pl.ds(half * n, half)], m["s_w"].at[0])
    ring_b1 = Ring(line, along_y, lambda k: wb.at[plane, k], lambda k, n: wb.at[plane, k, pl.ds(half * n, half)], m["s_w"].at[1])
    ring_a2 = Ring(line, along_y, lambda k: wa.at[:, k], lambda k, n: wa.at[pl.ds(2 * n, 2), k], m["s_w"].at[2])
    ring_b2 = Ring(plane, along_x, lambda k: wb.at[k], lambda k, n: wb.at[k, pl.ds(2 * n, 2)], m["s_w"].at[3])
    rings = (ring_a1, ring_b1, ring_a2, ring_b2)
    ring_a1.start()
    ring_b1.start()
    send_sw = SeqExchange(lambda p: swp, lambda k: m["sw_rx"].at[k], sems(m["s_sw"]))
    send_sw.start()
    m["sw_rx"][seq] = swp[...]

    def flip(q):
        m["tokt"][:, pl.ds(q * CHUNK, CHUNK)] = m["tok3"][pl.ds(4 * q, 4)].reshape(CHUNK, DM).T

    load_tok.wait()
    flip(0)
    ring_a1.forward()
    ring_b1.forward()
    ring_a1.finish()
    ring_a2.start()
    ring_b1.finish()
    ring_b2.start()

    i, j = iota((CHUNK, CHUNK), 0), iota((CHUNK, CHUNK), 1)
    m["tri"][0] = jnp.where(i >= j, 1.0, 0.0).astype(BF)
    it, jt = (i & 15) * 16 + (i >> 4), (j & 15) * 16 + (j >> 4)
    m["tri"][1] = jnp.where(it >= jt, 1.0, 0.0).astype(BF)
    m["tri"][2] = jnp.where(i <= j, 1.0, 0.0).astype(BF)
    m["tri"][3] = jnp.where(it <= jt, 1.0, 0.0).astype(BF)
    m["sw"][...] = jnp.zeros((LANES, DM), BF)
    m["R"]["RC"][...] = jnp.zeros((8, INNER), F32)
    m["T"]["RC"][...] = jnp.zeros((8, INNER), F32)
    m["lacc"][...] = jnp.zeros((CHUNK, LANES), F32)

    head_l = iota((1, LANES), 1)
    head_c = iota((1, INNER), 1) >> 6

    def lanes_of(value):
        v = jnp.zeros((1, LANES), F32)
        for h in range(HEADS):
            v = jnp.where((head_l < 8) & ((head_l & 3) == h), value(h), v)
        return v

    def features_of(value):
        v = jnp.zeros((1, INNER), F32)
        for h in range(HEADS):
            v = jnp.where(head_c == h, value(h), v)
        return v

    bias = lanes_of(lambda h: bias_s[h])
    rate_r, rate_t = lanes_of(lambda h: rate_s[0, h]), lanes_of(lambda h: rate_s[1, h])
    ratex_r = features_of(lambda h: rate_s[0, h]) * LOG2E
    ratex_t = features_of(lambda h: rate_s[1, h]) * LOG2E
    skip = features_of(lambda h: skip_s[h])

    load_cot.wait()
    flip(1)
    ring_a2.forward()
    ring_b2.forward()
    flip(2)
    flip(3)
    ring_a2.finish()
    ring_b2.finish()
    send_sw.wait_recv()
    for k in range(SEQ // 2):
        m["sw"][pl.ds(0, 16), pl.ds(k * LANES, LANES)] = m["sw_rx"][2 * k] + m["sw_rx"][2 * k + 1]

    def rows_of(q):
        return pl.ds(pl.multiple_of(q * CHUNK, CHUNK), CHUNK)

    def columns(ref, at, width):
        return ref[:, :, :, pl.ds(at, width)].reshape(DM, width)

    def rest(v):
        return v.reshape(4, WID, LANES)

    send_pay = SeqExchange(lambda p: m["pay"].at[p], lambda k: m["trx"].at[k], sems(m["s_pay"]))
    quarter = pl.ds(pl.multiple_of(chip * COLS, COLS), COLS)
    bcr, bct = m["bcr"], m["bct"]
    send_bc = SeqExchange(
        lambda p: bcr.at[core, p, quarter], lambda k: bct.at[core, k, quarter], sems(m["s_bc"])
    )

    def piece_of(ref, k):
        return ref.at[lax.rem(k, 2), :, pl.ds(pl.multiple_of(k // 2 * COLS, COLS), COLS)]

    send_bm = MpExchange(lambda p: piece_of(bct, mp), lambda k: piece_of(bct, k), sems(m["s_bm"]))
    m["wx"][:, pl.ds(0, LANES)] = jnp.where(core == 0, columns(wa, 256, 128), columns(wb, 256, 128))
    m["wx"][:, pl.ds(LANES, LANES)] = m["sw"][...].T

    def start_four(exchange, q):
        def one(n):
            d = lax.rem(4 * q + n - seq + SEQ, SEQ)

            @pl.when(d != 0)
            def _():
                exchange.copy(d).start()

        fori(0, 4, one)

    def project(n):
        q = lax.rem(plane + n, 4)
        rows = rows_of(q)
        u = m["tok3"][pl.ds(4 * q, 4)].reshape(CHUNK, DM)
        four = pl.ds(4 * q, 4)

        def put(block, v):
            v = v.astype(BF)
            for k in range(v.shape[1] // LANES):
                m["pay"][four, pl.ds((block + k) * WID, WID), :] = rest(v[:, k * LANES : (k + 1) * LANES])

        bcr[0, four] = rest(mm(u, columns(wa, 256, 128)).astype(BF))
        bcr[1, four] = rest(mm(u, columns(wb, 256, 128)).astype(BF))
        start_four(send_bc, q)
        z = mm(u, columns(wb, 0, 256)).astype(BF)
        m["z"][rows, :] = z
        zf = z.astype(F32)
        gate = zf * jax.nn.sigmoid(zf)
        put(BY, m["cot"][rows, :].astype(F32) * gate)
        put(BX, mm(u, columns(wa, 0, 256)))
        raw = mm(u, m["wx"][:, pl.ds(LANES, LANES)]) + bias
        m["sraw"][rows, :] = raw
        pair = as_pair(jnp.maximum(raw, 0.0) + jnp.log1p(jnp.exp(-jnp.abs(raw))))
        m["lp"][rows, :] = pair
        folded = jnp.zeros((64, LANES), F32)
        for g in range(4):
            part = rest(pair)[:, g * COLS : (g + 1) * COLS, :].reshape(64, LANES)
            folded += mm(part, pair_place(8 * g))
        m["pay"][four, pl.ds(ROWS_L, COLS), :] = folded.astype(BF).reshape(4, COLS, LANES)
        start_four(send_pay, q)

    fori(0, CHUNKS, project)
    m["trx"][seq] = m["pay"][seq]
    bct[core, seq, quarter] = bcr[core, seq, quarter]

    def load_r(block, q):
        if block >= BB:
            return bcr[block - BB, pl.ds(4 * q, 4)].reshape(CHUNK, LANES)
        return m["pay"][pl.ds(4 * q, 4), pl.ds(block * WID, WID), :].reshape(CHUNK, LANES)

    def pair_r(q):
        return m["lp"][rows_of(q), :], 0

    def cols_of(block, q):
        return pl.ds(pl.multiple_of(block * WID + q * COLS, COLS), COLS)

    def load_t(block, q):
        if block >= BB:
            return bct[block - BB, :, pl.ds(q * COLS, COLS), :].reshape(CHUNK, LANES)
        return m["trx"][:, cols_of(block, q), :].reshape(CHUNK, LANES)

    def pair_t(q):
        return m["trx"][:, pl.ds(ROWS_L, COLS), :].reshape(CHUNK, LANES), 8 * q

    def pieces_exchange(source, landing, sem):
        return SeqExchange(lambda p: source.at[p], lambda k: landing.at[k], sems(sem))

    r, t = m["R"], m["T"]
    tri_r, tri_t, up_r, up_t = (m["tri"].at[k] for k in range(4))

    def chunks(low, high, step):
        for q in range(low, high):
            step(q)


    def start_pieces(b, sem):
        pack_states(b)
        e = pieces_exchange(b["st"], b["sx"], sem)
        e.start()
        b["sx"][seq] = b["st"][seq]
        return e

    def start_entering(b, sem):
        chain_states(b)
        e = pieces_exchange(b["sy"], b["sz"], sem)
        e.start()
        b["sz"][seq] = b["sy"][seq]
        return e

    chunks(0, CHUNKS, lambda q: summary(r, tri_r[...], load_r, pair_r, rate_r * LOG2E, ratex_r, q))
    send_sr = start_pieces(r, m["s_sr"])
    send_bc.wait_recv()
    send_bm.start()
    chunks(0, CHUNKS, lambda q: inside(r, tri_r[...], load_r, q))
    send_sr.wait_recv()
    send_ur = start_entering(r, m["s_ur"])

    send_pay.wait_recv()
    send_bm.wait_recv()
    chunks(0, CHUNKS, lambda q: summary(t, tri_t[...], load_t, pair_t, rate_t * LOG2E, ratex_t, q))
    send_st = start_pieces(t, m["s_st"])
    chunks(0, 2, lambda q: inside(t, tri_t[...], load_t, q))
    send_st.wait_recv()
    send_ut = start_entering(t, m["s_ut"])
    chunks(2, CHUNKS, lambda q: inside(t, tri_t[...], load_t, q))
    send_ut.wait_recv()
    entering_states(t)

    def put_t(q, y, dx, db, dc, dd):
        def put(block, v):
            v = v.astype(BF)
            for k in range(v.shape[1] // LANES):
                part = v[:, k * LANES : (k + 1) * LANES]
                at = 128 * (q // 2) + 32 * (block + k) + COLS * (q % 2)
                m["bpay"][:, pl.ds(at, COLS), :] = part.reshape(SEQ, COLS, LANES)

        put(BX, y)
        put(BY, dx)
        m["tdb"][0, q] = db.astype(BF)
        m["tdb"][1, q] = dc.astype(BF)
        for n in range(2):
            d = lax.rem(2 * q + n - mp + MP, MP)

            @pl.when(d != 0)
            def _():
                send_tr.copy(d).start()

        m["lacc"][...] += mm(as_pair(dd), pair_place(8 * q))

    def half_back(at, count, sem):
        rows = pl.ds(at, count)
        return SeqExchange(lambda p: m["bpay"].at[p, rows], lambda k: m["brx"].at[k, rows], sems(sem))

    send_back = half_back(0, 128, m["s_back"])
    send_back2 = half_back(128, 144, m["s_back2"])
    send_tr = MpExchange(
        lambda p: m["tdb"].at[lax.rem(p, 2), p // 2], lambda k: m["trs"].at[k], sems(m["s_tr"])
    )
    send_bp = SeqExchange(lambda p: m["tpiece"].at[p], lambda k: m["rpiece"].at[k], sems(m["s_bp"]))
    send_rr = MpExchange(lambda p: piece_of(m["rdb"], p), lambda k: m["rrs"].at[k], sems(m["s_rr"]))

    def group_total(ref):
        v = ref[0].astype(F32)
        for k in range(1, MP):
            v += ref[k].astype(F32)
        return v

    chunks(0, 2, lambda q: outside(t, tri_t[...], up_t[...], load_t, pair_t, rate_t, q, put_t))
    send_back.start()
    chunks(2, 4, lambda q: outside(t, tri_t[...], up_t[...], load_t, pair_t, rate_t, q, put_t))
    m["bpay"][:, pl.ds(ROWS_L, COLS), :] = m["lacc"][...].astype(BF).reshape(SEQ, COLS, LANES)
    send_back2.start()
    m["brx"][seq] = m["bpay"][seq]
    m["trs"][mp] = m["tdb"][core, chip]

    send_ur.wait_recv()
    entering_states(r)

    def put_r(q, y, dx, db, dc, dd):
        r["y"][q] = y
        r["dx"][q] = dx
        m["rdb"][0, pl.ds(4 * q, 4)] = rest(db.astype(BF))
        m["rdb"][1, pl.ds(4 * q, 4)] = rest(dc.astype(BF))
        r["dd"][q] = dd

    def outside_r(q):
        outside(r, tri_r[...], up_r[...], load_r, pair_r, rate_r, q, put_r)

    chunks(0, 1, outside_r)
    send_tr.wait_recv()
    m["tpiece"][...] = group_total(m["trs"]).astype(BF).reshape(SEQ, COLS, LANES)
    send_bp.start()
    m["rpiece"][seq] = m["tpiece"][seq]
    chunks(1, CHUNKS, outside_r)
    send_rr.start()
    m["rrs"][mp] = m["rdb"][core, :, quarter]
    send_back.wait_recv()
    send_back2.wait_recv()
    send_bp.wait_recv()
    send_rr.wait_recv()
    m["dpiece"][...] = (group_total(m["rrs"]) + m["rpiece"][...].astype(F32)).astype(BF)

    def back(block, q):
        parts = [m["brx"][pl.ds(4 * q, 4), pl.ds(128 * n + 32 * block, 32), :] for n in range(2)]
        return jnp.concatenate(parts, axis=1).reshape(CHUNK, LANES)

    def combine(q):
        rows = rows_of(q)
        x = wide(load_r, BX, q).astype(F32)
        dy = wide(load_r, BY, q).astype(F32)
        z = m["z"][rows, :].astype(F32)
        cot = m["cot"][rows, :].astype(F32)
        y = r["y"][q] + wide(back, BX, q).astype(F32) + skip * x
        sigma = jax.nn.sigmoid(z)
        gated_o[rows, :] = (y * (z * sigma)).astype(BF)
        m["g"][rows, pl.ds(256, 256)] = (cot * y * sigma * (1.0 + z * (1.0 - sigma))).astype(BF)
        m["g"][rows, pl.ds(0, 256)] = (r["dx"][q] + wide(back, BY, q).astype(F32) + skip * dy).astype(BF)
        folded = m["brx"][pl.ds(4 * q, 4), pl.ds(ROWS_L, COLS), :].reshape(64, LANES)
        parts = [mm(folded, pair_merge(8 * g)).reshape(4, COLS, LANES) for g in range(4)]
        dd = r["dd"][q] + jnp.concatenate(parts, axis=1).reshape(CHUNK, LANES)
        dstep = dd * jax.nn.sigmoid(m["sraw"][rows, :])
        m["g"][rows, pl.ds(640, LANES)] = jnp.where(iota((CHUNK, LANES), 1) < HEADS, dstep, 0.0).astype(BF)

    def pair_copy(k, q):
        rows = rows_of(q)
        return mp_copy(
            m["ip"].at[2 * k + 1 - core, rows],
            m["prx"].at[k, rows],
            m["s_pair"].at[0, k, q],
            m["s_pair"].at[1, k, q],
            partner,
        )

    def z_peer(d):
        return lax.rem(chip + d, 4)

    def z_copy(d, q):
        return mp_copy(
            m["zs"].at[z_peer(d), rows_of(q)],
            m["zrx"].at[chip, rows_of(q)],
            m["s_z"].at[0, d, q],
            m["s_z"].at[1, d, q],
            2 * z_peer(d) + core,
        )

    def z_arrival(d, q):
        origin = lax.rem(chip - d + 4, 4)
        ref = m["zrx"].at[origin, rows_of(q)]
        return mp_copy(ref, ref, m["s_z"].at[0, d, q], m["s_z"].at[1, d, q], 2 * origin + core)

    def pair_sum(k, q):
        rows = rows_of(q)
        pair_copy(k, q).wait_recv()
        return (m["ip"][2 * k + core, rows, :].astype(F32) + m["prx"][k, rows, :].astype(F32)).astype(BF)

    def pass_on(q):
        def to(d):
            m["zs"][z_peer(d), rows_of(q), :] = pair_sum(z_peer(d), q)
            z_copy(d, q).start()

        fori(1, 4, to)
        m["zrx"][chip, rows_of(q), :] = pair_sum(chip, q)

    def finish(q):
        combine(q)
        rows = rows_of(q)
        piece = m["dpiece"][pl.ds(4 * q, 4)]
        here = (iota((4, WID, LANES), 1) >> 4) == chip
        piece = jnp.where(here, jnp.concatenate([piece] * 4, axis=1), jnp.zeros((), BF)).reshape(CHUNK, LANES)
        m["g"][rows, pl.ds(512, LANES)] = piece
        g = m["g"][rows, :]
        for c in range(4):
            cols = pl.ds(c * 256, 256)
            v = mm_nt(g[:, :256], wa[c, :, :, pl.ds(0, 256)].reshape(256, 256))
            v += mm_nt(g[:, 256:512], wb[c, :, :, pl.ds(0, 256)].reshape(256, 256))
            v += mm_nt(g[:, 512:], m["wx"][cols, :])
            v = v.astype(BF)
            m["ip"][2 * c, rows, :] = v[:, :LANES]
            m["ip"][2 * c + 1, rows, :] = v[:, LANES:]
        fori(0, 4, lambda k: pair_copy(k, q).start())

    for q in range(CHUNKS):
        finish(q)
        if q > 0:
            pass_on(q - 1)

    def shard_rows(ref):
        return lambda p: ref.at[pl.ds(pl.multiple_of(p * SHARD, SHARD), SHARD)]

    send_gp = SeqExchange(shard_rows(m["gp"]), lambda k: m["gp_rx"].at[k], sems(m["s_gp"]))
    send_gs = SeqExchange(lambda p: m["gs"].at[p // 2], lambda k: m["gs_rx"].at[k], sems(m["s_gs"]))

    def grads(n):
        k = lax.rem(plane + n, 4)
        cols = rows_of(k)
        v = mm(m["tokt"][cols, :], m["g"][...])
        m["gp"][cols, :] = v[:, :640].astype(BF)
        gs = v[:, 640:].T[:16].astype(BF)
        m["gs"][2 * k] = gs[:, :LANES]
        m["gs"][2 * k + 1] = gs[:, LANES:]
        start_four(send_gp, k)
        start_four(send_gs, k)

    grads(0)
    pass_on(CHUNKS - 1)
    fori(1, 4, grads)
    own = pl.ds(pl.multiple_of(seq * SHARD, SHARD), SHARD)
    m["gp_rx"][seq] = m["gp"][own, :]
    m["gs_rx"][seq] = m["gs"][seq // 2]

    def input_sum(q):
        rows = rows_of(q)
        fori(1, 4, lambda d: z_arrival(d, q).wait_recv())
        v = m["zrx"][0, rows, :].astype(F32)
        for k in range(1, 4):
            v += m["zrx"][k, rows, :].astype(F32)
        ig_o[rows, :] = v.astype(BF)

    fori(0, CHUNKS, input_sum)

    def total_of(ref):
        v = ref[0].astype(F32)
        for k in range(1, SEQ):
            v += ref[k].astype(F32)
        return v

    send_gp.wait_recv()
    main = total_of(m["gp_rx"])
    m["fsh"][...] = main[:, 512:]
    send_fin = MpExchange(lambda p: m["fsh"], lambda k: m["frx"].at[k], sems(m["s_fin"]))
    send_fin.start()
    m["frx"][mp] = main[:, 512:]
    gm_o[:, 0, :] = main[:, :INNER]
    gm_o[:, 1, :] = main[:, INNER : 2 * INNER]
    send_gs.wait_recv()
    step = total_of(m["gs_rx"])
    gst_o[...] = jnp.where(low == 0, step[:HEADS, :SHARD], step[:HEADS, SHARD:])
    send_fin.wait_recv()
    for n in range(2):
        gsh_o[:, n, :] = m["frx"][n] + m["frx"][2 + n] + m["frx"][4 + n] + m["frx"][6 + n]

    sent = rings + (send_sw, send_pay, send_bc, send_bm, send_sr, send_ur, send_st, send_ut)
    sent += (send_back, send_back2, send_tr, send_bp, send_rr, send_gp, send_gs, send_fin)
    for e in sent:
        e.wait_send()
    for q in range(CHUNKS):
        fori(0, 4, lambda k: pair_copy(k, q).wait_send())
        fori(1, 4, lambda d: z_copy(d, q).wait_send())


def hand_over(*refs):
    n = len(refs) // 2
    for k in range(n):
        refs[n + k][...] = refs[k][...]


def body(tokens, proj_main, proj_shared, proj_step, step_bias, decay_rate, skip_gain, cotangent):
    vm = pl.BlockSpec(memory_space=pltpu.VMEM)
    sm = pl.BlockSpec(memory_space=pltpu.SMEM)
    hbm = pl.BlockSpec(memory_space=pl.ANY)
    shapes = (
        jax.ShapeDtypeStruct((TOK, INNER), BF),
        jax.ShapeDtypeStruct((TOK, LANES), BF),
        jax.ShapeDtypeStruct((SHARD, 2, INNER), F32),
        jax.ShapeDtypeStruct((SHARD, 2, STATE), F32),
        jax.ShapeDtypeStruct((HEADS, SHARD), F32),
    )
    results = pl.pallas_call(
        kernel,
        out_shape=shapes,
        in_specs=[hbm, hbm, vm, vm, vm, sm, sm, sm],
        out_specs=(vm,) * 5,
        scratch_shapes=[main_scratch()],
        compiler_params=pltpu.CompilerParams(
            collective_id=0, has_side_effects=True, vmem_limit_bytes=62 * 1024 * 1024
        ),
    )(
        tokens.reshape(SEQ, WID, DM),
        cotangent.reshape(TOK, INNER),
        proj_main,
        proj_shared,
        proj_step.T,
        step_bias,
        decay_rate,
        skip_gain,
    )
    gated, ig, gm, gsh, gst = pl.pallas_call(
        hand_over,
        out_shape=shapes,
        in_specs=[vm] * 5,
        out_specs=(vm,) * 5,
    )(*results)
    return (
        gated.reshape(1, 16, WID, INNER),
        ig.reshape(1, 16, WID, LANES),
        gm,
        gsh,
        gst.T,
    )


def solution(mesh):
    placed = (
        P("seq", None, None, None),
        P("seq", None, "mp"),
        P("seq", None, None),
        P("seq", "mp"),
        P("mp"),
        P(None, "mp"),
        P("mp"),
        P("seq", None, None, "mp"),
    )
    return jax.shard_map(
        body,
        mesh=mesh,
        in_specs=placed,
        out_specs=(
            P("seq", None, None, "mp"),
            P("seq", None, None, "mp"),
            P("seq", None, "mp"),
            P("seq", None, None),
            P("seq", "mp"),
        ),
        check_vma=False,
    )
```

```python
import jax
import jax.numpy as jnp
from jax import lax
from jax.experimental import pallas as pl
from jax.experimental.pallas import tpu as pltpu
from jax.sharding import PartitionSpec as P

MESH = pl.DeviceIdType.MESH
BF = jnp.bfloat16
F32 = jnp.float32

SEQ = 16
MP = 8
TOK = 1024
WID = 64
DM = 1024
INNER = 256
HEADS = 4
STATE = 128
LANES = 128
CHUNK = 256
CHUNKS = TOK // CHUNK
COLS = CHUNK // SEQ
SHARD = DM // SEQ
BX, BY, BB, BC, ROWS_L, ROWS = 0, 2, 4, 5, 256, 272
PIECE = STATE // SEQ
HALF = 3 * LANES
LOG2E = 1.4426950408889634


def iota(shape, axis):
    return lax.broadcasted_iota(jnp.int32, shape, axis)


def mm(a, b):
    return lax.dot_general(a, b, (((1,), (0,)), ((), ())), preferred_element_type=F32)


def mm_nt(a, b):
    return lax.dot_general(a, b, (((1,), (1,)), ((), ())), preferred_element_type=F32)


def mm_tn(a, b):
    return lax.dot_general(a, b, (((0,), (0,)), ((), ())), preferred_element_type=F32)


def halves(v):
    hi = v.astype(BF)
    return hi, (v - hi.astype(F32)).astype(BF)


def as_pair(v):
    lane = iota(v.shape, 1)
    hi = v.astype(BF).astype(F32)
    return jnp.where(lane < 4, hi, jnp.where(lane < 8, v - hi, 0.0)).astype(BF)


def fori(low, high, step):
    def run(i, carry):
        step(i)
        return carry

    lax.fori_loop(low, high, run, 0)


class SeqExchange:
    def __init__(self, source, landing, sems):
        self.source, self.landing = source, landing
        self.send, self.recv = sems
        self.me = lax.axis_index("seq")

    def copy(self, d):
        peer = lax.rem(self.me + d, SEQ)
        return pltpu.make_async_remote_copy(
            src_ref=self.source(peer),
            dst_ref=self.landing(self.me),
            send_sem=self.send.at[d],
            recv_sem=self.recv.at[d],
            device_id={"seq": peer},
            device_id_type=MESH,
        )

    def arrival(self, d):
        origin = lax.rem(self.me - d + SEQ, SEQ)
        return pltpu.make_async_remote_copy(
            src_ref=self.landing(origin),
            dst_ref=self.landing(origin),
            send_sem=self.send.at[d],
            recv_sem=self.recv.at[d],
            device_id={"seq": origin},
            device_id_type=MESH,
        )

    def start(self):
        fori(1, SEQ, lambda d: self.copy(d).start())

    def wait_recv(self):
        fori(1, SEQ, lambda d: self.arrival(d).wait_recv())

    def wait_send(self):
        fori(1, SEQ, lambda d: self.copy(d).wait_send())


class Ring:
    def __init__(self, me, to, whole, part, sems):
        self.whole, self.part, self.sems, self.to = whole, part, sems, to
        self.me, self.right, self.left = me, lax.rem(me + 1, 4), lax.rem(me + 3, 4)
        self.far = lax.rem(me + 2, 4)

    def copy(self, ref, k, peer):
        return pltpu.make_async_remote_copy(
            src_ref=ref,
            dst_ref=ref,
            send_sem=self.sems.at[0, k],
            recv_sem=self.sems.at[1, k],
            device_id={"seq": self.to(peer)},
            device_id_type=MESH,
        )

    def start(self):
        self.copy(self.whole(self.me), 0, self.right).start()
        self.copy(self.whole(self.me), 1, self.left).start()

    def forward(self):
        self.copy(self.whole(self.left), 0, self.left).wait_recv()
        self.copy(self.part(self.left, 0), 2, self.right).start()
        self.copy(self.whole(self.right), 1, self.right).wait_recv()
        self.copy(self.part(self.right, 1), 3, self.left).start()

    def finish(self):
        self.copy(self.part(self.far, 0), 2, self.left).wait_recv()
        self.copy(self.part(self.far, 1), 3, self.right).wait_recv()

    def wait_send(self):
        self.copy(self.whole(self.me), 0, self.right).wait_send()
        self.copy(self.whole(self.me), 1, self.left).wait_send()
        self.copy(self.part(self.left, 0), 2, self.right).wait_send()
        self.copy(self.part(self.right, 1), 3, self.left).wait_send()


class RingSum:
    def __init__(self, me, to, part, raw, near, sems):
        self.part, self.raw, self.near, self.sems, self.to = part, raw, near, sems, to
        self.me, self.far = me, lax.rem(me + 2, 4)
        self.side = (lax.rem(me + 3, 4), lax.rem(me + 1, 4))

    def copy(self, source, landing, k, peer):
        return pltpu.make_async_remote_copy(
            src_ref=source,
            dst_ref=landing,
            send_sem=self.sems.at[0, k],
            recv_sem=self.sems.at[1, k],
            device_id=self.to(peer),
            device_id_type=MESH,
        )

    def far_copy(self, n):
        return self.copy(self.part(self.far, n), self.raw(n), n, self.side[1 - n])

    def own_copy(self, n):
        peer = self.side[1 - n]
        return self.copy(self.part(peer, 1 - n), self.near(n, 1 - n), 2 + n, peer)

    def sum_copy(self, n):
        peer = self.side[1 - n]
        return self.copy(self.part(peer, n), self.near(n, n), 4 + n, peer)

    def start_far(self):
        for n in range(2):
            self.far_copy(n).start()

    def start_near(self):
        for n in range(2):
            self.own_copy(n).start()

    def middle(self):
        for n in range(2):
            self.copy(self.raw(n), self.raw(n), n, self.side[n]).wait_recv()
            ref = self.part(self.side[1 - n], n)
            ref[...] = (ref[...].astype(F32) + self.raw(n)[...].astype(F32)).astype(BF)
            self.sum_copy(n).start()

    def finish(self):
        halves = []
        for n in range(2):
            for k in range(2):
                ref = self.near(k, n)
                self.copy(ref, ref, 2 + k if n != k else 4 + k, self.side[k]).wait_recv()
            v = self.part(self.me, n)[...].astype(F32)
            halves.append(v + self.near(0, n)[...].astype(F32) + self.near(1, n)[...].astype(F32))
        return halves

    def wait_send(self):
        for n in range(2):
            self.far_copy(n).wait_send()
            self.own_copy(n).wait_send()
            self.sum_copy(n).wait_send()


def mp_copy(source, landing, send, recv, peer):
    return pltpu.make_async_remote_copy(
        src_ref=source,
        dst_ref=landing,
        send_sem=send,
        recv_sem=recv,
        device_id={"mp": peer},
        device_id_type=MESH,
    )


class MpExchange:
    def __init__(self, source, landing, sems):
        self.source, self.landing = source, landing
        self.send, self.recv = sems
        self.me = lax.axis_index("mp")

    def copy(self, d):
        peer = lax.rem(self.me + d, MP)
        return mp_copy(self.source(peer), self.landing(self.me), self.send.at[d], self.recv.at[d], peer)

    def arrival(self, d):
        origin = lax.rem(self.me - d + MP, MP)
        ref = self.landing(origin)
        return mp_copy(ref, ref, self.send.at[d], self.recv.at[d], origin)

    def start(self):
        fori(1, MP, lambda d: self.copy(d).start())

    def wait_recv(self):
        fori(1, MP, lambda d: self.arrival(d).wait_recv())

    def wait_send(self):
        fori(1, MP, lambda d: self.copy(d).wait_send())


def scan_scratch():
    v = pltpu.VMEM
    return dict(
        xs=v((CHUNKS, CHUNK, INNER), BF),
        xt=v((CHUNKS, CHUNK, INNER), BF),
        ed=v((CHUNKS, CHUNK, INNER), BF),
        er=v((CHUNKS, CHUNK, INNER), F32),
        tail=v((CHUNKS, CHUNK, INNER), F32),
        rcol=v((CHUNKS, CHUNK, LANES), F32),
        fresh=v((CHUNKS, STATE, INNER), F32),
        back=v((CHUNKS, STATE, INNER), F32),
        eR=v((CHUNKS, 8, INNER), F32),
        RC=v((8, INNER), F32),
        st=v((SEQ, 4 * PIECE, INNER), BF),
        sx=v((SEQ, 4 * PIECE, INNER), BF),
        sy=v((SEQ, 2 * PIECE, INNER), BF),
        sz=v((SEQ, 2 * PIECE, INNER), BF),
        y=v((CHUNKS, CHUNK, INNER), F32),
        dx=v((CHUNKS, CHUNK, INNER), F32),
        dbc=v((CHUNKS, CHUNK, 2 * STATE), F32),
        dd=v((CHUNKS, CHUNK, LANES), F32),
        gin=v((CHUNKS, STATE, INNER), F32),
        sin=v((STATE, INNER), F32),
    )


def main_scratch():
    v = pltpu.VMEM
    dma = pltpu.SemaphoreType.DMA
    seq_sems = lambda: dma((2, SEQ))
    return dict(
        tok3=v((SEQ, WID, DM), BF),
        cot=v((TOK, INNER), BF),
        wa=v((4, 4, SHARD, HALF), BF),
        wb=v((4, 4, SHARD, HALF), BF),
        sw_rx=v((SEQ, 16, LANES), BF),
        sw=v((LANES, DM), BF),
        z=v((TOK, INNER), BF),
        sraw=v((TOK, LANES), F32),
        pay=v((SEQ, ROWS, LANES), BF),
        trx=v((SEQ, ROWS, LANES), BF),
        bpay=v((SEQ, ROWS, LANES), BF),
        brx=v((SEQ, ROWS, LANES), BF),
        tri=v((4, CHUNK, CHUNK), BF),
        lp=v((TOK, LANES), BF),
        bcr=v((2, SEQ, WID, LANES), BF),
        bct=v((2, SEQ, WID, LANES), BF),
        wx=v((DM, 2 * LANES), BF),
        tdb=v((2, CHUNKS, CHUNK, LANES), BF),
        trs=v((MP, CHUNK, LANES), BF),
        tpiece=v((SEQ, COLS, LANES), BF),
        rpiece=v((SEQ, COLS, LANES), BF),
        rdb=v((2, SEQ, WID, LANES), BF),
        rrs=v((MP, SEQ, COLS, LANES), BF),
        dpiece=v((SEQ, COLS, LANES), BF),
        lacc=v((CHUNK, LANES), F32),
        swp=v((16, LANES), BF),
        R=scan_scratch(),
        T=scan_scratch(),
        g=v((TOK, 768), BF),
        tokt=v((DM, TOK), BF),
        gp=v((4, 4, SHARD, 640), BF),
        g_raw=v((2, 2, 2, 32, 640), BF),
        g_near=v((2, 2, 4, 32, 640), BF),
        h_own=v((2, 4, 32, 640), BF),
        h_raw=v((2, 2, 16, 640), BF),
        h_near=v((2, 2, 32, 640), BF),
        z_raw=v((2, 2, CHUNK, LANES), BF),
        z_near=v((2, 2, 2 * CHUNK, LANES), BF),
        gs=v((MP, 16, LANES), BF),
        gs_rx=v((SEQ, 16, LANES), BF),
        ip=v((MP, TOK, LANES), BF),
        prx=v((4, TOK, LANES), BF),
        zs=v((4, TOK, LANES), BF),
        fsh=v((SHARD, LANES), F32),
        frx=v((MP, SHARD, LANES), F32),
        s_local=dma((4,)),
        s_w=dma((4, 2, 4)),
        s_sw=seq_sems(),
        s_pay=seq_sems(),
        s_sr=seq_sems(),
        s_st=seq_sems(),
        s_ur=seq_sems(),
        s_ut=seq_sems(),
        s_back=seq_sems(),
        s_back2=seq_sems(),
        s_gp=dma((4, 2, 6)),
        s_bc=seq_sems(),
        s_bp=seq_sems(),
        s_gs=seq_sems(),
        s_bm=dma((2, MP)),
        s_tr=dma((2, MP)),
        s_rr=dma((2, MP)),
        s_fin=dma((2, MP)),
        s_pair=dma((2, 4, CHUNKS)),
        s_z=dma((2, 2, 6)),
    )


def sems(ref):
    return ref.at[0], ref.at[1]


def head_sum():
    c, h = iota((INNER, LANES), 0), iota((INNER, LANES), 1)
    return jnp.where((h < 8) & ((h & 3) == (c >> 6)), 1.0, 0.0).astype(BF)


def pair_expand(shift):
    k, c = iota((LANES, INNER), 0) - shift, iota((LANES, INNER), 1)
    return jnp.where((k >= 0) & (k < 8) & ((k & 3) == (c >> 6)), 1.0, 0.0).astype(BF)


def pair_merge(shift):
    k, h = iota((LANES, LANES), 0) - shift, iota((LANES, LANES), 1)
    return jnp.where((k >= 0) & (k < 8) & (h < 8) & ((k & 3) == (h & 3)), 1.0, 0.0).astype(BF)


def pair_place(shift):
    k, lane = iota((LANES, LANES), 0), iota((LANES, LANES), 1)
    return jnp.where((k < 8) & (lane == k + shift), 1.0, 0.0).astype(BF)


def wide(load, block, q):
    return jnp.concatenate([load(block, q), load(block + 1, q)], axis=1)


def summary(b, tri, load, pair_of, rate, ratex, q):
    x = wide(load, BX, q).astype(F32)
    dy = wide(load, BY, q).astype(F32)
    pair, shift = pair_of(q)
    dexp = mm(pair, pair_expand(shift))
    logs = (-dexp * ratex).astype(BF)
    rexp = mm(tri, logs)
    b["rcol"][q] = mm(tri, (-mm(pair, pair_merge(shift)) * rate).astype(BF))
    total = jnp.sum(logs.astype(F32), axis=0, keepdims=True)
    er = jnp.exp2(rexp)
    tail = jnp.exp2(jnp.minimum(total - rexp, 0.0))
    xs = (x * dexp).astype(BF)
    xt = (xs.astype(F32) * tail).astype(BF)
    ed = (er * dy).astype(BF)
    b["er"][q] = er
    b["tail"][q] = tail
    b["xs"][q] = xs
    b["xt"][q] = xt
    b["ed"][q] = ed
    b["fresh"][q] = mm_tn(load(BB, q), xt)
    b["back"][q] = mm_tn(load(BC, q), ed)
    rows = jnp.broadcast_to(total, (8, INNER))
    b["eR"][q] = jnp.exp2(rows)
    b["RC"][...] += rows


def pack_states(b):
    e = [b["eR"][q][:1] for q in range(CHUNKS)]
    end = b["fresh"][0]
    for q in range(1, CHUNKS):
        end = end * e[q] + b["fresh"][q]
    first = b["back"][CHUNKS - 1]
    for q in range(CHUNKS - 2, -1, -1):
        first = first * e[q] + b["back"][q]
    rc = b["RC"][...]
    hi = rc.astype(BF).astype(F32)
    logs = jnp.concatenate([hi, rc - hi], axis=0).astype(BF)
    pieces = [v.reshape(SEQ, PIECE, INNER) for v in (end, first)]
    b["st"][:, pl.ds(0, 2 * PIECE), :] = jnp.concatenate(pieces, axis=1).astype(BF)
    for k in range(SEQ):
        b["st"][k, pl.ds(2 * PIECE, 2 * PIECE)] = logs


def chain_states(b):
    own = [b["sx"][k, pl.ds(0, 2 * PIECE)].astype(F32) for k in range(SEQ)]
    logs = [b["sx"][k, pl.ds(2 * PIECE, 2 * PIECE)].astype(F32) for k in range(SEQ)]
    decay = [jnp.exp2(v[:PIECE] + v[PIECE:]) for v in logs]
    state = [jnp.zeros((PIECE, INNER), F32)]
    grad = [jnp.zeros((PIECE, INNER), F32)]
    for k in range(SEQ - 1):
        state.append(state[k] * decay[k] + own[k][:PIECE])
        n = SEQ - 1 - k
        grad.append(grad[k] * decay[n] + own[n][PIECE:])
    for k in range(SEQ):
        b["sy"][k] = jnp.concatenate([state[k], grad[SEQ - 1 - k]], axis=0).astype(BF)


def entering_states(b):
    both = b["sz"][...].astype(F32)
    b["sin"][...] = both[:, :PIECE, :].reshape(STATE, INNER)
    grad = both[:, PIECE:, :].reshape(STATE, INNER)
    for q in range(CHUNKS - 1, -1, -1):
        b["gin"][q] = grad
        if q > 0:
            grad = grad * b["eR"][q][:1] + b["back"][q]


def head_rows(h):
    one = jnp.where((iota((16, INNER), 1) >> 6) == h, 1.0, 0.0).astype(BF)
    return jnp.concatenate([one] * (CHUNK // 16), axis=0)


def inside(b, tri, load, q):
    dy = wide(load, BY, q)
    bmat = load(BB, q)
    cmat = load(BC, q)
    xs = b["xs"][q]
    trif = tri.astype(F32)
    scores = mm_nt(cmat, bmat) * trif
    rcol = b["rcol"][q]
    rrow = rcol.T
    pairs = None
    ms, dys, xss = [], [], []
    for h in range(HEADS):
        decay = jnp.exp2(jnp.minimum(rcol[:, h : h + 1] - rrow[h : h + 1, :], 0.0))
        ms.append((decay * scores).astype(BF))
        mask = head_rows(h)
        dys.append(dy * mask)
        xss.append(xs * mask)
        term = decay * mm_nt(dys[h], xs)
        pairs = term if h == 0 else pairs + term
    dy4 = jnp.concatenate(dys, axis=0)
    y = mm(jnp.concatenate(ms, axis=1), jnp.concatenate(xss, axis=0))
    dxs = mm_tn(jnp.concatenate(ms, axis=0), dy4)
    pairs = (pairs * trif).astype(BF)
    b["y"][q] = y
    b["dx"][q] = dxs
    b["dbc"][q, :, pl.ds(0, STATE)] = mm_tn(pairs, cmat)
    b["dbc"][q, :, pl.ds(STATE, STATE)] = mm(pairs, bmat)


def outside(b, tri, tri_up, load, pair_of, rate, q, put):
    x = wide(load, BX, q).astype(F32)
    dy = wide(load, BY, q).astype(F32)
    bmat = load(BB, q)
    cmat = load(BC, q)
    pair, shift = pair_of(q)
    dexp = mm(pair, pair_expand(shift))
    xs = b["xs"][q].astype(F32)
    state = b["sin"][...]
    grad = b["gin"][q]
    state_b, grad_b = state.astype(BF), grad.astype(BF)
    sums = head_sum()
    y = b["y"][q] + b["er"][q] * mm(cmat, state_b)
    inner = b["dx"][q]
    outer = b["tail"][q] * mm(bmat, grad_b)
    dxs = inner + outer
    db = b["dbc"][q, :, pl.ds(0, STATE)] + mm_nt(b["xt"][q], grad_b)
    dc = b["dbc"][q, :, pl.ds(STATE, STATE)] + mm_nt(b["ed"][q], state_b)

    def by_head(v):
        return mm(v.astype(BF), sums)

    late = by_head(dy * y - xs * inner).astype(BF)
    early = by_head(xs * outer).astype(BF)
    decayed = b["eR"][q][:1] * state
    across = jnp.sum(decayed * grad, axis=0, keepdims=True)
    across = mm(jnp.broadcast_to(across, (16, INNER)).astype(BF), sums)[:1]
    dl = mm(tri_up, late) + mm(tri, early) - early.astype(F32) + across
    ddelta = by_head(x * dxs) - rate * dl
    b["sin"][...] = decayed + b["fresh"][q]
    put(q, y, dexp * dxs, db, dc, ddelta)


def kernel(tok_hbm, cot_hbm, pm, ps, pt, bias_s, rate_s, skip_s, gated_o, ig_o, gm_o, gsh_o, gst_o, m):
    seq, mp = lax.axis_index("seq"), lax.axis_index("mp")
    core = lax.rem(mp, 2)
    chip = mp // 2
    partner = mp + 1 - 2 * core
    plane, line = seq // 4, lax.rem(seq, 4)
    low = lax.rem(seq, 2)

    load_tok = pltpu.make_async_copy(tok_hbm, m["tok3"], m["s_local"].at[0])
    load_cot = pltpu.make_async_copy(cot_hbm, m["cot"], m["s_local"].at[1])
    load_tok.start()
    load_cot.start()

    barrier = pltpu.get_barrier_semaphore()

    def greet_seq(d):
        pl.semaphore_signal(
            barrier, inc=1, device_id={"seq": lax.rem(seq + d, SEQ)}, device_id_type=MESH
        )

    def greet_mp(d):
        pl.semaphore_signal(barrier, inc=1, device_id={"mp": lax.rem(mp + d, MP)}, device_id_type=MESH)

    fori(1, SEQ, greet_seq)
    fori(1, MP, greet_mp)

    wa, wb, swp = m["wa"], m["wb"], m["swp"]
    wa[plane, line, :, pl.ds(0, 256)] = pm[:, 0, :]
    wb[plane, line, :, pl.ds(0, 256)] = pm[:, 1, :]
    wa[plane, line, :, pl.ds(256, 128)] = ps[:, 0, :]
    wb[plane, line, :, pl.ds(256, 128)] = ps[:, 1, :]
    at, lane = iota((SHARD, LANES), 0), iota((SHARD, LANES), 1)
    place = jnp.where(lane == at + SHARD * low, 1.0, 0.0).astype(BF)
    shifted = mm(pt[...], place).astype(BF)
    swp[...] = jnp.concatenate([shifted, shifted, jnp.zeros((8, LANES), BF)], axis=0)
    pl.semaphore_wait(barrier, SEQ + MP - 2)

    def along_x(k):
        return 4 * k + line

    def along_y(k):
        return 4 * plane + k

    half = SHARD // 2
    ring_a1 = Ring(plane, along_x, lambda k: wa.at[k, line], lambda k, n: wa.at[k, line, pl.ds(half * n, half)], m["s_w"].at[0])
    ring_b1 = Ring(line, along_y, lambda k: wb.at[plane, k], lambda k, n: wb.at[plane, k, pl.ds(half * n, half)], m["s_w"].at[1])
    ring_a2 = Ring(line, along_y, lambda k: wa.at[:, k], lambda k, n: wa.at[pl.ds(2 * n, 2), k], m["s_w"].at[2])
    ring_b2 = Ring(plane, along_x, lambda k: wb.at[k], lambda k, n: wb.at[k, pl.ds(2 * n, 2)], m["s_w"].at[3])
    rings = (ring_a1, ring_b1, ring_a2, ring_b2)
    ring_a1.start()
    ring_b1.start()
    send_sw = SeqExchange(lambda p: swp, lambda k: m["sw_rx"].at[k], sems(m["s_sw"]))
    send_sw.start()
    m["sw_rx"][seq] = swp[...]

    def flip(q):
        m["tokt"][:, pl.ds(q * CHUNK, CHUNK)] = m["tok3"][pl.ds(4 * q, 4)].reshape(CHUNK, DM).T

    load_tok.wait()
    flip(0)
    ring_a1.forward()
    ring_b1.forward()
    ring_a1.finish()
    ring_a2.start()
    ring_b1.finish()
    ring_b2.start()

    i, j = iota((CHUNK, CHUNK), 0), iota((CHUNK, CHUNK), 1)
    m["tri"][0] = jnp.where(i >= j, 1.0, 0.0).astype(BF)
    it, jt = (i & 15) * 16 + (i >> 4), (j & 15) * 16 + (j >> 4)
    m["tri"][1] = jnp.where(it >= jt, 1.0, 0.0).astype(BF)
    m["tri"][2] = jnp.where(i <= j, 1.0, 0.0).astype(BF)
    m["tri"][3] = jnp.where(it <= jt, 1.0, 0.0).astype(BF)
    m["sw"][...] = jnp.zeros((LANES, DM), BF)
    m["R"]["RC"][...] = jnp.zeros((8, INNER), F32)
    m["T"]["RC"][...] = jnp.zeros((8, INNER), F32)
    m["lacc"][...] = jnp.zeros((CHUNK, LANES), F32)

    head_l = iota((1, LANES), 1)
    head_c = iota((1, INNER), 1) >> 6

    def lanes_of(value):
        v = jnp.zeros((1, LANES), F32)
        for h in range(HEADS):
            v = jnp.where((head_l < 8) & ((head_l & 3) == h), value(h), v)
        return v

    def features_of(value):
        v = jnp.zeros((1, INNER), F32)
        for h in range(HEADS):
            v = jnp.where(head_c == h, value(h), v)
        return v

    bias = lanes_of(lambda h: bias_s[h])
    rate_r, rate_t = lanes_of(lambda h: rate_s[0, h]), lanes_of(lambda h: rate_s[1, h])
    ratex_r = features_of(lambda h: rate_s[0, h]) * LOG2E
    ratex_t = features_of(lambda h: rate_s[1, h]) * LOG2E
    skip = features_of(lambda h: skip_s[h])

    load_cot.wait()
    flip(1)
    ring_a2.forward()
    ring_b2.forward()
    flip(2)
    flip(3)
    ring_a2.finish()
    ring_b2.finish()
    send_sw.wait_recv()
    for k in range(SEQ // 2):
        m["sw"][pl.ds(0, 16), pl.ds(k * LANES, LANES)] = m["sw_rx"][2 * k] + m["sw_rx"][2 * k + 1]

    def rows_of(q):
        return pl.ds(pl.multiple_of(q * CHUNK, CHUNK), CHUNK)

    def columns(ref, at, width):
        return ref[:, :, :, pl.ds(at, width)].reshape(DM, width)

    def rest(v):
        return v.reshape(4, WID, LANES)

    send_pay = SeqExchange(lambda p: m["pay"].at[p], lambda k: m["trx"].at[k], sems(m["s_pay"]))
    quarter = pl.ds(pl.multiple_of(chip * COLS, COLS), COLS)
    bcr, bct = m["bcr"], m["bct"]
    send_bc = SeqExchange(
        lambda p: bcr.at[core, p, quarter], lambda k: bct.at[core, k, quarter], sems(m["s_bc"])
    )

    def piece_of(ref, k):
        return ref.at[lax.rem(k, 2), :, pl.ds(pl.multiple_of(k // 2 * COLS, COLS), COLS)]

    send_bm = MpExchange(lambda p: piece_of(bct, mp), lambda k: piece_of(bct, k), sems(m["s_bm"]))
    m["wx"][:, pl.ds(0, LANES)] = jnp.where(core == 0, columns(wa, 256, 128), columns(wb, 256, 128))
    m["wx"][:, pl.ds(LANES, LANES)] = m["sw"][...].T

    def start_four(exchange, q):
        def one(n):
            d = lax.rem(4 * q + n - seq + SEQ, SEQ)

            @pl.when(d != 0)
            def _():
                exchange.copy(d).start()

        fori(0, 4, one)

    def project(n):
        q = lax.rem(plane + n, 4)
        rows = rows_of(q)
        u = m["tok3"][pl.ds(4 * q, 4)].reshape(CHUNK, DM)
        four = pl.ds(4 * q, 4)

        def put(block, v):
            v = v.astype(BF)
            for k in range(v.shape[1] // LANES):
                m["pay"][four, pl.ds((block + k) * WID, WID), :] = rest(v[:, k * LANES : (k + 1) * LANES])

        bcr[0, four] = rest(mm(u, columns(wa, 256, 128)).astype(BF))
        bcr[1, four] = rest(mm(u, columns(wb, 256, 128)).astype(BF))
        start_four(send_bc, q)
        z = mm(u, columns(wb, 0, 256)).astype(BF)
        m["z"][rows, :] = z
        zf = z.astype(F32)
        gate = zf * jax.nn.sigmoid(zf)
        put(BY, m["cot"][rows, :].astype(F32) * gate)
        put(BX, mm(u, columns(wa, 0, 256)))
        raw = mm(u, m["wx"][:, pl.ds(LANES, LANES)]) + bias
        m["sraw"][rows, :] = raw
        pair = as_pair(jnp.maximum(raw, 0.0) + jnp.log1p(jnp.exp(-jnp.abs(raw))))
        m["lp"][rows, :] = pair
        folded = jnp.zeros((64, LANES), F32)
        for g in range(4):
            part = rest(pair)[:, g * COLS : (g + 1) * COLS, :].reshape(64, LANES)
            folded += mm(part, pair_place(8 * g))
        m["pay"][four, pl.ds(ROWS_L, COLS), :] = folded.astype(BF).reshape(4, COLS, LANES)
        start_four(send_pay, q)

    fori(0, CHUNKS, project)
    m["trx"][seq] = m["pay"][seq]
    bct[core, seq, quarter] = bcr[core, seq, quarter]

    def load_r(block, q):
        if block >= BB:
            return bcr[block - BB, pl.ds(4 * q, 4)].reshape(CHUNK, LANES)
        return m["pay"][pl.ds(4 * q, 4), pl.ds(block * WID, WID), :].reshape(CHUNK, LANES)

    def pair_r(q):
        return m["lp"][rows_of(q), :], 0

    def cols_of(block, q):
        return pl.ds(pl.multiple_of(block * WID + q * COLS, COLS), COLS)

    def load_t(block, q):
        if block >= BB:
            return bct[block - BB, :, pl.ds(q * COLS, COLS), :].reshape(CHUNK, LANES)
        return m["trx"][:, cols_of(block, q), :].reshape(CHUNK, LANES)

    def pair_t(q):
        return m["trx"][:, pl.ds(ROWS_L, COLS), :].reshape(CHUNK, LANES), 8 * q

    def pieces_exchange(source, landing, sem):
        return SeqExchange(lambda p: source.at[p], lambda k: landing.at[k], sems(sem))

    r, t = m["R"], m["T"]
    tri_r, tri_t, up_r, up_t = (m["tri"].at[k] for k in range(4))

    def chunks(low, high, step):
        for q in range(low, high):
            step(q)


    def start_pieces(b, sem):
        pack_states(b)
        e = pieces_exchange(b["st"], b["sx"], sem)
        e.start()
        b["sx"][seq] = b["st"][seq]
        return e

    def start_entering(b, sem):
        chain_states(b)
        e = pieces_exchange(b["sy"], b["sz"], sem)
        e.start()
        b["sz"][seq] = b["sy"][seq]
        return e

    chunks(0, CHUNKS, lambda q: summary(r, tri_r[...], load_r, pair_r, rate_r * LOG2E, ratex_r, q))
    send_sr = start_pieces(r, m["s_sr"])
    send_bc.wait_recv()
    send_bm.start()
    chunks(0, CHUNKS, lambda q: inside(r, tri_r[...], load_r, q))
    send_sr.wait_recv()
    send_ur = start_entering(r, m["s_ur"])

    send_pay.wait_recv()
    send_bm.wait_recv()
    chunks(0, CHUNKS, lambda q: summary(t, tri_t[...], load_t, pair_t, rate_t * LOG2E, ratex_t, q))
    send_st = start_pieces(t, m["s_st"])
    chunks(0, 2, lambda q: inside(t, tri_t[...], load_t, q))
    send_st.wait_recv()
    send_ut = start_entering(t, m["s_ut"])
    chunks(2, CHUNKS, lambda q: inside(t, tri_t[...], load_t, q))
    send_ut.wait_recv()
    entering_states(t)

    def put_t(q, y, dx, db, dc, dd):
        def put(block, v):
            v = v.astype(BF)
            for k in range(v.shape[1] // LANES):
                part = v[:, k * LANES : (k + 1) * LANES]
                at = 128 * (q // 2) + 32 * (block + k) + COLS * (q % 2)
                m["bpay"][:, pl.ds(at, COLS), :] = part.reshape(SEQ, COLS, LANES)

        put(BX, y)
        put(BY, dx)
        m["tdb"][0, q] = db.astype(BF)
        m["tdb"][1, q] = dc.astype(BF)
        for n in range(2):
            d = lax.rem(2 * q + n - mp + MP, MP)

            @pl.when(d != 0)
            def _():
                send_tr.copy(d).start()

        m["lacc"][...] += mm(as_pair(dd), pair_place(8 * q))

    def half_back(at, count, sem):
        rows = pl.ds(at, count)
        return SeqExchange(lambda p: m["bpay"].at[p, rows], lambda k: m["brx"].at[k, rows], sems(sem))

    send_back = half_back(0, 128, m["s_back"])
    send_back2 = half_back(128, 144, m["s_back2"])
    send_tr = MpExchange(
        lambda p: m["tdb"].at[lax.rem(p, 2), p // 2], lambda k: m["trs"].at[k], sems(m["s_tr"])
    )
    send_bp = SeqExchange(lambda p: m["tpiece"].at[p], lambda k: m["rpiece"].at[k], sems(m["s_bp"]))
    send_rr = MpExchange(lambda p: piece_of(m["rdb"], p), lambda k: m["rrs"].at[k], sems(m["s_rr"]))

    def group_total(ref):
        v = ref[0].astype(F32)
        for k in range(1, MP):
            v += ref[k].astype(F32)
        return v

    chunks(0, 2, lambda q: outside(t, tri_t[...], up_t[...], load_t, pair_t, rate_t, q, put_t))
    send_back.start()
    chunks(2, 4, lambda q: outside(t, tri_t[...], up_t[...], load_t, pair_t, rate_t, q, put_t))
    m["bpay"][:, pl.ds(ROWS_L, COLS), :] = m["lacc"][...].astype(BF).reshape(SEQ, COLS, LANES)
    send_back2.start()
    m["brx"][seq] = m["bpay"][seq]
    m["trs"][mp] = m["tdb"][core, chip]

    send_ur.wait_recv()
    entering_states(r)

    def put_r(q, y, dx, db, dc, dd):
        r["y"][q] = y
        r["dx"][q] = dx
        m["rdb"][0, pl.ds(4 * q, 4)] = rest(db.astype(BF))
        m["rdb"][1, pl.ds(4 * q, 4)] = rest(dc.astype(BF))
        r["dd"][q] = dd

    def outside_r(q):
        outside(r, tri_r[...], up_r[...], load_r, pair_r, rate_r, q, put_r)

    chunks(0, 1, outside_r)
    send_tr.wait_recv()
    m["tpiece"][...] = group_total(m["trs"]).astype(BF).reshape(SEQ, COLS, LANES)
    send_bp.start()
    m["rpiece"][seq] = m["tpiece"][seq]
    chunks(1, CHUNKS, outside_r)
    send_rr.start()
    m["rrs"][mp] = m["rdb"][core, :, quarter]
    send_back.wait_recv()
    send_back2.wait_recv()
    send_bp.wait_recv()
    send_rr.wait_recv()
    m["dpiece"][...] = (group_total(m["rrs"]) + m["rpiece"][...].astype(F32)).astype(BF)

    def back(block, q):
        parts = [m["brx"][pl.ds(4 * q, 4), pl.ds(128 * n + 32 * block, 32), :] for n in range(2)]
        return jnp.concatenate(parts, axis=1).reshape(CHUNK, LANES)

    def combine(q):
        rows = rows_of(q)
        x = wide(load_r, BX, q).astype(F32)
        dy = wide(load_r, BY, q).astype(F32)
        z = m["z"][rows, :].astype(F32)
        cot = m["cot"][rows, :].astype(F32)
        y = r["y"][q] + wide(back, BX, q).astype(F32) + skip * x
        sigma = jax.nn.sigmoid(z)
        gated_o[rows, :] = (y * (z * sigma)).astype(BF)
        m["g"][rows, pl.ds(256, 256)] = (cot * y * sigma * (1.0 + z * (1.0 - sigma))).astype(BF)
        m["g"][rows, pl.ds(0, 256)] = (r["dx"][q] + wide(back, BY, q).astype(F32) + skip * dy).astype(BF)
        folded = m["brx"][pl.ds(4 * q, 4), pl.ds(ROWS_L, COLS), :].reshape(64, LANES)
        parts = [mm(folded, pair_merge(8 * g)).reshape(4, COLS, LANES) for g in range(4)]
        dd = r["dd"][q] + jnp.concatenate(parts, axis=1).reshape(CHUNK, LANES)
        dstep = dd * jax.nn.sigmoid(m["sraw"][rows, :])
        m["g"][rows, pl.ds(640, LANES)] = jnp.where(iota((CHUNK, LANES), 1) < HEADS, dstep, 0.0).astype(BF)

    def pair_copy(k, q):
        rows = rows_of(q)
        return mp_copy(
            m["ip"].at[2 * k + 1 - core, rows],
            m["prx"].at[k, rows],
            m["s_pair"].at[0, k, q],
            m["s_pair"].at[1, k, q],
            partner,
        )

    def z_ring(n):
        def part(k, h):
            return m["zs"].at[k, pl.ds(CHUNK * (2 * n + h), CHUNK)]

        return RingSum(
            chip,
            lambda k: {"mp": 2 * k + core},
            part,
            lambda h: m["z_raw"].at[n, h],
            lambda side, h: m["z_near"].at[n, side, pl.ds(CHUNK * h, CHUNK)],
            m["s_z"].at[n],
        )

    z_rings = [z_ring(0), z_ring(1)]

    def pair_sum(k, q):
        rows = rows_of(q)
        pair_copy(k, q).wait_recv()
        return (m["ip"][2 * k + core, rows, :].astype(F32) + m["prx"][k, rows, :].astype(F32)).astype(BF)

    def pass_on(q):
        for k in range(4):
            m["zs"][k, rows_of(q), :] = pair_sum(k, q)

    def z_start(n):
        z_rings[n].start_far()
        z_rings[n].start_near()

    def z_finish(n):
        for h, v in enumerate(z_rings[n].finish()):
            ig_o[rows_of(2 * n + h), :] = v.astype(BF)

    def finish(q):
        combine(q)
        rows = rows_of(q)
        piece = m["dpiece"][pl.ds(4 * q, 4)]
        here = (iota((4, WID, LANES), 1) >> 4) == chip
        piece = jnp.where(here, jnp.concatenate([piece] * 4, axis=1), jnp.zeros((), BF)).reshape(CHUNK, LANES)
        m["g"][rows, pl.ds(512, LANES)] = piece
        g = m["g"][rows, :]
        for c in range(4):
            cols = pl.ds(c * 256, 256)
            v = mm_nt(g[:, :256], wa[c, :, :, pl.ds(0, 256)].reshape(256, 256))
            v += mm_nt(g[:, 256:512], wb[c, :, :, pl.ds(0, 256)].reshape(256, 256))
            v += mm_nt(g[:, 512:], m["wx"][cols, :])
            v = v.astype(BF)
            m["ip"][2 * c, rows, :] = v[:, :LANES]
            m["ip"][2 * c + 1, rows, :] = v[:, LANES:]
        fori(0, 4, lambda k: pair_copy(k, q).start())

    for q in range(CHUNKS):
        finish(q)
        if q > 0:
            pass_on(q - 1)
        if q == 2:
            z_start(0)

    def g_ring(n):
        rows = pl.ds(32 * n, 32)

        def part(k, h):
            two = pl.ds(2 * h, 2)
            return m["gp"].at[k, two, rows] if n == 0 else m["gp"].at[two, k, rows]

        return RingSum(
            plane if n == 0 else line,
            lambda k: {"seq": along_x(k) if n == 0 else along_y(k)},
            part,
            lambda h: m["g_raw"].at[n, h],
            lambda side, h: m["g_near"].at[n, side, pl.ds(2 * h, 2)],
            m["s_gp"].at[n],
        )

    def h_ring(n):
        return RingSum(
            line if n == 0 else plane,
            lambda k: {"seq": along_y(k) if n == 0 else along_x(k)},
            lambda k, h: m["h_own"].at[n, k, pl.ds(16 * h, 16)],
            lambda h: m["h_raw"].at[n, h],
            lambda side, h: m["h_near"].at[n, side, pl.ds(16 * h, 16)],
            m["s_gp"].at[2 + n],
        )

    g_rings, h_rings = [g_ring(0), g_ring(1)], [h_ring(0), h_ring(1)]
    send_gs = SeqExchange(lambda p: m["gs"].at[p // 2], lambda k: m["gs_rx"].at[k], sems(m["s_gs"]))

    def grads(n):
        k = lax.rem(plane + n, 4)
        cols = rows_of(k)
        v = mm(m["tokt"][cols, :], m["g"][...])
        m["gp"][k] = v[:, :640].astype(BF).reshape(4, SHARD, 640)
        gs = v[:, 640:].T[:16].astype(BF)
        m["gs"][2 * k] = gs[:, :LANES]
        m["gs"][2 * k + 1] = gs[:, LANES:]
        start_four(send_gs, k)

    grads(2)
    g_rings[0].start_far()
    pass_on(CHUNKS - 1)
    z_start(1)
    grads(1)
    grads(3)
    g_rings[0].start_near()
    grads(0)
    g_rings[1].start_far()
    g_rings[1].start_near()
    m["gs_rx"][seq] = m["gs"][seq // 2]
    z_rings[0].middle()
    g_rings[0].middle()
    g_rings[1].middle()
    z_rings[1].middle()

    def g_next(n):
        for h, v in enumerate(g_rings[n].finish()):
            m["h_own"][n, pl.ds(2 * h, 2)] = v.astype(BF).reshape(2, 32, 640)
        h_rings[n].start_far()
        h_rings[n].start_near()

    g_next(0)
    g_next(1)
    h_rings[0].middle()
    h_rings[1].middle()
    z_finish(0)

    def total_of(ref):
        v = ref[0].astype(F32)
        for k in range(1, SEQ):
            v += ref[k].astype(F32)
        return v

    main = jnp.concatenate(h_rings[0].finish() + h_rings[1].finish(), axis=0)
    m["fsh"][...] = main[:, 512:]
    send_fin = MpExchange(lambda p: m["fsh"], lambda k: m["frx"].at[k], sems(m["s_fin"]))
    send_fin.start()
    m["frx"][mp] = main[:, 512:]
    gm_o[:, 0, :] = main[:, :INNER]
    gm_o[:, 1, :] = main[:, INNER : 2 * INNER]
    send_gs.wait_recv()
    step = total_of(m["gs_rx"])
    gst_o[...] = jnp.where(low == 0, step[:HEADS, :SHARD], step[:HEADS, SHARD:])
    z_finish(1)
    send_fin.wait_recv()
    for n in range(2):
        gsh_o[:, n, :] = m["frx"][n] + m["frx"][2 + n] + m["frx"][4 + n] + m["frx"][6 + n]

    sent = rings + (send_sw, send_pay, send_bc, send_bm, send_sr, send_ur, send_st, send_ut)
    sent += (send_back, send_back2, send_tr, send_bp, send_rr, send_gs, send_fin)
    sent += tuple(z_rings + g_rings + h_rings)
    for e in sent:
        e.wait_send()
    for q in range(CHUNKS):
        fori(0, 4, lambda k: pair_copy(k, q).wait_send())


def hand_over(*refs):
    n = len(refs) // 2
    for k in range(n):
        refs[n + k][...] = refs[k][...]


def body(tokens, proj_main, proj_shared, proj_step, step_bias, decay_rate, skip_gain, cotangent):
    vm = pl.BlockSpec(memory_space=pltpu.VMEM)
    sm = pl.BlockSpec(memory_space=pltpu.SMEM)
    hbm = pl.BlockSpec(memory_space=pl.ANY)
    shapes = (
        jax.ShapeDtypeStruct((TOK, INNER), BF),
        jax.ShapeDtypeStruct((TOK, LANES), BF),
        jax.ShapeDtypeStruct((SHARD, 2, INNER), F32),
        jax.ShapeDtypeStruct((SHARD, 2, STATE), F32),
        jax.ShapeDtypeStruct((HEADS, SHARD), F32),
    )
    results = pl.pallas_call(
        kernel,
        out_shape=shapes,
        in_specs=[hbm, hbm, vm, vm, vm, sm, sm, sm],
        out_specs=(vm,) * 5,
        scratch_shapes=[main_scratch()],
        compiler_params=pltpu.CompilerParams(
            collective_id=0, has_side_effects=True, vmem_limit_bytes=62 * 1024 * 1024
        ),
    )(
        tokens.reshape(SEQ, WID, DM),
        cotangent.reshape(TOK, INNER),
        proj_main,
        proj_shared,
        proj_step.T,
        step_bias,
        decay_rate,
        skip_gain,
    )
    gated, ig, gm, gsh, gst = pl.pallas_call(
        hand_over,
        out_shape=shapes,
        in_specs=[vm] * 5,
        out_specs=(vm,) * 5,
    )(*results)
    return (
        gated.reshape(1, 16, WID, INNER),
        ig.reshape(1, 16, WID, LANES),
        gm,
        gsh,
        gst.T,
    )


def solution(mesh):
    placed = (
        P("seq", None, None, None),
        P("seq", None, "mp"),
        P("seq", None, None),
        P("seq", "mp"),
        P("mp"),
        P(None, "mp"),
        P("mp"),
        P("seq", None, None, "mp"),
    )
    return jax.shard_map(
        body,
        mesh=mesh,
        in_specs=placed,
        out_specs=(
            P("seq", None, None, "mp"),
            P("seq", None, None, "mp"),
            P("seq", None, "mp"),
            P("seq", None, None),
            P("seq", "mp"),
        ),
        check_vma=False,
    )
```

```python
import jax
import jax.numpy as jnp
from jax import lax
from jax.experimental import pallas as pl
from jax.experimental.pallas import tpu as pltpu
from jax.sharding import PartitionSpec as P

MESH = pl.DeviceIdType.MESH
BF = jnp.bfloat16
F32 = jnp.float32

SEQ = 16
MP = 8
TOK = 1024
WID = 64
DM = 1024
INNER = 256
HEADS = 4
STATE = 128
LANES = 128
CHUNK = 256
CHUNKS = TOK // CHUNK
COLS = CHUNK // SEQ
SHARD = DM // SEQ
BX, BY, BB, BC, ROWS_L, ROWS = 0, 2, 4, 5, 256, 272
PIECE = STATE // SEQ
HALF = 3 * LANES
LOG2E = 1.4426950408889634


def iota(shape, axis):
    return lax.broadcasted_iota(jnp.int32, shape, axis)


def mm(a, b):
    return lax.dot_general(a, b, (((1,), (0,)), ((), ())), preferred_element_type=F32)


def mm_nt(a, b):
    return lax.dot_general(a, b, (((1,), (1,)), ((), ())), preferred_element_type=F32)


def mm_tn(a, b):
    return lax.dot_general(a, b, (((0,), (0,)), ((), ())), preferred_element_type=F32)


def halves(v):
    hi = v.astype(BF)
    return hi, (v - hi.astype(F32)).astype(BF)


def as_pair(v):
    lane = iota(v.shape, 1)
    hi = v.astype(BF).astype(F32)
    return jnp.where(lane < 4, hi, jnp.where(lane < 8, v - hi, 0.0)).astype(BF)


def fori(low, high, step):
    def run(i, carry):
        step(i)
        return carry

    lax.fori_loop(low, high, run, 0)


class SeqExchange:
    def __init__(self, source, landing, sems):
        self.source, self.landing = source, landing
        self.send, self.recv = sems
        self.me = lax.axis_index("seq")

    def copy(self, d):
        peer = lax.rem(self.me + d, SEQ)
        return pltpu.make_async_remote_copy(
            src_ref=self.source(peer),
            dst_ref=self.landing(self.me),
            send_sem=self.send.at[d],
            recv_sem=self.recv.at[d],
            device_id={"seq": peer},
            device_id_type=MESH,
        )

    def arrival(self, d):
        origin = lax.rem(self.me - d + SEQ, SEQ)
        return pltpu.make_async_remote_copy(
            src_ref=self.landing(origin),
            dst_ref=self.landing(origin),
            send_sem=self.send.at[d],
            recv_sem=self.recv.at[d],
            device_id={"seq": origin},
            device_id_type=MESH,
        )

    def start(self):
        fori(1, SEQ, lambda d: self.copy(d).start())

    def wait_recv(self):
        fori(1, SEQ, lambda d: self.arrival(d).wait_recv())

    def wait_send(self):
        fori(1, SEQ, lambda d: self.copy(d).wait_send())


class Ring:
    def __init__(self, me, to, whole, part, sems):
        self.whole, self.part, self.sems, self.to = whole, part, sems, to
        self.me, self.right, self.left = me, lax.rem(me + 1, 4), lax.rem(me + 3, 4)
        self.far = lax.rem(me + 2, 4)

    def copy(self, ref, k, peer):
        return pltpu.make_async_remote_copy(
            src_ref=ref,
            dst_ref=ref,
            send_sem=self.sems.at[0, k],
            recv_sem=self.sems.at[1, k],
            device_id={"seq": self.to(peer)},
            device_id_type=MESH,
        )

    def start(self):
        self.copy(self.whole(self.me), 0, self.right).start()
        self.copy(self.whole(self.me), 1, self.left).start()

    def forward(self):
        self.copy(self.whole(self.left), 0, self.left).wait_recv()
        self.copy(self.part(self.left, 0), 2, self.right).start()
        self.copy(self.whole(self.right), 1, self.right).wait_recv()
        self.copy(self.part(self.right, 1), 3, self.left).start()

    def finish(self):
        self.copy(self.part(self.far, 0), 2, self.left).wait_recv()
        self.copy(self.part(self.far, 1), 3, self.right).wait_recv()

    def wait_send(self):
        self.copy(self.whole(self.me), 0, self.right).wait_send()
        self.copy(self.whole(self.me), 1, self.left).wait_send()
        self.copy(self.part(self.left, 0), 2, self.right).wait_send()
        self.copy(self.part(self.right, 1), 3, self.left).wait_send()


class RingSum:
    def __init__(self, me, to, part, raw, near, sems):
        self.part, self.raw, self.near, self.sems, self.to = part, raw, near, sems, to
        self.me, self.far = me, lax.rem(me + 2, 4)
        self.side = (lax.rem(me + 3, 4), lax.rem(me + 1, 4))

    def copy(self, source, landing, k, peer):
        return pltpu.make_async_remote_copy(
            src_ref=source,
            dst_ref=landing,
            send_sem=self.sems.at[0, k],
            recv_sem=self.sems.at[1, k],
            device_id=self.to(peer),
            device_id_type=MESH,
        )

    def far_copy(self, n):
        return self.copy(self.part(self.far, n), self.raw(n), n, self.side[1 - n])

    def own_copy(self, n):
        peer = self.side[1 - n]
        return self.copy(self.part(peer, 1 - n), self.near(n, 1 - n), 2 + n, peer)

    def sum_copy(self, n):
        peer = self.side[1 - n]
        return self.copy(self.part(peer, n), self.near(n, n), 4 + n, peer)

    def start_far(self):
        for n in range(2):
            self.far_copy(n).start()

    def start_near(self):
        for n in range(2):
            self.own_copy(n).start()

    def middle(self):
        for n in range(2):
            self.copy(self.raw(n), self.raw(n), n, self.side[n]).wait_recv()
            ref = self.part(self.side[1 - n], n)
            ref[...] = (ref[...].astype(F32) + self.raw(n)[...].astype(F32)).astype(BF)
            self.sum_copy(n).start()

    def finish(self):
        halves = []
        for n in range(2):
            for k in range(2):
                ref = self.near(k, n)
                self.copy(ref, ref, 2 + k if n != k else 4 + k, self.side[k]).wait_recv()
            v = self.part(self.me, n)[...].astype(F32)
            halves.append(v + self.near(0, n)[...].astype(F32) + self.near(1, n)[...].astype(F32))
        return halves

    def wait_send(self):
        for n in range(2):
            self.far_copy(n).wait_send()
            self.own_copy(n).wait_send()
            self.sum_copy(n).wait_send()


def mp_copy(source, landing, send, recv, peer):
    return pltpu.make_async_remote_copy(
        src_ref=source,
        dst_ref=landing,
        send_sem=send,
        recv_sem=recv,
        device_id={"mp": peer},
        device_id_type=MESH,
    )


class MpExchange:
    def __init__(self, source, landing, sems):
        self.source, self.landing = source, landing
        self.send, self.recv = sems
        self.me = lax.axis_index("mp")

    def copy(self, d):
        peer = lax.rem(self.me + d, MP)
        return mp_copy(self.source(peer), self.landing(self.me), self.send.at[d], self.recv.at[d], peer)

    def arrival(self, d):
        origin = lax.rem(self.me - d + MP, MP)
        ref = self.landing(origin)
        return mp_copy(ref, ref, self.send.at[d], self.recv.at[d], origin)

    def start(self):
        fori(1, MP, lambda d: self.copy(d).start())

    def wait_recv(self):
        fori(1, MP, lambda d: self.arrival(d).wait_recv())

    def wait_send(self):
        fori(1, MP, lambda d: self.copy(d).wait_send())


def scan_scratch():
    v = pltpu.VMEM
    return dict(
        xs=v((CHUNKS, CHUNK, INNER), BF),
        xt=v((CHUNKS, CHUNK, INNER), BF),
        ed=v((CHUNKS, CHUNK, INNER), BF),
        er=v((CHUNKS, CHUNK, INNER), F32),
        tail=v((CHUNKS, CHUNK, INNER), F32),
        rcol=v((CHUNKS, CHUNK, LANES), F32),
        fresh=v((CHUNKS, STATE, INNER), F32),
        back=v((CHUNKS, STATE, INNER), F32),
        eR=v((CHUNKS, 8, INNER), F32),
        RC=v((8, INNER), F32),
        st=v((SEQ, 4 * PIECE, INNER), BF),
        sx=v((SEQ, 4 * PIECE, INNER), BF),
        sy=v((SEQ, 2 * PIECE, INNER), BF),
        sz=v((SEQ, 2 * PIECE, INNER), BF),
        y=v((CHUNKS, CHUNK, INNER), F32),
        dx=v((CHUNKS, CHUNK, INNER), F32),
        dbc=v((CHUNKS, CHUNK, 2 * STATE), F32),
        dd=v((CHUNKS, CHUNK, LANES), F32),
        gin=v((CHUNKS, STATE, INNER), F32),
        sin=v((STATE, INNER), F32),
    )


def main_scratch():
    v = pltpu.VMEM
    dma = pltpu.SemaphoreType.DMA
    seq_sems = lambda: dma((2, SEQ))
    return dict(
        tok3=v((SEQ, WID, DM), BF),
        cot=v((TOK, INNER), BF),
        wa=v((4, 4, SHARD, HALF), BF),
        wb=v((4, 4, SHARD, HALF), BF),
        sw_rx=v((SEQ, 16, LANES), BF),
        sw=v((LANES, DM), BF),
        z=v((TOK, INNER), BF),
        sraw=v((TOK, LANES), F32),
        pay=v((SEQ, ROWS, LANES), BF),
        trx=v((SEQ, ROWS, LANES), BF),
        bpay=v((SEQ, ROWS, LANES), BF),
        brx=v((SEQ, ROWS, LANES), BF),
        tri=v((4, CHUNK, CHUNK), BF),
        lp=v((TOK, LANES), BF),
        bcr=v((2, SEQ, WID, LANES), BF),
        bct=v((2, SEQ, WID, LANES), BF),
        wx=v((DM, 2 * LANES), BF),
        tdb=v((2, CHUNKS, CHUNK, LANES), BF),
        trs=v((MP, CHUNK, LANES), BF),
        tpiece=v((SEQ, COLS, LANES), BF),
        rpiece=v((SEQ, COLS, LANES), BF),
        rdb=v((2, SEQ, WID, LANES), BF),
        rrs=v((MP, SEQ, COLS, LANES), BF),
        dpiece=v((SEQ, COLS, LANES), BF),
        lacc=v((CHUNK, LANES), F32),
        swp=v((16, LANES), BF),
        R=scan_scratch(),
        T=scan_scratch(),
        g=v((TOK, 768), BF),
        tokt=v((DM, TOK), BF),
        gp=v((4, 4, SHARD, 640), BF),
        g_raw=v((2, 2, 2, 32, 640), BF),
        g_near=v((2, 2, 4, 32, 640), BF),
        h_own=v((2, 4, 32, 640), BF),
        h_raw=v((2, 2, 16, 640), BF),
        h_near=v((2, 2, 32, 640), BF),
        z_raw=v((2, 2, CHUNK, LANES), BF),
        z_near=v((2, 2, 2 * CHUNK, LANES), BF),
        gs=v((MP, 16, LANES), BF),
        gs_rx=v((SEQ, 16, LANES), BF),
        ip=v((MP, TOK, LANES), BF),
        prx=v((4, TOK, LANES), BF),
        zs=v((4, TOK, LANES), BF),
        fsh=v((SHARD, LANES), F32),
        frx=v((MP, SHARD, LANES), F32),
        s_local=dma((4,)),
        s_w=dma((4, 2, 4)),
        s_sw=seq_sems(),
        s_pay=seq_sems(),
        s_sr=seq_sems(),
        s_st=seq_sems(),
        s_ur=seq_sems(),
        s_ut=seq_sems(),
        s_back=seq_sems(),
        s_back2=seq_sems(),
        s_gp=dma((4, 2, 6)),
        s_bc=seq_sems(),
        s_bp=seq_sems(),
        s_gs=seq_sems(),
        s_bm=dma((2, MP)),
        s_tr=dma((2, MP)),
        s_rr=dma((2, MP)),
        s_fin=dma((2, MP)),
        s_pair=dma((2, 4, CHUNKS)),
        s_z=dma((2, 2, 6)),
    )


def sems(ref):
    return ref.at[0], ref.at[1]


def head_sum():
    c, h = iota((INNER, LANES), 0), iota((INNER, LANES), 1)
    return jnp.where((h < 8) & ((h & 3) == (c >> 6)), 1.0, 0.0).astype(BF)


def pair_expand(shift):
    k, c = iota((LANES, INNER), 0) - shift, iota((LANES, INNER), 1)
    return jnp.where((k >= 0) & (k < 8) & ((k & 3) == (c >> 6)), 1.0, 0.0).astype(BF)


def pair_merge(shift):
    k, h = iota((LANES, LANES), 0) - shift, iota((LANES, LANES), 1)
    return jnp.where((k >= 0) & (k < 8) & (h < 8) & ((k & 3) == (h & 3)), 1.0, 0.0).astype(BF)


def pair_place(shift):
    k, lane = iota((LANES, LANES), 0), iota((LANES, LANES), 1)
    return jnp.where((k < 8) & (lane == k + shift), 1.0, 0.0).astype(BF)


def wide(load, block, q):
    return jnp.concatenate([load(block, q), load(block + 1, q)], axis=1)


def summary(b, tri, load, pair_of, rate, ratex, q):
    x = wide(load, BX, q).astype(F32)
    dy = wide(load, BY, q).astype(F32)
    pair, shift = pair_of(q)
    dexp = mm(pair, pair_expand(shift))
    logs = (-dexp * ratex).astype(BF)
    rexp = mm(tri, logs)
    b["rcol"][q] = mm(tri, (-mm(pair, pair_merge(shift)) * rate).astype(BF))
    total = jnp.sum(logs.astype(F32), axis=0, keepdims=True)
    er = jnp.exp2(rexp)
    tail = jnp.exp2(jnp.minimum(total - rexp, 0.0))
    xs = (x * dexp).astype(BF)
    xt = (xs.astype(F32) * tail).astype(BF)
    ed = (er * dy).astype(BF)
    b["er"][q] = er
    b["tail"][q] = tail
    b["xs"][q] = xs
    b["xt"][q] = xt
    b["ed"][q] = ed
    b["fresh"][q] = mm_tn(load(BB, q), xt)
    b["back"][q] = mm_tn(load(BC, q), ed)
    rows = jnp.broadcast_to(total, (8, INNER))
    b["eR"][q] = jnp.exp2(rows)
    b["RC"][...] += rows


def pack_states(b):
    e = [b["eR"][q][:1] for q in range(CHUNKS)]
    end = b["fresh"][0]
    for q in range(1, CHUNKS):
        end = end * e[q] + b["fresh"][q]
    first = b["back"][CHUNKS - 1]
    for q in range(CHUNKS - 2, -1, -1):
        first = first * e[q] + b["back"][q]
    rc = b["RC"][...]
    hi = rc.astype(BF).astype(F32)
    logs = jnp.concatenate([hi, rc - hi], axis=0).astype(BF)
    pieces = [v.reshape(SEQ, PIECE, INNER) for v in (end, first)]
    b["st"][:, pl.ds(0, 2 * PIECE), :] = jnp.concatenate(pieces, axis=1).astype(BF)
    for k in range(SEQ):
        b["st"][k, pl.ds(2 * PIECE, 2 * PIECE)] = logs


def chain_states(b):
    own = [b["sx"][k, pl.ds(0, 2 * PIECE)].astype(F32) for k in range(SEQ)]
    logs = [b["sx"][k, pl.ds(2 * PIECE, 2 * PIECE)].astype(F32) for k in range(SEQ)]
    decay = [jnp.exp2(v[:PIECE] + v[PIECE:]) for v in logs]
    state = [jnp.zeros((PIECE, INNER), F32)]
    grad = [jnp.zeros((PIECE, INNER), F32)]
    for k in range(SEQ - 1):
        state.append(state[k] * decay[k] + own[k][:PIECE])
        n = SEQ - 1 - k
        grad.append(grad[k] * decay[n] + own[n][PIECE:])
    for k in range(SEQ):
        b["sy"][k] = jnp.concatenate([state[k], grad[SEQ - 1 - k]], axis=0).astype(BF)


def entering_states(b):
    both = b["sz"][...].astype(F32)
    b["sin"][...] = both[:, :PIECE, :].reshape(STATE, INNER)
    grad = both[:, PIECE:, :].reshape(STATE, INNER)
    for q in range(CHUNKS - 1, -1, -1):
        b["gin"][q] = grad
        if q > 0:
            grad = grad * b["eR"][q][:1] + b["back"][q]


def head_rows(h):
    one = jnp.where((iota((16, INNER), 1) >> 6) == h, 1.0, 0.0).astype(BF)
    return jnp.concatenate([one] * (CHUNK // 16), axis=0)


def inside(b, tri, load, q):
    dy = wide(load, BY, q)
    bmat = load(BB, q)
    cmat = load(BC, q)
    xs = b["xs"][q]
    trif = tri.astype(F32)
    scores = mm_nt(cmat, bmat) * trif
    rcol = b["rcol"][q]
    rrow = rcol.T
    pairs = None
    ms, dys, xss = [], [], []
    for h in range(HEADS):
        decay = jnp.exp2(jnp.minimum(rcol[:, h : h + 1] - rrow[h : h + 1, :], 0.0))
        ms.append((decay * scores).astype(BF))
        mask = head_rows(h)
        dys.append(dy * mask)
        xss.append(xs * mask)
        term = decay * mm_nt(dys[h], xs)
        pairs = term if h == 0 else pairs + term
    dy4 = jnp.concatenate(dys, axis=0)
    y = mm(jnp.concatenate(ms, axis=1), jnp.concatenate(xss, axis=0))
    dxs = mm_tn(jnp.concatenate(ms, axis=0), dy4)
    pairs = (pairs * trif).astype(BF)
    b["y"][q] = y
    b["dx"][q] = dxs
    b["dbc"][q, :, pl.ds(0, STATE)] = mm_tn(pairs, cmat)
    b["dbc"][q, :, pl.ds(STATE, STATE)] = mm(pairs, bmat)


def outside(b, tri, tri_up, load, pair_of, rate, q, put):
    x = wide(load, BX, q).astype(F32)
    dy = wide(load, BY, q).astype(F32)
    bmat = load(BB, q)
    cmat = load(BC, q)
    pair, shift = pair_of(q)
    dexp = mm(pair, pair_expand(shift))
    xs = b["xs"][q].astype(F32)
    state = b["sin"][...]
    grad = b["gin"][q]
    state_b, grad_b = state.astype(BF), grad.astype(BF)
    sums = head_sum()
    y = b["y"][q] + b["er"][q] * mm(cmat, state_b)
    inner = b["dx"][q]
    outer = b["tail"][q] * mm(bmat, grad_b)
    dxs = inner + outer
    db = b["dbc"][q, :, pl.ds(0, STATE)] + mm_nt(b["xt"][q], grad_b)
    dc = b["dbc"][q, :, pl.ds(STATE, STATE)] + mm_nt(b["ed"][q], state_b)

    def by_head(v):
        return mm(v.astype(BF), sums)

    late = by_head(dy * y - xs * inner).astype(BF)
    early = by_head(xs * outer).astype(BF)
    decayed = b["eR"][q][:1] * state
    across = jnp.sum(decayed * grad, axis=0, keepdims=True)
    across = mm(jnp.broadcast_to(across, (16, INNER)).astype(BF), sums)[:1]
    dl = mm(tri_up, late) + mm(tri, early) - early.astype(F32) + across
    ddelta = by_head(x * dxs) - rate * dl
    b["sin"][...] = decayed + b["fresh"][q]
    put(q, y, dexp * dxs, db, dc, ddelta)


def kernel(tok_hbm, cot_hbm, pm, ps, pt, bias_s, rate_s, skip_s, gated_o, ig_o, gm_o, gsh_o, gst_o, m):
    seq, mp = lax.axis_index("seq"), lax.axis_index("mp")
    core = lax.rem(mp, 2)
    chip = mp // 2
    partner = mp + 1 - 2 * core
    plane, line = seq // 4, lax.rem(seq, 4)
    low = lax.rem(seq, 2)

    load_tok = pltpu.make_async_copy(tok_hbm, m["tok3"], m["s_local"].at[0])
    load_cot = pltpu.make_async_copy(cot_hbm, m["cot"], m["s_local"].at[1])
    load_tok.start()
    load_cot.start()

    barrier = pltpu.get_barrier_semaphore()

    def greet_seq(d):
        pl.semaphore_signal(
            barrier, inc=1, device_id={"seq": lax.rem(seq + d, SEQ)}, device_id_type=MESH
        )

    def greet_mp(d):
        pl.semaphore_signal(barrier, inc=1, device_id={"mp": lax.rem(mp + d, MP)}, device_id_type=MESH)

    fori(1, SEQ, greet_seq)
    fori(1, MP, greet_mp)

    wa, wb, swp = m["wa"], m["wb"], m["swp"]
    wa[plane, line, :, pl.ds(0, 256)] = pm[:, 0, :]
    wb[plane, line, :, pl.ds(0, 256)] = pm[:, 1, :]
    wa[plane, line, :, pl.ds(256, 128)] = ps[:, 0, :]
    wb[plane, line, :, pl.ds(256, 128)] = ps[:, 1, :]
    at, lane = iota((SHARD, LANES), 0), iota((SHARD, LANES), 1)
    place = jnp.where(lane == at + SHARD * low, 1.0, 0.0).astype(BF)
    shifted = mm(pt[...], place).astype(BF)
    swp[...] = jnp.concatenate([shifted, shifted, jnp.zeros((8, LANES), BF)], axis=0)
    pl.semaphore_wait(barrier, SEQ + MP - 2)

    def along_x(k):
        return 4 * k + line

    def along_y(k):
        return 4 * plane + k

    half = SHARD // 2
    ring_a1 = Ring(plane, along_x, lambda k: wa.at[k, line], lambda k, n: wa.at[k, line, pl.ds(half * n, half)], m["s_w"].at[0])
    ring_b1 = Ring(line, along_y, lambda k: wb.at[plane, k], lambda k, n: wb.at[plane, k, pl.ds(half * n, half)], m["s_w"].at[1])
    ring_a2 = Ring(line, along_y, lambda k: wa.at[:, k], lambda k, n: wa.at[pl.ds(2 * n, 2), k], m["s_w"].at[2])
    ring_b2 = Ring(plane, along_x, lambda k: wb.at[k], lambda k, n: wb.at[k, pl.ds(2 * n, 2)], m["s_w"].at[3])
    rings = (ring_a1, ring_b1, ring_a2, ring_b2)
    ring_a1.start()
    ring_b1.start()
    send_sw = SeqExchange(lambda p: swp, lambda k: m["sw_rx"].at[k], sems(m["s_sw"]))
    send_sw.start()
    m["sw_rx"][seq] = swp[...]

    def flip(q):
        m["tokt"][:, pl.ds(q * CHUNK, CHUNK)] = m["tok3"][pl.ds(4 * q, 4)].reshape(CHUNK, DM).T

    load_tok.wait()
    flip(0)
    ring_a1.forward()
    ring_b1.forward()
    ring_a1.finish()
    ring_a2.start()
    ring_b1.finish()
    ring_b2.start()

    i, j = iota((CHUNK, CHUNK), 0), iota((CHUNK, CHUNK), 1)
    m["tri"][0] = jnp.where(i >= j, 1.0, 0.0).astype(BF)
    it, jt = (i & 15) * 16 + (i >> 4), (j & 15) * 16 + (j >> 4)
    m["tri"][1] = jnp.where(it >= jt, 1.0, 0.0).astype(BF)
    m["tri"][2] = jnp.where(i <= j, 1.0, 0.0).astype(BF)
    m["tri"][3] = jnp.where(it <= jt, 1.0, 0.0).astype(BF)
    m["sw"][...] = jnp.zeros((LANES, DM), BF)
    m["R"]["RC"][...] = jnp.zeros((8, INNER), F32)
    m["T"]["RC"][...] = jnp.zeros((8, INNER), F32)
    m["lacc"][...] = jnp.zeros((CHUNK, LANES), F32)

    head_l = iota((1, LANES), 1)
    head_c = iota((1, INNER), 1) >> 6

    def lanes_of(value):
        v = jnp.zeros((1, LANES), F32)
        for h in range(HEADS):
            v = jnp.where((head_l < 8) & ((head_l & 3) == h), value(h), v)
        return v

    def features_of(value):
        v = jnp.zeros((1, INNER), F32)
        for h in range(HEADS):
            v = jnp.where(head_c == h, value(h), v)
        return v

    bias = lanes_of(lambda h: bias_s[h])
    rate_r, rate_t = lanes_of(lambda h: rate_s[0, h]), lanes_of(lambda h: rate_s[1, h])
    ratex_r = features_of(lambda h: rate_s[0, h]) * LOG2E
    ratex_t = features_of(lambda h: rate_s[1, h]) * LOG2E
    skip = features_of(lambda h: skip_s[h])

    load_cot.wait()
    flip(1)
    ring_a2.forward()
    ring_b2.forward()
    flip(2)
    flip(3)
    ring_a2.finish()
    ring_b2.finish()
    send_sw.wait_recv()
    for k in range(SEQ // 2):
        m["sw"][pl.ds(0, 16), pl.ds(k * LANES, LANES)] = m["sw_rx"][2 * k] + m["sw_rx"][2 * k + 1]

    def rows_of(q):
        return pl.ds(pl.multiple_of(q * CHUNK, CHUNK), CHUNK)

    def columns(ref, at, width):
        return ref[:, :, :, pl.ds(at, width)].reshape(DM, width)

    def rest(v):
        return v.reshape(4, WID, LANES)

    send_pay = SeqExchange(lambda p: m["pay"].at[p], lambda k: m["trx"].at[k], sems(m["s_pay"]))
    quarter = pl.ds(pl.multiple_of(chip * COLS, COLS), COLS)
    bcr, bct = m["bcr"], m["bct"]
    send_bc = SeqExchange(
        lambda p: bcr.at[core, p, quarter], lambda k: bct.at[core, k, quarter], sems(m["s_bc"])
    )

    def piece_of(ref, k):
        return ref.at[lax.rem(k, 2), :, pl.ds(pl.multiple_of(k // 2 * COLS, COLS), COLS)]

    send_bm = MpExchange(lambda p: piece_of(bct, mp), lambda k: piece_of(bct, k), sems(m["s_bm"]))
    m["wx"][:, pl.ds(0, LANES)] = jnp.where(core == 0, columns(wa, 256, 128), columns(wb, 256, 128))
    m["wx"][:, pl.ds(LANES, LANES)] = m["sw"][...].T

    def start_four(exchange, q):
        def one(n):
            d = lax.rem(4 * q + n - seq + SEQ, SEQ)

            @pl.when(d != 0)
            def _():
                exchange.copy(d).start()

        fori(0, 4, one)

    def project_shared(n):
        q = lax.rem(plane + n, 4)
        u = m["tok3"][pl.ds(4 * q, 4)].reshape(CHUNK, DM)
        w = jnp.concatenate([columns(wa, 256, 128), columns(wb, 256, 128)], axis=1)
        v = mm(u, w).astype(BF)
        bcr[0, pl.ds(4 * q, 4)] = rest(v[:, :LANES])
        bcr[1, pl.ds(4 * q, 4)] = rest(v[:, LANES:])
        start_four(send_bc, q)

    def project(n):
        q = lax.rem(plane + n, 4)
        rows = rows_of(q)
        u = m["tok3"][pl.ds(4 * q, 4)].reshape(CHUNK, DM)
        four = pl.ds(4 * q, 4)

        def put(block, v):
            v = v.astype(BF)
            for k in range(v.shape[1] // LANES):
                m["pay"][four, pl.ds((block + k) * WID, WID), :] = rest(v[:, k * LANES : (k + 1) * LANES])

        z = mm(u, columns(wb, 0, 256)).astype(BF)
        m["z"][rows, :] = z
        zf = z.astype(F32)
        gate = zf * jax.nn.sigmoid(zf)
        put(BY, m["cot"][rows, :].astype(F32) * gate)
        put(BX, mm(u, columns(wa, 0, 256)))
        raw = mm(u, m["wx"][:, pl.ds(LANES, LANES)]) + bias
        m["sraw"][rows, :] = raw
        pair = as_pair(jnp.maximum(raw, 0.0) + jnp.log1p(jnp.exp(-jnp.abs(raw))))
        m["lp"][rows, :] = pair
        folded = jnp.zeros((64, LANES), F32)
        for g in range(4):
            part = rest(pair)[:, g * COLS : (g + 1) * COLS, :].reshape(64, LANES)
            folded += mm(part, pair_place(8 * g))
        m["pay"][four, pl.ds(ROWS_L, COLS), :] = folded.astype(BF).reshape(4, COLS, LANES)
        start_four(send_pay, q)

    fori(0, CHUNKS, project_shared)
    fori(0, CHUNKS, project)
    m["trx"][seq] = m["pay"][seq]
    bct[core, seq, quarter] = bcr[core, seq, quarter]

    def load_r(block, q):
        if block >= BB:
            return bcr[block - BB, pl.ds(4 * q, 4)].reshape(CHUNK, LANES)
        return m["pay"][pl.ds(4 * q, 4), pl.ds(block * WID, WID), :].reshape(CHUNK, LANES)

    def pair_r(q):
        return m["lp"][rows_of(q), :], 0

    def cols_of(block, q):
        return pl.ds(pl.multiple_of(block * WID + q * COLS, COLS), COLS)

    def load_t(block, q):
        if block >= BB:
            return bct[block - BB, :, pl.ds(q * COLS, COLS), :].reshape(CHUNK, LANES)
        return m["trx"][:, cols_of(block, q), :].reshape(CHUNK, LANES)

    def pair_t(q):
        return m["trx"][:, pl.ds(ROWS_L, COLS), :].reshape(CHUNK, LANES), 8 * q

    def pieces_exchange(source, landing, sem):
        return SeqExchange(lambda p: source.at[p], lambda k: landing.at[k], sems(sem))

    r, t = m["R"], m["T"]
    tri_r, tri_t, up_r, up_t = (m["tri"].at[k] for k in range(4))

    def chunks(low, high, step):
        for q in range(low, high):
            step(q)


    def start_pieces(b, sem):
        pack_states(b)
        e = pieces_exchange(b["st"], b["sx"], sem)
        e.start()
        b["sx"][seq] = b["st"][seq]
        return e

    def start_entering(b, sem):
        chain_states(b)
        e = pieces_exchange(b["sy"], b["sz"], sem)
        e.start()
        b["sz"][seq] = b["sy"][seq]
        return e

    chunks(0, CHUNKS, lambda q: summary(r, tri_r[...], load_r, pair_r, rate_r * LOG2E, ratex_r, q))
    send_sr = start_pieces(r, m["s_sr"])
    send_bc.wait_recv()
    send_bm.start()
    chunks(0, CHUNKS, lambda q: inside(r, tri_r[...], load_r, q))
    send_sr.wait_recv()
    send_ur = start_entering(r, m["s_ur"])

    send_pay.wait_recv()
    send_bm.wait_recv()
    chunks(0, CHUNKS, lambda q: summary(t, tri_t[...], load_t, pair_t, rate_t * LOG2E, ratex_t, q))
    send_st = start_pieces(t, m["s_st"])
    chunks(0, 2, lambda q: inside(t, tri_t[...], load_t, q))
    send_st.wait_recv()
    send_ut = start_entering(t, m["s_ut"])
    chunks(2, CHUNKS, lambda q: inside(t, tri_t[...], load_t, q))
    send_ut.wait_recv()
    entering_states(t)

    def put_t(q, y, dx, db, dc, dd):
        def put(block, v):
            v = v.astype(BF)
            for k in range(v.shape[1] // LANES):
                part = v[:, k * LANES : (k + 1) * LANES]
                at = 128 * (q // 2) + 32 * (block + k) + COLS * (q % 2)
                m["bpay"][:, pl.ds(at, COLS), :] = part.reshape(SEQ, COLS, LANES)

        put(BX, y)
        put(BY, dx)
        m["tdb"][0, q] = db.astype(BF)
        m["tdb"][1, q] = dc.astype(BF)
        for n in range(2):
            d = lax.rem(2 * q + n - mp + MP, MP)

            @pl.when(d != 0)
            def _():
                send_tr.copy(d).start()

        m["lacc"][...] += mm(as_pair(dd), pair_place(8 * q))

    def half_back(at, count, sem):
        rows = pl.ds(at, count)
        return SeqExchange(lambda p: m["bpay"].at[p, rows], lambda k: m["brx"].at[k, rows], sems(sem))

    send_back = half_back(0, 128, m["s_back"])
    send_back2 = half_back(128, 144, m["s_back2"])
    send_tr = MpExchange(
        lambda p: m["tdb"].at[lax.rem(p, 2), p // 2], lambda k: m["trs"].at[k], sems(m["s_tr"])
    )
    send_bp = SeqExchange(lambda p: m["tpiece"].at[p], lambda k: m["rpiece"].at[k], sems(m["s_bp"]))
    send_rr = MpExchange(lambda p: piece_of(m["rdb"], p), lambda k: m["rrs"].at[k], sems(m["s_rr"]))

    def group_total(ref):
        v = ref[0].astype(F32)
        for k in range(1, MP):
            v += ref[k].astype(F32)
        return v

    chunks(0, 2, lambda q: outside(t, tri_t[...], up_t[...], load_t, pair_t, rate_t, q, put_t))
    send_back.start()
    chunks(2, 4, lambda q: outside(t, tri_t[...], up_t[...], load_t, pair_t, rate_t, q, put_t))
    m["bpay"][:, pl.ds(ROWS_L, COLS), :] = m["lacc"][...].astype(BF).reshape(SEQ, COLS, LANES)
    send_back2.start()
    m["brx"][seq] = m["bpay"][seq]
    m["trs"][mp] = m["tdb"][core, chip]

    send_ur.wait_recv()
    entering_states(r)

    def put_r(q, y, dx, db, dc, dd):
        r["y"][q] = y
        r["dx"][q] = dx
        m["rdb"][0, pl.ds(4 * q, 4)] = rest(db.astype(BF))
        m["rdb"][1, pl.ds(4 * q, 4)] = rest(dc.astype(BF))
        r["dd"][q] = dd

    def outside_r(q):
        outside(r, tri_r[...], up_r[...], load_r, pair_r, rate_r, q, put_r)

    chunks(0, 1, outside_r)
    send_tr.wait_recv()
    m["tpiece"][...] = group_total(m["trs"]).astype(BF).reshape(SEQ, COLS, LANES)
    send_bp.start()
    m["rpiece"][seq] = m["tpiece"][seq]
    chunks(1, CHUNKS, outside_r)
    send_rr.start()
    m["rrs"][mp] = m["rdb"][core, :, quarter]
    send_back.wait_recv()
    send_back2.wait_recv()
    send_bp.wait_recv()
    send_rr.wait_recv()
    m["dpiece"][...] = (group_total(m["rrs"]) + m["rpiece"][...].astype(F32)).astype(BF)

    def back(block, q):
        parts = [m["brx"][pl.ds(4 * q, 4), pl.ds(128 * n + 32 * block, 32), :] for n in range(2)]
        return jnp.concatenate(parts, axis=1).reshape(CHUNK, LANES)

    def combine(q):
        rows = rows_of(q)
        x = wide(load_r, BX, q).astype(F32)
        dy = wide(load_r, BY, q).astype(F32)
        z = m["z"][rows, :].astype(F32)
        cot = m["cot"][rows, :].astype(F32)
        y = r["y"][q] + wide(back, BX, q).astype(F32) + skip * x
        sigma = jax.nn.sigmoid(z)
        gated_o[rows, :] = (y * (z * sigma)).astype(BF)
        m["g"][rows, pl.ds(256, 256)] = (cot * y * sigma * (1.0 + z * (1.0 - sigma))).astype(BF)
        m["g"][rows, pl.ds(0, 256)] = (r["dx"][q] + wide(back, BY, q).astype(F32) + skip * dy).astype(BF)
        folded = m["brx"][pl.ds(4 * q, 4), pl.ds(ROWS_L, COLS), :].reshape(64, LANES)
        parts = [mm(folded, pair_merge(8 * g)).reshape(4, COLS, LANES) for g in range(4)]
        dd = r["dd"][q] + jnp.concatenate(parts, axis=1).reshape(CHUNK, LANES)
        dstep = dd * jax.nn.sigmoid(m["sraw"][rows, :])
        m["g"][rows, pl.ds(640, LANES)] = jnp.where(iota((CHUNK, LANES), 1) < HEADS, dstep, 0.0).astype(BF)

    def pair_copy(k, q):
        rows = rows_of(q)
        return mp_copy(
            m["ip"].at[2 * k + 1 - core, rows],
            m["prx"].at[k, rows],
            m["s_pair"].at[0, k, q],
            m["s_pair"].at[1, k, q],
            partner,
        )

    def z_ring(n):
        def part(k, h):
            return m["zs"].at[k, pl.ds(CHUNK * (2 * n + h), CHUNK)]

        return RingSum(
            chip,
            lambda k: {"mp": 2 * k + core},
            part,
            lambda h: m["z_raw"].at[n, h],
            lambda side, h: m["z_near"].at[n, side, pl.ds(CHUNK * h, CHUNK)],
            m["s_z"].at[n],
        )

    z_rings = [z_ring(0), z_ring(1)]

    def pair_sum(k, q):
        rows = rows_of(q)
        pair_copy(k, q).wait_recv()
        return (m["ip"][2 * k + core, rows, :].astype(F32) + m["prx"][k, rows, :].astype(F32)).astype(BF)

    def pass_on(q):
        for k in range(4):
            m["zs"][k, rows_of(q), :] = pair_sum(k, q)

    def z_start(n):
        z_rings[n].start_far()
        z_rings[n].start_near()

    def z_finish(n):
        for h, v in enumerate(z_rings[n].finish()):
            ig_o[rows_of(2 * n + h), :] = v.astype(BF)

    def combine_all(q):
        combine(q)
        rows = rows_of(q)
        piece = m["dpiece"][pl.ds(4 * q, 4)]
        here = (iota((4, WID, LANES), 1) >> 4) == chip
        piece = jnp.where(here, jnp.concatenate([piece] * 4, axis=1), jnp.zeros((), BF)).reshape(CHUNK, LANES)
        m["g"][rows, pl.ds(512, LANES)] = piece

    def input_part(q):
        rows = rows_of(q)
        g = m["g"][rows, :]
        for c in range(4):
            cols = pl.ds(c * 256, 256)
            v = mm_nt(g[:, :256], wa[c, :, :, pl.ds(0, 256)].reshape(256, 256))
            v += mm_nt(g[:, 256:512], wb[c, :, :, pl.ds(0, 256)].reshape(256, 256))
            v += mm_nt(g[:, 512:], m["wx"][cols, :])
            v = v.astype(BF)
            m["ip"][2 * c, rows, :] = v[:, :LANES]
            m["ip"][2 * c + 1, rows, :] = v[:, LANES:]
        fori(0, 4, lambda k: pair_copy(k, q).start())

    chunks(0, CHUNKS, combine_all)

    def g_ring(n):
        rows = pl.ds(32 * n, 32)

        def part(k, h):
            two = pl.ds(2 * h, 2)
            return m["gp"].at[k, two, rows] if n == 0 else m["gp"].at[two, k, rows]

        return RingSum(
            plane if n == 0 else line,
            lambda k: {"seq": along_x(k) if n == 0 else along_y(k)},
            part,
            lambda h: m["g_raw"].at[n, h],
            lambda side, h: m["g_near"].at[n, side, pl.ds(2 * h, 2)],
            m["s_gp"].at[n],
        )

    def h_ring(n):
        return RingSum(
            line if n == 0 else plane,
            lambda k: {"seq": along_y(k) if n == 0 else along_x(k)},
            lambda k, h: m["h_own"].at[n, k, pl.ds(16 * h, 16)],
            lambda h: m["h_raw"].at[n, h],
            lambda side, h: m["h_near"].at[n, side, pl.ds(16 * h, 16)],
            m["s_gp"].at[2 + n],
        )

    g_rings, h_rings = [g_ring(0), g_ring(1)], [h_ring(0), h_ring(1)]
    send_gs = SeqExchange(lambda p: m["gs"].at[p // 2], lambda k: m["gs_rx"].at[k], sems(m["s_gs"]))

    def grads(n):
        k = lax.rem(plane + n, 4)
        cols = rows_of(k)
        v = mm(m["tokt"][cols, :], m["g"][...])
        m["gp"][k] = v[:, :640].astype(BF).reshape(4, SHARD, 640)
        gs = v[:, 640:].T[:16].astype(BF)
        m["gs"][2 * k] = gs[:, :LANES]
        m["gs"][2 * k + 1] = gs[:, LANES:]
        start_four(send_gs, k)

    grads(2)
    g_rings[0].start_far()
    grads(1)
    grads(3)
    g_rings[0].start_near()
    grads(0)
    g_rings[1].start_far()
    g_rings[1].start_near()
    m["gs_rx"][seq] = m["gs"][seq // 2]
    input_part(0)
    input_part(1)
    g_rings[0].middle()
    g_rings[1].middle()
    pass_on(0)
    pass_on(1)
    z_start(0)
    input_part(2)
    input_part(3)

    def g_next(n):
        for h, v in enumerate(g_rings[n].finish()):
            m["h_own"][n, pl.ds(2 * h, 2)] = v.astype(BF).reshape(2, 32, 640)
        h_rings[n].start_far()
        h_rings[n].start_near()

    g_next(0)
    g_next(1)
    pass_on(2)
    pass_on(3)
    z_start(1)
    z_rings[0].middle()
    h_rings[0].middle()
    h_rings[1].middle()
    z_rings[1].middle()

    def total_of(ref):
        v = ref[0].astype(F32)
        for k in range(1, SEQ):
            v += ref[k].astype(F32)
        return v

    main = jnp.concatenate(h_rings[0].finish() + h_rings[1].finish(), axis=0)
    m["fsh"][...] = main[:, 512:]
    send_fin = MpExchange(lambda p: m["fsh"], lambda k: m["frx"].at[k], sems(m["s_fin"]))
    send_fin.start()
    m["frx"][mp] = main[:, 512:]
    gm_o[:, 0, :] = main[:, :INNER]
    gm_o[:, 1, :] = main[:, INNER : 2 * INNER]
    send_gs.wait_recv()
    step = total_of(m["gs_rx"])
    gst_o[...] = jnp.where(low == 0, step[:HEADS, :SHARD], step[:HEADS, SHARD:])
    z_finish(0)
    z_finish(1)
    send_fin.wait_recv()
    for n in range(2):
        gsh_o[:, n, :] = m["frx"][n] + m["frx"][2 + n] + m["frx"][4 + n] + m["frx"][6 + n]

    sent = rings + (send_sw, send_pay, send_bc, send_bm, send_sr, send_ur, send_st, send_ut)
    sent += (send_back, send_back2, send_tr, send_bp, send_rr, send_gs, send_fin)
    sent += tuple(z_rings + g_rings + h_rings)
    for e in sent:
        e.wait_send()
    for q in range(CHUNKS):
        fori(0, 4, lambda k: pair_copy(k, q).wait_send())


def hand_over(*refs):
    n = len(refs) // 2
    for k in range(n):
        refs[n + k][...] = refs[k][...]


def body(tokens, proj_main, proj_shared, proj_step, step_bias, decay_rate, skip_gain, cotangent):
    vm = pl.BlockSpec(memory_space=pltpu.VMEM)
    sm = pl.BlockSpec(memory_space=pltpu.SMEM)
    hbm = pl.BlockSpec(memory_space=pl.ANY)
    shapes = (
        jax.ShapeDtypeStruct((TOK, INNER), BF),
        jax.ShapeDtypeStruct((TOK, LANES), BF),
        jax.ShapeDtypeStruct((SHARD, 2, INNER), F32),
        jax.ShapeDtypeStruct((SHARD, 2, STATE), F32),
        jax.ShapeDtypeStruct((HEADS, SHARD), F32),
    )
    results = pl.pallas_call(
        kernel,
        out_shape=shapes,
        in_specs=[hbm, hbm, vm, vm, vm, sm, sm, sm],
        out_specs=(vm,) * 5,
        scratch_shapes=[main_scratch()],
        compiler_params=pltpu.CompilerParams(
            collective_id=0, has_side_effects=True, vmem_limit_bytes=62 * 1024 * 1024
        ),
    )(
        tokens.reshape(SEQ, WID, DM),
        cotangent.reshape(TOK, INNER),
        proj_main,
        proj_shared,
        proj_step.T,
        step_bias,
        decay_rate,
        skip_gain,
    )
    gated, ig, gm, gsh, gst = pl.pallas_call(
        hand_over,
        out_shape=shapes,
        in_specs=[vm] * 5,
        out_specs=(vm,) * 5,
    )(*results)
    return (
        gated.reshape(1, 16, WID, INNER),
        ig.reshape(1, 16, WID, LANES),
        gm,
        gsh,
        gst.T,
    )


def solution(mesh):
    placed = (
        P("seq", None, None, None),
        P("seq", None, "mp"),
        P("seq", None, None),
        P("seq", "mp"),
        P("mp"),
        P(None, "mp"),
        P("mp"),
        P("seq", None, None, "mp"),
    )
    return jax.shard_map(
        body,
        mesh=mesh,
        in_specs=placed,
        out_specs=(
            P("seq", None, None, "mp"),
            P("seq", None, None, "mp"),
            P("seq", None, "mp"),
            P("seq", None, None),
            P("seq", "mp"),
        ),
        check_vma=False,
    )
```

```python
import jax
import jax.numpy as jnp
from jax import lax
from jax.experimental import pallas as pl
from jax.experimental.pallas import tpu as pltpu
from jax.sharding import PartitionSpec as P

MESH = pl.DeviceIdType.MESH
BF = jnp.bfloat16
F32 = jnp.float32

SEQ = 16
MP = 8
TOK = 1024
WID = 64
DM = 1024
INNER = 256
HEADS = 4
STATE = 128
LANES = 128
CHUNK = 256
CHUNKS = TOK // CHUNK
COLS = CHUNK // SEQ
SHARD = DM // SEQ
BX, BY, BB, BC, ROWS_L, ROWS = 0, 2, 4, 5, 256, 272
PIECE = STATE // SEQ
HALF = 3 * LANES
LOG2E = 1.4426950408889634


def iota(shape, axis):
    return lax.broadcasted_iota(jnp.int32, shape, axis)


def mm(a, b):
    return lax.dot_general(a, b, (((1,), (0,)), ((), ())), preferred_element_type=F32)


def mm_nt(a, b):
    return lax.dot_general(a, b, (((1,), (1,)), ((), ())), preferred_element_type=F32)


def mm_tn(a, b):
    return lax.dot_general(a, b, (((0,), (0,)), ((), ())), preferred_element_type=F32)


def halves(v):
    hi = v.astype(BF)
    return hi, (v - hi.astype(F32)).astype(BF)


def as_pair(v):
    lane = iota(v.shape, 1)
    hi = v.astype(BF).astype(F32)
    return jnp.where(lane < 4, hi, jnp.where(lane < 8, v - hi, 0.0)).astype(BF)


def fori(low, high, step):
    def run(i, carry):
        step(i)
        return carry

    lax.fori_loop(low, high, run, 0)


class SeqExchange:
    def __init__(self, source, landing, many, sems):
        self.source, self.landing, self.many = source, landing, many
        self.send, self.recv = sems
        self.me = lax.axis_index("seq")

    def copy(self, d):
        peer = lax.rem(self.me + d, SEQ)
        return pltpu.make_async_remote_copy(
            src_ref=self.source(peer),
            dst_ref=self.landing(self.me),
            send_sem=self.send,
            recv_sem=self.recv,
            device_id={"seq": peer},
            device_id_type=MESH,
        )

    def all(self):
        return pltpu.make_async_remote_copy(
            src_ref=self.many,
            dst_ref=self.many,
            send_sem=self.send,
            recv_sem=self.recv,
            device_id={"seq": lax.rem(self.me + 1, SEQ)},
            device_id_type=MESH,
        )

    def start(self):
        def one(i):
            step = i // 2
            self.copy(SEQ // 2 + jnp.where(lax.rem(i, 2) == 0, step, -step)).start()

        fori(1, SEQ, one)

    def wait_recv(self):
        self.all().wait_recv()

    def wait_send(self):
        self.all().wait_send()


class Ring:
    def __init__(self, me, to, whole, part, sems):
        self.whole, self.part, self.sems, self.to = whole, part, sems, to
        self.me, self.right, self.left = me, lax.rem(me + 1, 4), lax.rem(me + 3, 4)
        self.far = lax.rem(me + 2, 4)

    def copy(self, ref, k, peer):
        return pltpu.make_async_remote_copy(
            src_ref=ref,
            dst_ref=ref,
            send_sem=self.sems.at[0, k],
            recv_sem=self.sems.at[1, k],
            device_id={"seq": self.to(peer)},
            device_id_type=MESH,
        )

    def start(self):
        self.copy(self.whole(self.me), 0, self.right).start()
        self.copy(self.whole(self.me), 1, self.left).start()

    def forward(self):
        self.copy(self.whole(self.left), 0, self.left).wait_recv()
        self.copy(self.part(self.left, 0), 2, self.right).start()
        self.copy(self.whole(self.right), 1, self.right).wait_recv()
        self.copy(self.part(self.right, 1), 3, self.left).start()

    def finish(self):
        self.copy(self.part(self.far, 0), 2, self.left).wait_recv()
        self.copy(self.part(self.far, 1), 3, self.right).wait_recv()

    def wait_send(self):
        self.copy(self.whole(self.me), 0, self.right).wait_send()
        self.copy(self.whole(self.me), 1, self.left).wait_send()
        self.copy(self.part(self.left, 0), 2, self.right).wait_send()
        self.copy(self.part(self.right, 1), 3, self.left).wait_send()


class RingSum:
    def __init__(self, me, to, part, raw, near, sems):
        self.part, self.raw, self.near, self.sems, self.to = part, raw, near, sems, to
        self.me, self.far = me, lax.rem(me + 2, 4)
        self.side = (lax.rem(me + 3, 4), lax.rem(me + 1, 4))

    def copy(self, source, landing, k, peer):
        return pltpu.make_async_remote_copy(
            src_ref=source,
            dst_ref=landing,
            send_sem=self.sems.at[0, k],
            recv_sem=self.sems.at[1, k],
            device_id=self.to(peer),
            device_id_type=MESH,
        )

    def far_copy(self, n):
        return self.copy(self.part(self.far, n), self.raw(n), n, self.side[1 - n])

    def own_copy(self, n):
        peer = self.side[1 - n]
        return self.copy(self.part(peer, 1 - n), self.near(n, 1 - n), 2 + n, peer)

    def sum_copy(self, n):
        peer = self.side[1 - n]
        return self.copy(self.part(peer, n), self.near(n, n), 4 + n, peer)

    def start_far(self):
        for n in range(2):
            self.far_copy(n).start()

    def start_near(self):
        for n in range(2):
            self.own_copy(n).start()

    def middle(self):
        for n in range(2):
            self.copy(self.raw(n), self.raw(n), n, self.side[n]).wait_recv()
            ref = self.part(self.side[1 - n], n)
            ref[...] = (ref[...].astype(F32) + self.raw(n)[...].astype(F32)).astype(BF)
            self.sum_copy(n).start()

    def finish(self):
        halves = []
        for n in range(2):
            for k in range(2):
                ref = self.near(k, n)
                self.copy(ref, ref, 2 + k if n != k else 4 + k, self.side[k]).wait_recv()
            v = self.part(self.me, n)[...].astype(F32)
            halves.append(v + self.near(0, n)[...].astype(F32) + self.near(1, n)[...].astype(F32))
        return halves

    def wait_send(self):
        for n in range(2):
            self.far_copy(n).wait_send()
            self.own_copy(n).wait_send()
            self.sum_copy(n).wait_send()


def mp_copy(source, landing, send, recv, peer):
    return pltpu.make_async_remote_copy(
        src_ref=source,
        dst_ref=landing,
        send_sem=send,
        recv_sem=recv,
        device_id={"mp": peer},
        device_id_type=MESH,
    )


class MpExchange:
    def __init__(self, source, landing, sems):
        self.source, self.landing = source, landing
        self.send, self.recv = sems
        self.me = lax.axis_index("mp")

    def copy(self, d):
        peer = lax.rem(self.me + d, MP)
        return mp_copy(self.source(peer), self.landing(self.me), self.send.at[d], self.recv.at[d], peer)

    def arrival(self, d):
        origin = lax.rem(self.me - d + MP, MP)
        ref = self.landing(origin)
        return mp_copy(ref, ref, self.send.at[d], self.recv.at[d], origin)

    def start(self):
        fori(1, MP, lambda d: self.copy(d).start())

    def wait_recv(self):
        fori(1, MP, lambda d: self.arrival(d).wait_recv())

    def wait_send(self):
        fori(1, MP, lambda d: self.copy(d).wait_send())


def scan_scratch():
    v = pltpu.VMEM
    return dict(
        xs=v((CHUNKS, CHUNK, INNER), BF),
        xt=v((CHUNKS, CHUNK, INNER), BF),
        ed=v((CHUNKS, CHUNK, INNER), BF),
        er=v((CHUNKS, CHUNK, INNER), F32),
        tail=v((CHUNKS, CHUNK, INNER), F32),
        rcol=v((CHUNKS, CHUNK, LANES), F32),
        fresh=v((CHUNKS, STATE, INNER), F32),
        back=v((CHUNKS, STATE, INNER), F32),
        eR=v((CHUNKS, 8, INNER), F32),
        RC=v((8, INNER), F32),
        st=v((SEQ, 4 * PIECE, INNER), BF),
        sx=v((SEQ, 4 * PIECE, INNER), BF),
        sy=v((SEQ, 2 * PIECE, INNER), BF),
        sz=v((SEQ, 2 * PIECE, INNER), BF),
        y=v((CHUNKS, CHUNK, INNER), F32),
        dx=v((CHUNKS, CHUNK, INNER), F32),
        dbc=v((CHUNKS, CHUNK, 2 * STATE), F32),
        dd=v((CHUNKS, CHUNK, LANES), F32),
        gin=v((CHUNKS, STATE, INNER), F32),
        sin=v((STATE, INNER), F32),
    )


def main_scratch():
    v = pltpu.VMEM
    dma = pltpu.SemaphoreType.DMA
    seq_sems = lambda: dma((2,))
    return dict(
        tok3=v((SEQ, WID, DM), BF),
        cot=v((TOK, INNER), BF),
        wa=v((4, 4, SHARD, HALF), BF),
        wb=v((4, 4, SHARD, HALF), BF),
        sw_rx=v((SEQ, 16, LANES), BF),
        sw=v((LANES, DM), BF),
        z=v((TOK, INNER), BF),
        sraw=v((TOK, LANES), F32),
        pay=v((SEQ, ROWS, LANES), BF),
        trx=v((SEQ, ROWS, LANES), BF),
        bpay=v((SEQ, ROWS, LANES), BF),
        brx=v((SEQ, ROWS, LANES), BF),
        tri=v((4, CHUNK, CHUNK), BF),
        lp=v((TOK, LANES), BF),
        bcr=v((2, SEQ, WID, LANES), BF),
        bct=v((2, SEQ, WID, LANES), BF),
        wx=v((DM, 2 * LANES), BF),
        tdb=v((2, CHUNKS, CHUNK, LANES), BF),
        trs=v((MP, CHUNK, LANES), BF),
        tpiece=v((SEQ, COLS, LANES), BF),
        rpiece=v((SEQ, COLS, LANES), BF),
        rdb=v((2, SEQ, WID, LANES), BF),
        rrs=v((MP, SEQ, COLS, LANES), BF),
        dpiece=v((SEQ, COLS, LANES), BF),
        lacc=v((CHUNK, LANES), F32),
        swp=v((16, LANES), BF),
        R=scan_scratch(),
        T=scan_scratch(),
        g=v((TOK, 768), BF),
        tokt=v((DM, TOK), BF),
        gp=v((4, 4, SHARD, 640), BF),
        g_raw=v((2, 2, 2, 32, 640), BF),
        g_near=v((2, 2, 4, 32, 640), BF),
        h_own=v((2, 4, 32, 640), BF),
        h_raw=v((2, 2, 16, 640), BF),
        h_near=v((2, 2, 32, 640), BF),
        z_raw=v((2, 2, CHUNK, LANES), BF),
        z_near=v((2, 2, 2 * CHUNK, LANES), BF),
        gs=v((MP, 16, LANES), BF),
        gs_rx=v((SEQ, 16, LANES), BF),
        ip=v((MP, TOK, LANES), BF),
        prx=v((4, TOK, LANES), BF),
        zs=v((4, TOK, LANES), BF),
        fsh=v((SHARD, LANES), F32),
        frx=v((MP, SHARD, LANES), F32),
        s_local=dma((4,)),
        s_w=dma((4, 2, 4)),
        s_sw=seq_sems(),
        s_pay=seq_sems(),
        s_sr=seq_sems(),
        s_st=seq_sems(),
        s_ur=seq_sems(),
        s_ut=seq_sems(),
        s_back=seq_sems(),
        s_back2=seq_sems(),
        s_gp=dma((4, 2, 6)),
        s_bc=seq_sems(),
        s_bp=seq_sems(),
        s_gs=seq_sems(),
        s_bm=dma((2, MP)),
        s_tr=dma((2, MP)),
        s_rr=dma((2, MP)),
        s_fin=dma((2, MP)),
        s_pair=dma((2, 4, CHUNKS)),
        s_z=dma((2, 2, 6)),
    )


def sems(ref):
    return ref.at[0], ref.at[1]


def head_sum():
    c, h = iota((INNER, LANES), 0), iota((INNER, LANES), 1)
    return jnp.where((h < 8) & ((h & 3) == (c >> 6)), 1.0, 0.0).astype(BF)


def pair_expand(shift):
    k, c = iota((LANES, INNER), 0) - shift, iota((LANES, INNER), 1)
    return jnp.where((k >= 0) & (k < 8) & ((k & 3) == (c >> 6)), 1.0, 0.0).astype(BF)


def pair_merge(shift):
    k, h = iota((LANES, LANES), 0) - shift, iota((LANES, LANES), 1)
    return jnp.where((k >= 0) & (k < 8) & (h < 8) & ((k & 3) == (h & 3)), 1.0, 0.0).astype(BF)


def pair_place(shift):
    k, lane = iota((LANES, LANES), 0), iota((LANES, LANES), 1)
    return jnp.where((k < 8) & (lane == k + shift), 1.0, 0.0).astype(BF)


def wide(load, block, q):
    return jnp.concatenate([load(block, q), load(block + 1, q)], axis=1)


def summary(b, tri, load, pair_of, rate, ratex, q):
    x = wide(load, BX, q).astype(F32)
    dy = wide(load, BY, q).astype(F32)
    pair, shift = pair_of(q)
    dexp = mm(pair, pair_expand(shift))
    logs = (-dexp * ratex).astype(BF)
    rexp = mm(tri, logs)
    b["rcol"][q] = mm(tri, (-mm(pair, pair_merge(shift)) * rate).astype(BF))
    total = jnp.sum(logs.astype(F32), axis=0, keepdims=True)
    er = jnp.exp2(rexp)
    tail = jnp.exp2(jnp.minimum(total - rexp, 0.0))
    xs = (x * dexp).astype(BF)
    xt = (xs.astype(F32) * tail).astype(BF)
    ed = (er * dy).astype(BF)
    b["er"][q] = er
    b["tail"][q] = tail
    b["xs"][q] = xs
    b["xt"][q] = xt
    b["ed"][q] = ed
    b["fresh"][q] = mm_tn(load(BB, q), xt)
    b["back"][q] = mm_tn(load(BC, q), ed)
    rows = jnp.broadcast_to(total, (8, INNER))
    b["eR"][q] = jnp.exp2(rows)
    b["RC"][...] += rows


def pack_states(b):
    e = [b["eR"][q][:1] for q in range(CHUNKS)]
    end = b["fresh"][0]
    for q in range(1, CHUNKS):
        end = end * e[q] + b["fresh"][q]
    first = b["back"][CHUNKS - 1]
    for q in range(CHUNKS - 2, -1, -1):
        first = first * e[q] + b["back"][q]
    rc = b["RC"][...]
    hi = rc.astype(BF).astype(F32)
    logs = jnp.concatenate([hi, rc - hi], axis=0).astype(BF)
    pieces = [v.reshape(SEQ, PIECE, INNER) for v in (end, first)]
    b["st"][:, pl.ds(0, 2 * PIECE), :] = jnp.concatenate(pieces, axis=1).astype(BF)
    for k in range(SEQ):
        b["st"][k, pl.ds(2 * PIECE, 2 * PIECE)] = logs


def chain_states(b):
    own = [b["sx"][k, pl.ds(0, 2 * PIECE)].astype(F32) for k in range(SEQ)]
    logs = [b["sx"][k, pl.ds(2 * PIECE, 2 * PIECE)].astype(F32) for k in range(SEQ)]
    decay = [jnp.exp2(v[:PIECE] + v[PIECE:]) for v in logs]
    state = [jnp.zeros((PIECE, INNER), F32)]
    grad = [jnp.zeros((PIECE, INNER), F32)]
    for k in range(SEQ - 1):
        state.append(state[k] * decay[k] + own[k][:PIECE])
        n = SEQ - 1 - k
        grad.append(grad[k] * decay[n] + own[n][PIECE:])
    for k in range(SEQ):
        b["sy"][k] = jnp.concatenate([state[k], grad[SEQ - 1 - k]], axis=0).astype(BF)


def entering_states(b):
    both = b["sz"][...].astype(F32)
    b["sin"][...] = both[:, :PIECE, :].reshape(STATE, INNER)
    grad = both[:, PIECE:, :].reshape(STATE, INNER)
    for q in range(CHUNKS - 1, -1, -1):
        b["gin"][q] = grad
        if q > 0:
            grad = grad * b["eR"][q][:1] + b["back"][q]


def head_rows(h):
    one = jnp.where((iota((16, INNER), 1) >> 6) == h, 1.0, 0.0).astype(BF)
    return jnp.concatenate([one] * (CHUNK // 16), axis=0)


def inside(b, tri, load, q):
    dy = wide(load, BY, q)
    bmat = load(BB, q)
    cmat = load(BC, q)
    xs = b["xs"][q]
    trif = tri.astype(F32)
    scores = mm_nt(cmat, bmat) * trif
    rcol = b["rcol"][q]
    rrow = rcol.T
    pairs = None
    ms, dys, xss = [], [], []
    for h in range(HEADS):
        decay = jnp.exp2(jnp.minimum(rcol[:, h : h + 1] - rrow[h : h + 1, :], 0.0))
        ms.append((decay * scores).astype(BF))
        mask = head_rows(h)
        dys.append(dy * mask)
        xss.append(xs * mask)
        term = decay * mm_nt(dys[h], xs)
        pairs = term if h == 0 else pairs + term
    dy4 = jnp.concatenate(dys, axis=0)
    y = mm(jnp.concatenate(ms, axis=1), jnp.concatenate(xss, axis=0))
    dxs = mm_tn(jnp.concatenate(ms, axis=0), dy4)
    pairs = (pairs * trif).astype(BF)
    b["y"][q] = y
    b["dx"][q] = dxs
    b["dbc"][q, :, pl.ds(0, STATE)] = mm_tn(pairs, cmat)
    b["dbc"][q, :, pl.ds(STATE, STATE)] = mm(pairs, bmat)


def outside(b, tri, tri_up, load, pair_of, rate, q, put):
    x = wide(load, BX, q).astype(F32)
    dy = wide(load, BY, q).astype(F32)
    bmat = load(BB, q)
    cmat = load(BC, q)
    pair, shift = pair_of(q)
    dexp = mm(pair, pair_expand(shift))
    xs = b["xs"][q].astype(F32)
    state = b["sin"][...]
    grad = b["gin"][q]
    state_b, grad_b = state.astype(BF), grad.astype(BF)
    sums = head_sum()
    y = b["y"][q] + b["er"][q] * mm(cmat, state_b)
    inner = b["dx"][q]
    outer = b["tail"][q] * mm(bmat, grad_b)
    dxs = inner + outer
    db = b["dbc"][q, :, pl.ds(0, STATE)] + mm_nt(b["xt"][q], grad_b)
    dc = b["dbc"][q, :, pl.ds(STATE, STATE)] + mm_nt(b["ed"][q], state_b)

    def by_head(v):
        return mm(v.astype(BF), sums)

    late = by_head(dy * y - xs * inner).astype(BF)
    early = by_head(xs * outer).astype(BF)
    decayed = b["eR"][q][:1] * state
    across = jnp.sum(decayed * grad, axis=0, keepdims=True)
    across = mm(jnp.broadcast_to(across, (16, INNER)).astype(BF), sums)[:1]
    dl = mm(tri_up, late) + mm(tri, early) - early.astype(F32) + across
    ddelta = by_head(x * dxs) - rate * dl
    b["sin"][...] = decayed + b["fresh"][q]
    put(q, y, dexp * dxs, db, dc, ddelta)


def kernel(tok_hbm, cot_hbm, pm, ps, pt, bias_s, rate_s, skip_s, gated_o, ig_o, gm_o, gsh_o, gst_o, m):
    seq, mp = lax.axis_index("seq"), lax.axis_index("mp")
    core = lax.rem(mp, 2)
    chip = mp // 2
    partner = mp + 1 - 2 * core
    plane, line = seq // 4, lax.rem(seq, 4)
    low = lax.rem(seq, 2)

    load_tok = pltpu.make_async_copy(tok_hbm, m["tok3"], m["s_local"].at[0])
    load_cot = pltpu.make_async_copy(cot_hbm, m["cot"], m["s_local"].at[1])
    load_tok.start()
    load_cot.start()

    barrier = pltpu.get_barrier_semaphore()

    def greet_seq(d):
        pl.semaphore_signal(
            barrier, inc=1, device_id={"seq": lax.rem(seq + d, SEQ)}, device_id_type=MESH
        )

    def greet_mp(d):
        pl.semaphore_signal(barrier, inc=1, device_id={"mp": lax.rem(mp + d, MP)}, device_id_type=MESH)

    fori(1, SEQ, greet_seq)
    fori(1, MP, greet_mp)

    wa, wb, swp = m["wa"], m["wb"], m["swp"]
    wa[plane, line, :, pl.ds(0, 256)] = pm[:, 0, :]
    wb[plane, line, :, pl.ds(0, 256)] = pm[:, 1, :]
    wa[plane, line, :, pl.ds(256, 128)] = ps[:, 0, :]
    wb[plane, line, :, pl.ds(256, 128)] = ps[:, 1, :]
    at, lane = iota((SHARD, LANES), 0), iota((SHARD, LANES), 1)
    place = jnp.where(lane == at + SHARD * low, 1.0, 0.0).astype(BF)
    shifted = mm(pt[...], place).astype(BF)
    swp[...] = jnp.concatenate([shifted, shifted, jnp.zeros((8, LANES), BF)], axis=0)
    pl.semaphore_wait(barrier, SEQ + MP - 2)

    most = pl.ds(0, SEQ - 1)

    def along_x(k):
        return 4 * k + line

    def along_y(k):
        return 4 * plane + k

    half = SHARD // 2
    ring_a1 = Ring(plane, along_x, lambda k: wa.at[k, line], lambda k, n: wa.at[k, line, pl.ds(half * n, half)], m["s_w"].at[0])
    ring_b1 = Ring(line, along_y, lambda k: wb.at[plane, k], lambda k, n: wb.at[plane, k, pl.ds(half * n, half)], m["s_w"].at[1])
    ring_a2 = Ring(line, along_y, lambda k: wa.at[:, k], lambda k, n: wa.at[pl.ds(2 * n, 2), k], m["s_w"].at[2])
    ring_b2 = Ring(plane, along_x, lambda k: wb.at[k], lambda k, n: wb.at[k, pl.ds(2 * n, 2)], m["s_w"].at[3])
    rings = (ring_a1, ring_b1, ring_a2, ring_b2)
    ring_a1.start()
    ring_b1.start()
    send_sw = SeqExchange(lambda p: swp, lambda k: m["sw_rx"].at[k], m["sw_rx"].at[most], sems(m["s_sw"]))
    send_sw.start()
    m["sw_rx"][seq] = swp[...]

    def flip(q):
        m["tokt"][:, pl.ds(q * CHUNK, CHUNK)] = m["tok3"][pl.ds(4 * q, 4)].reshape(CHUNK, DM).T

    load_tok.wait()
    flip(0)
    ring_a1.forward()
    ring_b1.forward()
    ring_a1.finish()
    ring_a2.start()
    ring_b1.finish()
    ring_b2.start()

    i, j = iota((CHUNK, CHUNK), 0), iota((CHUNK, CHUNK), 1)
    m["tri"][0] = jnp.where(i >= j, 1.0, 0.0).astype(BF)
    it, jt = (i & 15) * 16 + (i >> 4), (j & 15) * 16 + (j >> 4)
    m["tri"][1] = jnp.where(it >= jt, 1.0, 0.0).astype(BF)
    m["tri"][2] = jnp.where(i <= j, 1.0, 0.0).astype(BF)
    m["tri"][3] = jnp.where(it <= jt, 1.0, 0.0).astype(BF)
    m["sw"][...] = jnp.zeros((LANES, DM), BF)
    m["R"]["RC"][...] = jnp.zeros((8, INNER), F32)
    m["T"]["RC"][...] = jnp.zeros((8, INNER), F32)
    m["lacc"][...] = jnp.zeros((CHUNK, LANES), F32)

    head_l = iota((1, LANES), 1)
    head_c = iota((1, INNER), 1) >> 6

    def lanes_of(value):
        v = jnp.zeros((1, LANES), F32)
        for h in range(HEADS):
            v = jnp.where((head_l < 8) & ((head_l & 3) == h), value(h), v)
        return v

    def features_of(value):
        v = jnp.zeros((1, INNER), F32)
        for h in range(HEADS):
            v = jnp.where(head_c == h, value(h), v)
        return v

    bias = lanes_of(lambda h: bias_s[h])
    rate_r, rate_t = lanes_of(lambda h: rate_s[0, h]), lanes_of(lambda h: rate_s[1, h])
    ratex_r = features_of(lambda h: rate_s[0, h]) * LOG2E
    ratex_t = features_of(lambda h: rate_s[1, h]) * LOG2E
    skip = features_of(lambda h: skip_s[h])

    load_cot.wait()
    flip(1)
    ring_a2.forward()
    ring_b2.forward()
    flip(2)
    flip(3)
    ring_a2.finish()
    ring_b2.finish()
    send_sw.wait_recv()
    for k in range(SEQ // 2):
        m["sw"][pl.ds(0, 16), pl.ds(k * LANES, LANES)] = m["sw_rx"][2 * k] + m["sw_rx"][2 * k + 1]

    def rows_of(q):
        return pl.ds(pl.multiple_of(q * CHUNK, CHUNK), CHUNK)

    def columns(ref, at, width):
        return ref[:, :, :, pl.ds(at, width)].reshape(DM, width)

    def rest(v):
        return v.reshape(4, WID, LANES)

    send_pay = SeqExchange(lambda p: m["pay"].at[p], lambda k: m["trx"].at[k], m["trx"].at[most], sems(m["s_pay"]))
    quarter = pl.ds(pl.multiple_of(chip * COLS, COLS), COLS)
    bcr, bct = m["bcr"], m["bct"]
    send_bc = SeqExchange(
        lambda p: bcr.at[core, p, quarter],
        lambda k: bct.at[core, k, quarter],
        bct.at[core, most, quarter],
        sems(m["s_bc"]),
    )

    def piece_of(ref, k):
        return ref.at[lax.rem(k, 2), :, pl.ds(pl.multiple_of(k // 2 * COLS, COLS), COLS)]

    send_bm = MpExchange(lambda p: piece_of(bct, mp), lambda k: piece_of(bct, k), sems(m["s_bm"]))
    m["wx"][:, pl.ds(0, LANES)] = jnp.where(core == 0, columns(wa, 256, 128), columns(wb, 256, 128))
    m["wx"][:, pl.ds(LANES, LANES)] = m["sw"][...].T

    def start_four(exchange, q):
        def one(n):
            d = lax.rem(4 * q + n - seq + SEQ, SEQ)

            @pl.when(d != 0)
            def _():
                exchange.copy(d).start()

        fori(0, 4, one)

    def far_first(n):
        step = jnp.where(n == 0, 2, jnp.where(n == 3, 0, 2 * n - 1))
        return lax.rem(plane + step, 4)

    def project_shared(n):
        q = far_first(n)
        u = m["tok3"][pl.ds(4 * q, 4)].reshape(CHUNK, DM)
        w = jnp.concatenate([columns(wa, 256, 128), columns(wb, 256, 128)], axis=1)
        v = mm(u, w).astype(BF)
        bcr[0, pl.ds(4 * q, 4)] = rest(v[:, :LANES])
        bcr[1, pl.ds(4 * q, 4)] = rest(v[:, LANES:])
        start_four(send_bc, q)

    def project(n):
        q = far_first(n)
        rows = rows_of(q)
        u = m["tok3"][pl.ds(4 * q, 4)].reshape(CHUNK, DM)
        four = pl.ds(4 * q, 4)

        def put(block, v):
            v = v.astype(BF)
            for k in range(v.shape[1] // LANES):
                m["pay"][four, pl.ds((block + k) * WID, WID), :] = rest(v[:, k * LANES : (k + 1) * LANES])

        z = mm(u, columns(wb, 0, 256)).astype(BF)
        m["z"][rows, :] = z
        zf = z.astype(F32)
        gate = zf * jax.nn.sigmoid(zf)
        put(BY, m["cot"][rows, :].astype(F32) * gate)
        put(BX, mm(u, columns(wa, 0, 256)))
        raw = mm(u, m["wx"][:, pl.ds(LANES, LANES)]) + bias
        m["sraw"][rows, :] = raw
        pair = as_pair(jnp.maximum(raw, 0.0) + jnp.log1p(jnp.exp(-jnp.abs(raw))))
        m["lp"][rows, :] = pair
        folded = jnp.zeros((64, LANES), F32)
        for g in range(4):
            part = rest(pair)[:, g * COLS : (g + 1) * COLS, :].reshape(64, LANES)
            folded += mm(part, pair_place(8 * g))
        m["pay"][four, pl.ds(ROWS_L, COLS), :] = folded.astype(BF).reshape(4, COLS, LANES)
        start_four(send_pay, q)

    fori(0, CHUNKS, project_shared)
    fori(0, CHUNKS, project)
    m["trx"][seq] = m["pay"][seq]
    bct[core, seq, quarter] = bcr[core, seq, quarter]

    def load_r(block, q):
        if block >= BB:
            return bcr[block - BB, pl.ds(4 * q, 4)].reshape(CHUNK, LANES)
        return m["pay"][pl.ds(4 * q, 4), pl.ds(block * WID, WID), :].reshape(CHUNK, LANES)

    def pair_r(q):
        return m["lp"][rows_of(q), :], 0

    def cols_of(block, q):
        return pl.ds(pl.multiple_of(block * WID + q * COLS, COLS), COLS)

    def load_t(block, q):
        if block >= BB:
            return bct[block - BB, :, pl.ds(q * COLS, COLS), :].reshape(CHUNK, LANES)
        return m["trx"][:, cols_of(block, q), :].reshape(CHUNK, LANES)

    def pair_t(q):
        return m["trx"][:, pl.ds(ROWS_L, COLS), :].reshape(CHUNK, LANES), 8 * q

    def pieces_exchange(source, landing, sem):
        return SeqExchange(lambda p: source.at[p], lambda k: landing.at[k], landing.at[most], sems(sem))

    r, t = m["R"], m["T"]
    tri_r, tri_t, up_r, up_t = (m["tri"].at[k] for k in range(4))

    def chunks(low, high, step):
        for q in range(low, high):
            step(q)


    def start_pieces(b, sem):
        e = pieces_exchange(b["st"], b["sx"], sem)
        e.start()
        b["sx"][seq] = b["st"][seq]
        return e

    def start_entering(b, sem):
        chain_states(b)
        e = pieces_exchange(b["sy"], b["sz"], sem)
        e.start()
        b["sz"][seq] = b["sy"][seq]
        return e

    chunks(0, CHUNKS, lambda q: summary(r, tri_r[...], load_r, pair_r, rate_r * LOG2E, ratex_r, q))
    pack_states(r)
    send_bc.wait_recv()
    send_bm.start()
    chunks(0, 2, lambda q: inside(r, tri_r[...], load_r, q))
    send_sw.wait_send()
    for e in rings:
        e.wait_send()

    send_pay.wait_recv()
    send_sr = start_pieces(r, m["s_sr"])
    send_bm.wait_recv()
    chunks(0, CHUNKS, lambda q: summary(t, tri_t[...], load_t, pair_t, rate_t * LOG2E, ratex_t, q))
    pack_states(t)
    send_st = start_pieces(t, m["s_st"])
    send_sr.wait_recv()
    send_ur = start_entering(r, m["s_ur"])
    chunks(0, 2, lambda q: inside(t, tri_t[...], load_t, q))
    chunks(2, 3, lambda q: inside(r, tri_r[...], load_r, q))
    send_st.wait_recv()
    send_ut = start_entering(t, m["s_ut"])
    chunks(2, CHUNKS, lambda q: inside(t, tri_t[...], load_t, q))
    chunks(3, CHUNKS, lambda q: inside(r, tri_r[...], load_r, q))
    send_ut.wait_recv()
    entering_states(t)

    def put_t(q, y, dx, db, dc, dd):
        def put(block, v):
            v = v.astype(BF)
            for k in range(v.shape[1] // LANES):
                part = v[:, k * LANES : (k + 1) * LANES]
                at = 128 * (q // 2) + 32 * (block + k) + COLS * (q % 2)
                m["bpay"][:, pl.ds(at, COLS), :] = part.reshape(SEQ, COLS, LANES)

        put(BX, y)
        put(BY, dx)
        m["tdb"][0, q] = db.astype(BF)
        m["tdb"][1, q] = dc.astype(BF)
        for n in range(2):
            d = lax.rem(2 * q + n - mp + MP, MP)

            @pl.when(d != 0)
            def _():
                send_tr.copy(d).start()

        m["lacc"][...] += mm(as_pair(dd), pair_place(8 * q))

    def half_back(at, count, sem):
        rows = pl.ds(at, count)
        return SeqExchange(
            lambda p: m["bpay"].at[p, rows], lambda k: m["brx"].at[k, rows], m["brx"].at[most, rows], sems(sem)
        )

    send_back = half_back(0, 128, m["s_back"])
    send_back2 = half_back(128, 144, m["s_back2"])
    send_tr = MpExchange(
        lambda p: m["tdb"].at[lax.rem(p, 2), p // 2], lambda k: m["trs"].at[k], sems(m["s_tr"])
    )
    send_bp = SeqExchange(lambda p: m["tpiece"].at[p], lambda k: m["rpiece"].at[k], m["rpiece"].at[most], sems(m["s_bp"]))
    send_rr = MpExchange(lambda p: piece_of(m["rdb"], p), lambda k: m["rrs"].at[k], sems(m["s_rr"]))

    def group_total(ref):
        v = ref[0].astype(F32)
        for k in range(1, MP):
            v += ref[k].astype(F32)
        return v

    chunks(0, 2, lambda q: outside(t, tri_t[...], up_t[...], load_t, pair_t, rate_t, q, put_t))
    send_back.start()
    chunks(2, 4, lambda q: outside(t, tri_t[...], up_t[...], load_t, pair_t, rate_t, q, put_t))
    m["bpay"][:, pl.ds(ROWS_L, COLS), :] = m["lacc"][...].astype(BF).reshape(SEQ, COLS, LANES)
    send_back2.start()
    m["brx"][seq] = m["bpay"][seq]
    m["trs"][mp] = m["tdb"][core, chip]

    send_ur.wait_recv()
    entering_states(r)

    def put_r(q, y, dx, db, dc, dd):
        r["y"][q] = y
        r["dx"][q] = dx
        m["rdb"][0, pl.ds(4 * q, 4)] = rest(db.astype(BF))
        m["rdb"][1, pl.ds(4 * q, 4)] = rest(dc.astype(BF))
        r["dd"][q] = dd

    def outside_r(q):
        outside(r, tri_r[...], up_r[...], load_r, pair_r, rate_r, q, put_r)

    chunks(0, 1, outside_r)
    send_tr.wait_recv()
    m["tpiece"][...] = group_total(m["trs"]).astype(BF).reshape(SEQ, COLS, LANES)
    send_bp.start()
    m["rpiece"][seq] = m["tpiece"][seq]
    chunks(1, CHUNKS, outside_r)
    send_rr.start()
    m["rrs"][mp] = m["rdb"][core, :, quarter]
    for e in (send_pay, send_bc, send_bm, send_sr, send_ur, send_st, send_ut):
        e.wait_send()
    send_back.wait_recv()
    send_back2.wait_recv()
    send_bp.wait_recv()
    send_rr.wait_recv()
    m["dpiece"][...] = (group_total(m["rrs"]) + m["rpiece"][...].astype(F32)).astype(BF)

    def back(block, q):
        parts = [m["brx"][pl.ds(4 * q, 4), pl.ds(128 * n + 32 * block, 32), :] for n in range(2)]
        return jnp.concatenate(parts, axis=1).reshape(CHUNK, LANES)

    def combine(q):
        rows = rows_of(q)
        x = wide(load_r, BX, q).astype(F32)
        dy = wide(load_r, BY, q).astype(F32)
        z = m["z"][rows, :].astype(F32)
        cot = m["cot"][rows, :].astype(F32)
        y = r["y"][q] + wide(back, BX, q).astype(F32) + skip * x
        sigma = jax.nn.sigmoid(z)
        gated_o[rows, :] = (y * (z * sigma)).astype(BF)
        m["g"][rows, pl.ds(256, 256)] = (cot * y * sigma * (1.0 + z * (1.0 - sigma))).astype(BF)
        m["g"][rows, pl.ds(0, 256)] = (r["dx"][q] + wide(back, BY, q).astype(F32) + skip * dy).astype(BF)
        folded = m["brx"][pl.ds(4 * q, 4), pl.ds(ROWS_L, COLS), :].reshape(64, LANES)
        parts = [mm(folded, pair_merge(8 * g)).reshape(4, COLS, LANES) for g in range(4)]
        dd = r["dd"][q] + jnp.concatenate(parts, axis=1).reshape(CHUNK, LANES)
        dstep = dd * jax.nn.sigmoid(m["sraw"][rows, :])
        m["g"][rows, pl.ds(640, LANES)] = jnp.where(iota((CHUNK, LANES), 1) < HEADS, dstep, 0.0).astype(BF)

    def pair_copy(k, q):
        rows = rows_of(q)
        return mp_copy(
            m["ip"].at[2 * k + 1 - core, rows],
            m["prx"].at[k, rows],
            m["s_pair"].at[0, k, q],
            m["s_pair"].at[1, k, q],
            partner,
        )

    def z_ring(n):
        def part(k, h):
            return m["zs"].at[k, pl.ds(CHUNK * (2 * n + h), CHUNK)]

        return RingSum(
            chip,
            lambda k: {"mp": 2 * k + core},
            part,
            lambda h: m["z_raw"].at[n, h],
            lambda side, h: m["z_near"].at[n, side, pl.ds(CHUNK * h, CHUNK)],
            m["s_z"].at[n],
        )

    z_rings = [z_ring(0), z_ring(1)]

    def pair_sum(k, q):
        rows = rows_of(q)
        pair_copy(k, q).wait_recv()
        return (m["ip"][2 * k + core, rows, :].astype(F32) + m["prx"][k, rows, :].astype(F32)).astype(BF)

    def pass_on(q):
        for k in range(4):
            m["zs"][k, rows_of(q), :] = pair_sum(k, q)

    def z_start(n):
        z_rings[n].start_far()
        z_rings[n].start_near()

    def z_finish(n):
        for h, v in enumerate(z_rings[n].finish()):
            ig_o[rows_of(2 * n + h), :] = v.astype(BF)

    def combine_all(q):
        combine(q)
        rows = rows_of(q)
        piece = m["dpiece"][pl.ds(4 * q, 4)]
        here = (iota((4, WID, LANES), 1) >> 4) == chip
        piece = jnp.where(here, jnp.concatenate([piece] * 4, axis=1), jnp.zeros((), BF)).reshape(CHUNK, LANES)
        m["g"][rows, pl.ds(512, LANES)] = piece

    def input_part(q):
        rows = rows_of(q)
        g = m["g"][rows, :]
        for c in range(4):
            cols = pl.ds(c * 256, 256)
            v = mm_nt(g[:, :256], wa[c, :, :, pl.ds(0, 256)].reshape(256, 256))
            v += mm_nt(g[:, 256:512], wb[c, :, :, pl.ds(0, 256)].reshape(256, 256))
            v += mm_nt(g[:, 512:], m["wx"][cols, :])
            v = v.astype(BF)
            m["ip"][2 * c, rows, :] = v[:, :LANES]
            m["ip"][2 * c + 1, rows, :] = v[:, LANES:]
        fori(0, 4, lambda k: pair_copy(k, q).start())

    chunks(0, CHUNKS, combine_all)

    def g_ring(n):
        rows = pl.ds(32 * n, 32)

        def part(k, h):
            two = pl.ds(2 * h, 2)
            return m["gp"].at[k, two, rows] if n == 0 else m["gp"].at[two, k, rows]

        return RingSum(
            plane if n == 0 else line,
            lambda k: {"seq": along_x(k) if n == 0 else along_y(k)},
            part,
            lambda h: m["g_raw"].at[n, h],
            lambda side, h: m["g_near"].at[n, side, pl.ds(2 * h, 2)],
            m["s_gp"].at[n],
        )

    def h_ring(n):
        return RingSum(
            line if n == 0 else plane,
            lambda k: {"seq": along_y(k) if n == 0 else along_x(k)},
            lambda k, h: m["h_own"].at[n, k, pl.ds(16 * h, 16)],
            lambda h: m["h_raw"].at[n, h],
            lambda side, h: m["h_near"].at[n, side, pl.ds(16 * h, 16)],
            m["s_gp"].at[2 + n],
        )

    g_rings, h_rings = [g_ring(0), g_ring(1)], [h_ring(0), h_ring(1)]
    send_gs = SeqExchange(lambda p: m["gs"].at[p // 2], lambda k: m["gs_rx"].at[k], m["gs_rx"].at[most], sems(m["s_gs"]))

    def grads(n):
        k = lax.rem(plane + n, 4)
        cols = rows_of(k)
        v = mm(m["tokt"][cols, :], m["g"][...])
        m["gp"][k] = v[:, :640].astype(BF).reshape(4, SHARD, 640)
        gs = v[:, 640:].T[:16].astype(BF)
        m["gs"][2 * k] = gs[:, :LANES]
        m["gs"][2 * k + 1] = gs[:, LANES:]
        start_four(send_gs, k)

    grads(2)
    g_rings[0].start_far()
    grads(1)
    grads(3)
    g_rings[0].start_near()
    grads(0)
    g_rings[1].start_far()
    g_rings[1].start_near()
    m["gs_rx"][seq] = m["gs"][seq // 2]
    input_part(0)
    input_part(1)
    g_rings[0].middle()
    g_rings[1].middle()
    pass_on(0)
    pass_on(1)
    z_start(0)
    input_part(2)
    input_part(3)
    for e in (send_back, send_back2, send_tr, send_bp, send_rr, send_gs):
        e.wait_send()

    def g_next(n):
        for h, v in enumerate(g_rings[n].finish()):
            m["h_own"][n, pl.ds(2 * h, 2)] = v.astype(BF).reshape(2, 32, 640)
        h_rings[n].start_far()
        h_rings[n].start_near()

    g_next(0)
    g_next(1)
    pass_on(2)
    pass_on(3)
    z_start(1)
    z_rings[0].middle()
    h_rings[0].middle()
    h_rings[1].middle()
    z_rings[1].middle()

    def total_of(ref):
        v = ref[0].astype(F32)
        for k in range(1, SEQ):
            v += ref[k].astype(F32)
        return v

    main = jnp.concatenate(h_rings[0].finish() + h_rings[1].finish(), axis=0)
    m["fsh"][...] = main[:, 512:]
    send_fin = MpExchange(lambda p: m["fsh"], lambda k: m["frx"].at[k], sems(m["s_fin"]))
    send_fin.start()
    m["frx"][mp] = main[:, 512:]
    gm_o[:, 0, :] = main[:, :INNER]
    gm_o[:, 1, :] = main[:, INNER : 2 * INNER]
    send_gs.wait_recv()
    step = total_of(m["gs_rx"])
    gst_o[...] = jnp.where(low == 0, step[:HEADS, :SHARD], step[:HEADS, SHARD:])
    z_finish(0)
    z_finish(1)
    send_fin.wait_recv()
    for n in range(2):
        gsh_o[:, n, :] = m["frx"][n] + m["frx"][2 + n] + m["frx"][4 + n] + m["frx"][6 + n]

    sent = [send_fin] + z_rings + g_rings + h_rings
    for e in sent:
        e.wait_send()
    for q in range(CHUNKS):
        fori(0, 4, lambda k: pair_copy(k, q).wait_send())


def hand_over(*refs):
    n = len(refs) // 2
    for k in range(n):
        refs[n + k][...] = refs[k][...]


def body(tokens, proj_main, proj_shared, proj_step, step_bias, decay_rate, skip_gain, cotangent):
    vm = pl.BlockSpec(memory_space=pltpu.VMEM)
    sm = pl.BlockSpec(memory_space=pltpu.SMEM)
    hbm = pl.BlockSpec(memory_space=pl.ANY)
    shapes = (
        jax.ShapeDtypeStruct((TOK, INNER), BF),
        jax.ShapeDtypeStruct((TOK, LANES), BF),
        jax.ShapeDtypeStruct((SHARD, 2, INNER), F32),
        jax.ShapeDtypeStruct((SHARD, 2, STATE), F32),
        jax.ShapeDtypeStruct((HEADS, SHARD), F32),
    )
    results = pl.pallas_call(
        kernel,
        out_shape=shapes,
        in_specs=[hbm, hbm, vm, vm, vm, sm, sm, sm],
        out_specs=(vm,) * 5,
        scratch_shapes=[main_scratch()],
        compiler_params=pltpu.CompilerParams(
            collective_id=0, has_side_effects=True, vmem_limit_bytes=62 * 1024 * 1024
        ),
    )(
        tokens.reshape(SEQ, WID, DM),
        cotangent.reshape(TOK, INNER),
        proj_main,
        proj_shared,
        proj_step.T,
        step_bias,
        decay_rate,
        skip_gain,
    )
    gated, ig, gm, gsh, gst = pl.pallas_call(
        hand_over,
        out_shape=shapes,
        in_specs=[vm] * 5,
        out_specs=(vm,) * 5,
    )(*results)
    return (
        gated.reshape(1, 16, WID, INNER),
        ig.reshape(1, 16, WID, LANES),
        gm,
        gsh,
        gst.T,
    )


def solution(mesh):
    placed = (
        P("seq", None, None, None),
        P("seq", None, "mp"),
        P("seq", None, None),
        P("seq", "mp"),
        P("mp"),
        P(None, "mp"),
        P("mp"),
        P("seq", None, None, "mp"),
    )
    return jax.shard_map(
        body,
        mesh=mesh,
        in_specs=placed,
        out_specs=(
            P("seq", None, None, "mp"),
            P("seq", None, None, "mp"),
            P("seq", None, "mp"),
            P("seq", None, None),
            P("seq", "mp"),
        ),
        check_vma=False,
    )
```

```python
import jax
import jax.numpy as jnp
from jax import lax
from jax.experimental import pallas as pl
from jax.experimental.pallas import tpu as pltpu
from jax.sharding import PartitionSpec as P

MESH = pl.DeviceIdType.MESH
BF = jnp.bfloat16
F32 = jnp.float32

SEQ = 16
MP = 8
TOK = 1024
WID = 64
DM = 1024
INNER = 256
HEADS = 4
STATE = 128
LANES = 128
CHUNK = 256
CHUNKS = TOK // CHUNK
COLS = CHUNK // SEQ
SHARD = DM // SEQ
BX, BY, BB, BC, ROWS_L, ROWS = 0, 2, 4, 5, 256, 272
PIECE = STATE // SEQ
HALF = 3 * LANES
LOG2E = 1.4426950408889634


def iota(shape, axis):
    return lax.broadcasted_iota(jnp.int32, shape, axis)


def mm(a, b):
    return lax.dot_general(a, b, (((1,), (0,)), ((), ())), preferred_element_type=F32)


def mm_nt(a, b):
    return lax.dot_general(a, b, (((1,), (1,)), ((), ())), preferred_element_type=F32)


def mm_tn(a, b):
    return lax.dot_general(a, b, (((0,), (0,)), ((), ())), preferred_element_type=F32)


def halves(v):
    hi = v.astype(BF)
    return hi, (v - hi.astype(F32)).astype(BF)


def as_pair(v):
    lane = iota(v.shape, 1)
    hi = v.astype(BF).astype(F32)
    return jnp.where(lane < 4, hi, jnp.where(lane < 8, v - hi, 0.0)).astype(BF)


def fori(low, high, step):
    def run(i, carry):
        step(i)
        return carry

    lax.fori_loop(low, high, run, 0)


class SeqExchange:
    def __init__(self, source, landing, many, sems):
        self.source, self.landing, self.many = source, landing, many
        self.send, self.recv = sems
        self.me = lax.axis_index("seq")

    def copy(self, d):
        peer = lax.rem(self.me + d, SEQ)
        return pltpu.make_async_remote_copy(
            src_ref=self.source(peer),
            dst_ref=self.landing(self.me),
            send_sem=self.send,
            recv_sem=self.recv,
            device_id={"seq": peer},
            device_id_type=MESH,
        )

    def all(self):
        return pltpu.make_async_remote_copy(
            src_ref=self.many,
            dst_ref=self.many,
            send_sem=self.send,
            recv_sem=self.recv,
            device_id={"seq": lax.rem(self.me + 1, SEQ)},
            device_id_type=MESH,
        )

    def start(self):
        def one(i):
            step = i // 2
            self.copy(SEQ // 2 + jnp.where(lax.rem(i, 2) == 0, step, -step)).start()

        fori(1, SEQ, one)

    def wait_recv(self):
        self.all().wait_recv()

    def wait_send(self):
        self.all().wait_send()


class Ring:
    def __init__(self, me, to, whole, part, sems):
        self.whole, self.part, self.sems, self.to = whole, part, sems, to
        self.me, self.right, self.left = me, lax.rem(me + 1, 4), lax.rem(me + 3, 4)
        self.far = lax.rem(me + 2, 4)

    def copy(self, ref, k, peer):
        return pltpu.make_async_remote_copy(
            src_ref=ref,
            dst_ref=ref,
            send_sem=self.sems.at[0, k],
            recv_sem=self.sems.at[1, k],
            device_id={"seq": self.to(peer)},
            device_id_type=MESH,
        )

    def start(self):
        self.copy(self.whole(self.me), 0, self.right).start()
        self.copy(self.whole(self.me), 1, self.left).start()

    def forward(self):
        self.copy(self.whole(self.left), 0, self.left).wait_recv()
        self.copy(self.part(self.left, 0), 2, self.right).start()
        self.copy(self.whole(self.right), 1, self.right).wait_recv()
        self.copy(self.part(self.right, 1), 3, self.left).start()

    def finish(self):
        self.copy(self.part(self.far, 0), 2, self.left).wait_recv()
        self.copy(self.part(self.far, 1), 3, self.right).wait_recv()

    def wait_send(self):
        self.copy(self.whole(self.me), 0, self.right).wait_send()
        self.copy(self.whole(self.me), 1, self.left).wait_send()
        self.copy(self.part(self.left, 0), 2, self.right).wait_send()
        self.copy(self.part(self.right, 1), 3, self.left).wait_send()


class RingSum:
    def __init__(self, me, to, part, raw, near, sems):
        self.part, self.raw, self.near, self.sems, self.to = part, raw, near, sems, to
        self.me, self.far = me, lax.rem(me + 2, 4)
        self.side = (lax.rem(me + 3, 4), lax.rem(me + 1, 4))

    def copy(self, source, landing, k, peer):
        return pltpu.make_async_remote_copy(
            src_ref=source,
            dst_ref=landing,
            send_sem=self.sems.at[0, k],
            recv_sem=self.sems.at[1, k],
            device_id=self.to(peer),
            device_id_type=MESH,
        )

    def far_copy(self, n):
        return self.copy(self.part(self.far, n), self.raw(n), n, self.side[1 - n])

    def own_copy(self, n):
        peer = self.side[1 - n]
        return self.copy(self.part(peer, 1 - n), self.near(n, 1 - n), 2 + n, peer)

    def sum_copy(self, n):
        peer = self.side[1 - n]
        return self.copy(self.part(peer, n), self.near(n, n), 4 + n, peer)

    def start_far(self):
        for n in range(2):
            self.far_copy(n).start()

    def start_near(self):
        for n in range(2):
            self.own_copy(n).start()

    def middle(self):
        for n in range(2):
            self.copy(self.raw(n), self.raw(n), n, self.side[n]).wait_recv()
            ref = self.part(self.side[1 - n], n)
            ref[...] = (ref[...].astype(F32) + self.raw(n)[...].astype(F32)).astype(BF)
            self.sum_copy(n).start()

    def finish(self):
        halves = []
        for n in range(2):
            for k in range(2):
                ref = self.near(k, n)
                self.copy(ref, ref, 2 + k if n != k else 4 + k, self.side[k]).wait_recv()
            v = self.part(self.me, n)[...].astype(F32)
            halves.append(v + self.near(0, n)[...].astype(F32) + self.near(1, n)[...].astype(F32))
        return halves

    def wait_send(self):
        for n in range(2):
            self.far_copy(n).wait_send()
            self.own_copy(n).wait_send()
            self.sum_copy(n).wait_send()


def mp_copy(source, landing, send, recv, peer):
    return pltpu.make_async_remote_copy(
        src_ref=source,
        dst_ref=landing,
        send_sem=send,
        recv_sem=recv,
        device_id={"mp": peer},
        device_id_type=MESH,
    )


class MpExchange:
    def __init__(self, source, landing, sems):
        self.source, self.landing = source, landing
        self.send, self.recv = sems
        self.me = lax.axis_index("mp")

    def copy(self, d):
        peer = lax.rem(self.me + d, MP)
        return mp_copy(self.source(peer), self.landing(self.me), self.send.at[d], self.recv.at[d], peer)

    def arrival(self, d):
        origin = lax.rem(self.me - d + MP, MP)
        ref = self.landing(origin)
        return mp_copy(ref, ref, self.send.at[d], self.recv.at[d], origin)

    def start(self):
        fori(1, MP, lambda d: self.copy(d).start())

    def wait_recv(self):
        fori(1, MP, lambda d: self.arrival(d).wait_recv())

    def wait_send(self):
        fori(1, MP, lambda d: self.copy(d).wait_send())


def scan_scratch():
    v = pltpu.VMEM
    return dict(
        xs=v((CHUNKS, CHUNK, INNER), BF),
        xt=v((CHUNKS, CHUNK, INNER), BF),
        ed=v((CHUNKS, CHUNK, INNER), BF),
        er=v((CHUNKS, CHUNK, INNER), F32),
        tail=v((CHUNKS, CHUNK, INNER), F32),
        rcol=v((CHUNKS, CHUNK, LANES), F32),
        fresh=v((CHUNKS, STATE, INNER), F32),
        back=v((CHUNKS, STATE, INNER), F32),
        eR=v((CHUNKS, 8, INNER), F32),
        RC=v((8, INNER), F32),
        st=v((SEQ, 4 * PIECE, INNER), BF),
        sx=v((SEQ, 4 * PIECE, INNER), BF),
        sy=v((SEQ, 2 * PIECE, INNER), BF),
        sz=v((SEQ, 2 * PIECE, INNER), BF),
        y=v((CHUNKS, CHUNK, INNER), F32),
        dx=v((CHUNKS, CHUNK, INNER), F32),
        dbc=v((CHUNKS, CHUNK, 2 * STATE), F32),
        dd=v((CHUNKS, CHUNK, LANES), F32),
        gin=v((CHUNKS, STATE, INNER), F32),
        sin=v((STATE, INNER), F32),
    )


def main_scratch():
    v = pltpu.VMEM
    dma = pltpu.SemaphoreType.DMA
    seq_sems = lambda: dma((2,))
    return dict(
        tok3=v((SEQ, WID, DM), BF),
        cot=v((TOK, INNER), BF),
        wa=v((4, 4, SHARD, HALF), BF),
        wb=v((4, 4, SHARD, HALF), BF),
        sw_rx=v((SEQ, 16, LANES), BF),
        sw=v((LANES, DM), BF),
        z=v((TOK, INNER), BF),
        sraw=v((TOK, LANES), F32),
        gate=v((TOK, INNER), F32),
        slope=v((TOK, INNER), F32),
        pay=v((SEQ, ROWS, LANES), BF),
        trx=v((SEQ, ROWS, LANES), BF),
        bpay=v((SEQ, ROWS, LANES), BF),
        brx=v((SEQ, ROWS, LANES), BF),
        tri=v((4, CHUNK, CHUNK), BF),
        lp=v((TOK, LANES), BF),
        bcr=v((2, SEQ, WID, LANES), BF),
        bct=v((2, SEQ, WID, LANES), BF),
        wx=v((DM, 2 * LANES), BF),
        tdb=v((2, CHUNKS, CHUNK, LANES), BF),
        trs=v((MP, CHUNK, LANES), BF),
        tpiece=v((SEQ, COLS, LANES), BF),
        rpiece=v((SEQ, COLS, LANES), BF),
        rdb=v((2, SEQ, WID, LANES), BF),
        rrs=v((MP, SEQ, COLS, LANES), BF),
        dpiece=v((SEQ, COLS, LANES), BF),
        lacc=v((CHUNK, LANES), F32),
        swp=v((16, LANES), BF),
        R=scan_scratch(),
        T=scan_scratch(),
        g=v((TOK, 768), BF),
        tokt=v((DM, TOK), BF),
        gp=v((4, 4, SHARD, 640), BF),
        g_raw=v((2, 2, 2, 32, 640), BF),
        g_near=v((2, 2, 4, 32, 640), BF),
        h_own=v((2, 4, 32, 640), BF),
        h_raw=v((2, 2, 16, 640), BF),
        h_near=v((2, 2, 32, 640), BF),
        z_raw=v((2, 2, CHUNK, LANES), BF),
        z_near=v((2, 2, 2 * CHUNK, LANES), BF),
        gs=v((MP, 16, LANES), BF),
        gs_rx=v((SEQ, 16, LANES), BF),
        ip=v((MP, TOK, LANES), BF),
        prx=v((4, TOK, LANES), BF),
        zs=v((4, TOK, LANES), BF),
        fsh=v((SHARD, LANES), F32),
        frx=v((MP, SHARD, LANES), F32),
        s_local=dma((4,)),
        s_w=dma((4, 2, 4)),
        s_sw=seq_sems(),
        s_pay=seq_sems(),
        s_sr=seq_sems(),
        s_st=seq_sems(),
        s_ur=seq_sems(),
        s_ut=seq_sems(),
        s_back=seq_sems(),
        s_back2=seq_sems(),
        s_gp=dma((4, 2, 6)),
        s_bc=seq_sems(),
        s_bp=seq_sems(),
        s_gs=seq_sems(),
        s_bm=dma((2, MP)),
        s_tr=dma((2, MP)),
        s_rr=dma((2, MP)),
        s_fin=dma((2, MP)),
        s_pair=dma((2, 4, CHUNKS)),
        s_z=dma((2, 2, 6)),
    )


def sems(ref):
    return ref.at[0], ref.at[1]


def head_sum():
    c, h = iota((INNER, LANES), 0), iota((INNER, LANES), 1)
    return jnp.where((h < 8) & ((h & 3) == (c >> 6)), 1.0, 0.0).astype(BF)


def pair_expand(shift):
    k, c = iota((LANES, INNER), 0) - shift, iota((LANES, INNER), 1)
    return jnp.where((k >= 0) & (k < 8) & ((k & 3) == (c >> 6)), 1.0, 0.0).astype(BF)


def pair_merge(shift):
    k, h = iota((LANES, LANES), 0) - shift, iota((LANES, LANES), 1)
    return jnp.where((k >= 0) & (k < 8) & (h < 8) & ((k & 3) == (h & 3)), 1.0, 0.0).astype(BF)


def pair_place(shift):
    k, lane = iota((LANES, LANES), 0), iota((LANES, LANES), 1)
    return jnp.where((k < 8) & (lane == k + shift), 1.0, 0.0).astype(BF)


def wide(load, block, q):
    return jnp.concatenate([load(block, q), load(block + 1, q)], axis=1)


def summary(b, tri, load, pair_of, rate, ratex, q):
    x = wide(load, BX, q).astype(F32)
    dy = wide(load, BY, q).astype(F32)
    pair, shift = pair_of(q)
    dexp = mm(pair, pair_expand(shift))
    logs = (-dexp * ratex).astype(BF)
    rexp = mm(tri, logs)
    b["rcol"][q] = mm(tri, (-mm(pair, pair_merge(shift)) * rate).astype(BF))
    total = jnp.sum(logs.astype(F32), axis=0, keepdims=True)
    er = jnp.exp2(rexp)
    tail = jnp.exp2(jnp.minimum(total - rexp, 0.0))
    xs = (x * dexp).astype(BF)
    xt = (xs.astype(F32) * tail).astype(BF)
    ed = (er * dy).astype(BF)
    b["er"][q] = er
    b["tail"][q] = tail
    b["xs"][q] = xs
    b["xt"][q] = xt
    b["ed"][q] = ed
    b["fresh"][q] = mm_tn(load(BB, q), xt)
    b["back"][q] = mm_tn(load(BC, q), ed)
    rows = jnp.broadcast_to(total, (8, INNER))
    b["eR"][q] = jnp.exp2(rows)
    b["RC"][...] += rows


def pack_states(b):
    e = [b["eR"][q][:1] for q in range(CHUNKS)]
    end = b["fresh"][0]
    for q in range(1, CHUNKS):
        end = end * e[q] + b["fresh"][q]
    first = b["back"][CHUNKS - 1]
    for q in range(CHUNKS - 2, -1, -1):
        first = first * e[q] + b["back"][q]
    rc = b["RC"][...]
    hi = rc.astype(BF).astype(F32)
    logs = jnp.concatenate([hi, rc - hi], axis=0).astype(BF)
    pieces = [v.reshape(SEQ, PIECE, INNER) for v in (end, first)]
    b["st"][:, pl.ds(0, 2 * PIECE), :] = jnp.concatenate(pieces, axis=1).astype(BF)
    for k in range(SEQ):
        b["st"][k, pl.ds(2 * PIECE, 2 * PIECE)] = logs


def chain_states(b):
    own = [b["sx"][k, pl.ds(0, 2 * PIECE)].astype(F32) for k in range(SEQ)]
    logs = [b["sx"][k, pl.ds(2 * PIECE, 2 * PIECE)].astype(F32) for k in range(SEQ)]
    decay = [jnp.exp2(v[:PIECE] + v[PIECE:]) for v in logs]
    state = [jnp.zeros((PIECE, INNER), F32)]
    grad = [jnp.zeros((PIECE, INNER), F32)]
    for k in range(SEQ - 1):
        state.append(state[k] * decay[k] + own[k][:PIECE])
        n = SEQ - 1 - k
        grad.append(grad[k] * decay[n] + own[n][PIECE:])
    for k in range(SEQ):
        b["sy"][k] = jnp.concatenate([state[k], grad[SEQ - 1 - k]], axis=0).astype(BF)


def entering_states(b):
    both = b["sz"][...].astype(F32)
    b["sin"][...] = both[:, :PIECE, :].reshape(STATE, INNER)
    grad = both[:, PIECE:, :].reshape(STATE, INNER)
    for q in range(CHUNKS - 1, -1, -1):
        b["gin"][q] = grad
        if q > 0:
            grad = grad * b["eR"][q][:1] + b["back"][q]


def head_rows(h):
    one = jnp.where((iota((16, INNER), 1) >> 6) == h, 1.0, 0.0).astype(BF)
    return jnp.concatenate([one] * (CHUNK // 16), axis=0)


def inside(b, tri, load, q):
    dy = wide(load, BY, q)
    bmat = load(BB, q)
    cmat = load(BC, q)
    xs = b["xs"][q]
    trif = tri.astype(F32)
    scores = mm_nt(cmat, bmat) * trif
    rcol = b["rcol"][q]
    rrow = rcol.T
    pairs = None
    ms, dys, xss = [], [], []
    for h in range(HEADS):
        decay = jnp.exp2(jnp.minimum(rcol[:, h : h + 1] - rrow[h : h + 1, :], 0.0))
        ms.append((decay * scores).astype(BF))
        mask = head_rows(h)
        dys.append(dy * mask)
        xss.append(xs * mask)
        term = decay * mm_nt(dys[h], xs)
        pairs = term if h == 0 else pairs + term
    dy4 = jnp.concatenate(dys, axis=0)
    y = mm(jnp.concatenate(ms, axis=1), jnp.concatenate(xss, axis=0))
    dxs = mm_tn(jnp.concatenate(ms, axis=0), dy4)
    pairs = (pairs * trif).astype(BF)
    b["y"][q] = y
    b["dx"][q] = dxs
    b["dbc"][q, :, pl.ds(0, STATE)] = mm_tn(pairs, cmat)
    b["dbc"][q, :, pl.ds(STATE, STATE)] = mm(pairs, bmat)


def outside(b, tri, tri_up, load, pair_of, rate, q, put):
    x = wide(load, BX, q).astype(F32)
    dy = wide(load, BY, q).astype(F32)
    bmat = load(BB, q)
    cmat = load(BC, q)
    pair, shift = pair_of(q)
    dexp = mm(pair, pair_expand(shift))
    xs = b["xs"][q].astype(F32)
    state = b["sin"][...]
    grad = b["gin"][q]
    state_b, grad_b = state.astype(BF), grad.astype(BF)
    sums = head_sum()
    y = b["y"][q] + b["er"][q] * mm(cmat, state_b)
    inner = b["dx"][q]
    outer = b["tail"][q] * mm(bmat, grad_b)
    dxs = inner + outer
    db = b["dbc"][q, :, pl.ds(0, STATE)] + mm_nt(b["xt"][q], grad_b)
    dc = b["dbc"][q, :, pl.ds(STATE, STATE)] + mm_nt(b["ed"][q], state_b)

    def by_head(v):
        return mm(v.astype(BF), sums)

    late = by_head(dy * y - xs * inner).astype(BF)
    early = by_head(xs * outer).astype(BF)
    decayed = b["eR"][q][:1] * state
    across = jnp.sum(decayed * grad, axis=0, keepdims=True)
    across = mm(jnp.broadcast_to(across, (16, INNER)).astype(BF), sums)[:1]
    dl = mm(tri_up, late) + mm(tri, early) - early.astype(F32) + across
    ddelta = by_head(x * dxs) - rate * dl
    b["sin"][...] = decayed + b["fresh"][q]
    put(q, y, dexp * dxs, db, dc, ddelta)


def kernel(tok_hbm, cot_hbm, pm, ps, pt, bias_s, rate_s, skip_s, gated_o, ig_o, gm_o, gsh_o, gst_o, m):
    seq, mp = lax.axis_index("seq"), lax.axis_index("mp")
    core = lax.rem(mp, 2)
    chip = mp // 2
    partner = mp + 1 - 2 * core
    plane, line = seq // 4, lax.rem(seq, 4)
    low = lax.rem(seq, 2)

    load_tok = pltpu.make_async_copy(tok_hbm, m["tok3"], m["s_local"].at[0])
    load_cot = pltpu.make_async_copy(cot_hbm, m["cot"], m["s_local"].at[1])
    load_tok.start()
    load_cot.start()

    barrier = pltpu.get_barrier_semaphore()

    def greet_seq(d):
        pl.semaphore_signal(
            barrier, inc=1, device_id={"seq": lax.rem(seq + d, SEQ)}, device_id_type=MESH
        )

    def greet_mp(d):
        pl.semaphore_signal(barrier, inc=1, device_id={"mp": lax.rem(mp + d, MP)}, device_id_type=MESH)

    fori(1, SEQ, greet_seq)
    fori(1, MP, greet_mp)

    wa, wb, swp = m["wa"], m["wb"], m["swp"]
    wa[plane, line, :, pl.ds(0, 256)] = pm[:, 0, :]
    wb[plane, line, :, pl.ds(0, 256)] = pm[:, 1, :]
    wa[plane, line, :, pl.ds(256, 128)] = ps[:, 0, :]
    wb[plane, line, :, pl.ds(256, 128)] = ps[:, 1, :]
    at, lane = iota((SHARD, LANES), 0), iota((SHARD, LANES), 1)
    place = jnp.where(lane == at + SHARD * low, 1.0, 0.0).astype(BF)
    shifted = mm(pt[...], place).astype(BF)
    swp[...] = jnp.concatenate([shifted, shifted, jnp.zeros((8, LANES), BF)], axis=0)
    pl.semaphore_wait(barrier, SEQ + MP - 2)

    most = pl.ds(0, SEQ - 1)

    def along_x(k):
        return 4 * k + line

    def along_y(k):
        return 4 * plane + k

    half = SHARD // 2
    ring_a1 = Ring(plane, along_x, lambda k: wa.at[k, line], lambda k, n: wa.at[k, line, pl.ds(half * n, half)], m["s_w"].at[0])
    ring_b1 = Ring(line, along_y, lambda k: wb.at[plane, k], lambda k, n: wb.at[plane, k, pl.ds(half * n, half)], m["s_w"].at[1])
    ring_a2 = Ring(line, along_y, lambda k: wa.at[:, k], lambda k, n: wa.at[pl.ds(2 * n, 2), k], m["s_w"].at[2])
    ring_b2 = Ring(plane, along_x, lambda k: wb.at[k], lambda k, n: wb.at[k, pl.ds(2 * n, 2)], m["s_w"].at[3])
    rings = (ring_a1, ring_b1, ring_a2, ring_b2)
    ring_a1.start()
    ring_b1.start()
    send_sw = SeqExchange(lambda p: swp, lambda k: m["sw_rx"].at[k], m["sw_rx"].at[most], sems(m["s_sw"]))
    send_sw.start()
    m["sw_rx"][seq] = swp[...]

    def flip(q):
        m["tokt"][:, pl.ds(q * CHUNK, CHUNK)] = m["tok3"][pl.ds(4 * q, 4)].reshape(CHUNK, DM).T

    load_tok.wait()
    flip(0)
    ring_a1.forward()
    ring_b1.forward()
    ring_a1.finish()
    ring_a2.start()
    ring_b1.finish()
    ring_b2.start()

    i, j = iota((CHUNK, CHUNK), 0), iota((CHUNK, CHUNK), 1)
    m["tri"][0] = jnp.where(i >= j, 1.0, 0.0).astype(BF)
    it, jt = (i & 15) * 16 + (i >> 4), (j & 15) * 16 + (j >> 4)
    m["tri"][1] = jnp.where(it >= jt, 1.0, 0.0).astype(BF)
    m["tri"][2] = jnp.where(i <= j, 1.0, 0.0).astype(BF)
    m["tri"][3] = jnp.where(it <= jt, 1.0, 0.0).astype(BF)
    m["sw"][...] = jnp.zeros((LANES, DM), BF)
    m["R"]["RC"][...] = jnp.zeros((8, INNER), F32)
    m["T"]["RC"][...] = jnp.zeros((8, INNER), F32)
    m["lacc"][...] = jnp.zeros((CHUNK, LANES), F32)

    head_l = iota((1, LANES), 1)
    head_c = iota((1, INNER), 1) >> 6

    def lanes_of(value):
        v = jnp.zeros((1, LANES), F32)
        for h in range(HEADS):
            v = jnp.where((head_l < 8) & ((head_l & 3) == h), value(h), v)
        return v

    def features_of(value):
        v = jnp.zeros((1, INNER), F32)
        for h in range(HEADS):
            v = jnp.where(head_c == h, value(h), v)
        return v

    bias = lanes_of(lambda h: bias_s[h])
    rate_r, rate_t = lanes_of(lambda h: rate_s[0, h]), lanes_of(lambda h: rate_s[1, h])
    ratex_r = features_of(lambda h: rate_s[0, h]) * LOG2E
    ratex_t = features_of(lambda h: rate_s[1, h]) * LOG2E
    skip = features_of(lambda h: skip_s[h])

    load_cot.wait()
    flip(1)
    ring_a2.forward()
    ring_b2.forward()
    flip(2)
    flip(3)
    ring_a2.finish()
    ring_b2.finish()
    send_sw.wait_recv()
    for k in range(SEQ // 2):
        m["sw"][pl.ds(0, 16), pl.ds(k * LANES, LANES)] = m["sw_rx"][2 * k] + m["sw_rx"][2 * k + 1]

    def rows_of(q):
        return pl.ds(pl.multiple_of(q * CHUNK, CHUNK), CHUNK)

    def columns(ref, at, width):
        return ref[:, :, :, pl.ds(at, width)].reshape(DM, width)

    def rest(v):
        return v.reshape(4, WID, LANES)

    send_pay = SeqExchange(lambda p: m["pay"].at[p], lambda k: m["trx"].at[k], m["trx"].at[most], sems(m["s_pay"]))
    quarter = pl.ds(pl.multiple_of(chip * COLS, COLS), COLS)
    bcr, bct = m["bcr"], m["bct"]
    send_bc = SeqExchange(
        lambda p: bcr.at[core, p, quarter],
        lambda k: bct.at[core, k, quarter],
        bct.at[core, most, quarter],
        sems(m["s_bc"]),
    )

    def piece_of(ref, k):
        return ref.at[lax.rem(k, 2), :, pl.ds(pl.multiple_of(k // 2 * COLS, COLS), COLS)]

    send_bm = MpExchange(lambda p: piece_of(bct, mp), lambda k: piece_of(bct, k), sems(m["s_bm"]))
    m["wx"][:, pl.ds(0, LANES)] = jnp.where(core == 0, columns(wa, 256, 128), columns(wb, 256, 128))
    m["wx"][:, pl.ds(LANES, LANES)] = m["sw"][...].T

    def start_four(exchange, q):
        def one(n):
            d = lax.rem(4 * q + n - seq + SEQ, SEQ)

            @pl.when(d != 0)
            def _():
                exchange.copy(d).start()

        fori(0, 4, one)

    def far_first(n):
        step = jnp.where(n == 0, 2, jnp.where(n == 3, 0, 2 * n - 1))
        return lax.rem(plane + step, 4)

    def project_shared(n):
        q = far_first(n)
        u = m["tok3"][pl.ds(4 * q, 4)].reshape(CHUNK, DM)
        w = jnp.concatenate([columns(wa, 256, 128), columns(wb, 256, 128)], axis=1)
        v = mm(u, w).astype(BF)
        bcr[0, pl.ds(4 * q, 4)] = rest(v[:, :LANES])
        bcr[1, pl.ds(4 * q, 4)] = rest(v[:, LANES:])
        start_four(send_bc, q)

    def project(n):
        q = far_first(n)
        rows = rows_of(q)
        u = m["tok3"][pl.ds(4 * q, 4)].reshape(CHUNK, DM)
        four = pl.ds(4 * q, 4)

        def put(block, v):
            v = v.astype(BF)
            for k in range(v.shape[1] // LANES):
                m["pay"][four, pl.ds((block + k) * WID, WID), :] = rest(v[:, k * LANES : (k + 1) * LANES])

        z = mm(u, columns(wb, 0, 256)).astype(BF)
        m["z"][rows, :] = z
        zf = z.astype(F32)
        gate = zf * jax.nn.sigmoid(zf)
        put(BY, m["cot"][rows, :].astype(F32) * gate)
        put(BX, mm(u, columns(wa, 0, 256)))
        raw = mm(u, m["wx"][:, pl.ds(LANES, LANES)]) + bias
        m["sraw"][rows, :] = raw
        pair = as_pair(jnp.maximum(raw, 0.0) + jnp.log1p(jnp.exp(-jnp.abs(raw))))
        m["lp"][rows, :] = pair
        folded = jnp.zeros((64, LANES), F32)
        for g in range(4):
            part = rest(pair)[:, g * COLS : (g + 1) * COLS, :].reshape(64, LANES)
            folded += mm(part, pair_place(8 * g))
        m["pay"][four, pl.ds(ROWS_L, COLS), :] = folded.astype(BF).reshape(4, COLS, LANES)
        start_four(send_pay, q)

    fori(0, CHUNKS, project_shared)
    fori(0, CHUNKS, project)
    m["trx"][seq] = m["pay"][seq]
    bct[core, seq, quarter] = bcr[core, seq, quarter]

    def load_r(block, q):
        if block >= BB:
            return bcr[block - BB, pl.ds(4 * q, 4)].reshape(CHUNK, LANES)
        return m["pay"][pl.ds(4 * q, 4), pl.ds(block * WID, WID), :].reshape(CHUNK, LANES)

    def pair_r(q):
        return m["lp"][rows_of(q), :], 0

    def cols_of(block, q):
        return pl.ds(pl.multiple_of(block * WID + q * COLS, COLS), COLS)

    def load_t(block, q):
        if block >= BB:
            return bct[block - BB, :, pl.ds(q * COLS, COLS), :].reshape(CHUNK, LANES)
        return m["trx"][:, cols_of(block, q), :].reshape(CHUNK, LANES)

    def pair_t(q):
        return m["trx"][:, pl.ds(ROWS_L, COLS), :].reshape(CHUNK, LANES), 8 * q

    def pieces_exchange(source, landing, sem):
        return SeqExchange(lambda p: source.at[p], lambda k: landing.at[k], landing.at[most], sems(sem))

    r, t = m["R"], m["T"]
    tri_r, tri_t, up_r, up_t = (m["tri"].at[k] for k in range(4))

    def chunks(low, high, step):
        for q in range(low, high):
            step(q)


    def start_pieces(b, sem):
        e = pieces_exchange(b["st"], b["sx"], sem)
        e.start()
        b["sx"][seq] = b["st"][seq]
        return e

    def start_entering(b, sem):
        chain_states(b)
        e = pieces_exchange(b["sy"], b["sz"], sem)
        e.start()
        b["sz"][seq] = b["sy"][seq]
        return e

    chunks(0, CHUNKS, lambda q: summary(r, tri_r[...], load_r, pair_r, rate_r * LOG2E, ratex_r, q))
    pack_states(r)
    send_bc.wait_recv()
    send_bm.start()
    chunks(0, 2, lambda q: inside(r, tri_r[...], load_r, q))
    send_sw.wait_send()
    for e in rings:
        e.wait_send()

    send_pay.wait_recv()
    send_sr = start_pieces(r, m["s_sr"])
    send_bm.wait_recv()
    chunks(0, CHUNKS, lambda q: summary(t, tri_t[...], load_t, pair_t, rate_t * LOG2E, ratex_t, q))
    pack_states(t)
    send_st = start_pieces(t, m["s_st"])
    send_sr.wait_recv()
    send_ur = start_entering(r, m["s_ur"])
    chunks(0, 2, lambda q: inside(t, tri_t[...], load_t, q))
    chunks(2, 3, lambda q: inside(r, tri_r[...], load_r, q))
    send_st.wait_recv()
    send_ut = start_entering(t, m["s_ut"])
    chunks(2, CHUNKS, lambda q: inside(t, tri_t[...], load_t, q))
    chunks(3, CHUNKS, lambda q: inside(r, tri_r[...], load_r, q))
    send_ut.wait_recv()
    entering_states(t)

    def put_t(q, y, dx, db, dc, dd):
        def put(block, v):
            v = v.astype(BF)
            for k in range(v.shape[1] // LANES):
                part = v[:, k * LANES : (k + 1) * LANES]
                at = 128 * (q // 2) + 32 * (block + k) + COLS * (q % 2)
                m["bpay"][:, pl.ds(at, COLS), :] = part.reshape(SEQ, COLS, LANES)

        put(BX, y)
        put(BY, dx)
        m["tdb"][0, q] = db.astype(BF)
        m["tdb"][1, q] = dc.astype(BF)
        for n in range(2):
            d = lax.rem(2 * q + n - mp + MP, MP)

            @pl.when(d != 0)
            def _():
                send_tr.copy(d).start()

        m["lacc"][...] += mm(as_pair(dd), pair_place(8 * q))

    def half_back(at, count, sem):
        rows = pl.ds(at, count)
        return SeqExchange(
            lambda p: m["bpay"].at[p, rows], lambda k: m["brx"].at[k, rows], m["brx"].at[most, rows], sems(sem)
        )

    send_back = half_back(0, 128, m["s_back"])
    send_back2 = half_back(128, 144, m["s_back2"])
    send_tr = MpExchange(
        lambda p: m["tdb"].at[lax.rem(p, 2), p // 2], lambda k: m["trs"].at[k], sems(m["s_tr"])
    )
    send_bp = SeqExchange(lambda p: m["tpiece"].at[p], lambda k: m["rpiece"].at[k], m["rpiece"].at[most], sems(m["s_bp"]))
    send_rr = MpExchange(lambda p: piece_of(m["rdb"], p), lambda k: m["rrs"].at[k], sems(m["s_rr"]))

    def group_total(ref):
        v = ref[0].astype(F32)
        for k in range(1, MP):
            v += ref[k].astype(F32)
        return v

    chunks(0, 2, lambda q: outside(t, tri_t[...], up_t[...], load_t, pair_t, rate_t, q, put_t))
    send_back.start()
    chunks(2, 4, lambda q: outside(t, tri_t[...], up_t[...], load_t, pair_t, rate_t, q, put_t))
    m["bpay"][:, pl.ds(ROWS_L, COLS), :] = m["lacc"][...].astype(BF).reshape(SEQ, COLS, LANES)
    send_back2.start()
    m["brx"][seq] = m["bpay"][seq]
    m["trs"][mp] = m["tdb"][core, chip]

    send_ur.wait_recv()
    entering_states(r)

    def put_r(q, y, dx, db, dc, dd):
        rows = rows_of(q)
        r["y"][q] = y + skip * wide(load_r, BX, q).astype(F32)
        r["dx"][q] = dx + skip * wide(load_r, BY, q).astype(F32)
        z = m["z"][rows, :].astype(F32)
        sigma = jax.nn.sigmoid(z)
        m["gate"][rows, :] = z * sigma
        m["slope"][rows, :] = m["cot"][rows, :].astype(F32) * sigma * (1.0 + z * (1.0 - sigma))
        m["sraw"][rows, :] = jax.nn.sigmoid(m["sraw"][rows, :])
        m["rdb"][0, pl.ds(4 * q, 4)] = rest(db.astype(BF))
        m["rdb"][1, pl.ds(4 * q, 4)] = rest(dc.astype(BF))
        r["dd"][q] = dd

    def outside_r(q):
        outside(r, tri_r[...], up_r[...], load_r, pair_r, rate_r, q, put_r)

    chunks(0, 1, outside_r)
    send_tr.wait_recv()
    m["tpiece"][...] = group_total(m["trs"]).astype(BF).reshape(SEQ, COLS, LANES)
    send_bp.start()
    m["rpiece"][seq] = m["tpiece"][seq]
    chunks(1, CHUNKS, outside_r)
    send_rr.start()
    m["rrs"][mp] = m["rdb"][core, :, quarter]
    for e in (send_pay, send_bc, send_bm, send_sr, send_ur, send_st, send_ut):
        e.wait_send()
    send_back.wait_recv()
    send_back2.wait_recv()
    send_bp.wait_recv()
    send_rr.wait_recv()
    m["dpiece"][...] = (group_total(m["rrs"]) + m["rpiece"][...].astype(F32)).astype(BF)

    def back(block, q):
        parts = [m["brx"][pl.ds(4 * q, 4), pl.ds(128 * n + 32 * block, 32), :] for n in range(2)]
        return jnp.concatenate(parts, axis=1).reshape(CHUNK, LANES)

    def combine(q):
        rows = rows_of(q)
        y = r["y"][q] + wide(back, BX, q).astype(F32)
        gated_o[rows, :] = (y * m["gate"][rows, :]).astype(BF)
        m["g"][rows, pl.ds(256, 256)] = (y * m["slope"][rows, :]).astype(BF)
        m["g"][rows, pl.ds(0, 256)] = (r["dx"][q] + wide(back, BY, q).astype(F32)).astype(BF)
        folded = m["brx"][pl.ds(4 * q, 4), pl.ds(ROWS_L, COLS), :].reshape(64, LANES)
        parts = [mm(folded, pair_merge(8 * g)).reshape(4, COLS, LANES) for g in range(4)]
        dd = r["dd"][q] + jnp.concatenate(parts, axis=1).reshape(CHUNK, LANES)
        dstep = dd * m["sraw"][rows, :]
        m["g"][rows, pl.ds(640, LANES)] = jnp.where(iota((CHUNK, LANES), 1) < HEADS, dstep, 0.0).astype(BF)

    def pair_copy(k, q):
        rows = rows_of(q)
        return mp_copy(
            m["ip"].at[2 * k + 1 - core, rows],
            m["prx"].at[k, rows],
            m["s_pair"].at[0, k, q],
            m["s_pair"].at[1, k, q],
            partner,
        )

    def z_ring(n):
        def part(k, h):
            return m["zs"].at[k, pl.ds(CHUNK * (2 * n + h), CHUNK)]

        return RingSum(
            chip,
            lambda k: {"mp": 2 * k + core},
            part,
            lambda h: m["z_raw"].at[n, h],
            lambda side, h: m["z_near"].at[n, side, pl.ds(CHUNK * h, CHUNK)],
            m["s_z"].at[n],
        )

    z_rings = [z_ring(0), z_ring(1)]

    def pair_sum(k, q):
        rows = rows_of(q)
        pair_copy(k, q).wait_recv()
        return (m["ip"][2 * k + core, rows, :].astype(F32) + m["prx"][k, rows, :].astype(F32)).astype(BF)

    def pass_on(q):
        for k in range(4):
            m["zs"][k, rows_of(q), :] = pair_sum(k, q)

    def z_start(n):
        z_rings[n].start_far()
        z_rings[n].start_near()

    def z_finish(n):
        for h, v in enumerate(z_rings[n].finish()):
            ig_o[rows_of(2 * n + h), :] = v.astype(BF)

    def combine_all(q):
        combine(q)
        rows = rows_of(q)
        piece = m["dpiece"][pl.ds(4 * q, 4)]
        here = (iota((4, WID, LANES), 1) >> 4) == chip
        piece = jnp.where(here, jnp.concatenate([piece] * 4, axis=1), jnp.zeros((), BF)).reshape(CHUNK, LANES)
        m["g"][rows, pl.ds(512, LANES)] = piece

    def input_part(q):
        rows = rows_of(q)
        g = m["g"][rows, :]
        for c in range(4):
            cols = pl.ds(c * 256, 256)
            v = mm_nt(g[:, :256], wa[c, :, :, pl.ds(0, 256)].reshape(256, 256))
            v += mm_nt(g[:, 256:512], wb[c, :, :, pl.ds(0, 256)].reshape(256, 256))
            v += mm_nt(g[:, 512:], m["wx"][cols, :])
            v = v.astype(BF)
            m["ip"][2 * c, rows, :] = v[:, :LANES]
            m["ip"][2 * c + 1, rows, :] = v[:, LANES:]
        fori(0, 4, lambda k: pair_copy(k, q).start())

    chunks(0, CHUNKS, combine_all)

    def g_ring(n):
        rows = pl.ds(32 * n, 32)

        def part(k, h):
            two = pl.ds(2 * h, 2)
            return m["gp"].at[k, two, rows] if n == 0 else m["gp"].at[two, k, rows]

        return RingSum(
            plane if n == 0 else line,
            lambda k: {"seq": along_x(k) if n == 0 else along_y(k)},
            part,
            lambda h: m["g_raw"].at[n, h],
            lambda side, h: m["g_near"].at[n, side, pl.ds(2 * h, 2)],
            m["s_gp"].at[n],
        )

    def h_ring(n):
        return RingSum(
            line if n == 0 else plane,
            lambda k: {"seq": along_y(k) if n == 0 else along_x(k)},
            lambda k, h: m["h_own"].at[n, k, pl.ds(16 * h, 16)],
            lambda h: m["h_raw"].at[n, h],
            lambda side, h: m["h_near"].at[n, side, pl.ds(16 * h, 16)],
            m["s_gp"].at[2 + n],
        )

    g_rings, h_rings = [g_ring(0), g_ring(1)], [h_ring(0), h_ring(1)]
    send_gs = SeqExchange(lambda p: m["gs"].at[p // 2], lambda k: m["gs_rx"].at[k], m["gs_rx"].at[most], sems(m["s_gs"]))

    def grads(n):
        k = lax.rem(plane + n, 4)
        cols = rows_of(k)
        v = mm(m["tokt"][cols, :], m["g"][...])
        m["gp"][k] = v[:, :640].astype(BF).reshape(4, SHARD, 640)
        gs = v[:, 640:].T[:16].astype(BF)
        m["gs"][2 * k] = gs[:, :LANES]
        m["gs"][2 * k + 1] = gs[:, LANES:]
        start_four(send_gs, k)

    grads(2)
    g_rings[0].start_far()
    grads(1)
    grads(3)
    g_rings[0].start_near()
    grads(0)
    g_rings[1].start_far()
    g_rings[1].start_near()
    m["gs_rx"][seq] = m["gs"][seq // 2]
    input_part(0)
    input_part(1)
    g_rings[0].middle()
    g_rings[1].middle()
    input_part(2)
    pass_on(0)
    pass_on(1)
    z_start(0)
    input_part(3)
    for e in (send_back, send_back2, send_tr, send_bp, send_rr, send_gs):
        e.wait_send()
    pass_on(2)
    pass_on(3)
    z_start(1)

    def g_next(n):
        for h, v in enumerate(g_rings[n].finish()):
            m["h_own"][n, pl.ds(2 * h, 2)] = v.astype(BF).reshape(2, 32, 640)
        h_rings[n].start_far()
        h_rings[n].start_near()

    g_next(0)
    g_next(1)
    z_rings[0].middle()
    h_rings[0].middle()
    h_rings[1].middle()
    z_rings[1].middle()

    def total_of(ref):
        v = ref[0].astype(F32)
        for k in range(1, SEQ):
            v += ref[k].astype(F32)
        return v

    main = jnp.concatenate(h_rings[0].finish() + h_rings[1].finish(), axis=0)
    m["fsh"][...] = main[:, 512:]
    send_fin = MpExchange(lambda p: m["fsh"], lambda k: m["frx"].at[k], sems(m["s_fin"]))
    send_fin.start()
    m["frx"][mp] = main[:, 512:]
    gm_o[:, 0, :] = main[:, :INNER]
    gm_o[:, 1, :] = main[:, INNER : 2 * INNER]
    send_gs.wait_recv()
    step = total_of(m["gs_rx"])
    gst_o[...] = jnp.where(low == 0, step[:HEADS, :SHARD], step[:HEADS, SHARD:])
    z_finish(0)
    z_finish(1)
    send_fin.wait_recv()
    for n in range(2):
        gsh_o[:, n, :] = m["frx"][n] + m["frx"][2 + n] + m["frx"][4 + n] + m["frx"][6 + n]

    sent = [send_fin] + z_rings + g_rings + h_rings
    for e in sent:
        e.wait_send()
    for q in range(CHUNKS):
        fori(0, 4, lambda k: pair_copy(k, q).wait_send())


def hand_over(*refs):
    n = len(refs) // 2
    for k in range(n):
        refs[n + k][...] = refs[k][...]


def body(tokens, proj_main, proj_shared, proj_step, step_bias, decay_rate, skip_gain, cotangent):
    vm = pl.BlockSpec(memory_space=pltpu.VMEM)
    sm = pl.BlockSpec(memory_space=pltpu.SMEM)
    hbm = pl.BlockSpec(memory_space=pl.ANY)
    shapes = (
        jax.ShapeDtypeStruct((TOK, INNER), BF),
        jax.ShapeDtypeStruct((TOK, LANES), BF),
        jax.ShapeDtypeStruct((SHARD, 2, INNER), F32),
        jax.ShapeDtypeStruct((SHARD, 2, STATE), F32),
        jax.ShapeDtypeStruct((HEADS, SHARD), F32),
    )
    results = pl.pallas_call(
        kernel,
        out_shape=shapes,
        in_specs=[hbm, hbm, vm, vm, vm, sm, sm, sm],
        out_specs=(vm,) * 5,
        scratch_shapes=[main_scratch()],
        compiler_params=pltpu.CompilerParams(
            collective_id=0, has_side_effects=True, vmem_limit_bytes=62 * 1024 * 1024
        ),
    )(
        tokens.reshape(SEQ, WID, DM),
        cotangent.reshape(TOK, INNER),
        proj_main,
        proj_shared,
        proj_step.T,
        step_bias,
        decay_rate,
        skip_gain,
    )
    gated, ig, gm, gsh, gst = pl.pallas_call(
        hand_over,
        out_shape=shapes,
        in_specs=[vm] * 5,
        out_specs=(vm,) * 5,
    )(*results)
    return (
        gated.reshape(1, 16, WID, INNER),
        ig.reshape(1, 16, WID, LANES),
        gm,
        gsh,
        gst.T,
    )


def solution(mesh):
    placed = (
        P("seq", None, None, None),
        P("seq", None, "mp"),
        P("seq", None, None),
        P("seq", "mp"),
        P("mp"),
        P(None, "mp"),
        P("mp"),
        P("seq", None, None, "mp"),
    )
    return jax.shard_map(
        body,
        mesh=mesh,
        in_specs=placed,
        out_specs=(
            P("seq", None, None, "mp"),
            P("seq", None, None, "mp"),
            P("seq", None, "mp"),
            P("seq", None, None),
            P("seq", "mp"),
        ),
        check_vma=False,
    )
```

```python
import jax
import jax.numpy as jnp
from jax import lax
from jax.experimental import pallas as pl
from jax.experimental.pallas import tpu as pltpu
from jax.sharding import PartitionSpec as P

MESH = pl.DeviceIdType.MESH
BF = jnp.bfloat16
F32 = jnp.float32

SEQ = 16
MP = 8
TOK = 1024
WID = 64
DM = 1024
INNER = 256
HEADS = 4
STATE = 128
LANES = 128
CHUNK = 256
CHUNKS = TOK // CHUNK
COLS = CHUNK // SEQ
SHARD = DM // SEQ
BX, BY, BB, BC, ROWS_L, ROWS = 0, 2, 4, 5, 256, 272
PIECE = STATE // SEQ
HALF = 3 * LANES
LOG2E = 1.4426950408889634


def iota(shape, axis):
    return lax.broadcasted_iota(jnp.int32, shape, axis)


def mm(a, b):
    return lax.dot_general(a, b, (((1,), (0,)), ((), ())), preferred_element_type=F32)


def mm_nt(a, b):
    return lax.dot_general(a, b, (((1,), (1,)), ((), ())), preferred_element_type=F32)


def mm_tn(a, b):
    return lax.dot_general(a, b, (((0,), (0,)), ((), ())), preferred_element_type=F32)


def halves(v):
    hi = v.astype(BF)
    return hi, (v - hi.astype(F32)).astype(BF)


def as_pair(v):
    lane = iota(v.shape, 1)
    hi = v.astype(BF).astype(F32)
    return jnp.where(lane < 4, hi, jnp.where(lane < 8, v - hi, 0.0)).astype(BF)


def fori(low, high, step):
    def run(i, carry):
        step(i)
        return carry

    lax.fori_loop(low, high, run, 0)


class SeqExchange:
    def __init__(self, source, landing, many, sems):
        self.source, self.landing, self.many = source, landing, many
        self.send, self.recv = sems
        self.me = lax.axis_index("seq")

    def copy(self, d):
        peer = lax.rem(self.me + d, SEQ)
        return pltpu.make_async_remote_copy(
            src_ref=self.source(peer),
            dst_ref=self.landing(self.me),
            send_sem=self.send,
            recv_sem=self.recv,
            device_id={"seq": peer},
            device_id_type=MESH,
        )

    def all(self):
        return pltpu.make_async_remote_copy(
            src_ref=self.many,
            dst_ref=self.many,
            send_sem=self.send,
            recv_sem=self.recv,
            device_id={"seq": lax.rem(self.me + 1, SEQ)},
            device_id_type=MESH,
        )

    def start(self):
        def one(i):
            step = i // 2
            self.copy(SEQ // 2 + jnp.where(lax.rem(i, 2) == 0, step, -step)).start()

        fori(1, SEQ, one)

    def wait_recv(self):
        self.all().wait_recv()

    def wait_send(self):
        self.all().wait_send()


class Ring:
    def __init__(self, me, to, whole, part, sems):
        self.whole, self.part, self.sems, self.to = whole, part, sems, to
        self.me, self.right, self.left = me, lax.rem(me + 1, 4), lax.rem(me + 3, 4)
        self.far = lax.rem(me + 2, 4)

    def copy(self, ref, k, peer):
        return pltpu.make_async_remote_copy(
            src_ref=ref,
            dst_ref=ref,
            send_sem=self.sems.at[0, k],
            recv_sem=self.sems.at[1, k],
            device_id={"seq": self.to(peer)},
            device_id_type=MESH,
        )

    def start(self):
        self.copy(self.whole(self.me), 0, self.right).start()
        self.copy(self.whole(self.me), 1, self.left).start()

    def forward(self):
        self.copy(self.whole(self.left), 0, self.left).wait_recv()
        self.copy(self.part(self.left, 0), 2, self.right).start()
        self.copy(self.whole(self.right), 1, self.right).wait_recv()
        self.copy(self.part(self.right, 1), 3, self.left).start()

    def finish(self):
        self.copy(self.part(self.far, 0), 2, self.left).wait_recv()
        self.copy(self.part(self.far, 1), 3, self.right).wait_recv()

    def wait_send(self):
        self.copy(self.whole(self.me), 0, self.right).wait_send()
        self.copy(self.whole(self.me), 1, self.left).wait_send()
        self.copy(self.part(self.left, 0), 2, self.right).wait_send()
        self.copy(self.part(self.right, 1), 3, self.left).wait_send()


class RingSum:
    def __init__(self, me, to, part, raw, near, sems):
        self.part, self.raw, self.near, self.sems, self.to = part, raw, near, sems, to
        self.me, self.far = me, lax.rem(me + 2, 4)
        self.side = (lax.rem(me + 3, 4), lax.rem(me + 1, 4))

    def copy(self, source, landing, k, peer):
        return pltpu.make_async_remote_copy(
            src_ref=source,
            dst_ref=landing,
            send_sem=self.sems.at[0, k],
            recv_sem=self.sems.at[1, k],
            device_id=self.to(peer),
            device_id_type=MESH,
        )

    def far_copy(self, n):
        return self.copy(self.part(self.far, n), self.raw(n), n, self.side[1 - n])

    def own_copy(self, n):
        peer = self.side[1 - n]
        return self.copy(self.part(peer, 1 - n), self.near(n, 1 - n), 2 + n, peer)

    def sum_copy(self, n):
        peer = self.side[1 - n]
        return self.copy(self.part(peer, n), self.near(n, n), 4 + n, peer)

    def start_far(self):
        for n in range(2):
            self.far_copy(n).start()

    def start_near(self):
        for n in range(2):
            self.own_copy(n).start()

    def middle(self):
        for n in range(2):
            self.copy(self.raw(n), self.raw(n), n, self.side[n]).wait_recv()
            ref = self.part(self.side[1 - n], n)
            ref[...] = (ref[...].astype(F32) + self.raw(n)[...].astype(F32)).astype(BF)
            self.sum_copy(n).start()

    def finish(self):
        halves = []
        for n in range(2):
            for k in range(2):
                ref = self.near(k, n)
                self.copy(ref, ref, 2 + k if n != k else 4 + k, self.side[k]).wait_recv()
            v = self.part(self.me, n)[...].astype(F32)
            halves.append(v + self.near(0, n)[...].astype(F32) + self.near(1, n)[...].astype(F32))
        return halves

    def wait_send(self):
        for n in range(2):
            self.far_copy(n).wait_send()
            self.own_copy(n).wait_send()
            self.sum_copy(n).wait_send()


def mp_copy(source, landing, send, recv, peer):
    return pltpu.make_async_remote_copy(
        src_ref=source,
        dst_ref=landing,
        send_sem=send,
        recv_sem=recv,
        device_id={"mp": peer},
        device_id_type=MESH,
    )


class MpExchange:
    def __init__(self, source, landing, sems):
        self.source, self.landing = source, landing
        self.send, self.recv = sems
        self.me = lax.axis_index("mp")

    def copy(self, d):
        peer = lax.rem(self.me + d, MP)
        return mp_copy(self.source(peer), self.landing(self.me), self.send.at[d], self.recv.at[d], peer)

    def arrival(self, d):
        origin = lax.rem(self.me - d + MP, MP)
        ref = self.landing(origin)
        return mp_copy(ref, ref, self.send.at[d], self.recv.at[d], origin)

    def start(self):
        fori(1, MP, lambda d: self.copy(d).start())

    def wait_recv(self):
        fori(1, MP, lambda d: self.arrival(d).wait_recv())

    def wait_send(self):
        fori(1, MP, lambda d: self.copy(d).wait_send())


def scan_scratch():
    v = pltpu.VMEM
    return dict(
        xs=v((CHUNKS, CHUNK, INNER), BF),
        xt=v((CHUNKS, CHUNK, INNER), BF),
        ed=v((CHUNKS, CHUNK, INNER), BF),
        er=v((CHUNKS, CHUNK, INNER), F32),
        tail=v((CHUNKS, CHUNK, INNER), F32),
        rcol=v((CHUNKS, CHUNK, LANES), F32),
        fresh=v((CHUNKS, STATE, INNER), F32),
        back=v((CHUNKS, STATE, INNER), F32),
        eR=v((CHUNKS, 8, INNER), F32),
        RC=v((8, INNER), F32),
        st=v((SEQ, 4 * PIECE, INNER), BF),
        sx=v((SEQ, 4 * PIECE, INNER), BF),
        sy=v((SEQ, 2 * PIECE, INNER), BF),
        sz=v((SEQ, 2 * PIECE, INNER), BF),
        y=v((CHUNKS, CHUNK, INNER), F32),
        dx=v((CHUNKS, CHUNK, INNER), F32),
        dbc=v((CHUNKS, CHUNK, 2 * STATE), F32),
        dd=v((CHUNKS, CHUNK, LANES), F32),
        gin=v((CHUNKS, STATE, INNER), F32),
        sin=v((STATE, INNER), F32),
    )


def main_scratch():
    v = pltpu.VMEM
    dma = pltpu.SemaphoreType.DMA
    seq_sems = lambda: dma((2,))
    return dict(
        tok3=v((SEQ, WID, DM), BF),
        cot=v((TOK, INNER), BF),
        wa=v((4, 4, SHARD, HALF), BF),
        wb=v((4, 4, SHARD, HALF), BF),
        sw_rx=v((SEQ, 16, LANES), BF),
        sw=v((LANES, DM), BF),
        z=v((TOK, INNER), BF),
        sraw=v((TOK, LANES), F32),
        gate=v((TOK, INNER), F32),
        slope=v((TOK, INNER), F32),
        pay=v((SEQ, ROWS, LANES), BF),
        trx=v((SEQ, ROWS, LANES), BF),
        bpay=v((SEQ, ROWS, LANES), BF),
        brx=v((SEQ, ROWS, LANES), BF),
        tri=v((4, CHUNK, CHUNK), BF),
        lp=v((TOK, LANES), BF),
        bcr=v((2, SEQ, WID, LANES), BF),
        bct=v((2, SEQ, WID, LANES), BF),
        wx=v((DM, 2 * LANES), BF),
        tdb=v((2, CHUNKS, CHUNK, LANES), BF),
        trs=v((MP, CHUNK, LANES), BF),
        tpiece=v((SEQ, COLS, LANES), BF),
        rpiece=v((SEQ, COLS, LANES), BF),
        rdb=v((2, SEQ, WID, LANES), BF),
        rrs=v((MP, SEQ, COLS, LANES), BF),
        dpiece=v((SEQ, COLS, LANES), BF),
        lacc=v((CHUNK, LANES), F32),
        swp=v((16, LANES), BF),
        R=scan_scratch(),
        T=scan_scratch(),
        g=v((TOK, 768), BF),
        tokt=v((DM, TOK), BF),
        gp=v((4, 4, SHARD, 640), BF),
        g_raw=v((2, 2, 2, 32, 640), BF),
        g_near=v((2, 2, 4, 32, 640), BF),
        h_own=v((2, 4, 32, 640), BF),
        h_raw=v((2, 2, 16, 640), BF),
        h_near=v((2, 2, 32, 640), BF),
        z_raw=v((2, 2, CHUNK, LANES), BF),
        z_near=v((2, 2, 2 * CHUNK, LANES), BF),
        gs=v((MP, 16, LANES), BF),
        gs_rx=v((SEQ, 16, LANES), BF),
        ip=v((MP, TOK, LANES), BF),
        prx=v((4, TOK, LANES), BF),
        zs=v((4, TOK, LANES), BF),
        fsh=v((SHARD, LANES), F32),
        frx=v((MP, SHARD, LANES), F32),
        s_local=dma((4,)),
        s_w=dma((4, 2, 4)),
        s_sw=seq_sems(),
        s_pay=seq_sems(),
        s_sr=seq_sems(),
        s_st=seq_sems(),
        s_ur=seq_sems(),
        s_ut=seq_sems(),
        s_back=seq_sems(),
        s_back2=seq_sems(),
        s_gp=dma((4, 2, 6)),
        s_bc=seq_sems(),
        s_bp=seq_sems(),
        s_gs=seq_sems(),
        s_bm=dma((2, MP)),
        s_tr=dma((2, MP)),
        s_rr=dma((2, MP)),
        s_fin=dma((2, MP)),
        s_pair=dma((2, 4, CHUNKS)),
        s_z=dma((2, 2, 6)),
    )


def sems(ref):
    return ref.at[0], ref.at[1]


def head_sum():
    c, h = iota((INNER, LANES), 0), iota((INNER, LANES), 1)
    return jnp.where((h < 8) & ((h & 3) == (c >> 6)), 1.0, 0.0).astype(BF)


def pair_expand(shift):
    k, c = iota((LANES, INNER), 0) - shift, iota((LANES, INNER), 1)
    return jnp.where((k >= 0) & (k < 8) & ((k & 3) == (c >> 6)), 1.0, 0.0).astype(BF)


def pair_merge(shift):
    k, h = iota((LANES, LANES), 0) - shift, iota((LANES, LANES), 1)
    return jnp.where((k >= 0) & (k < 8) & (h < 8) & ((k & 3) == (h & 3)), 1.0, 0.0).astype(BF)


def pair_place(shift):
    k, lane = iota((LANES, LANES), 0), iota((LANES, LANES), 1)
    return jnp.where((k < 8) & (lane == k + shift), 1.0, 0.0).astype(BF)


def wide(load, block, q):
    return jnp.concatenate([load(block, q), load(block + 1, q)], axis=1)


def summary(b, tri, load, pair_of, rate, ratex, q):
    x = wide(load, BX, q).astype(F32)
    dy = wide(load, BY, q).astype(F32)
    pair, shift = pair_of(q)
    dexp = mm(pair, pair_expand(shift))
    logs = (-dexp * ratex).astype(BF)
    rexp = mm(tri, logs)
    b["rcol"][q] = mm(tri, (-mm(pair, pair_merge(shift)) * rate).astype(BF))
    total = jnp.sum(logs.astype(F32), axis=0, keepdims=True)
    er = jnp.exp2(rexp)
    tail = jnp.exp2(jnp.minimum(total - rexp, 0.0))
    xs = (x * dexp).astype(BF)
    xt = (xs.astype(F32) * tail).astype(BF)
    ed = (er * dy).astype(BF)
    b["er"][q] = er
    b["tail"][q] = tail
    b["xs"][q] = xs
    b["xt"][q] = xt
    b["ed"][q] = ed
    b["fresh"][q] = mm_tn(load(BB, q), xt)
    b["back"][q] = mm_tn(load(BC, q), ed)
    rows = jnp.broadcast_to(total, (8, INNER))
    b["eR"][q] = jnp.exp2(rows)
    b["RC"][...] += rows


def pack_states(b):
    e = [b["eR"][q][:1] for q in range(CHUNKS)]
    end = b["fresh"][0]
    for q in range(1, CHUNKS):
        end = end * e[q] + b["fresh"][q]
    first = b["back"][CHUNKS - 1]
    for q in range(CHUNKS - 2, -1, -1):
        first = first * e[q] + b["back"][q]
    rc = b["RC"][...]
    hi = rc.astype(BF).astype(F32)
    logs = jnp.concatenate([hi, rc - hi], axis=0).astype(BF)
    pieces = [v.reshape(SEQ, PIECE, INNER) for v in (end, first)]
    b["st"][:, pl.ds(0, 2 * PIECE), :] = jnp.concatenate(pieces, axis=1).astype(BF)
    for k in range(SEQ):
        b["st"][k, pl.ds(2 * PIECE, 2 * PIECE)] = logs


def chain_states(b):
    own = [b["sx"][k, pl.ds(0, 2 * PIECE)].astype(F32) for k in range(SEQ)]
    logs = [b["sx"][k, pl.ds(2 * PIECE, 2 * PIECE)].astype(F32) for k in range(SEQ)]
    decay = [jnp.exp2(v[:PIECE] + v[PIECE:]) for v in logs]
    state = [jnp.zeros((PIECE, INNER), F32)]
    grad = [jnp.zeros((PIECE, INNER), F32)]
    for k in range(SEQ - 1):
        state.append(state[k] * decay[k] + own[k][:PIECE])
        n = SEQ - 1 - k
        grad.append(grad[k] * decay[n] + own[n][PIECE:])
    for k in range(SEQ):
        b["sy"][k] = jnp.concatenate([state[k], grad[SEQ - 1 - k]], axis=0).astype(BF)


def entering_states(b):
    both = b["sz"][...].astype(F32)
    b["sin"][...] = both[:, :PIECE, :].reshape(STATE, INNER)
    grad = both[:, PIECE:, :].reshape(STATE, INNER)
    for q in range(CHUNKS - 1, -1, -1):
        b["gin"][q] = grad
        if q > 0:
            grad = grad * b["eR"][q][:1] + b["back"][q]


def head_rows(h):
    one = jnp.where((iota((16, INNER), 1) >> 6) == h, 1.0, 0.0).astype(BF)
    return jnp.concatenate([one] * (CHUNK // 16), axis=0)


def inside(b, tri, load, q):
    dy = wide(load, BY, q)
    bmat = load(BB, q)
    cmat = load(BC, q)
    xs = b["xs"][q]
    trif = tri.astype(F32)
    scores = mm_nt(cmat, bmat) * trif
    rcol = b["rcol"][q]
    rrow = rcol.T
    pairs = None
    ms, dys, xss = [], [], []
    for h in range(HEADS):
        decay = jnp.exp2(jnp.minimum(rcol[:, h : h + 1] - rrow[h : h + 1, :], 0.0))
        ms.append((decay * scores).astype(BF))
        mask = head_rows(h)
        dys.append(dy * mask)
        xss.append(xs * mask)
        term = decay * mm_nt(dys[h], xs)
        pairs = term if h == 0 else pairs + term
    dy4 = jnp.concatenate(dys, axis=0)
    y = mm(jnp.concatenate(ms, axis=1), jnp.concatenate(xss, axis=0))
    dxs = mm_tn(jnp.concatenate(ms, axis=0), dy4)
    pairs = (pairs * trif).astype(BF)
    b["y"][q] = y
    b["dx"][q] = dxs
    b["dbc"][q, :, pl.ds(0, STATE)] = mm_tn(pairs, cmat)
    b["dbc"][q, :, pl.ds(STATE, STATE)] = mm(pairs, bmat)


def outside(b, tri, tri_up, load, pair_of, rate, q, put):
    x = wide(load, BX, q).astype(F32)
    dy = wide(load, BY, q).astype(F32)
    bmat = load(BB, q)
    cmat = load(BC, q)
    pair, shift = pair_of(q)
    dexp = mm(pair, pair_expand(shift))
    xs = b["xs"][q].astype(F32)
    state = b["sin"][...]
    grad = b["gin"][q]
    state_b, grad_b = state.astype(BF), grad.astype(BF)
    sums = head_sum()
    y = b["y"][q] + b["er"][q] * mm(cmat, state_b)
    inner = b["dx"][q]
    outer = b["tail"][q] * mm(bmat, grad_b)
    dxs = inner + outer
    db = b["dbc"][q, :, pl.ds(0, STATE)] + mm_nt(b["xt"][q], grad_b)
    dc = b["dbc"][q, :, pl.ds(STATE, STATE)] + mm_nt(b["ed"][q], state_b)

    def by_head(v):
        return mm(v.astype(BF), sums)

    late = by_head(dy * y - xs * inner).astype(BF)
    early = by_head(xs * outer).astype(BF)
    decayed = b["eR"][q][:1] * state
    across = jnp.sum(decayed * grad, axis=0, keepdims=True)
    across = mm(jnp.broadcast_to(across, (16, INNER)).astype(BF), sums)[:1]
    dl = mm(tri_up, late) + mm(tri, early) - early.astype(F32) + across
    ddelta = by_head(x * dxs) - rate * dl
    b["sin"][...] = decayed + b["fresh"][q]
    put(q, y, dexp * dxs, db, dc, ddelta)


def kernel(tok_hbm, cot_hbm, pm, ps, pt, bias_s, rate_s, skip_s, gated_o, ig_o, gm_o, gsh_o, gst_o, m):
    seq, mp = lax.axis_index("seq"), lax.axis_index("mp")
    core = lax.rem(mp, 2)
    chip = mp // 2
    partner = mp + 1 - 2 * core
    plane, line = seq // 4, lax.rem(seq, 4)
    low = lax.rem(seq, 2)

    load_tok = pltpu.make_async_copy(tok_hbm, m["tok3"], m["s_local"].at[0])
    load_cot = pltpu.make_async_copy(cot_hbm, m["cot"], m["s_local"].at[1])
    load_tok.start()
    load_cot.start()

    barrier = pltpu.get_barrier_semaphore()

    def greet_seq(d):
        pl.semaphore_signal(
            barrier, inc=1, device_id={"seq": lax.rem(seq + d, SEQ)}, device_id_type=MESH
        )

    def greet_mp(d):
        pl.semaphore_signal(barrier, inc=1, device_id={"mp": lax.rem(mp + d, MP)}, device_id_type=MESH)

    fori(1, SEQ, greet_seq)
    fori(1, MP, greet_mp)

    wa, wb, swp = m["wa"], m["wb"], m["swp"]
    wa[plane, line, :, pl.ds(0, 256)] = pm[:, 0, :]
    wb[plane, line, :, pl.ds(0, 256)] = pm[:, 1, :]
    wa[plane, line, :, pl.ds(256, 128)] = ps[:, 0, :]
    wb[plane, line, :, pl.ds(256, 128)] = ps[:, 1, :]
    at, lane = iota((SHARD, LANES), 0), iota((SHARD, LANES), 1)
    place = jnp.where(lane == at + SHARD * low, 1.0, 0.0).astype(BF)
    shifted = mm(pt[...], place).astype(BF)
    swp[...] = jnp.concatenate([shifted, shifted, jnp.zeros((8, LANES), BF)], axis=0)
    pl.semaphore_wait(barrier, SEQ + MP - 2)

    most = pl.ds(0, SEQ - 1)

    def along_x(k):
        return 4 * k + line

    def along_y(k):
        return 4 * plane + k

    half = SHARD // 2
    ring_a1 = Ring(plane, along_x, lambda k: wa.at[k, line], lambda k, n: wa.at[k, line, pl.ds(half * n, half)], m["s_w"].at[0])
    ring_b1 = Ring(line, along_y, lambda k: wb.at[plane, k], lambda k, n: wb.at[plane, k, pl.ds(half * n, half)], m["s_w"].at[1])
    ring_a2 = Ring(line, along_y, lambda k: wa.at[:, k], lambda k, n: wa.at[pl.ds(2 * n, 2), k], m["s_w"].at[2])
    ring_b2 = Ring(plane, along_x, lambda k: wb.at[k], lambda k, n: wb.at[k, pl.ds(2 * n, 2)], m["s_w"].at[3])
    rings = (ring_a1, ring_b1, ring_a2, ring_b2)
    ring_a1.start()
    ring_b1.start()
    send_sw = SeqExchange(lambda p: swp, lambda k: m["sw_rx"].at[k], m["sw_rx"].at[most], sems(m["s_sw"]))
    send_sw.start()
    m["sw_rx"][seq] = swp[...]

    def flip(q):
        m["tokt"][:, pl.ds(q * CHUNK, CHUNK)] = m["tok3"][pl.ds(4 * q, 4)].reshape(CHUNK, DM).T

    load_tok.wait()
    flip(0)
    ring_a1.forward()
    ring_b1.forward()
    ring_a1.finish()
    ring_a2.start()
    ring_b1.finish()
    ring_b2.start()

    i, j = iota((CHUNK, CHUNK), 0), iota((CHUNK, CHUNK), 1)
    m["tri"][0] = jnp.where(i >= j, 1.0, 0.0).astype(BF)
    it, jt = (i & 15) * 16 + (i >> 4), (j & 15) * 16 + (j >> 4)
    m["tri"][1] = jnp.where(it >= jt, 1.0, 0.0).astype(BF)
    m["tri"][2] = jnp.where(i <= j, 1.0, 0.0).astype(BF)
    m["tri"][3] = jnp.where(it <= jt, 1.0, 0.0).astype(BF)
    m["sw"][...] = jnp.zeros((LANES, DM), BF)
    m["R"]["RC"][...] = jnp.zeros((8, INNER), F32)
    m["T"]["RC"][...] = jnp.zeros((8, INNER), F32)
    m["lacc"][...] = jnp.zeros((CHUNK, LANES), F32)

    head_l = iota((1, LANES), 1)
    head_c = iota((1, INNER), 1) >> 6

    def lanes_of(value):
        v = jnp.zeros((1, LANES), F32)
        for h in range(HEADS):
            v = jnp.where((head_l < 8) & ((head_l & 3) == h), value(h), v)
        return v

    def features_of(value):
        v = jnp.zeros((1, INNER), F32)
        for h in range(HEADS):
            v = jnp.where(head_c == h, value(h), v)
        return v

    bias = lanes_of(lambda h: bias_s[h])
    rate_r, rate_t = lanes_of(lambda h: rate_s[0, h]), lanes_of(lambda h: rate_s[1, h])
    ratex_r = features_of(lambda h: rate_s[0, h]) * LOG2E
    ratex_t = features_of(lambda h: rate_s[1, h]) * LOG2E
    skip = features_of(lambda h: skip_s[h])

    load_cot.wait()
    flip(1)
    ring_a2.forward()
    ring_b2.forward()
    flip(2)
    flip(3)
    ring_a2.finish()
    ring_b2.finish()
    send_sw.wait_recv()
    for k in range(SEQ // 2):
        m["sw"][pl.ds(0, 16), pl.ds(k * LANES, LANES)] = m["sw_rx"][2 * k] + m["sw_rx"][2 * k + 1]

    def rows_of(q):
        return pl.ds(pl.multiple_of(q * CHUNK, CHUNK), CHUNK)

    def columns(ref, at, width):
        return ref[:, :, :, pl.ds(at, width)].reshape(DM, width)

    def rest(v):
        return v.reshape(4, WID, LANES)

    send_pay = SeqExchange(lambda p: m["pay"].at[p], lambda k: m["trx"].at[k], m["trx"].at[most], sems(m["s_pay"]))
    quarter = pl.ds(pl.multiple_of(chip * COLS, COLS), COLS)
    bcr, bct = m["bcr"], m["bct"]
    send_bc = SeqExchange(
        lambda p: bcr.at[core, p, quarter],
        lambda k: bct.at[core, k, quarter],
        bct.at[core, most, quarter],
        sems(m["s_bc"]),
    )

    def piece_of(ref, k):
        return ref.at[lax.rem(k, 2), :, pl.ds(pl.multiple_of(k // 2 * COLS, COLS), COLS)]

    send_bm = MpExchange(lambda p: piece_of(bct, mp), lambda k: piece_of(bct, k), sems(m["s_bm"]))
    m["wx"][:, pl.ds(0, LANES)] = jnp.where(core == 0, columns(wa, 256, 128), columns(wb, 256, 128))
    m["wx"][:, pl.ds(LANES, LANES)] = m["sw"][...].T

    def start_four(exchange, q):
        def one(n):
            d = lax.rem(4 * q + n - seq + SEQ, SEQ)

            @pl.when(d != 0)
            def _():
                exchange.copy(d).start()

        fori(0, 4, one)

    def far_first(n):
        step = jnp.where(n == 0, 2, jnp.where(n == 3, 0, 2 * n - 1))
        return lax.rem(plane + step, 4)

    def project_shared(n):
        q = far_first(n)
        u = m["tok3"][pl.ds(4 * q, 4)].reshape(CHUNK, DM)
        w = jnp.concatenate([columns(wa, 256, 128), columns(wb, 256, 128)], axis=1)
        v = mm(u, w).astype(BF)
        bcr[0, pl.ds(4 * q, 4)] = rest(v[:, :LANES])
        bcr[1, pl.ds(4 * q, 4)] = rest(v[:, LANES:])
        start_four(send_bc, q)

    def project(n):
        q = far_first(n)
        rows = rows_of(q)
        u = m["tok3"][pl.ds(4 * q, 4)].reshape(CHUNK, DM)
        four = pl.ds(4 * q, 4)

        def put(block, v):
            v = v.astype(BF)
            for k in range(v.shape[1] // LANES):
                m["pay"][four, pl.ds((block + k) * WID, WID), :] = rest(v[:, k * LANES : (k + 1) * LANES])

        z = mm(u, columns(wb, 0, 256)).astype(BF)
        m["z"][rows, :] = z
        zf = z.astype(F32)
        gate = zf * jax.nn.sigmoid(zf)
        put(BY, m["cot"][rows, :].astype(F32) * gate)
        put(BX, mm(u, columns(wa, 0, 256)))
        raw = mm(u, m["wx"][:, pl.ds(LANES, LANES)]) + bias
        m["sraw"][rows, :] = raw
        pair = as_pair(jnp.maximum(raw, 0.0) + jnp.log1p(jnp.exp(-jnp.abs(raw))))
        m["lp"][rows, :] = pair
        folded = jnp.zeros((64, LANES), F32)
        for g in range(4):
            part = rest(pair)[:, g * COLS : (g + 1) * COLS, :].reshape(64, LANES)
            folded += mm(part, pair_place(8 * g))
        m["pay"][four, pl.ds(ROWS_L, COLS), :] = folded.astype(BF).reshape(4, COLS, LANES)
        start_four(send_pay, q)

    fori(0, CHUNKS, project_shared)
    fori(0, CHUNKS, project)
    m["trx"][seq] = m["pay"][seq]
    bct[core, seq, quarter] = bcr[core, seq, quarter]

    def load_r(block, q):
        if block >= BB:
            return bcr[block - BB, pl.ds(4 * q, 4)].reshape(CHUNK, LANES)
        return m["pay"][pl.ds(4 * q, 4), pl.ds(block * WID, WID), :].reshape(CHUNK, LANES)

    def pair_r(q):
        return m["lp"][rows_of(q), :], 0

    def cols_of(block, q):
        return pl.ds(pl.multiple_of(block * WID + q * COLS, COLS), COLS)

    def load_t(block, q):
        if block >= BB:
            return bct[block - BB, :, pl.ds(q * COLS, COLS), :].reshape(CHUNK, LANES)
        return m["trx"][:, cols_of(block, q), :].reshape(CHUNK, LANES)

    def pair_t(q):
        return m["trx"][:, pl.ds(ROWS_L, COLS), :].reshape(CHUNK, LANES), 8 * q

    def pieces_exchange(source, landing, sem):
        return SeqExchange(lambda p: source.at[p], lambda k: landing.at[k], landing.at[most], sems(sem))

    r, t = m["R"], m["T"]
    tri_r, tri_t, up_r, up_t = (m["tri"].at[k] for k in range(4))

    def chunks(low, high, step):
        for q in range(low, high):
            step(q)


    def start_pieces(b, sem):
        e = pieces_exchange(b["st"], b["sx"], sem)
        e.start()
        b["sx"][seq] = b["st"][seq]
        return e

    def start_entering(b, sem):
        chain_states(b)
        e = pieces_exchange(b["sy"], b["sz"], sem)
        e.start()
        b["sz"][seq] = b["sy"][seq]
        return e

    chunks(0, CHUNKS, lambda q: summary(r, tri_r[...], load_r, pair_r, rate_r * LOG2E, ratex_r, q))
    pack_states(r)
    send_bc.wait_recv()
    send_bm.start()
    chunks(0, 2, lambda q: inside(r, tri_r[...], load_r, q))
    send_sw.wait_send()
    for e in rings:
        e.wait_send()

    send_pay.wait_recv()
    send_sr = start_pieces(r, m["s_sr"])
    send_bm.wait_recv()
    chunks(0, CHUNKS, lambda q: summary(t, tri_t[...], load_t, pair_t, rate_t * LOG2E, ratex_t, q))
    pack_states(t)
    send_st = start_pieces(t, m["s_st"])
    send_sr.wait_recv()
    send_ur = start_entering(r, m["s_ur"])
    chunks(0, 2, lambda q: inside(t, tri_t[...], load_t, q))
    send_st.wait_recv()
    send_ut = start_entering(t, m["s_ut"])
    chunks(2, CHUNKS, lambda q: inside(t, tri_t[...], load_t, q))
    send_ut.wait_recv()
    entering_states(t)

    def put_t(q, y, dx, db, dc, dd):
        def put(block, v):
            v = v.astype(BF)
            for k in range(v.shape[1] // LANES):
                part = v[:, k * LANES : (k + 1) * LANES]
                at = 128 * (q // 2) + 32 * (block + k) + COLS * (q % 2)
                m["bpay"][:, pl.ds(at, COLS), :] = part.reshape(SEQ, COLS, LANES)

        put(BX, y)
        put(BY, dx)
        m["tdb"][0, q] = db.astype(BF)
        m["tdb"][1, q] = dc.astype(BF)
        for n in range(2):
            d = lax.rem(2 * q + n - mp + MP, MP)

            @pl.when(d != 0)
            def _():
                send_tr.copy(d).start()

        m["lacc"][...] += mm(as_pair(dd), pair_place(8 * q))

    def half_back(at, count, sem):
        rows = pl.ds(at, count)
        return SeqExchange(
            lambda p: m["bpay"].at[p, rows], lambda k: m["brx"].at[k, rows], m["brx"].at[most, rows], sems(sem)
        )

    send_back = half_back(0, 128, m["s_back"])
    send_back2 = half_back(128, 144, m["s_back2"])
    send_tr = MpExchange(
        lambda p: m["tdb"].at[lax.rem(p, 2), p // 2], lambda k: m["trs"].at[k], sems(m["s_tr"])
    )
    send_bp = SeqExchange(lambda p: m["tpiece"].at[p], lambda k: m["rpiece"].at[k], m["rpiece"].at[most], sems(m["s_bp"]))
    send_rr = MpExchange(lambda p: piece_of(m["rdb"], p), lambda k: m["rrs"].at[k], sems(m["s_rr"]))

    def group_total(ref):
        v = ref[0].astype(F32)
        for k in range(1, MP):
            v += ref[k].astype(F32)
        return v

    chunks(0, 2, lambda q: outside(t, tri_t[...], up_t[...], load_t, pair_t, rate_t, q, put_t))
    send_back.start()
    chunks(2, 4, lambda q: outside(t, tri_t[...], up_t[...], load_t, pair_t, rate_t, q, put_t))
    m["bpay"][:, pl.ds(ROWS_L, COLS), :] = m["lacc"][...].astype(BF).reshape(SEQ, COLS, LANES)
    send_back2.start()
    m["brx"][seq] = m["bpay"][seq]
    m["trs"][mp] = m["tdb"][core, chip]

    inside(r, tri_r[...], load_r, 2)
    send_tr.wait_recv()
    m["tpiece"][...] = group_total(m["trs"]).astype(BF).reshape(SEQ, COLS, LANES)
    send_bp.start()
    m["rpiece"][seq] = m["tpiece"][seq]
    inside(r, tri_r[...], load_r, 3)
    send_ur.wait_recv()
    entering_states(r)

    def put_r(q, y, dx, db, dc, dd):
        rows = rows_of(q)
        r["y"][q] = y + skip * wide(load_r, BX, q).astype(F32)
        r["dx"][q] = dx + skip * wide(load_r, BY, q).astype(F32)
        z = m["z"][rows, :].astype(F32)
        sigma = jax.nn.sigmoid(z)
        m["gate"][rows, :] = z * sigma
        m["slope"][rows, :] = m["cot"][rows, :].astype(F32) * sigma * (1.0 + z * (1.0 - sigma))
        m["sraw"][rows, :] = jax.nn.sigmoid(m["sraw"][rows, :])
        m["rdb"][0, pl.ds(4 * q, 4)] = rest(db.astype(BF))
        m["rdb"][1, pl.ds(4 * q, 4)] = rest(dc.astype(BF))
        r["dd"][q] = dd

    def outside_r(q):
        outside(r, tri_r[...], up_r[...], load_r, pair_r, rate_r, q, put_r)

    chunks(0, CHUNKS, outside_r)
    send_rr.start()
    m["rrs"][mp] = m["rdb"][core, :, quarter]
    for e in (send_pay, send_bc, send_bm, send_sr, send_ur, send_st, send_ut):
        e.wait_send()
    send_back.wait_recv()
    send_back2.wait_recv()
    send_bp.wait_recv()
    send_rr.wait_recv()
    m["dpiece"][...] = (group_total(m["rrs"]) + m["rpiece"][...].astype(F32)).astype(BF)

    def back(block, q):
        parts = [m["brx"][pl.ds(4 * q, 4), pl.ds(128 * n + 32 * block, 32), :] for n in range(2)]
        return jnp.concatenate(parts, axis=1).reshape(CHUNK, LANES)

    def combine(q):
        rows = rows_of(q)
        y = r["y"][q] + wide(back, BX, q).astype(F32)
        gated_o[rows, :] = (y * m["gate"][rows, :]).astype(BF)
        m["g"][rows, pl.ds(256, 256)] = (y * m["slope"][rows, :]).astype(BF)
        m["g"][rows, pl.ds(0, 256)] = (r["dx"][q] + wide(back, BY, q).astype(F32)).astype(BF)
        folded = m["brx"][pl.ds(4 * q, 4), pl.ds(ROWS_L, COLS), :].reshape(64, LANES)
        parts = [mm(folded, pair_merge(8 * g)).reshape(4, COLS, LANES) for g in range(4)]
        dd = r["dd"][q] + jnp.concatenate(parts, axis=1).reshape(CHUNK, LANES)
        dstep = dd * m["sraw"][rows, :]
        m["g"][rows, pl.ds(640, LANES)] = jnp.where(iota((CHUNK, LANES), 1) < HEADS, dstep, 0.0).astype(BF)

    def pair_copy(k, q):
        rows = rows_of(q)
        return mp_copy(
            m["ip"].at[2 * k + 1 - core, rows],
            m["prx"].at[k, rows],
            m["s_pair"].at[0, k, q],
            m["s_pair"].at[1, k, q],
            partner,
        )

    def z_ring(n):
        def part(k, h):
            return m["zs"].at[k, pl.ds(CHUNK * (2 * n + h), CHUNK)]

        return RingSum(
            chip,
            lambda k: {"mp": 2 * k + core},
            part,
            lambda h: m["z_raw"].at[n, h],
            lambda side, h: m["z_near"].at[n, side, pl.ds(CHUNK * h, CHUNK)],
            m["s_z"].at[n],
        )

    z_rings = [z_ring(0), z_ring(1)]

    def pair_sum(k, q):
        rows = rows_of(q)
        pair_copy(k, q).wait_recv()
        return (m["ip"][2 * k + core, rows, :].astype(F32) + m["prx"][k, rows, :].astype(F32)).astype(BF)

    def pass_on(q):
        for k in range(4):
            m["zs"][k, rows_of(q), :] = pair_sum(k, q)

    def z_start(n):
        z_rings[n].start_far()
        z_rings[n].start_near()

    def z_finish(n):
        for h, v in enumerate(z_rings[n].finish()):
            ig_o[rows_of(2 * n + h), :] = v.astype(BF)

    def combine_all(q):
        combine(q)
        rows = rows_of(q)
        piece = m["dpiece"][pl.ds(4 * q, 4)]
        here = (iota((4, WID, LANES), 1) >> 4) == chip
        piece = jnp.where(here, jnp.concatenate([piece] * 4, axis=1), jnp.zeros((), BF)).reshape(CHUNK, LANES)
        m["g"][rows, pl.ds(512, LANES)] = piece

    def input_part(q):
        rows = rows_of(q)
        g = m["g"][rows, :]
        for c in range(4):
            cols = pl.ds(c * 256, 256)
            v = mm_nt(g[:, :256], wa[c, :, :, pl.ds(0, 256)].reshape(256, 256))
            v += mm_nt(g[:, 256:512], wb[c, :, :, pl.ds(0, 256)].reshape(256, 256))
            v += mm_nt(g[:, 512:], m["wx"][cols, :])
            v = v.astype(BF)
            m["ip"][2 * c, rows, :] = v[:, :LANES]
            m["ip"][2 * c + 1, rows, :] = v[:, LANES:]
        fori(0, 4, lambda k: pair_copy(k, q).start())

    chunks(0, CHUNKS, combine_all)

    def g_ring(n):
        rows = pl.ds(32 * n, 32)

        def part(k, h):
            two = pl.ds(2 * h, 2)
            return m["gp"].at[k, two, rows] if n == 0 else m["gp"].at[two, k, rows]

        return RingSum(
            plane if n == 0 else line,
            lambda k: {"seq": along_x(k) if n == 0 else along_y(k)},
            part,
            lambda h: m["g_raw"].at[n, h],
            lambda side, h: m["g_near"].at[n, side, pl.ds(2 * h, 2)],
            m["s_gp"].at[n],
        )

    def h_ring(n):
        return RingSum(
            line if n == 0 else plane,
            lambda k: {"seq": along_y(k) if n == 0 else along_x(k)},
            lambda k, h: m["h_own"].at[n, k, pl.ds(16 * h, 16)],
            lambda h: m["h_raw"].at[n, h],
            lambda side, h: m["h_near"].at[n, side, pl.ds(16 * h, 16)],
            m["s_gp"].at[2 + n],
        )

    g_rings, h_rings = [g_ring(0), g_ring(1)], [h_ring(0), h_ring(1)]
    send_gs = SeqExchange(lambda p: m["gs"].at[p // 2], lambda k: m["gs_rx"].at[k], m["gs_rx"].at[most], sems(m["s_gs"]))

    def grads(n):
        k = lax.rem(plane + n, 4)
        cols = rows_of(k)
        v = mm(m["tokt"][cols, :], m["g"][...])
        m["gp"][k] = v[:, :640].astype(BF).reshape(4, SHARD, 640)
        gs = v[:, 640:].T[:16].astype(BF)
        m["gs"][2 * k] = gs[:, :LANES]
        m["gs"][2 * k + 1] = gs[:, LANES:]
        start_four(send_gs, k)

    grads(2)
    g_rings[0].start_far()
    grads(1)
    grads(3)
    g_rings[0].start_near()
    grads(0)
    g_rings[1].start_far()
    g_rings[1].start_near()
    m["gs_rx"][seq] = m["gs"][seq // 2]
    input_part(0)
    input_part(1)
    g_rings[0].middle()
    g_rings[1].middle()
    input_part(2)
    pass_on(0)
    pass_on(1)
    z_start(0)
    input_part(3)
    for e in (send_back, send_back2, send_tr, send_bp, send_rr, send_gs):
        e.wait_send()
    pass_on(2)
    pass_on(3)
    z_start(1)

    def g_next(n):
        for h, v in enumerate(g_rings[n].finish()):
            m["h_own"][n, pl.ds(2 * h, 2)] = v.astype(BF).reshape(2, 32, 640)
        h_rings[n].start_far()
        h_rings[n].start_near()

    g_next(0)
    g_next(1)
    z_rings[0].middle()
    h_rings[0].middle()
    h_rings[1].middle()
    z_rings[1].middle()

    def total_of(ref):
        v = ref[0].astype(F32)
        for k in range(1, SEQ):
            v += ref[k].astype(F32)
        return v

    main = jnp.concatenate(h_rings[0].finish() + h_rings[1].finish(), axis=0)
    m["fsh"][...] = main[:, 512:]
    send_fin = MpExchange(lambda p: m["fsh"], lambda k: m["frx"].at[k], sems(m["s_fin"]))
    send_fin.start()
    m["frx"][mp] = main[:, 512:]
    gm_o[:, 0, :] = main[:, :INNER]
    gm_o[:, 1, :] = main[:, INNER : 2 * INNER]
    send_gs.wait_recv()
    step = total_of(m["gs_rx"])
    gst_o[...] = jnp.where(low == 0, step[:HEADS, :SHARD], step[:HEADS, SHARD:])
    z_finish(0)
    z_finish(1)
    send_fin.wait_recv()
    for n in range(2):
        gsh_o[:, n, :] = m["frx"][n] + m["frx"][2 + n] + m["frx"][4 + n] + m["frx"][6 + n]

    sent = [send_fin] + z_rings + g_rings + h_rings
    for e in sent:
        e.wait_send()
    for q in range(CHUNKS):
        fori(0, 4, lambda k: pair_copy(k, q).wait_send())


def hand_over(*refs):
    n = len(refs) // 2
    for k in range(n):
        refs[n + k][...] = refs[k][...]


def body(tokens, proj_main, proj_shared, proj_step, step_bias, decay_rate, skip_gain, cotangent):
    vm = pl.BlockSpec(memory_space=pltpu.VMEM)
    sm = pl.BlockSpec(memory_space=pltpu.SMEM)
    hbm = pl.BlockSpec(memory_space=pl.ANY)
    shapes = (
        jax.ShapeDtypeStruct((TOK, INNER), BF),
        jax.ShapeDtypeStruct((TOK, LANES), BF),
        jax.ShapeDtypeStruct((SHARD, 2, INNER), F32),
        jax.ShapeDtypeStruct((SHARD, 2, STATE), F32),
        jax.ShapeDtypeStruct((HEADS, SHARD), F32),
    )
    results = pl.pallas_call(
        kernel,
        out_shape=shapes,
        in_specs=[hbm, hbm, vm, vm, vm, sm, sm, sm],
        out_specs=(vm,) * 5,
        scratch_shapes=[main_scratch()],
        compiler_params=pltpu.CompilerParams(
            collective_id=0, has_side_effects=True, vmem_limit_bytes=62 * 1024 * 1024
        ),
    )(
        tokens.reshape(SEQ, WID, DM),
        cotangent.reshape(TOK, INNER),
        proj_main,
        proj_shared,
        proj_step.T,
        step_bias,
        decay_rate,
        skip_gain,
    )
    gated, ig, gm, gsh, gst = pl.pallas_call(
        hand_over,
        out_shape=shapes,
        in_specs=[vm] * 5,
        out_specs=(vm,) * 5,
    )(*results)
    return (
        gated.reshape(1, 16, WID, INNER),
        ig.reshape(1, 16, WID, LANES),
        gm,
        gsh,
        gst.T,
    )


def solution(mesh):
    placed = (
        P("seq", None, None, None),
        P("seq", None, "mp"),
        P("seq", None, None),
        P("seq", "mp"),
        P("mp"),
        P(None, "mp"),
        P("mp"),
        P("seq", None, None, "mp"),
    )
    return jax.shard_map(
        body,
        mesh=mesh,
        in_specs=placed,
        out_specs=(
            P("seq", None, None, "mp"),
            P("seq", None, None, "mp"),
            P("seq", None, "mp"),
            P("seq", None, None),
            P("seq", "mp"),
        ),
        check_vma=False,
    )
```

```python
import jax
import jax.numpy as jnp
from jax import lax
from jax.experimental import pallas as pl
from jax.experimental.pallas import tpu as pltpu
from jax.sharding import PartitionSpec as P

MESH = pl.DeviceIdType.MESH
BF = jnp.bfloat16
F32 = jnp.float32

SEQ = 16
MP = 8
TOK = 1024
WID = 64
DM = 1024
INNER = 256
HEADS = 4
STATE = 128
LANES = 128
CHUNK = 256
CHUNKS = TOK // CHUNK
COLS = CHUNK // SEQ
SHARD = DM // SEQ
BX, BY, BB, BC, ROWS_L, ROWS = 0, 2, 4, 5, 256, 272
PIECE = STATE // SEQ
HALF = 3 * LANES
LOG2E = 1.4426950408889634


def iota(shape, axis):
    return lax.broadcasted_iota(jnp.int32, shape, axis)


def mm(a, b):
    return lax.dot_general(a, b, (((1,), (0,)), ((), ())), preferred_element_type=F32)


def mm_nt(a, b):
    return lax.dot_general(a, b, (((1,), (1,)), ((), ())), preferred_element_type=F32)


def mm_tn(a, b):
    return lax.dot_general(a, b, (((0,), (0,)), ((), ())), preferred_element_type=F32)


def halves(v):
    hi = v.astype(BF)
    return hi, (v - hi.astype(F32)).astype(BF)


def as_pair(v):
    lane = iota(v.shape, 1)
    hi = v.astype(BF).astype(F32)
    return jnp.where(lane < 4, hi, jnp.where(lane < 8, v - hi, 0.0)).astype(BF)


def fori(low, high, step):
    def run(i, carry):
        step(i)
        return carry

    lax.fori_loop(low, high, run, 0)


class SeqExchange:
    def __init__(self, source, landing, many, sems):
        self.source, self.landing, self.many = source, landing, many
        self.send, self.recv = sems
        self.me = lax.axis_index("seq")

    def copy(self, d):
        peer = lax.rem(self.me + d, SEQ)
        return pltpu.make_async_remote_copy(
            src_ref=self.source(peer),
            dst_ref=self.landing(self.me),
            send_sem=self.send,
            recv_sem=self.recv,
            device_id={"seq": peer},
            device_id_type=MESH,
        )

    def all(self):
        return pltpu.make_async_remote_copy(
            src_ref=self.many,
            dst_ref=self.many,
            send_sem=self.send,
            recv_sem=self.recv,
            device_id={"seq": lax.rem(self.me + 1, SEQ)},
            device_id_type=MESH,
        )

    def start(self):
        def one(i):
            step = i // 2
            self.copy(SEQ // 2 + jnp.where(lax.rem(i, 2) == 0, step, -step)).start()

        fori(1, SEQ, one)

    def wait_recv(self):
        self.all().wait_recv()

    def wait_send(self):
        self.all().wait_send()


class Ring:
    def __init__(self, me, to, whole, part, sems):
        self.whole, self.part, self.sems, self.to = whole, part, sems, to
        self.me, self.right, self.left = me, lax.rem(me + 1, 4), lax.rem(me + 3, 4)
        self.far = lax.rem(me + 2, 4)

    def copy(self, ref, k, peer):
        return pltpu.make_async_remote_copy(
            src_ref=ref,
            dst_ref=ref,
            send_sem=self.sems.at[0, k],
            recv_sem=self.sems.at[1, k],
            device_id={"seq": self.to(peer)},
            device_id_type=MESH,
        )

    def start(self):
        self.copy(self.whole(self.me), 0, self.right).start()
        self.copy(self.whole(self.me), 1, self.left).start()

    def forward(self):
        self.copy(self.whole(self.left), 0, self.left).wait_recv()
        self.copy(self.part(self.left, 0), 2, self.right).start()
        self.copy(self.whole(self.right), 1, self.right).wait_recv()
        self.copy(self.part(self.right, 1), 3, self.left).start()

    def finish(self):
        self.copy(self.part(self.far, 0), 2, self.left).wait_recv()
        self.copy(self.part(self.far, 1), 3, self.right).wait_recv()

    def wait_send(self):
        self.copy(self.whole(self.me), 0, self.right).wait_send()
        self.copy(self.whole(self.me), 1, self.left).wait_send()
        self.copy(self.part(self.left, 0), 2, self.right).wait_send()
        self.copy(self.part(self.right, 1), 3, self.left).wait_send()


class RingSum:
    def __init__(self, me, to, part, raw, near, sems):
        self.part, self.raw, self.near, self.sems, self.to = part, raw, near, sems, to
        self.me, self.far = me, lax.rem(me + 2, 4)
        self.side = (lax.rem(me + 3, 4), lax.rem(me + 1, 4))

    def copy(self, source, landing, k, peer):
        return pltpu.make_async_remote_copy(
            src_ref=source,
            dst_ref=landing,
            send_sem=self.sems.at[0, k],
            recv_sem=self.sems.at[1, k],
            device_id=self.to(peer),
            device_id_type=MESH,
        )

    def far_copy(self, n):
        return self.copy(self.part(self.far, n), self.raw(n), n, self.side[1 - n])

    def own_copy(self, n):
        peer = self.side[1 - n]
        return self.copy(self.part(peer, 1 - n), self.near(n, 1 - n), 2 + n, peer)

    def sum_copy(self, n):
        peer = self.side[1 - n]
        return self.copy(self.part(peer, n), self.near(n, n), 4 + n, peer)

    def start_far(self):
        for n in range(2):
            self.far_copy(n).start()

    def start_near(self):
        for n in range(2):
            self.own_copy(n).start()

    def middle(self):
        for n in range(2):
            self.copy(self.raw(n), self.raw(n), n, self.side[n]).wait_recv()
            ref = self.part(self.side[1 - n], n)
            ref[...] = (ref[...].astype(F32) + self.raw(n)[...].astype(F32)).astype(BF)
            self.sum_copy(n).start()

    def finish(self):
        halves = []
        for n in range(2):
            for k in range(2):
                ref = self.near(k, n)
                self.copy(ref, ref, 2 + k if n != k else 4 + k, self.side[k]).wait_recv()
            v = self.part(self.me, n)[...].astype(F32)
            halves.append(v + self.near(0, n)[...].astype(F32) + self.near(1, n)[...].astype(F32))
        return halves

    def wait_send(self):
        for n in range(2):
            self.far_copy(n).wait_send()
            self.own_copy(n).wait_send()
            self.sum_copy(n).wait_send()


def mp_copy(source, landing, send, recv, peer):
    return pltpu.make_async_remote_copy(
        src_ref=source,
        dst_ref=landing,
        send_sem=send,
        recv_sem=recv,
        device_id={"mp": peer},
        device_id_type=MESH,
    )


class MpExchange:
    def __init__(self, source, landing, sems):
        self.source, self.landing = source, landing
        self.send, self.recv = sems
        self.me = lax.axis_index("mp")

    def copy(self, d):
        peer = lax.rem(self.me + d, MP)
        return mp_copy(self.source(peer), self.landing(self.me), self.send.at[d], self.recv.at[d], peer)

    def arrival(self, d):
        origin = lax.rem(self.me - d + MP, MP)
        ref = self.landing(origin)
        return mp_copy(ref, ref, self.send.at[d], self.recv.at[d], origin)

    def start(self):
        fori(1, MP, lambda d: self.copy(d).start())

    def wait_recv(self):
        fori(1, MP, lambda d: self.arrival(d).wait_recv())

    def wait_send(self):
        fori(1, MP, lambda d: self.copy(d).wait_send())


def scan_scratch():
    v = pltpu.VMEM
    return dict(
        xs=v((CHUNKS, CHUNK, INNER), BF),
        xt=v((CHUNKS, CHUNK, INNER), BF),
        ed=v((CHUNKS, CHUNK, INNER), BF),
        er=v((CHUNKS, CHUNK, INNER), F32),
        tail=v((CHUNKS, CHUNK, INNER), F32),
        rcol=v((CHUNKS, CHUNK, LANES), F32),
        fresh=v((CHUNKS, STATE, INNER), F32),
        back=v((CHUNKS, STATE, INNER), F32),
        eR=v((CHUNKS, 8, INNER), F32),
        RC=v((8, INNER), F32),
        st=v((SEQ, 4 * PIECE, INNER), BF),
        sx=v((SEQ, 4 * PIECE, INNER), BF),
        sy=v((SEQ, 2 * PIECE, INNER), BF),
        sz=v((SEQ, 2 * PIECE, INNER), BF),
        y=v((CHUNKS, CHUNK, INNER), F32),
        dx=v((CHUNKS, CHUNK, INNER), F32),
        dbc=v((CHUNKS, CHUNK, 2 * STATE), F32),
        dd=v((CHUNKS, CHUNK, LANES), F32),
        gin=v((CHUNKS, STATE, INNER), F32),
        sin=v((STATE, INNER), F32),
    )


def main_scratch():
    v = pltpu.VMEM
    dma = pltpu.SemaphoreType.DMA
    seq_sems = lambda: dma((2,))
    return dict(
        tok3=v((SEQ, WID, DM), BF),
        cot=v((TOK, INNER), BF),
        wa=v((4, 4, SHARD, HALF), BF),
        wb=v((4, 4, SHARD, HALF), BF),
        sw_rx=v((SEQ, 16, LANES), BF),
        sw=v((LANES, DM), BF),
        z=v((TOK, INNER), BF),
        sraw=v((TOK, LANES), F32),
        gate=v((TOK, INNER), F32),
        slope=v((TOK, INNER), F32),
        pay=v((SEQ, ROWS, LANES), BF),
        trx=v((SEQ, ROWS, LANES), BF),
        bpay=v((SEQ, ROWS, LANES), BF),
        brx=v((SEQ, ROWS, LANES), BF),
        tri=v((4, CHUNK, CHUNK), BF),
        lp=v((TOK, LANES), BF),
        bcr=v((2, SEQ, WID, LANES), BF),
        bct=v((2, SEQ, WID, LANES), BF),
        wx=v((DM, 2 * LANES), BF),
        tdb=v((2, CHUNKS, CHUNK, LANES), BF),
        trs=v((MP, CHUNK, LANES), BF),
        tpiece=v((SEQ, COLS, LANES), BF),
        rpiece=v((SEQ, COLS, LANES), BF),
        rdb=v((2, SEQ, WID, LANES), BF),
        rrs=v((MP, SEQ, COLS, LANES), BF),
        dpiece=v((SEQ, COLS, LANES), BF),
        lacc=v((CHUNK, LANES), F32),
        swp=v((16, LANES), BF),
        R=scan_scratch(),
        T=scan_scratch(),
        g=v((TOK, 768), BF),
        tokt=v((DM, TOK), BF),
        gp=v((4, 4, SHARD, 640), BF),
        g_raw=v((2, 2, 2, 32, 640), BF),
        g_near=v((2, 2, 4, 32, 640), BF),
        h_own=v((2, 4, 32, 640), BF),
        h_raw=v((2, 2, 16, 640), BF),
        h_near=v((2, 2, 32, 640), BF),
        z_raw=v((2, 2, CHUNK, LANES), BF),
        z_near=v((2, 2, 2 * CHUNK, LANES), BF),
        gs=v((MP, 16, LANES), BF),
        gs_rx=v((SEQ, 16, LANES), BF),
        ip=v((MP, TOK, LANES), BF),
        prx=v((4, TOK, LANES), BF),
        zs=v((4, TOK, LANES), BF),
        fsh=v((SHARD, LANES), F32),
        frx=v((MP, SHARD, LANES), F32),
        s_local=dma((4,)),
        s_w=dma((4, 2, 4)),
        s_sw=seq_sems(),
        s_pay=seq_sems(),
        s_sr=seq_sems(),
        s_st=seq_sems(),
        s_ur=seq_sems(),
        s_ut=seq_sems(),
        s_back=seq_sems(),
        s_back2=seq_sems(),
        s_gp=dma((4, 2, 6)),
        s_bc=seq_sems(),
        s_bp=seq_sems(),
        s_gs=seq_sems(),
        s_bm=dma((2, MP)),
        s_tr=dma((2, MP)),
        s_rr=dma((2, MP)),
        s_fin=dma((2, MP)),
        s_pair=dma((2, 4, CHUNKS)),
        s_z=dma((2, 2, 6)),
    )


def sems(ref):
    return ref.at[0], ref.at[1]


def head_sum():
    c, h = iota((INNER, LANES), 0), iota((INNER, LANES), 1)
    return jnp.where((h < 8) & ((h & 3) == (c >> 6)), 1.0, 0.0).astype(BF)


def pair_expand(shift):
    k, c = iota((LANES, INNER), 0) - shift, iota((LANES, INNER), 1)
    return jnp.where((k >= 0) & (k < 8) & ((k & 3) == (c >> 6)), 1.0, 0.0).astype(BF)


def pair_merge(shift):
    k, h = iota((LANES, LANES), 0) - shift, iota((LANES, LANES), 1)
    return jnp.where((k >= 0) & (k < 8) & (h < 8) & ((k & 3) == (h & 3)), 1.0, 0.0).astype(BF)


def pair_place(shift):
    k, lane = iota((LANES, LANES), 0), iota((LANES, LANES), 1)
    return jnp.where((k < 8) & (lane == k + shift), 1.0, 0.0).astype(BF)


def wide(load, block, q):
    return jnp.concatenate([load(block, q), load(block + 1, q)], axis=1)


def summary(b, tri, load, pair_of, rate, ratex, q):
    x = wide(load, BX, q).astype(F32)
    dy = wide(load, BY, q).astype(F32)
    pair, shift = pair_of(q)
    dexp = mm(pair, pair_expand(shift))
    logs = (-dexp * ratex).astype(BF)
    rexp = mm(tri, logs)
    b["rcol"][q] = mm(tri, (-mm(pair, pair_merge(shift)) * rate).astype(BF))
    total = jnp.sum(logs.astype(F32), axis=0, keepdims=True)
    er = jnp.exp2(rexp)
    tail = jnp.exp2(jnp.minimum(total - rexp, 0.0))
    xs = (x * dexp).astype(BF)
    xt = (xs.astype(F32) * tail).astype(BF)
    ed = (er * dy).astype(BF)
    b["er"][q] = er
    b["tail"][q] = tail
    b["xs"][q] = xs
    b["xt"][q] = xt
    b["ed"][q] = ed
    b["fresh"][q] = mm_tn(load(BB, q), xt)
    b["back"][q] = mm_tn(load(BC, q), ed)
    rows = jnp.broadcast_to(total, (8, INNER))
    b["eR"][q] = jnp.exp2(rows)
    b["RC"][...] += rows


def pack_states(b):
    e = [b["eR"][q][:1] for q in range(CHUNKS)]
    end = b["fresh"][0]
    for q in range(1, CHUNKS):
        end = end * e[q] + b["fresh"][q]
    first = b["back"][CHUNKS - 1]
    for q in range(CHUNKS - 2, -1, -1):
        first = first * e[q] + b["back"][q]
    rc = b["RC"][...]
    hi = rc.astype(BF).astype(F32)
    logs = jnp.concatenate([hi, rc - hi], axis=0).astype(BF)
    pieces = [v.reshape(SEQ, PIECE, INNER) for v in (end, first)]
    b["st"][:, pl.ds(0, 2 * PIECE), :] = jnp.concatenate(pieces, axis=1).astype(BF)
    for k in range(SEQ):
        b["st"][k, pl.ds(2 * PIECE, 2 * PIECE)] = logs


def chain_states(b):
    own = [b["sx"][k, pl.ds(0, 2 * PIECE)].astype(F32) for k in range(SEQ)]
    logs = [b["sx"][k, pl.ds(2 * PIECE, 2 * PIECE)].astype(F32) for k in range(SEQ)]
    decay = [jnp.exp2(v[:PIECE] + v[PIECE:]) for v in logs]
    state = [jnp.zeros((PIECE, INNER), F32)]
    grad = [jnp.zeros((PIECE, INNER), F32)]
    for k in range(SEQ - 1):
        state.append(state[k] * decay[k] + own[k][:PIECE])
        n = SEQ - 1 - k
        grad.append(grad[k] * decay[n] + own[n][PIECE:])
    for k in range(SEQ):
        b["sy"][k] = jnp.concatenate([state[k], grad[SEQ - 1 - k]], axis=0).astype(BF)


def entering_states(b):
    both = b["sz"][...].astype(F32)
    b["sin"][...] = both[:, :PIECE, :].reshape(STATE, INNER)
    grad = both[:, PIECE:, :].reshape(STATE, INNER)
    for q in range(CHUNKS - 1, -1, -1):
        b["gin"][q] = grad
        if q > 0:
            grad = grad * b["eR"][q][:1] + b["back"][q]


def head_rows(h):
    one = jnp.where((iota((16, INNER), 1) >> 6) == h, 1.0, 0.0).astype(BF)
    return jnp.concatenate([one] * (CHUNK // 16), axis=0)


def inside(b, tri, load, q):
    dy = wide(load, BY, q)
    bmat = load(BB, q)
    cmat = load(BC, q)
    xs = b["xs"][q]
    trif = tri.astype(F32)
    scores = mm_nt(cmat, bmat) * trif
    rcol = b["rcol"][q]
    rrow = rcol.T
    pairs = None
    ms, dys, xss = [], [], []
    for h in range(HEADS):
        decay = jnp.exp2(jnp.minimum(rcol[:, h : h + 1] - rrow[h : h + 1, :], 0.0))
        ms.append((decay * scores).astype(BF))
        mask = head_rows(h)
        dys.append(dy * mask)
        xss.append(xs * mask)
        term = decay * mm_nt(dys[h], xs)
        pairs = term if h == 0 else pairs + term
    dy4 = jnp.concatenate(dys, axis=0)
    y = mm(jnp.concatenate(ms, axis=1), jnp.concatenate(xss, axis=0))
    dxs = mm_tn(jnp.concatenate(ms, axis=0), dy4)
    pairs = (pairs * trif).astype(BF)
    b["y"][q] = y
    b["dx"][q] = dxs
    b["dbc"][q, :, pl.ds(0, STATE)] = mm_tn(pairs, cmat)
    b["dbc"][q, :, pl.ds(STATE, STATE)] = mm(pairs, bmat)


def outside(b, tri, tri_up, load, pair_of, rate, q, put):
    x = wide(load, BX, q).astype(F32)
    dy = wide(load, BY, q).astype(F32)
    bmat = load(BB, q)
    cmat = load(BC, q)
    pair, shift = pair_of(q)
    dexp = mm(pair, pair_expand(shift))
    xs = b["xs"][q].astype(F32)
    state = b["sin"][...]
    grad = b["gin"][q]
    state_b, grad_b = state.astype(BF), grad.astype(BF)
    sums = head_sum()
    y = b["y"][q] + b["er"][q] * mm(cmat, state_b)
    inner = b["dx"][q]
    outer = b["tail"][q] * mm(bmat, grad_b)
    dxs = inner + outer
    db = b["dbc"][q, :, pl.ds(0, STATE)] + mm_nt(b["xt"][q], grad_b)
    dc = b["dbc"][q, :, pl.ds(STATE, STATE)] + mm_nt(b["ed"][q], state_b)

    def by_head(v):
        return mm(v.astype(BF), sums)

    late = by_head(dy * y - xs * inner).astype(BF)
    early = by_head(xs * outer).astype(BF)
    decayed = b["eR"][q][:1] * state
    across = jnp.sum(decayed * grad, axis=0, keepdims=True)
    across = mm(jnp.broadcast_to(across, (16, INNER)).astype(BF), sums)[:1]
    dl = mm(tri_up, late) + mm(tri, early) - early.astype(F32) + across
    ddelta = by_head(x * dxs) - rate * dl
    b["sin"][...] = decayed + b["fresh"][q]
    put(q, y, dexp * dxs, db, dc, ddelta)


def kernel(tok_hbm, cot_hbm, pm, ps, pt, bias_s, rate_s, skip_s, gated_o, ig_o, gm_o, gsh_o, gst_o, m):
    seq, mp = lax.axis_index("seq"), lax.axis_index("mp")
    core = lax.rem(mp, 2)
    chip = mp // 2
    partner = mp + 1 - 2 * core
    plane, line = seq // 4, lax.rem(seq, 4)
    low = lax.rem(seq, 2)

    load_tok = pltpu.make_async_copy(tok_hbm, m["tok3"], m["s_local"].at[0])
    load_cot = pltpu.make_async_copy(cot_hbm, m["cot"], m["s_local"].at[1])
    load_tok.start()
    load_cot.start()

    barrier = pltpu.get_barrier_semaphore()

    def greet_seq(d):
        pl.semaphore_signal(
            barrier, inc=1, device_id={"seq": lax.rem(seq + d, SEQ)}, device_id_type=MESH
        )

    def greet_mp(d):
        pl.semaphore_signal(barrier, inc=1, device_id={"mp": lax.rem(mp + d, MP)}, device_id_type=MESH)

    fori(1, SEQ, greet_seq)
    fori(1, MP, greet_mp)

    wa, wb, swp = m["wa"], m["wb"], m["swp"]
    wa[plane, line, :, pl.ds(0, 256)] = pm[:, 0, :]
    wb[plane, line, :, pl.ds(0, 256)] = pm[:, 1, :]
    wa[plane, line, :, pl.ds(256, 128)] = ps[:, 0, :]
    wb[plane, line, :, pl.ds(256, 128)] = ps[:, 1, :]
    at, lane = iota((SHARD, LANES), 0), iota((SHARD, LANES), 1)
    place = jnp.where(lane == at + SHARD * low, 1.0, 0.0).astype(BF)
    shifted = mm(pt[...], place).astype(BF)
    swp[...] = jnp.concatenate([shifted, shifted, jnp.zeros((8, LANES), BF)], axis=0)
    pl.semaphore_wait(barrier, SEQ + MP - 2)

    most = pl.ds(0, SEQ - 1)

    def along_x(k):
        return 4 * k + line

    def along_y(k):
        return 4 * plane + k

    half = SHARD // 2
    ring_a1 = Ring(plane, along_x, lambda k: wa.at[k, line], lambda k, n: wa.at[k, line, pl.ds(half * n, half)], m["s_w"].at[0])
    ring_b1 = Ring(line, along_y, lambda k: wb.at[plane, k], lambda k, n: wb.at[plane, k, pl.ds(half * n, half)], m["s_w"].at[1])
    ring_a2 = Ring(line, along_y, lambda k: wa.at[:, k], lambda k, n: wa.at[pl.ds(2 * n, 2), k], m["s_w"].at[2])
    ring_b2 = Ring(plane, along_x, lambda k: wb.at[k], lambda k, n: wb.at[k, pl.ds(2 * n, 2)], m["s_w"].at[3])
    rings = (ring_a1, ring_b1, ring_a2, ring_b2)
    ring_a1.start()
    ring_b1.start()
    send_sw = SeqExchange(lambda p: swp, lambda k: m["sw_rx"].at[k], m["sw_rx"].at[most], sems(m["s_sw"]))
    send_sw.start()
    m["sw_rx"][seq] = swp[...]

    def flip(q):
        m["tokt"][:, pl.ds(q * CHUNK, CHUNK)] = m["tok3"][pl.ds(4 * q, 4)].reshape(CHUNK, DM).T

    load_tok.wait()
    flip(0)
    ring_a1.forward()
    ring_b1.forward()
    ring_a1.finish()
    ring_a2.start()
    ring_b1.finish()
    ring_b2.start()

    i, j = iota((CHUNK, CHUNK), 0), iota((CHUNK, CHUNK), 1)
    m["tri"][0] = jnp.where(i >= j, 1.0, 0.0).astype(BF)
    it, jt = (i & 15) * 16 + (i >> 4), (j & 15) * 16 + (j >> 4)
    m["tri"][1] = jnp.where(it >= jt, 1.0, 0.0).astype(BF)
    m["tri"][2] = jnp.where(i <= j, 1.0, 0.0).astype(BF)
    m["tri"][3] = jnp.where(it <= jt, 1.0, 0.0).astype(BF)
    m["sw"][...] = jnp.zeros((LANES, DM), BF)
    m["R"]["RC"][...] = jnp.zeros((8, INNER), F32)
    m["T"]["RC"][...] = jnp.zeros((8, INNER), F32)
    m["lacc"][...] = jnp.zeros((CHUNK, LANES), F32)

    head_l = iota((1, LANES), 1)
    head_c = iota((1, INNER), 1) >> 6

    def lanes_of(value):
        v = jnp.zeros((1, LANES), F32)
        for h in range(HEADS):
            v = jnp.where((head_l < 8) & ((head_l & 3) == h), value(h), v)
        return v

    def features_of(value):
        v = jnp.zeros((1, INNER), F32)
        for h in range(HEADS):
            v = jnp.where(head_c == h, value(h), v)
        return v

    bias = lanes_of(lambda h: bias_s[h])
    rate_r, rate_t = lanes_of(lambda h: rate_s[0, h]), lanes_of(lambda h: rate_s[1, h])
    ratex_r = features_of(lambda h: rate_s[0, h]) * LOG2E
    ratex_t = features_of(lambda h: rate_s[1, h]) * LOG2E
    skip = features_of(lambda h: skip_s[h])

    load_cot.wait()
    flip(1)
    ring_a2.forward()
    ring_b2.forward()
    flip(2)
    flip(3)
    ring_a2.finish()
    ring_b2.finish()
    send_sw.wait_recv()
    for k in range(SEQ // 2):
        m["sw"][pl.ds(0, 16), pl.ds(k * LANES, LANES)] = m["sw_rx"][2 * k] + m["sw_rx"][2 * k + 1]

    def rows_of(q):
        return pl.ds(pl.multiple_of(q * CHUNK, CHUNK), CHUNK)

    def columns(ref, at, width):
        return ref[:, :, :, pl.ds(at, width)].reshape(DM, width)

    def rest(v):
        return v.reshape(4, WID, LANES)

    send_pay = SeqExchange(lambda p: m["pay"].at[p], lambda k: m["trx"].at[k], m["trx"].at[most], sems(m["s_pay"]))
    quarter = pl.ds(pl.multiple_of(chip * COLS, COLS), COLS)
    bcr, bct = m["bcr"], m["bct"]
    send_bc = SeqExchange(
        lambda p: bcr.at[core, p, quarter],
        lambda k: bct.at[core, k, quarter],
        bct.at[core, most, quarter],
        sems(m["s_bc"]),
    )

    def piece_of(ref, k):
        return ref.at[lax.rem(k, 2), :, pl.ds(pl.multiple_of(k // 2 * COLS, COLS), COLS)]

    send_bm = MpExchange(lambda p: piece_of(bct, mp), lambda k: piece_of(bct, k), sems(m["s_bm"]))
    m["wx"][:, pl.ds(0, LANES)] = jnp.where(core == 0, columns(wa, 256, 128), columns(wb, 256, 128))
    m["wx"][:, pl.ds(LANES, LANES)] = m["sw"][...].T

    def start_four(exchange, q):
        def one(n):
            d = lax.rem(4 * q + n - seq + SEQ, SEQ)

            @pl.when(d != 0)
            def _():
                exchange.copy(d).start()

        fori(0, 4, one)

    def far_first(n):
        step = jnp.where(n == 0, 2, jnp.where(n == 3, 0, 2 * n - 1))
        return lax.rem(plane + step, 4)

    def project_shared(n):
        q = far_first(n)
        u = m["tok3"][pl.ds(4 * q, 4)].reshape(CHUNK, DM)
        w = jnp.concatenate([columns(wa, 256, 128), columns(wb, 256, 128)], axis=1)
        v = mm(u, w).astype(BF)
        bcr[0, pl.ds(4 * q, 4)] = rest(v[:, :LANES])
        bcr[1, pl.ds(4 * q, 4)] = rest(v[:, LANES:])
        start_four(send_bc, q)

    def project(n):
        q = far_first(n)
        rows = rows_of(q)
        u = m["tok3"][pl.ds(4 * q, 4)].reshape(CHUNK, DM)
        four = pl.ds(4 * q, 4)

        def put(block, v):
            v = v.astype(BF)
            for k in range(v.shape[1] // LANES):
                m["pay"][four, pl.ds((block + k) * WID, WID), :] = rest(v[:, k * LANES : (k + 1) * LANES])

        z = mm(u, columns(wb, 0, 256)).astype(BF)
        m["z"][rows, :] = z
        zf = z.astype(F32)
        gate = zf * jax.nn.sigmoid(zf)
        put(BY, m["cot"][rows, :].astype(F32) * gate)
        put(BX, mm(u, columns(wa, 0, 256)))
        raw = mm(u, m["wx"][:, pl.ds(LANES, LANES)]) + bias
        m["sraw"][rows, :] = raw
        pair = as_pair(jnp.maximum(raw, 0.0) + jnp.log1p(jnp.exp(-jnp.abs(raw))))
        m["lp"][rows, :] = pair
        folded = jnp.zeros((64, LANES), F32)
        for g in range(4):
            part = rest(pair)[:, g * COLS : (g + 1) * COLS, :].reshape(64, LANES)
            folded += mm(part, pair_place(8 * g))
        m["pay"][four, pl.ds(ROWS_L, COLS), :] = folded.astype(BF).reshape(4, COLS, LANES)
        start_four(send_pay, q)

    fori(0, CHUNKS, project_shared)
    fori(0, CHUNKS, project)
    m["trx"][seq] = m["pay"][seq]
    bct[core, seq, quarter] = bcr[core, seq, quarter]

    def load_r(block, q):
        if block >= BB:
            return bcr[block - BB, pl.ds(4 * q, 4)].reshape(CHUNK, LANES)
        return m["pay"][pl.ds(4 * q, 4), pl.ds(block * WID, WID), :].reshape(CHUNK, LANES)

    def pair_r(q):
        return m["lp"][rows_of(q), :], 0

    def cols_of(block, q):
        return pl.ds(pl.multiple_of(block * WID + q * COLS, COLS), COLS)

    def load_t(block, q):
        if block >= BB:
            return bct[block - BB, :, pl.ds(q * COLS, COLS), :].reshape(CHUNK, LANES)
        return m["trx"][:, cols_of(block, q), :].reshape(CHUNK, LANES)

    def pair_t(q):
        return m["trx"][:, pl.ds(ROWS_L, COLS), :].reshape(CHUNK, LANES), 8 * q

    def pieces_exchange(source, landing, sem):
        return SeqExchange(lambda p: source.at[p], lambda k: landing.at[k], landing.at[most], sems(sem))

    r, t = m["R"], m["T"]
    tri_r, tri_t, up_r, up_t = (m["tri"].at[k] for k in range(4))

    def chunks(low, high, step):
        for q in range(low, high):
            step(q)


    def start_pieces(b, sem):
        e = pieces_exchange(b["st"], b["sx"], sem)
        e.start()
        b["sx"][seq] = b["st"][seq]
        return e

    def start_entering(b, sem):
        chain_states(b)
        e = pieces_exchange(b["sy"], b["sz"], sem)
        e.start()
        b["sz"][seq] = b["sy"][seq]
        return e

    chunks(0, CHUNKS, lambda q: summary(r, tri_r[...], load_r, pair_r, rate_r * LOG2E, ratex_r, q))
    pack_states(r)
    send_bc.wait_recv()
    send_bm.start()
    chunks(0, 2, lambda q: inside(r, tri_r[...], load_r, q))
    def gates(q):
        rows = rows_of(q)
        z = m["z"][rows, :].astype(F32)
        sigma = jax.nn.sigmoid(z)
        m["gate"][rows, :] = z * sigma
        m["slope"][rows, :] = m["cot"][rows, :].astype(F32) * sigma * (1.0 + z * (1.0 - sigma))
        m["sraw"][rows, :] = jax.nn.sigmoid(m["sraw"][rows, :])

    chunks(0, CHUNKS, gates)
    send_sw.wait_send()
    for e in rings:
        e.wait_send()

    send_pay.wait_recv()
    send_sr = start_pieces(r, m["s_sr"])
    send_bm.wait_recv()
    chunks(0, CHUNKS, lambda q: summary(t, tri_t[...], load_t, pair_t, rate_t * LOG2E, ratex_t, q))
    pack_states(t)
    send_st = start_pieces(t, m["s_st"])
    send_sr.wait_recv()
    send_ur = start_entering(r, m["s_ur"])
    chunks(0, 2, lambda q: inside(t, tri_t[...], load_t, q))
    chunks(2, 3, lambda q: inside(r, tri_r[...], load_r, q))
    send_st.wait_recv()
    send_ut = start_entering(t, m["s_ut"])
    chunks(2, CHUNKS, lambda q: inside(t, tri_t[...], load_t, q))
    chunks(3, CHUNKS, lambda q: inside(r, tri_r[...], load_r, q))
    send_ut.wait_recv()
    entering_states(t)

    def put_t(q, y, dx, db, dc, dd):
        def put(block, v):
            v = v.astype(BF)
            for k in range(v.shape[1] // LANES):
                part = v[:, k * LANES : (k + 1) * LANES]
                at = 128 * (q // 2) + 32 * (block + k) + COLS * (q % 2)
                m["bpay"][:, pl.ds(at, COLS), :] = part.reshape(SEQ, COLS, LANES)

        put(BX, y)
        put(BY, dx)
        m["tdb"][0, q] = db.astype(BF)
        m["tdb"][1, q] = dc.astype(BF)
        for n in range(2):
            d = lax.rem(2 * q + n - mp + MP, MP)

            @pl.when(d != 0)
            def _():
                send_tr.copy(d).start()

        m["lacc"][...] += mm(as_pair(dd), pair_place(8 * q))

    def half_back(at, count, sem):
        rows = pl.ds(at, count)
        return SeqExchange(
            lambda p: m["bpay"].at[p, rows], lambda k: m["brx"].at[k, rows], m["brx"].at[most, rows], sems(sem)
        )

    send_back = half_back(0, 128, m["s_back"])
    send_back2 = half_back(128, 144, m["s_back2"])
    send_tr = MpExchange(
        lambda p: m["tdb"].at[lax.rem(p, 2), p // 2], lambda k: m["trs"].at[k], sems(m["s_tr"])
    )
    send_bp = SeqExchange(lambda p: m["tpiece"].at[p], lambda k: m["rpiece"].at[k], m["rpiece"].at[most], sems(m["s_bp"]))
    send_rr = MpExchange(lambda p: piece_of(m["rdb"], p), lambda k: m["rrs"].at[k], sems(m["s_rr"]))

    def group_total(ref):
        v = ref[0].astype(F32)
        for k in range(1, MP):
            v += ref[k].astype(F32)
        return v

    chunks(0, 2, lambda q: outside(t, tri_t[...], up_t[...], load_t, pair_t, rate_t, q, put_t))
    send_back.start()
    chunks(2, 4, lambda q: outside(t, tri_t[...], up_t[...], load_t, pair_t, rate_t, q, put_t))
    m["bpay"][:, pl.ds(ROWS_L, COLS), :] = m["lacc"][...].astype(BF).reshape(SEQ, COLS, LANES)
    send_back2.start()
    m["brx"][seq] = m["bpay"][seq]
    m["trs"][mp] = m["tdb"][core, chip]

    send_ur.wait_recv()
    entering_states(r)

    def put_r(q, y, dx, db, dc, dd):
        rows = rows_of(q)
        r["y"][q] = y + skip * wide(load_r, BX, q).astype(F32)
        r["dx"][q] = dx + skip * wide(load_r, BY, q).astype(F32)
        m["rdb"][0, pl.ds(4 * q, 4)] = rest(db.astype(BF))
        m["rdb"][1, pl.ds(4 * q, 4)] = rest(dc.astype(BF))
        r["dd"][q] = dd

    def outside_r(q):
        outside(r, tri_r[...], up_r[...], load_r, pair_r, rate_r, q, put_r)

    chunks(0, 1, outside_r)
    send_tr.wait_recv()
    m["tpiece"][...] = group_total(m["trs"]).astype(BF).reshape(SEQ, COLS, LANES)
    send_bp.start()
    m["rpiece"][seq] = m["tpiece"][seq]
    chunks(1, CHUNKS, outside_r)
    send_rr.start()
    m["rrs"][mp] = m["rdb"][core, :, quarter]
    for e in (send_pay, send_bc, send_bm, send_sr, send_ur, send_st, send_ut):
        e.wait_send()
    send_back.wait_recv()
    send_back2.wait_recv()
    send_bp.wait_recv()
    send_rr.wait_recv()
    m["dpiece"][...] = (group_total(m["rrs"]) + m["rpiece"][...].astype(F32)).astype(BF)

    def back(block, q):
        parts = [m["brx"][pl.ds(4 * q, 4), pl.ds(128 * n + 32 * block, 32), :] for n in range(2)]
        return jnp.concatenate(parts, axis=1).reshape(CHUNK, LANES)

    def combine(q):
        rows = rows_of(q)
        y = r["y"][q] + wide(back, BX, q).astype(F32)
        gated_o[rows, :] = (y * m["gate"][rows, :]).astype(BF)
        m["g"][rows, pl.ds(256, 256)] = (y * m["slope"][rows, :]).astype(BF)
        m["g"][rows, pl.ds(0, 256)] = (r["dx"][q] + wide(back, BY, q).astype(F32)).astype(BF)
        folded = m["brx"][pl.ds(4 * q, 4), pl.ds(ROWS_L, COLS), :].reshape(64, LANES)
        parts = [mm(folded, pair_merge(8 * g)).reshape(4, COLS, LANES) for g in range(4)]
        dd = r["dd"][q] + jnp.concatenate(parts, axis=1).reshape(CHUNK, LANES)
        dstep = dd * m["sraw"][rows, :]
        m["g"][rows, pl.ds(640, LANES)] = jnp.where(iota((CHUNK, LANES), 1) < HEADS, dstep, 0.0).astype(BF)

    def pair_copy(k, q):
        rows = rows_of(q)
        return mp_copy(
            m["ip"].at[2 * k + 1 - core, rows],
            m["prx"].at[k, rows],
            m["s_pair"].at[0, k, q],
            m["s_pair"].at[1, k, q],
            partner,
        )

    def z_ring(n):
        def part(k, h):
            return m["zs"].at[k, pl.ds(CHUNK * (2 * n + h), CHUNK)]

        return RingSum(
            chip,
            lambda k: {"mp": 2 * k + core},
            part,
            lambda h: m["z_raw"].at[n, h],
            lambda side, h: m["z_near"].at[n, side, pl.ds(CHUNK * h, CHUNK)],
            m["s_z"].at[n],
        )

    z_rings = [z_ring(0), z_ring(1)]

    def pair_sum(k, q):
        rows = rows_of(q)
        pair_copy(k, q).wait_recv()
        return (m["ip"][2 * k + core, rows, :].astype(F32) + m["prx"][k, rows, :].astype(F32)).astype(BF)

    def pass_on(q):
        for k in range(4):
            m["zs"][k, rows_of(q), :] = pair_sum(k, q)

    def z_start(n):
        z_rings[n].start_far()
        z_rings[n].start_near()

    def z_finish(n):
        for h, v in enumerate(z_rings[n].finish()):
            ig_o[rows_of(2 * n + h), :] = v.astype(BF)

    def combine_all(q):
        combine(q)
        rows = rows_of(q)
        piece = m["dpiece"][pl.ds(4 * q, 4)]
        here = (iota((4, WID, LANES), 1) >> 4) == chip
        piece = jnp.where(here, jnp.concatenate([piece] * 4, axis=1), jnp.zeros((), BF)).reshape(CHUNK, LANES)
        m["g"][rows, pl.ds(512, LANES)] = piece

    def input_part(q):
        rows = rows_of(q)
        g = m["g"][rows, :]
        for c in range(4):
            cols = pl.ds(c * 256, 256)
            v = mm_nt(g[:, :256], wa[c, :, :, pl.ds(0, 256)].reshape(256, 256))
            v += mm_nt(g[:, 256:512], wb[c, :, :, pl.ds(0, 256)].reshape(256, 256))
            v += mm_nt(g[:, 512:], m["wx"][cols, :])
            v = v.astype(BF)
            m["ip"][2 * c, rows, :] = v[:, :LANES]
            m["ip"][2 * c + 1, rows, :] = v[:, LANES:]
        fori(0, 4, lambda k: pair_copy(k, q).start())

    chunks(0, CHUNKS, combine_all)

    def g_ring(n):
        rows = pl.ds(32 * n, 32)

        def part(k, h):
            two = pl.ds(2 * h, 2)
            return m["gp"].at[k, two, rows] if n == 0 else m["gp"].at[two, k, rows]

        return RingSum(
            plane if n == 0 else line,
            lambda k: {"seq": along_x(k) if n == 0 else along_y(k)},
            part,
            lambda h: m["g_raw"].at[n, h],
            lambda side, h: m["g_near"].at[n, side, pl.ds(2 * h, 2)],
            m["s_gp"].at[n],
        )

    def h_ring(n):
        return RingSum(
            line if n == 0 else plane,
            lambda k: {"seq": along_y(k) if n == 0 else along_x(k)},
            lambda k, h: m["h_own"].at[n, k, pl.ds(16 * h, 16)],
            lambda h: m["h_raw"].at[n, h],
            lambda side, h: m["h_near"].at[n, side, pl.ds(16 * h, 16)],
            m["s_gp"].at[2 + n],
        )

    g_rings, h_rings = [g_ring(0), g_ring(1)], [h_ring(0), h_ring(1)]
    send_gs = SeqExchange(lambda p: m["gs"].at[p // 2], lambda k: m["gs_rx"].at[k], m["gs_rx"].at[most], sems(m["s_gs"]))

    def grads(n):
        k = lax.rem(plane + n, 4)
        cols = rows_of(k)
        v = mm(m["tokt"][cols, :], m["g"][...])
        m["gp"][k] = v[:, :640].astype(BF).reshape(4, SHARD, 640)
        gs = v[:, 640:].T[:16].astype(BF)
        m["gs"][2 * k] = gs[:, :LANES]
        m["gs"][2 * k + 1] = gs[:, LANES:]
        start_four(send_gs, k)

    grads(2)
    g_rings[0].start_far()
    grads(1)
    grads(3)
    g_rings[0].start_near()
    grads(0)
    g_rings[1].start_far()
    g_rings[1].start_near()
    m["gs_rx"][seq] = m["gs"][seq // 2]
    input_part(0)
    input_part(1)
    g_rings[0].middle()
    g_rings[1].middle()
    input_part(2)
    pass_on(0)
    pass_on(1)
    z_start(0)
    input_part(3)
    for e in (send_back, send_back2, send_tr, send_bp, send_rr, send_gs):
        e.wait_send()
    pass_on(2)
    pass_on(3)
    z_start(1)

    def g_next(n):
        for h, v in enumerate(g_rings[n].finish()):
            m["h_own"][n, pl.ds(2 * h, 2)] = v.astype(BF).reshape(2, 32, 640)
        h_rings[n].start_far()
        h_rings[n].start_near()

    g_next(0)
    g_next(1)
    z_rings[0].middle()
    h_rings[0].middle()
    h_rings[1].middle()
    z_rings[1].middle()

    def total_of(ref):
        v = ref[0].astype(F32)
        for k in range(1, SEQ):
            v += ref[k].astype(F32)
        return v

    main = jnp.concatenate(h_rings[0].finish() + h_rings[1].finish(), axis=0)
    m["fsh"][...] = main[:, 512:]
    send_fin = MpExchange(lambda p: m["fsh"], lambda k: m["frx"].at[k], sems(m["s_fin"]))
    send_fin.start()
    m["frx"][mp] = main[:, 512:]
    gm_o[:, 0, :] = main[:, :INNER]
    gm_o[:, 1, :] = main[:, INNER : 2 * INNER]
    send_gs.wait_recv()
    step = total_of(m["gs_rx"])
    gst_o[...] = jnp.where(low == 0, step[:HEADS, :SHARD], step[:HEADS, SHARD:])
    z_finish(0)
    z_finish(1)
    send_fin.wait_recv()
    for n in range(2):
        gsh_o[:, n, :] = m["frx"][n] + m["frx"][2 + n] + m["frx"][4 + n] + m["frx"][6 + n]

    sent = [send_fin] + z_rings + g_rings + h_rings
    for e in sent:
        e.wait_send()
    for q in range(CHUNKS):
        fori(0, 4, lambda k: pair_copy(k, q).wait_send())


def hand_over(*refs):
    n = len(refs) // 2
    for k in range(n):
        refs[n + k][...] = refs[k][...]


def body(tokens, proj_main, proj_shared, proj_step, step_bias, decay_rate, skip_gain, cotangent):
    vm = pl.BlockSpec(memory_space=pltpu.VMEM)
    sm = pl.BlockSpec(memory_space=pltpu.SMEM)
    hbm = pl.BlockSpec(memory_space=pl.ANY)
    shapes = (
        jax.ShapeDtypeStruct((TOK, INNER), BF),
        jax.ShapeDtypeStruct((TOK, LANES), BF),
        jax.ShapeDtypeStruct((SHARD, 2, INNER), F32),
        jax.ShapeDtypeStruct((SHARD, 2, STATE), F32),
        jax.ShapeDtypeStruct((HEADS, SHARD), F32),
    )
    results = pl.pallas_call(
        kernel,
        out_shape=shapes,
        in_specs=[hbm, hbm, vm, vm, vm, sm, sm, sm],
        out_specs=(vm,) * 5,
        scratch_shapes=[main_scratch()],
        compiler_params=pltpu.CompilerParams(
            collective_id=0, has_side_effects=True, vmem_limit_bytes=62 * 1024 * 1024
        ),
    )(
        tokens.reshape(SEQ, WID, DM),
        cotangent.reshape(TOK, INNER),
        proj_main,
        proj_shared,
        proj_step.T,
        step_bias,
        decay_rate,
        skip_gain,
    )
    gated, ig, gm, gsh, gst = pl.pallas_call(
        hand_over,
        out_shape=shapes,
        in_specs=[vm] * 5,
        out_specs=(vm,) * 5,
    )(*results)
    return (
        gated.reshape(1, 16, WID, INNER),
        ig.reshape(1, 16, WID, LANES),
        gm,
        gsh,
        gst.T,
    )


def solution(mesh):
    placed = (
        P("seq", None, None, None),
        P("seq", None, "mp"),
        P("seq", None, None),
        P("seq", "mp"),
        P("mp"),
        P(None, "mp"),
        P("mp"),
        P("seq", None, None, "mp"),
    )
    return jax.shard_map(
        body,
        mesh=mesh,
        in_specs=placed,
        out_specs=(
            P("seq", None, None, "mp"),
            P("seq", None, None, "mp"),
            P("seq", None, "mp"),
            P("seq", None, None),
            P("seq", "mp"),
        ),
        check_vma=False,
    )
```
